128 devices in a mesh: region: 8 (over y, core), dev: 16 (over z, x).
Axes of the slice: x: 4, y: 4, z: 4, core: 2. Of those that a mesh axis runs over, the one named last changes fastest.
Arguments:
- positions: float32 [3, 8192, 256], P(None, ('region', 'dev')), may hold values from 0 to 1
- velocity: float32 [3, 8192, 256], P(None, ('region', 'dev')), may hold values from -6 to 6
- smoothing: float32 [8192, 256], P(('region', 'dev')), may hold values from 0.25 to 0.5
- masses: float32 [8192, 256], P(('region', 'dev')), may hold values from 0.004 to 0.016
- energy: float32 [8192, 256], P(('region', 'dev')), may hold values from 0.5 to 2
- occupancy: int32 [8192], P(('region', 'dev')), may hold values from 128 to 256
- active: int32 [8192, 256], P(('region', 'dev')), may hold values 0 or 1
- send_cells: int32 [128, 16, 16], P(('region', 'dev')), may hold values from 0 to 63
- send_fill: int32 [128, 16], P(('region', 'dev')), may hold values from 0 to 16, as said below
- pair_cell: int32 [128, 16, 16], P(('region', 'dev')), may hold values from 0 to 63
Outputs:
- density: float32 [8192, 256], P(('region', 'dev'))
- forces: float32 [4, 8192, 256], P(None, ('region', 'dev'))
The draws below stay inside these ranges and needn't reach their ends.
Inputs may be any that keep to these rules, and one draw needn't show every extreme that they name: `send_fill`: entry [d, j] is how many leading slots of device d's list for the device at index j of its region hold cells; it is 0 for d's own index, and in every region some device receives 16 cells from every other device of the region. Slots beyond it are ignored.
All inputs are finite; a program needn't handle non-finite values. No bound on the sum of `active` on one device may be relied on, other than what follows from the above.
Results may differ from the reference program's by a relative error of at most 0.0003.
Values sent between devices are 32-bit elements; how exact they have to be, the bound alone decides.
No kernel may reach another device: no remote copies, remote signals or barrier semaphores. Data moves between devices by JAX's collectives and lax.ppermute only.
A program may use at most 64 MiB of HBM per device.

```python
import math
import jax
import jax.numpy as jnp
from jax import lax

P_SIZE = 256
CELLS_DEV = 64
SLOTS = 16
FACE = 4
CELLS = 8192
N_REGION = 8
N_DEV = 16
DEVICES = 128


def draw_send_fill(key, part):
    key = jax.random.fold_in(key, 7)
    key_hot, key_base = jax.random.split(key)
    offset_table = jax.random.randint(key_hot, (N_REGION, 1), 0, 8)
    dest_ids = jnp.arange(N_DEV, dtype=jnp.int32)[None, :]
    hot_dest = (dest_ids + offset_table) % 8 == 0
    hot_rows = jnp.repeat(hot_dest, N_DEV, axis=0)
    base_fill = jax.random.randint(key_base, (DEVICES, N_DEV), 1, max(SLOTS // 4, 1) + 1)
    filled = jnp.where(hot_rows, SLOTS, base_fill)
    own_index = (jnp.arange(DEVICES, dtype=jnp.int32) % N_DEV)[:, None] == dest_ids
    return jnp.where(own_index, 0, filled).astype(jnp.int32)


def with_ends(drawn, rng, least, high):
    longest = drawn.shape.index(max(drawn.shape))
    spots = []
    for shift in (0, 1):
        where = [jax.random.randint(jax.random.fold_in(rng, axis), (), 0, length) for axis, length in enumerate(drawn.shape)]
        where[longest] = (where[longest] + shift) % drawn.shape[longest]
        spots.append(tuple(where))
    return drawn.at[spots[0]].set(least).at[spots[1]].set(high)


def levels(stream_key, shape, pieces, smallest, largest):
    gain, own = 1.0, jax.random.fold_in(stream_key, 6)
    for position, shards_of in pieces:
        draws = jnp.exp(jax.random.uniform(jax.random.fold_in(own, position), (shards_of,), jnp.float32, smallest / len(pieces), largest / len(pieces)))
        gain = gain * jnp.repeat(draws, shape[position] // shards_of).reshape([-1 if axis == position else 1 for axis in range(len(shape))])
    return gain


def normal_values(own_key, dims, scale, bound, pieces=(), kind=jnp.bfloat16):
    values = scale * jax.random.normal(own_key, dims, jnp.float32)
    if pieces:
        values = values * levels(own_key, dims, pieces, -0.22, 0.18)
    return jnp.clip(values, -bound, bound).astype(kind)


def setup_inputs(seed: int = 0) -> dict:
    keys = jax.random.split(jax.random.key(seed), 11)
    positions = jnp.clip(1.0 * jax.random.uniform(keys[0], (3, CELLS, P_SIZE), jnp.float32) ** levels(keys[0], (3, CELLS, P_SIZE), ((1, 128),), -0.2, 0.2), 0.0, 1.0)
    velocity = normal_values(keys[1], (3, CELLS, P_SIZE), 1.0, 6.0, ((1, 128),), jnp.float32)
    smoothing = jnp.clip(0.25 + 0.25 * jax.random.uniform(keys[2], (CELLS, P_SIZE), jnp.float32) ** levels(keys[2], (CELLS, P_SIZE), ((0, 128),), -0.2, 0.2), 0.25, 0.5)
    masses = jnp.clip(jnp.exp(math.log(0.016) - 1.3862944 * jax.random.uniform(keys[3], (CELLS, P_SIZE), jnp.float32) ** levels(keys[3], (CELLS, P_SIZE), ((0, 128),), -0.2, 0.2)), 0.004, 0.016)
    energy = jnp.clip(jnp.exp(math.log(2.0) - 1.3862944 * jax.random.uniform(keys[4], (CELLS, P_SIZE), jnp.float32) ** levels(keys[4], (CELLS, P_SIZE), ((0, 128),), -0.2, 0.2)), 0.5, 2.0)
    occupancy = with_ends(jax.random.randint(keys[5], (CELLS,), P_SIZE // 2, P_SIZE + 1), jax.random.fold_in(keys[5], 1), P_SIZE // 2, P_SIZE).astype(jnp.int32)
    active = with_ends((jax.random.randint(keys[6], (CELLS, P_SIZE), 0, 2) < 1).astype(jnp.int32), jax.random.fold_in(keys[6], 1), 0, 1)
    send_cells = with_ends(jax.random.randint(keys[7], (DEVICES, N_DEV, SLOTS), 0, CELLS_DEV), jax.random.fold_in(keys[7], 1), 0, CELLS_DEV - 1).astype(jnp.int32)
    send_fill = draw_send_fill(jax.random.fold_in(keys[10], 71), 0)
    pair_cell = with_ends(jax.random.randint(keys[9], (DEVICES, N_DEV, SLOTS), 0, CELLS_DEV), jax.random.fold_in(keys[9], 1), 0, CELLS_DEV - 1).astype(jnp.int32)
    return {"positions": positions, "velocity": velocity, "smoothing": smoothing, "masses": masses, "energy": energy, "occupancy": occupancy, "active": active, "send_cells": send_cells, "send_fill": send_fill, "pair_cell": pair_cell}


KERNEL_NORM = 21.0 / (2.0 * math.pi)
GAMMA_LESS = 2.0 / 3.0
pair_block = 64

def kernel_terms(first_side, second_side):
    offsets = [first_side[:, axis_id, :, None] - second_side[:, axis_id, None, :] for axis_id in range(3)]
    distance = jnp.sqrt(offsets[0] * offsets[0] + offsets[1] * offsets[1] + offsets[2] * offsets[2])
    support = 0.5 * (first_side[:, 6, :, None] + second_side[:, 6, None, :])
    scaled = distance / support
    remain = jnp.maximum(1.0 - scaled, 0.0)
    return (offsets, support, scaled, remain)

def density_pair(first_side, second_side):
    offsets, support, scaled, remain = kernel_terms(first_side, second_side)
    weight = KERNEL_NORM / (support * support * support) * remain ** 4 * (1.0 + 4.0 * scaled)
    to_first = lax.optimization_barrier(jnp.sum(weight * second_side[:, 7, None, :], axis=2))
    to_second = lax.optimization_barrier(jnp.sum(weight * first_side[:, 7, :, None], axis=1))
    return (to_first, to_second)

def force_pair(first_side, second_side, first_term, second_term):
    offsets, support, scaled, remain = kernel_terms(first_side, second_side)
    slope = -20.0 * KERNEL_NORM / support ** 5 * remain ** 3
    velocity_gap = [first_side[:, 3 + axis_id, :, None] - second_side[:, 3 + axis_id, None, :] for axis_id in range(3)]
    closing = velocity_gap[0] * offsets[0] + velocity_gap[1] * offsets[1] + velocity_gap[2] * offsets[2]
    pushing = (first_term[:, :, None] + second_term[:, None, :]) * slope
    first_mass = first_side[:, 7, :, None]
    second_mass = second_side[:, 7, None, :]
    push_first = pushing * second_mass
    push_second = pushing * first_mass
    acc_first = jnp.stack([-lax.optimization_barrier(jnp.sum(push_first * offsets[axis_id], axis=2)) for axis_id in range(3)], axis=1)
    acc_second = jnp.stack([lax.optimization_barrier(jnp.sum(push_second * offsets[axis_id], axis=1)) for axis_id in range(3)], axis=1)
    heating = closing * slope
    heat_first = first_term * lax.optimization_barrier(jnp.sum(heating * second_mass, axis=2))
    heat_second = second_term * lax.optimization_barrier(jnp.sum(heating * first_mass, axis=1))
    return (jnp.concatenate([acc_first, heat_first[:, None]], axis=1), jnp.concatenate([acc_second, heat_second[:, None]], axis=1))

def reference(positions, velocity, smoothing, masses, energy, occupancy, active, send_cells, send_fill, pair_cell):
    cell_total = smoothing.shape[0]
    slot_width = smoothing.shape[1]
    occupied = (jnp.arange(slot_width, dtype=jnp.int32)[None, :] < occupancy[:, None]).astype(jnp.float32)
    packed = jnp.concatenate([jnp.transpose(positions, (1, 0, 2)), jnp.transpose(velocity, (1, 0, 2)), smoothing[:, None], (masses * occupied)[:, None], energy[:, None]], axis=1)
    per_dev = CELLS_DEV
    self_ids = jnp.arange(cell_total, dtype=jnp.int32)
    near_ids = jnp.arange(DEVICES * (per_dev - 1), dtype=jnp.int32)
    near_first = near_ids // (per_dev - 1) * per_dev + near_ids % (per_dev - 1)
    receiver = jnp.arange(DEVICES, dtype=jnp.int32)[:, None, None]
    source_dev = jnp.arange(N_DEV, dtype=jnp.int32)[None, :, None]
    slot_ids = jnp.arange(SLOTS, dtype=jnp.int32)[None, None, :]
    sender = receiver // N_DEV * N_DEV + source_dev
    far_first = (receiver * per_dev + pair_cell).reshape(-1)
    far_second = (sender * per_dev + send_cells[sender, receiver % N_DEV, slot_ids]).reshape(-1)
    far_valid = (slot_ids < send_fill[sender, receiver % N_DEV]).astype(jnp.int32).reshape(-1)
    device_ids = jnp.arange(DEVICES, dtype=jnp.int32)[:, None]
    face_ids = jnp.arange(FACE, dtype=jnp.int32)[None, :]
    below = (device_ids // N_DEV - 1) % N_REGION * N_DEV + device_ids % N_DEV
    face_first = (device_ids * per_dev + face_ids).reshape(-1)
    face_second = (below * per_dev + per_dev - FACE + face_ids).reshape(-1)
    near_count = near_first.shape[0]
    face_count = face_first.shape[0]
    firsts = jnp.concatenate([self_ids, near_first, far_first, face_first])
    seconds = jnp.concatenate([self_ids, near_first + 1, far_second, face_second])
    live_int = jnp.concatenate([jnp.ones((cell_total,), jnp.int32), jnp.ones((near_count,), jnp.int32), far_valid, jnp.ones((face_count,), jnp.int32)])
    second_gate = jnp.concatenate([jnp.zeros((cell_total,), jnp.int32), jnp.ones((near_count,), jnp.int32), far_valid, jnp.ones((face_count,), jnp.int32)])
    ordering = jnp.argsort(1 - live_int, stable=True)
    firsts = firsts[ordering]
    seconds = seconds[ordering]
    live_int = live_int[ordering]
    second_gate = second_gate[ordering]
    padding = -firsts.shape[0] % pair_block
    firsts = jnp.pad(firsts, (0, padding)).reshape(-1, pair_block)
    seconds = jnp.pad(seconds, (0, padding)).reshape(-1, pair_block)
    first_weight = jnp.pad(live_int, (0, padding)).astype(jnp.float32).reshape(-1, pair_block)
    second_weight = jnp.pad(second_gate, (0, padding)).astype(jnp.float32).reshape(-1, pair_block)
    blocks_all = (firsts, seconds, first_weight, second_weight)

    def density_step(running, block_data):
        first_ids, second_ids, weight_one, weight_two = block_data

        def compute(totals):
            to_first, to_second = density_pair(packed[first_ids], packed[second_ids])
            totals = totals.at[first_ids].add(to_first * weight_one[:, None])
            return totals.at[second_ids].add(to_second * weight_two[:, None])
        return (lax.cond(jnp.max(weight_one) > 0.0, compute, lambda totals: totals, running), None)
    rho_start = jnp.zeros((cell_total, slot_width), jnp.float32)
    density = lax.scan(density_step, rho_start, blocks_all)[0] * occupied
    pterm = jnp.where(occupied > 0.0, GAMMA_LESS * energy / jnp.where(occupied > 0.0, density, 1.0), 0.0)

    def force_step(running, block_data):
        first_ids, second_ids, weight_one, weight_two = block_data

        def compute(totals):
            to_first, to_second = force_pair(packed[first_ids], packed[second_ids], pterm[first_ids], pterm[second_ids])
            totals = totals.at[first_ids].add(to_first * weight_one[:, None, None])
            return totals.at[second_ids].add(to_second * weight_two[:, None, None])
        return (lax.cond(jnp.max(weight_one) > 0.0, compute, lambda totals: totals, running), None)
    force_start = jnp.zeros((cell_total, 4, slot_width), jnp.float32)
    totals_force = lax.scan(force_step, force_start, blocks_all)[0]
    gate = active.astype(jnp.float32) * occupied
    forces = jnp.transpose(totals_force, (1, 0, 2)) * gate[None]
    return (density, forces)
```

```python
import functools
import math

import jax
import jax.numpy as jnp
from jax import lax
from jax.experimental import pallas as pl
from jax.experimental.pallas import tpu as pltpu
from jax.sharding import PartitionSpec as P

BF = jnp.bfloat16
F32 = jnp.float32
FACE = 4
CELLS = 64
WIDTH = 256
PEERS = 16
SLOTS = 16
LISTED = PEERS * SLOTS
GAMMA_LESS = 2.0 / 3.0
W_SCALE = 84.0 / math.pi
G_SCALE = 6720.0 / math.pi
TINY = 1e-14
EMPTY = 1e8
CHUNK = 32
NN = (((1,), (0,)), ((), ()))
NT = (((1,), (1,)), ((), ()))
VM = pl.BlockSpec(memory_space=pltpu.VMEM)
SM = pl.BlockSpec(memory_space=pltpu.SMEM)
ROWS = 5


def params():
    return pltpu.CompilerParams(vmem_limit_bytes=50 * 2**20)


def split2(x):
    a = x.astype(BF)
    return a, (x - a.astype(F32)).astype(BF)


def split3(x):
    a = x.astype(BF).astype(F32)
    rest = x - a
    b = rest.astype(BF).astype(F32)
    return a, b, rest - b


def rows_of(cell):
    x, y, z, h, m = [cell[k : k + 1] for k in range(5)]
    norm = 4.0 * (x * x + y * y + z * z)
    root = lax.rsqrt(jnp.where(m > 0.0, m, 1.0))
    mu = jnp.where(m > 0.0, root * lax.rsqrt(root), EMPTY)
    return x, y, z, h, norm, mu


def first_rows(cell):
    x, y, z, h, norm, mu = rows_of(cell)
    one = jnp.ones_like(x)
    return jnp.concatenate(
        [-8.0 * x, -8.0 * y, -8.0 * z, norm, one, h * h * mu, 2.0 * h * mu, mu], 0
    )


def second_rows(cell):
    x, y, z, h, norm, mu = rows_of(cell)
    one = jnp.ones_like(x)
    return jnp.concatenate([x, y, z, one, norm, mu, h * mu, h * h * mu], 0)


def first_operand(rows):
    a1, a2, a3 = split3(rows)
    return jnp.concatenate([a1, a1, a2, a2, a1, a3, jnp.zeros((80, WIDTH), F32)], 0).T.astype(BF)


def second_operands(rows, both):
    b1, b2, b3 = split3(rows)
    stacked = jnp.concatenate([b1, b2, b1, b2, b3, b1, jnp.zeros((80, WIDTH), F32)], 0)
    part = lax.broadcasted_iota(jnp.int32, stacked.shape, 0) % 8
    near = jnp.where(part < 5, stacked, 0.0).astype(BF)
    if not both:
        return near
    return near, jnp.where(part >= 5, stacked, 0.0).astype(BF)


def support_columns(row):
    return jnp.broadcast_to(row, (128, WIDTH)).T


def density_weights(left, near, mixed, columns, row, one_sided):
    second = jnp.zeros((8, WIDTH), F32)
    firsts = []
    for start in range(0, WIDTH, CHUNK):
        part = left[start : start + CHUNK]
        s = jnp.dot(part, near, preferred_element_type=F32)
        mix = jnp.dot(part, mixed, preferred_element_type=F32)
        s = jnp.maximum(s, TINY)
        dist = s * lax.rsqrt(s)
        wide = columns[start : start + CHUNK]
        support = jnp.concatenate([wide, wide], 1) + row
        d = jnp.maximum(support - dist, 0.0)
        x = pl.reciprocal(mix, approx=True) * d
        x = x * x
        x = x * x
        w = x * (support + 4.0 * dist)
        for k in range(CHUNK // 8):
            second = second + w[8 * k : 8 * k + 8]
        if not one_sided:
            firsts.append(w[:, :128] + w[:, 128:])
    if one_sided:
        return second
    turned = jnp.concatenate(firsts, 0).T
    first = turned[:8]
    for k in range(1, 16):
        first = first + turned[8 * k : 8 * k + 8]
    return second, first


def inverse_mass(m):
    return jnp.where(m > 0.0, W_SCALE / jnp.where(m > 0.0, m, 1.0), 0.0)


def prepare_kernel(occ, pair, pos, vel, smooth, mass, own, out):
    lane = lax.broadcasted_iota(jnp.int32, (1, WIDTH), 1)

    def cell_step(c, _):
        one = pl.ds(c, 1)
        rows = [pos[k, one, :] - 0.5 for k in range(3)]
        rows.append(smooth[one, :])
        rows.append(jnp.where(lane < occ[c], mass[one, :], 0.0))
        rows += [vel[k, one, :] for k in range(3)]
        own[c] = jnp.concatenate(rows, 0)
        return 0

    lax.fori_loop(0, CELLS, cell_step, 0)

    def slot_step(p, _):
        out[p] = own[pair[p], 0:ROWS]
        return 0

    lax.fori_loop(0, LISTED, slot_step, 0)


def prepare(occ, pair, pos, vel, smooth, mass):
    return pl.pallas_call(
        prepare_kernel,
        in_specs=[SM, SM, VM, VM, VM, VM],
        out_specs=[VM, VM],
        out_shape=[
            jax.ShapeDtypeStruct((CELLS, 8, WIDTH), F32),
            jax.ShapeDtypeStruct((LISTED, ROWS, WIDTH), F32),
        ],
        compiler_params=params(),
    )(occ, pair, pos, vel, smooth, mass)


def local_density_kernel(own, rho, second, total):
    def cell_step(c, _):
        second[c] = second_rows(own[c])
        return 0

    lax.fori_loop(0, CELLS, cell_step, 0)
    empty = jnp.concatenate([jnp.zeros((4, WIDTH), F32)] + [jnp.ones((1, WIDTH), F32)], 0)
    second[CELLS] = second_rows(empty * jnp.zeros((ROWS, WIDTH), F32))
    total[...] = jnp.zeros_like(total)

    def pairs(c):
        cell = own[c]
        left = first_operand(first_rows(cell))
        columns = support_columns(cell[3:4])
        row_self = cell[3:4]
        near, mixed = second_operands(second[c], True)
        own_sum = density_weights(left, near, mixed, columns, row_self, True)
        after = jnp.minimum(c + 1, CELLS - 1)
        near, mixed = second_operands(second[c + 1], True)
        to_second, to_first = density_weights(left, near, mixed, columns, own[after, 3:4], False)
        return own_sum + to_first, to_second

    def step(i, _):
        here0, next0 = pairs(2 * i)
        here1, next1 = pairs(2 * i + 1)
        total[2 * i] += here0
        total[2 * i + 1] += here1 + next0
        total[2 * i + 2] += next1
        return 0

    lax.fori_loop(0, CELLS // 2, step, 0)

    def finish(c, _):
        rho[c] = jnp.sum(total[c], axis=0, keepdims=True) * inverse_mass(own[c, 4:5])
        return 0

    lax.fori_loop(0, CELLS, finish, 0)


def local_density(own):
    return pl.pallas_call(
        local_density_kernel,
        in_specs=[VM],
        out_specs=VM,
        out_shape=jax.ShapeDtypeStruct((CELLS, 1, WIDTH), F32),
        scratch_shapes=[
            pltpu.VMEM((CELLS + 1, 8, WIDTH), F32),
            pltpu.VMEM((CELLS + 2, 8, WIDTH), F32),
        ],
        cost_estimate=pl.CostEstimate(
            flops=127 * 65536 * 60, bytes_accessed=2 * 2**20, transcendentals=0
        ),
        compiler_params=params(),
    )(own)


def list_pairs(fill, cells, slot_of, cell_of):
    def peer_step(e, count):
        def slot_step(s, count):
            slot_of[count] = e * SLOTS + s
            cell_of[count] = cells[e * SLOTS + s]
            return count + 1

        return lax.fori_loop(0, fill[e], slot_step, count)

    count = lax.fori_loop(0, PEERS, peer_step, 0)
    for f in range(FACE):
        slot_of[count + f] = LISTED + f
        cell_of[count + f] = f
        slot_of[count + FACE + f] = LISTED + FACE + f
        cell_of[count + FACE + f] = CELLS - FACE + f
    for f in range(3):
        slot_of[count + 2 * FACE + f] = LISTED + 2 * FACE
        cell_of[count + 2 * FACE + f] = 0
    return (count + 2 * FACE + 3) // 4


def arrived_cell(slot, listed, faces):
    is_listed = slot < LISTED
    inner = listed[jnp.minimum(slot, LISTED - 1)]
    face = slot - LISTED
    outer = faces[jnp.clip(face, 0, 2 * FACE - 1), 0:ROWS]
    cell = jnp.where(is_listed, inner, outer)
    return jnp.where(face < 2 * FACE, cell, 0.0)


def cross_density_kernel(fill, cells, own, listed, faces, rho, back, total, slot_of, cell_of):
    total[...] = jnp.zeros_like(total)
    back[...] = jnp.zeros_like(back)
    trips = list_pairs(fill, cells, slot_of, cell_of)

    def pair(n):
        slot = slot_of[n]
        mine = own[cell_of[n]]
        other = arrived_cell(slot, listed, faces)
        left = first_operand(first_rows(mine))
        near, mixed = second_operands(second_rows(other), True)
        to_second, to_first = density_weights(
            left, near, mixed, support_columns(mine[3:4]), other[3:4], False
        )
        sent = jnp.sum(to_second, axis=0, keepdims=True) * inverse_mass(other[4:5])
        return slot, cell_of[n], to_first, sent

    def step(i, _):
        results = [pair(4 * i + k) for k in range(4)]
        for slot, cell, to_first, sent in results:
            total[cell] += to_first
            back[pl.ds(slot, 1), :] = sent
        return 0

    lax.fori_loop(0, trips, step, 0)

    def finish(c, _):
        rho[c] = jnp.sum(total[c], axis=0, keepdims=True) * inverse_mass(own[c, 4:5])
        return 0

    lax.fori_loop(0, CELLS, finish, 0)


def cross_density(fill, cells, own, listed, faces):
    return pl.pallas_call(
        cross_density_kernel,
        in_specs=[SM, SM, VM, VM, VM],
        out_specs=[VM, VM],
        out_shape=[
            jax.ShapeDtypeStruct((CELLS, 1, WIDTH), F32),
            jax.ShapeDtypeStruct((LISTED + 16, WIDTH), F32),
        ],
        scratch_shapes=[
            pltpu.VMEM((CELLS, 8, WIDTH), F32),
            pltpu.SMEM((LISTED + 16,), jnp.int32),
            pltpu.SMEM((LISTED + 16,), jnp.int32),
        ],
        cost_estimate=pl.CostEstimate(
            flops=80 * 65536 * 60, bytes_accessed=2 * 2**20, transcendentals=0
        ),
        compiler_params=params(),
    )(fill, cells, own, listed, faces)


def pressure_kernel(occ, pair, near, cross, returned, energy, own, density, term, out):
    lane = lax.broadcasted_iota(jnp.int32, (1, WIDTH), 1)
    term[...] = near[...] + cross[...]

    def slot_step(p, _):
        term[pair[p]] += returned[pl.ds(p, 1), :]
        return 0

    lax.fori_loop(0, LISTED, slot_step, 0)

    def cell_step(c, _):
        one = pl.ds(c, 1)
        full = lane < occ[c]
        rho = jnp.where(full, term[c], 0.0)
        density[one, :] = rho
        term[c] = jnp.where(full, GAMMA_LESS * energy[one, :] / jnp.where(full, rho, 1.0), 0.0)
        return 0

    lax.fori_loop(0, CELLS, cell_step, 0)

    def send_step(p, _):
        c = pair[p]
        out[p] = jnp.concatenate([own[c, 5:8], term[c]], 0)
        return 0

    lax.fori_loop(0, LISTED, send_step, 0)


def pressure(occ, pair, near, cross, returned, energy, own):
    return pl.pallas_call(
        pressure_kernel,
        in_specs=[SM, SM, VM, VM, VM, VM, VM],
        out_specs=[VM, VM, VM],
        out_shape=[
            jax.ShapeDtypeStruct((CELLS, WIDTH), F32),
            jax.ShapeDtypeStruct((CELLS, 1, WIDTH), F32),
            jax.ShapeDtypeStruct((LISTED, 4, WIDTH), F32),
        ],
        compiler_params=params(),
    )(occ, pair, near, cross, returned, energy, own)


def force_rows(cell, velocity, term):
    x, y, z, _, m = [cell[k : k + 1] for k in range(5)]
    u, v, w = [velocity[k : k + 1] for k in range(3)]
    mp = m * term
    blank = jnp.zeros_like(m)
    rows = jnp.concatenate(
        [m, m * x, m * y, m * z, mp, mp * x, mp * y, mp * z]
        + [m * u, m * v, m * w, m * (u * x + v * y + w * z)]
        + [blank] * 4,
        0,
    )
    high, low = split2(rows)
    return jnp.concatenate([high, low], 0)


def force_of(sums, cell, velocity, term):
    sums = sums[:16] + sums[16:]
    one, p_one = sums[0:1], sums[4:5]
    place, speed = cell[0:3], velocity
    acc = term * (place * one - sums[1:4]) + (place * p_one - sums[5:8])
    mixed = jnp.sum(
        speed * (place * one - sums[1:4]) - place * sums[8:11], axis=0, keepdims=True
    )
    rate = -term * (mixed + sums[11:12])
    return G_SCALE * jnp.concatenate([acc, rate], 0)


def slopes(left, near, columns, row, high, low):
    for start in range(0, WIDTH, CHUNK):
        s = jnp.dot(left[start : start + CHUNK], near, preferred_element_type=F32)
        s = jnp.maximum(s, TINY)
        dist = s * lax.rsqrt(s)
        wide = columns[start : start + CHUNK]
        support = jnp.concatenate([wide, wide], 1) + row
        d = jnp.maximum(support - dist, 0.0)
        e = pl.reciprocal(support * support, approx=True)
        x = e * d
        g = (x * x) * (x * e)
        top = g.astype(BF)
        high[start : start + CHUNK] = top
        low[start : start + CHUNK] = (g - top.astype(F32)).astype(BF)


def slope_sums(rows, high, low, dims):
    top = lax.dot_general(rows, high[...], dims, preferred_element_type=F32)
    return top + lax.dot_general(rows, low[...], dims, preferred_element_type=F32)


def local_force_kernel(start, stop, own, term, out, second, rows, total, *slots):
    def cell_step(c, _):
        cell = own[c]
        second[c] = second_rows(cell)
        rows[c] = force_rows(cell, cell[5:8], term[c])
        return 0

    lax.fori_loop(0, CELLS, cell_step, 0)
    second[CELLS] = second_rows(jnp.zeros((ROWS, WIDTH), F32))
    rows[CELLS] = jnp.zeros((32, WIDTH), BF)
    total[...] = jnp.zeros_like(total)

    def make(c, held):
        cell = own[c]
        left = first_operand(first_rows(cell))
        columns = support_columns(cell[3:4])
        slopes(left, second_operands(second[c], False), columns, cell[3:4], held[0], held[1])
        after = jnp.minimum(c + 1, CELLS - 1)
        slopes(
            left, second_operands(second[c + 1], False), columns, own[after, 3:4], held[2], held[3]
        )

    def use(c, held):
        mine, other = rows[c], rows[c + 1]
        total[c] += slope_sums(mine, held[0], held[1], NN) + slope_sums(other, held[2], held[3], NT)
        total[c + 1] += slope_sums(mine, held[2], held[3], NN)

    def step(i, _):
        make(2 * i, slots[:4])
        make(2 * i + 1, slots[4:])
        use(2 * i, slots[:4])
        use(2 * i + 1, slots[4:])
        return 0

    lax.fori_loop(start // 2, stop // 2, step, 0)

    def finish(c, _):
        cell = own[c]
        out[c] = force_of(total[c], cell, cell[5:8], term[c])
        return 0

    lax.fori_loop(0, CELLS, finish, 0)


def local_force(own, term, start, stop):
    return pl.pallas_call(
        functools.partial(local_force_kernel, start, stop),
        in_specs=[VM, VM],
        out_specs=VM,
        out_shape=jax.ShapeDtypeStruct((CELLS, 4, WIDTH), F32),
        scratch_shapes=[
            pltpu.VMEM((CELLS + 1, 8, WIDTH), F32),
            pltpu.VMEM((CELLS + 1, 32, WIDTH), BF),
            pltpu.VMEM((CELLS + 1, 32, WIDTH), F32),
        ]
        + [pltpu.VMEM((WIDTH, WIDTH), BF)] * 8,
        cost_estimate=pl.CostEstimate(
            flops=2 * (stop - start) * 65536 * 80, bytes_accessed=2 * 2**20, transcendentals=0
        ),
        compiler_params=params(),
    )(own, term)


def cross_force_kernel(
    fill, cells, own, term, listed, second_part, faces, face_terms, out, back,
    rows, total, slot_of, cell_of, *slots
):
    def cell_step(c, _):
        cell = own[c]
        rows[c] = force_rows(cell, cell[5:8], term[c])
        return 0

    lax.fori_loop(0, CELLS, cell_step, 0)
    total[...] = jnp.zeros_like(total)
    back[...] = jnp.zeros_like(back)
    trips = list_pairs(fill, cells, slot_of, cell_of)

    def make(n, held):
        slot = slot_of[n]
        mine = own[cell_of[n]]
        other = arrived_cell(slot, listed, faces)
        is_listed = slot < LISTED
        inner = second_part[jnp.minimum(slot, LISTED - 1)]
        face = jnp.clip(slot - LISTED, 0, 2 * FACE - 1)
        outer = jnp.concatenate([faces[face, 5:8], face_terms[face]], 0)
        moving = jnp.where(is_listed, inner, outer)
        left = first_operand(first_rows(mine))
        slopes(
            left, second_operands(second_rows(other), False), support_columns(mine[3:4]),
            other[3:4], held[0], held[1],
        )
        return slot, cell_of[n], other, moving

    def use(made, held):
        slot, cell, other, moving = made
        sums = slope_sums(rows[cell], held[0], held[1], NN)
        back[slot] = force_of(sums, other, moving[0:3], moving[3:4])
        theirs = force_rows(other, moving[0:3], moving[3:4])
        total[cell] += slope_sums(theirs, held[0], held[1], NT)

    def step(i, _):
        made = [make(4 * i + k, slots[2 * k : 2 * k + 2]) for k in range(4)]
        for k in range(4):
            use(made[k], slots[2 * k : 2 * k + 2])
        return 0

    lax.fori_loop(0, trips, step, 0)

    def finish(c, _):
        cell = own[c]
        out[c] = force_of(total[c], cell, cell[5:8], term[c])
        return 0

    lax.fori_loop(0, CELLS, finish, 0)


def cross_force(fill, cells, own, term, listed, second_part, faces, face_terms):
    return pl.pallas_call(
        cross_force_kernel,
        in_specs=[SM, SM] + [VM] * 6,
        out_specs=[VM, VM],
        out_shape=[
            jax.ShapeDtypeStruct((CELLS, 4, WIDTH), F32),
            jax.ShapeDtypeStruct((LISTED + 16, 4, WIDTH), F32),
        ],
        scratch_shapes=[
            pltpu.VMEM((CELLS, 32, WIDTH), BF),
            pltpu.VMEM((CELLS, 32, WIDTH), F32),
            pltpu.SMEM((LISTED + 16,), jnp.int32),
            pltpu.SMEM((LISTED + 16,), jnp.int32),
        ]
        + [pltpu.VMEM((WIDTH, WIDTH), BF)] * 8,
        cost_estimate=pl.CostEstimate(
            flops=80 * 65536 * 80, bytes_accessed=2 * 2**20, transcendentals=0
        ),
        compiler_params=params(),
    )(fill, cells, own, term, listed, second_part, faces, face_terms)


def finish_kernel(occ, pair, early, late, cross, returned, active, out, total):
    lane = lax.broadcasted_iota(jnp.int32, (1, WIDTH), 1)
    total[...] = early[...] + late[...] + cross[...]

    def slot_step(p, _):
        total[pair[p]] += returned[p]
        return 0

    lax.fori_loop(0, LISTED, slot_step, 0)

    def cell_step(c, _):
        one = pl.ds(c, 1)
        gate = jnp.where(lane < occ[c], active[one, :].astype(F32), 0.0)
        gated = total[c] * gate
        for k in range(4):
            out[k, one, :] = gated[k : k + 1]
        return 0

    lax.fori_loop(0, CELLS, cell_step, 0)


def finish(occ, pair, early, late, cross, returned, active):
    return pl.pallas_call(
        finish_kernel,
        in_specs=[SM, SM] + [VM] * 5,
        out_specs=VM,
        out_shape=jax.ShapeDtypeStruct((4, CELLS, WIDTH), F32),
        scratch_shapes=[pltpu.VMEM((CELLS, 4, WIDTH), F32)],
        compiler_params=params(),
    )(occ, pair, early, late, cross, returned, active)


def to_peers(block):
    flat = block.reshape((PEERS, -1, WIDTH))
    moved = lax.all_to_all(flat, "dev", split_axis=0, concat_axis=0, tiled=True)
    return moved.reshape(block.shape)


def with_neighbours(block):
    count = lax.axis_size("region")
    up = [(i, (i + 1) % count) for i in range(count)]
    down = [(i, (i - 1) % count) for i in range(count)]
    return jnp.concatenate(
        [
            lax.ppermute(block[CELLS - FACE :], "region", up),
            lax.ppermute(block[:FACE], "region", down),
        ],
        0,
    )


def local(
    positions, velocity, smoothing, masses, energy, occupancy, active, send_cells, send_fill,
    pair_cell,
):
    pair = pair_cell.reshape(-1)
    cells = send_cells.reshape(-1)
    fill = send_fill.reshape(-1)
    own, listed = prepare(occupancy, pair, positions, velocity, smoothing, masses)
    arrived = to_peers(listed)
    faces = with_neighbours(own)
    near_rho = local_density(own)
    cross_rho, back = cross_density(fill, cells, own, arrived, faces)
    returned = to_peers(back[:LISTED])
    density, term, moving = pressure(
        occupancy, pair, near_rho, cross_rho, returned, energy, own
    )
    arrived_moving = to_peers(moving)
    face_terms = with_neighbours(term)
    early = local_force(own, term, 0, CELLS // 2)
    cross, force_back = cross_force(
        fill, cells, own, term, arrived, arrived_moving, faces, face_terms
    )
    returned_force = to_peers(force_back[:LISTED])
    late = local_force(own, term, CELLS // 2, CELLS)
    forces = finish(occupancy, pair, early, late, cross, returned_force, active)
    return (density, forces)


def solution(mesh):
    cells = P(("region", "dev"), None)
    vectors = P(None, ("region", "dev"), None)
    lists = P(("region", "dev"), None, None)
    in_specs = (
        vectors, vectors, cells, cells, cells, P(("region", "dev")), cells, lists, cells, lists,
    )
    return jax.shard_map(
        local, mesh=mesh, in_specs=in_specs, out_specs=(cells, vectors), check_vma=False
    )
```

```python
import functools
import math

import jax
import jax.numpy as jnp
from jax import lax
from jax.experimental import pallas as pl
from jax.experimental.pallas import tpu as pltpu
from jax.sharding import PartitionSpec as P

BF = jnp.bfloat16
F32 = jnp.float32
FACE = 4
CELLS = 64
WIDTH = 256
PEERS = 16
SLOTS = 16
LISTED = PEERS * SLOTS
GAMMA_LESS = 2.0 / 3.0
W_SCALE = 84.0 / math.pi
G_SCALE = 6720.0 / math.pi
TINY = 1e-14
EMPTY = 1e8
CHUNK = 32
NN = (((1,), (0,)), ((), ()))
NT = (((1,), (1,)), ((), ()))
VM = pl.BlockSpec(memory_space=pltpu.VMEM)
SM = pl.BlockSpec(memory_space=pltpu.SMEM)
ROWS = 5
MOVING = 4
SPLIT = 40
LOCAL_ROWS = (160, 192, 224, 256)
CROSS_ROWS = (192, 256)
UNIT = 4
LOCAL_AT = 16
LOCAL_LIST = 72
CROSS_AT = LOCAL_AT + 2 * len(LOCAL_ROWS) * LOCAL_LIST
CROSS_LIST = LISTED + 16
PLAN = CROSS_AT + 2 * len(CROSS_ROWS) * CROSS_LIST
ANYWHERE = pl.BlockSpec(memory_space=pl.ANY)


def params():
    return pltpu.CompilerParams(vmem_limit_bytes=50 * 2**20)


def split2(x):
    a = x.astype(BF)
    return a, (x - a.astype(F32)).astype(BF)


def split3(x):
    a = x.astype(BF).astype(F32)
    rest = x - a
    b = rest.astype(BF).astype(F32)
    return a, b, rest - b


def rows_of(cell):
    x, y, z, h, m = [cell[k : k + 1] for k in range(5)]
    norm = 4.0 * (x * x + y * y + z * z)
    root = lax.rsqrt(jnp.where(m > 0.0, m, 1.0))
    mu = jnp.where(m > 0.0, root * lax.rsqrt(root), EMPTY)
    return x, y, z, h, norm, mu


def first_rows(cell):
    x, y, z, h, norm, mu = rows_of(cell)
    one = jnp.ones_like(x)
    return jnp.concatenate(
        [-8.0 * x, -8.0 * y, -8.0 * z, norm, one, h * h * mu, 2.0 * h * mu, mu], 0
    )


def second_rows(cell):
    x, y, z, h, norm, mu = rows_of(cell)
    one = jnp.ones_like(x)
    return jnp.concatenate([x, y, z, one, norm, mu, h * mu, h * h * mu], 0)


def first_operand(rows):
    a1, a2, a3 = split3(rows)
    return jnp.concatenate([a1, a1, a2, a2, a1, a3, jnp.zeros((80, WIDTH), F32)], 0).T.astype(BF)


def second_operands(rows, both):
    b1, b2, b3 = split3(rows)
    stacked = jnp.concatenate([b1, b2, b1, b2, b3, b1, jnp.zeros((80, WIDTH), F32)], 0)
    part = lax.broadcasted_iota(jnp.int32, stacked.shape, 0) % 8
    near = jnp.where(part < 5, stacked, 0.0).astype(BF)
    if not both:
        return near
    return near, jnp.where(part >= 5, stacked, 0.0).astype(BF)


def support_columns(row):
    return jnp.broadcast_to(row, (128, WIDTH)).T


def density_products(left, operands, count, s_ref, mix_ref):
    part = left[:count]
    s_ref[0:count] = jnp.dot(part, operands[0], preferred_element_type=F32)
    mix_ref[0:count] = jnp.dot(part, operands[1], preferred_element_type=F32)


def density_weights(count, s_ref, mix_ref, columns, row, one_sided):
    second = jnp.zeros((8, WIDTH), F32)
    firsts = []
    for start in range(0, count, CHUNK):
        s = jnp.maximum(s_ref[start : start + CHUNK], TINY)
        dist = s * lax.rsqrt(s)
        wide = columns[start : start + CHUNK]
        support = jnp.concatenate([wide, wide], 1) + row
        d = jnp.maximum(support - dist, 0.0)
        x = pl.reciprocal(mix_ref[start : start + CHUNK], approx=True) * d
        x = x * x
        x = x * x
        w = x * (support + 4.0 * dist)
        for k in range(CHUNK // 8):
            second = second + w[8 * k : 8 * k + 8]
        if not one_sided:
            firsts.append(w[:, :128] + w[:, 128:])
    if one_sided:
        return second
    if count < WIDTH:
        firsts.append(jnp.zeros((WIDTH - count, 128), F32))
    turned = jnp.concatenate(firsts, 0).T
    first = turned[:8]
    for k in range(1, 16):
        first = first + turned[8 * k : 8 * k + 8]
    return second, first


def inverse_mass(m):
    return jnp.where(m > 0.0, W_SCALE / jnp.where(m > 0.0, m, 1.0), 0.0)


def make_plan(occ, fill, cells, plan):
    for k in range(LOCAL_AT):
        plan[k] = 0
    classes = len(LOCAL_ROWS)

    def local_step(c, _):
        size = occ[c]
        kind = sum((size > rows).astype(jnp.int32) for rows in LOCAL_ROWS[:-1])
        kind = kind + jnp.where(c >= SPLIT, classes, 0)
        count = plan[kind]
        plan[LOCAL_AT + kind * LOCAL_LIST + count] = c
        plan[kind] = count + 1
        return 0

    lax.fori_loop(0, CELLS, local_step, 0)
    for kind in range(2 * classes):
        count = plan[kind]
        plan[LOCAL_AT + kind * LOCAL_LIST + count] = CELLS
        plan[kind] = (count + 1) // 2

    base = 2 * classes

    unused = jnp.int32(0)
    for e in range(PEERS):
        unused = jnp.where(fill[0, e] == 0, e * SLOTS, unused)
    for kind in range(len(CROSS_ROWS)):
        at = CROSS_AT + 2 * kind * CROSS_LIST
        for k in range(UNIT - 1):
            plan[at + k] = unused
            plan[at + CROSS_LIST + k] = CELLS

    def peer_step(e, counts):
        def slot_step(s, counts):
            cell = cells[e, s]
            wide = (occ[cell] > CROSS_ROWS[0]).astype(jnp.int32)
            at = CROSS_AT + 2 * wide * CROSS_LIST + jnp.where(wide > 0, counts[1], counts[0])
            plan[at + UNIT - 1] = e * SLOTS + s
            plan[at + CROSS_LIST + UNIT - 1] = cell
            return (counts[0] + 1 - wide, counts[1] + wide)

        return lax.fori_loop(0, fill[0, e], slot_step, counts)

    counts = lax.fori_loop(0, PEERS, peer_step, (jnp.int32(0), jnp.int32(0)))
    for kind in range(len(CROSS_ROWS)):
        trips = (counts[kind] + UNIT - 1) // UNIT
        plan[base + 2 * kind] = trips
        plan[base + 2 * kind + 1] = UNIT - 1 + counts[kind] - UNIT * trips


def fetch(pairs, sem):
    copies = [
        pltpu.make_async_copy(source, target, sem.at[k])
        for k, (source, target) in enumerate(pairs)
    ]
    for copy in copies:
        copy.start()
    return copies


def prepare_kernel(
    occ, fill, cells, pair, pos_in, vel_in, smooth_in, mass_in, own, out, plan,
    pos, vel, smooth, mass, sem,
):
    copies = fetch(
        [(pos_in, pos), (vel_in, vel), (smooth_in, smooth), (mass_in, mass)], sem
    )
    lane = lax.broadcasted_iota(jnp.int32, (1, WIDTH), 1)
    for copy in copies:
        copy.wait()

    def cell_step(c, _):
        one = pl.ds(c, 1)
        rows = [pos[k, one, :] - 0.5 for k in range(3)]
        rows.append(smooth[one, :])
        rows.append(jnp.where(lane < occ[c], mass[one, :], 0.0))
        rows += [vel[k, one, :] for k in range(3)]
        own[c] = jnp.concatenate(rows, 0)
        return 0

    lax.fori_loop(0, CELLS, cell_step, 0, unroll=8)
    own[CELLS] = jnp.zeros((8, WIDTH), F32)

    def peer_step(e, _):
        for s in range(SLOTS):
            out[e, s * ROWS : (s + 1) * ROWS] = own[pair[e, s], 0:ROWS]
        return 0

    lax.fori_loop(0, PEERS, peer_step, 0)
    make_plan(occ, fill, cells, plan)


def prepare(occ, fill, cells, pair, pos, vel, smooth, mass):
    return pl.pallas_call(
        prepare_kernel,
        in_specs=[SM] * 4 + [ANYWHERE] * 4,
        out_specs=[VM, VM, SM],
        out_shape=[
            jax.ShapeDtypeStruct((CELLS + 1, 8, WIDTH), F32),
            jax.ShapeDtypeStruct((PEERS, SLOTS * ROWS, WIDTH), F32),
            jax.ShapeDtypeStruct((PLAN,), jnp.int32),
        ],
        scratch_shapes=[
            pltpu.VMEM((3, CELLS, WIDTH), F32),
            pltpu.VMEM((3, CELLS, WIDTH), F32),
            pltpu.VMEM((CELLS, WIDTH), F32),
            pltpu.VMEM((CELLS, WIDTH), F32),
            pltpu.SemaphoreType.DMA((4,)),
        ],
        compiler_params=params(),
    )(occ, fill, cells, pair, pos, vel, smooth, mass)


def fold(total, own, cells, out, carried):
    def cell_step(c, _):
        mine = jnp.sum(total[c], axis=0, keepdims=True) * inverse_mass(own[c, 4:5])
        one = pl.ds(c, 1)
        out[one, :] = mine if carried is None else carried[one, :] + mine
        return 0

    lax.fori_loop(0, cells, cell_step, 0, unroll=8)


def local_density_kernel(part, plan, own, *rest):
    if part:
        faces, carried, rho, second, total, *slots = rest
    else:
        faces = carried = None
        rho, second, total, *slots = rest

    def cell_step(c, _):
        second[c] = second_rows(own[c])
        return 0

    lax.fori_loop(0, CELLS + 1, cell_step, 0, unroll=5)
    total[...] = jnp.zeros_like(total)

    def unit(count, places):
        plans = []
        for k, c in enumerate(places):
            after = jnp.minimum(c + 1, CELLS)
            left = first_operand(first_rows(own[c]))
            one, two = slots[4 * k : 4 * k + 2], slots[4 * k + 2 : 4 * k + 4]
            density_products(left, second_operands(second[c], True), count, *one)
            density_products(left, second_operands(second[after], True), count, *two)
            plans.append((c, after, one, two))
        sums = []
        for c, after, one, two in plans:
            row = own[c, 3:4]
            columns = support_columns(row)
            own_sum = density_weights(count, *one, columns, row, True)
            to_second, to_first = density_weights(
                count, *two, columns, own[after, 3:4], False
            )
            sums.append((c, after, own_sum + to_first, to_second))
        for c, after, here, there in sums:
            total[c] += here
            total[after] += there

    for kind, count in enumerate(LOCAL_ROWS):
        at = kind + part * len(LOCAL_ROWS)
        start = LOCAL_AT + at * LOCAL_LIST

        def step(i, _):
            unit(count, [plan[start + 2 * i], plan[start + 2 * i + 1]])
            return 0

        lax.fori_loop(0, plan[at], step, 0)

    if part:

        def face_step(i, _):
            made = []
            for k in range(FACE):
                cell = faces[i * FACE + k]
                c = i * (CELLS - FACE) + k
                held = slots[2 * k : 2 * k + 2]
                left = first_operand(first_rows(cell))
                density_products(left, second_operands(second[c], True), WIDTH, *held)
                made.append((cell, c, held))
            for cell, c, held in made:
                total[c] += density_weights(
                    WIDTH, *held, support_columns(cell[3:4]), own[c, 3:4], True
                )
            return 0

        lax.fori_loop(0, 2, face_step, 0)

    fold(total, own, CELLS, rho, carried)


def local_density(part, plan, own, *rest):
    return pl.pallas_call(
        functools.partial(local_density_kernel, part),
        in_specs=[SM] + [VM] * (1 + len(rest)),
        out_specs=VM,
        out_shape=jax.ShapeDtypeStruct((CELLS, WIDTH), F32),
        scratch_shapes=[
            pltpu.VMEM((CELLS + 1, 8, WIDTH), F32),
            pltpu.VMEM((CELLS + 1, 8, WIDTH), F32),
        ]
        + [pltpu.VMEM((WIDTH, WIDTH), F32)] * 8,
        cost_estimate=pl.CostEstimate(
            flops=64 * 65536 * 60, bytes_accessed=2 * 2**20, transcendentals=0
        ),
        compiler_params=params(),
    )(plan, own, *rest)


def listed_rows(slot, block, count):
    return [block[slot // SLOTS, pl.ds((slot % SLOTS) * count + k, 1), :] for k in range(count)]


def listed_cell(slot, listed):
    return jnp.concatenate(listed_rows(slot, listed, ROWS), 0)


def over_pairs(plan, unit):
    for kind, count in enumerate(CROSS_ROWS):
        base = 2 * len(LOCAL_ROWS) + 2 * kind
        at = CROSS_AT + 2 * kind * CROSS_LIST + plan[base + 1]

        def step(i, _):
            unit(
                count,
                [
                    (plan[at + UNIT * i + k], plan[at + CROSS_LIST + UNIT * i + k])
                    for k in range(UNIT)
                ],
            )
            return 0

        lax.fori_loop(0, plan[base], step, 0)


def cross_density_kernel(plan, own, listed, carried, rho, back, total, *slots):
    total[...] = jnp.zeros_like(total)
    back[...] = jnp.zeros_like(back)

    def unit(count, pairs):
        made = []
        for k, (slot, c) in enumerate(pairs):
            other = listed_cell(slot, listed)
            held = slots[2 * k : 2 * k + 2]
            left = first_operand(first_rows(own[c]))
            density_products(left, second_operands(second_rows(other), True), count, *held)
            made.append((slot, c, other, held))
        sums = []
        for slot, c, other, held in made:
            to_second, to_first = density_weights(
                count, *held, support_columns(own[c, 3:4]), other[3:4], False
            )
            sent = jnp.sum(to_second, axis=0, keepdims=True) * inverse_mass(other[4:5])
            sums.append((slot, c, to_first, sent))
        for slot, c, to_first, sent in sums:
            total[c] += to_first
            back[slot // SLOTS, pl.ds(slot % SLOTS, 1), :] = sent

    over_pairs(plan, unit)
    fold(total, own, CELLS, rho, carried)


def cross_density(plan, own, listed, carried):
    return pl.pallas_call(
        cross_density_kernel,
        in_specs=[SM, VM, VM, VM],
        out_specs=[VM, VM],
        out_shape=[
            jax.ShapeDtypeStruct((CELLS, WIDTH), F32),
            jax.ShapeDtypeStruct((PEERS, SLOTS, WIDTH), F32),
        ],
        scratch_shapes=[pltpu.VMEM((CELLS + 1, 8, WIDTH), F32)]
        + [pltpu.VMEM((WIDTH, WIDTH), F32)] * 8,
        cost_estimate=pl.CostEstimate(
            flops=80 * 65536 * 60, bytes_accessed=2 * 2**20, transcendentals=0
        ),
        compiler_params=params(),
    )(plan, own, listed, carried)


def pressure_kernel(
    occ, pair, near, returned, energy_in, own, density, moving, out, energy, sum_of, sem
):
    copies = fetch([(energy_in, energy)], sem)
    lane = lax.broadcasted_iota(jnp.int32, (1, WIDTH), 1)

    def read_step(c, _):
        sum_of[c] = near[pl.ds(c, 1), :]
        return 0

    lax.fori_loop(0, CELLS, read_step, 0, unroll=8)

    def peer_step(e, _):
        for s in range(SLOTS):
            sum_of[pair[e, s]] += returned[e, s : s + 1]
        return 0

    lax.fori_loop(0, PEERS, peer_step, 0)
    copies[0].wait()

    def cell_step(c, _):
        one = pl.ds(c, 1)
        full = lane < occ[c]
        rho = jnp.where(full, sum_of[c], 0.0)
        density[one, :] = rho
        term = jnp.where(full, GAMMA_LESS * energy[one, :] / jnp.where(full, rho, 1.0), 0.0)
        moving[c] = jnp.concatenate([own[c, 5:8], term], 0)
        return 0

    lax.fori_loop(0, CELLS, cell_step, 0, unroll=8)
    moving[CELLS] = jnp.zeros((MOVING, WIDTH), F32)

    def send_step(e, _):
        for s in range(SLOTS):
            out[e, s * MOVING : (s + 1) * MOVING] = moving[pair[e, s]]
        return 0

    lax.fori_loop(0, PEERS, send_step, 0)


def pressure(occ, pair, near, returned, energy, own):
    return pl.pallas_call(
        pressure_kernel,
        in_specs=[SM, SM, VM, VM, ANYWHERE, VM],
        out_specs=[VM, VM, VM],
        out_shape=[
            jax.ShapeDtypeStruct((CELLS, WIDTH), F32),
            jax.ShapeDtypeStruct((CELLS + 1, MOVING, WIDTH), F32),
            jax.ShapeDtypeStruct((PEERS, SLOTS * MOVING, WIDTH), F32),
        ],
        scratch_shapes=[
            pltpu.VMEM((CELLS, WIDTH), F32),
            pltpu.VMEM((CELLS, 1, WIDTH), F32),
            pltpu.SemaphoreType.DMA((1,)),
        ],
        compiler_params=params(),
    )(occ, pair, near, returned, energy, own)


def force_rows(cell, moving):
    x, y, z, _, m = [cell[k : k + 1] for k in range(5)]
    u, v, w, term = [moving[k : k + 1] for k in range(4)]
    mp = m * term
    blank = jnp.zeros_like(m)
    rows = jnp.concatenate(
        [m, m * x, m * y, m * z, mp, mp * x, mp * y, mp * z]
        + [m * u, m * v, m * w, m * (u * x + v * y + w * z)]
        + [blank] * 4,
        0,
    )
    high, low = split2(rows)
    return jnp.concatenate([high, low], 0)


def force_of(sums, cell, moving):
    sums = sums[:16] + sums[16:]
    one, p_one = sums[0:1], sums[4:5]
    place, speed, term = cell[0:3], moving[0:3], moving[3:4]
    lean = place * one - sums[1:4]
    acc = term * lean + (place * p_one - sums[5:8])
    mixed = jnp.sum(speed * lean - place * sums[8:11], axis=0, keepdims=True)
    rate = -term * (mixed + sums[11:12])
    return G_SCALE * jnp.concatenate([acc, rate], 0)


def slopes(left, near, columns, row, count, s_ref, high, low):
    s_ref[0:count] = jnp.dot(left[:count], near, preferred_element_type=F32)
    for start in range(0, count, CHUNK):
        s = jnp.maximum(s_ref[start : start + CHUNK], TINY)
        dist = s * lax.rsqrt(s)
        wide = columns[start : start + CHUNK]
        support = jnp.concatenate([wide, wide], 1) + row
        d = jnp.maximum(support - dist, 0.0)
        e = pl.reciprocal(support * support, approx=True)
        x = e * d
        g = (x * x) * (x * e)
        top = g.astype(BF)
        high[start : start + CHUNK] = top
        low[start : start + CHUNK] = (g - top.astype(F32)).astype(BF)


def to_seconds(rows, count, high, low):
    part = rows[:, :count]
    top = lax.dot_general(part, high[0:count], NN, preferred_element_type=F32)
    return top + lax.dot_general(part, low[0:count], NN, preferred_element_type=F32)


def to_firsts(rows, count, high, low):
    top = lax.dot_general(rows, high[0:count], NT, preferred_element_type=F32)
    return top + lax.dot_general(rows, low[0:count], NT, preferred_element_type=F32)


def add_forces(total, own, moving, out, carried):
    def cell_step(c, _):
        mine = force_of(total[c], own[c], moving[c])
        out[c] = mine if carried is None else carried[c] + mine
        return 0

    lax.fori_loop(0, CELLS, cell_step, 0, unroll=4)


def local_force_kernel(part, plan, own, moving, *rest):
    if part:
        faces, face_terms, carried, out, second, rows, total, *slots = rest
    else:
        faces = face_terms = carried = None
        out, second, rows, total, *slots = rest

    def cell_step(c, _):
        cell = own[c]
        second[c] = second_rows(cell)
        rows[c] = force_rows(cell, moving[c])
        return 0

    lax.fori_loop(0, CELLS + 1, cell_step, 0, unroll=5)
    total[...] = jnp.zeros_like(total)

    def unit(count, places):
        made = []
        for k, c in enumerate(places):
            after = jnp.minimum(c + 1, CELLS)
            one, two = slots[6 * k : 6 * k + 3], slots[6 * k + 3 : 6 * k + 6]
            row = own[c, 3:4]
            left = first_operand(first_rows(own[c]))
            columns = support_columns(row)
            slopes(left, second_operands(second[c], False), columns, row, count, *one)
            slopes(
                left, second_operands(second[after], False), columns, own[after, 3:4], count, *two
            )
            made.append((c, after, one[1:], two[1:]))
        for c, after, one, two in made:
            mine, other = rows[c], rows[after]
            total[c] += to_seconds(mine, count, *one)
            total[c, :, 0:count] += to_firsts(other, count, *two)
            total[after] += to_seconds(mine, count, *two)

    for kind, count in enumerate(LOCAL_ROWS):
        at = kind + part * len(LOCAL_ROWS)
        start = LOCAL_AT + at * LOCAL_LIST

        def step(i, _):
            unit(count, [plan[start + 2 * i], plan[start + 2 * i + 1]])
            return 0

        lax.fori_loop(0, plan[at], step, 0)

    if part:

        def face_step(i, _):
            made = []
            for k in range(FACE):
                cell = faces[i * FACE + k]
                c = i * (CELLS - FACE) + k
                held = slots[3 * k : 3 * k + 3]
                left = first_operand(first_rows(cell))
                slopes(
                    left, second_operands(second[c], False), support_columns(cell[3:4]),
                    own[c, 3:4], WIDTH, *held,
                )
                theirs = jnp.concatenate([cell[5:8], face_terms[i * FACE + k, 3:4]], 0)
                made.append((force_rows(cell, theirs), c, held[1:]))
            for theirs, c, held in made:
                total[c] += to_seconds(theirs, WIDTH, *held)
            return 0

        lax.fori_loop(0, 2, face_step, 0)

    add_forces(total, own, moving, out, carried)


PAIR_SLOT = [
    pltpu.VMEM((WIDTH, WIDTH), F32),
    pltpu.VMEM((WIDTH, WIDTH), BF),
    pltpu.VMEM((WIDTH, WIDTH), BF),
]


def local_force(part, plan, own, moving, *rest):
    return pl.pallas_call(
        functools.partial(local_force_kernel, part),
        in_specs=[SM] + [VM] * (2 + len(rest)),
        out_specs=VM,
        out_shape=jax.ShapeDtypeStruct((CELLS, 4, WIDTH), F32),
        scratch_shapes=[
            pltpu.VMEM((CELLS + 1, 8, WIDTH), F32),
            pltpu.VMEM((CELLS + 1, 32, WIDTH), BF),
            pltpu.VMEM((CELLS + 1, 32, WIDTH), F32),
        ]
        + PAIR_SLOT * 4,
        cost_estimate=pl.CostEstimate(
            flops=64 * 65536 * 80, bytes_accessed=2 * 2**20, transcendentals=0
        ),
        compiler_params=params(),
    )(plan, own, moving, *rest)


def cross_force_kernel(
    plan, own, moving, listed, arrived, carried, out, back, rows, total, *slots
):
    def cell_step(c, _):
        rows[c] = force_rows(own[c], moving[c])
        return 0

    lax.fori_loop(0, CELLS + 1, cell_step, 0, unroll=5)
    total[...] = jnp.zeros_like(total)
    back[...] = jnp.zeros_like(back)

    def unit(count, pairs):
        made = []
        for k, (slot, c) in enumerate(pairs):
            other = listed_cell(slot, listed)
            held = slots[3 * k : 3 * k + 3]
            left = first_operand(first_rows(own[c]))
            slopes(
                left, second_operands(second_rows(other), False), support_columns(own[c, 3:4]),
                other[3:4], count, *held,
            )
            made.append((slot, c, other, held[1:]))
        for slot, c, other, held in made:
            theirs = jnp.concatenate(listed_rows(slot, arrived, MOVING), 0)
            sums = to_seconds(rows[c], count, *held)
            sent = force_of(sums, other, theirs)
            for k in range(MOVING):
                at = pl.ds((slot % SLOTS) * MOVING + k, 1)
                back[slot // SLOTS, at, :] = sent[k : k + 1]
            total[c, :, 0:count] += to_firsts(force_rows(other, theirs), count, *held)

    over_pairs(plan, unit)
    add_forces(total, own, moving, out, carried)


def cross_force(plan, own, moving, listed, arrived, carried):
    return pl.pallas_call(
        cross_force_kernel,
        in_specs=[SM] + [VM] * 5,
        out_specs=[VM, VM],
        out_shape=[
            jax.ShapeDtypeStruct((CELLS, 4, WIDTH), F32),
            jax.ShapeDtypeStruct((PEERS, SLOTS * MOVING, WIDTH), F32),
        ],
        scratch_shapes=[
            pltpu.VMEM((CELLS + 1, 32, WIDTH), BF),
            pltpu.VMEM((CELLS + 1, 32, WIDTH), F32),
        ]
        + PAIR_SLOT * 4,
        cost_estimate=pl.CostEstimate(
            flops=80 * 65536 * 80, bytes_accessed=2 * 2**20, transcendentals=0
        ),
        compiler_params=params(),
    )(plan, own, moving, listed, arrived, carried)


def finish_kernel(occ, pair, near, returned, active_in, out, total, active, sem):
    copies = fetch([(active_in, active)], sem)
    lane = lax.broadcasted_iota(jnp.int32, (1, WIDTH), 1)
    total[...] = near[...]

    def peer_step(e, _):
        for s in range(SLOTS):
            total[pair[e, s]] += returned[e, s * MOVING : (s + 1) * MOVING]
        return 0

    lax.fori_loop(0, PEERS, peer_step, 0)
    copies[0].wait()

    def cell_step(c, _):
        one = pl.ds(c, 1)
        gate = jnp.where(lane < occ[c], active[one, :].astype(F32), 0.0)
        gated = total[c] * gate
        for k in range(4):
            out[k, one, :] = gated[k : k + 1]
        return 0

    lax.fori_loop(0, CELLS, cell_step, 0, unroll=8)


def finish(occ, pair, near, returned, active):
    return pl.pallas_call(
        finish_kernel,
        in_specs=[SM, SM, VM, VM, ANYWHERE],
        out_specs=VM,
        out_shape=jax.ShapeDtypeStruct((4, CELLS, WIDTH), F32),
        scratch_shapes=[
            pltpu.VMEM((CELLS, 4, WIDTH), F32),
            pltpu.VMEM((CELLS, WIDTH), jnp.int32),
            pltpu.SemaphoreType.DMA((1,)),
        ],
        compiler_params=params(),
    )(occ, pair, near, returned, active)


def to_peers(block):
    return lax.all_to_all(block, "dev", split_axis=0, concat_axis=0, tiled=True)


def with_neighbours(block):
    count = lax.axis_size("region")
    up = [(i, (i + 1) % count) for i in range(count)]
    down = [(i, (i - 1) % count) for i in range(count)]
    return jnp.concatenate(
        [
            lax.ppermute(block[CELLS - FACE : CELLS], "region", up),
            lax.ppermute(block[:FACE], "region", down),
        ],
        0,
    )


def local(
    positions, velocity, smoothing, masses, energy, occupancy, active, send_cells, send_fill,
    pair_cell,
):
    pair = pair_cell[0]
    own, listed, plan = prepare(
        occupancy, send_fill, send_cells[0], pair, positions, velocity, smoothing, masses
    )
    arrived = to_peers(listed)
    faces = with_neighbours(own)
    rho = local_density(0, plan, own)
    rho, back = cross_density(plan, own, arrived, rho)
    returned = to_peers(back)
    rho = local_density(1, plan, own, faces, rho)
    density, moving, leaving = pressure(occupancy, pair, rho, returned, energy, own)
    arrived_moving = to_peers(leaving)
    face_terms = with_neighbours(moving)
    sums = local_force(0, plan, own, moving)
    sums, force_back = cross_force(plan, own, moving, arrived, arrived_moving, sums)
    returned_force = to_peers(force_back)
    sums = local_force(1, plan, own, moving, faces, face_terms, sums)
    forces = finish(occupancy, pair, sums, returned_force, active)
    return (density, forces)


def solution(mesh):
    cells = P(("region", "dev"), None)
    vectors = P(None, ("region", "dev"), None)
    lists = P(("region", "dev"), None, None)
    in_specs = (
        vectors, vectors, cells, cells, cells, P(("region", "dev")), cells, lists, cells, lists,
    )
    return jax.shard_map(
        local, mesh=mesh, in_specs=in_specs, out_specs=(cells, vectors), check_vma=False
    )
```

```python
import functools
import math

import jax
import jax.numpy as jnp
from jax import lax
from jax.experimental import pallas as pl
from jax.experimental.pallas import tpu as pltpu
from jax.sharding import PartitionSpec as P

BF = jnp.bfloat16
F32 = jnp.float32
FACE = 4
CELLS = 64
WIDTH = 256
PEERS = 16
SLOTS = 16
LISTED = PEERS * SLOTS
GAMMA_LESS = 2.0 / 3.0
W_SCALE = 84.0 / math.pi
G_SCALE = 6720.0 / math.pi
TINY = 1e-14
EMPTY = 1e8
CHUNK = 32
CELL = 8
SUMS = 16
NN = (((1,), (0,)), ((), ()))
NT = (((1,), (1,)), ((), ()))
VM = pl.BlockSpec(memory_space=pltpu.VMEM)
SM = pl.BlockSpec(memory_space=pltpu.SMEM)
ROWS = 5
MOVING = 4
SPLIT = 40
LOCAL_ROWS = (192, 224, 256)
CROSS_ROWS = (192, 256)
UNIT = 4
LOCAL_AT = 16
LOCAL_LIST = 72
LEAD = UNIT + 3
CROSS_AT = LOCAL_AT + 2 * len(LOCAL_ROWS) * LOCAL_LIST
CROSS_LIST = LISTED + 16
PLAN = CROSS_AT + 2 * len(CROSS_ROWS) * CROSS_LIST
ANYWHERE = pl.BlockSpec(memory_space=pl.ANY)


def params():
    return pltpu.CompilerParams(vmem_limit_bytes=50 * 2**20)


def split2(x):
    a = x.astype(BF)
    return a, (x - a.astype(F32)).astype(BF)


def split3(x):
    a = x.astype(BF).astype(F32)
    rest = x - a
    b = rest.astype(BF).astype(F32)
    return a, b, rest - b


def pair_terms(x, y, z, h, m):
    norm = 4.0 * (x * x + y * y + z * z)
    root = lax.rsqrt(jnp.where(m > 0.0, m, 1.0))
    mu = jnp.where(m > 0.0, root * lax.rsqrt(root), EMPTY)
    one = jnp.ones_like(x)
    first = [-8.0 * x, -8.0 * y, -8.0 * z, norm, one, h * h * mu, 2.0 * h * mu, mu]
    second = [x, y, z, one, norm, mu, h * mu, h * h * mu]
    return first, second


def both(read):
    return jnp.concatenate([read(0), read(1)], -1)


def half(value, h):
    return value[..., 128 * h : 128 * (h + 1)]


def put(ref, planes, start, count, stride):
    for k, plane in enumerate(planes):
        for h in range(2):
            ref[h, pl.ds(start + k, count, stride=stride), :] = half(plane, h)


def planes_of(ref, ids, start, count, stride):
    return [both(lambda h: ref[h, pl.ds(start + k, count, stride=stride), :]) for k in ids]


def rows_at(index, size):
    return pl.ds(pl.multiple_of(index * size, size), size)


def block(ref, index, size):
    return both(lambda h: ref[h, rows_at(index, size), :])


def set_block(ref, index, size, value):
    for h in range(2):
        ref[h, rows_at(index, size), :] = half(value, h)


def add_block(ref, index, size, value):
    for h in range(2):
        ref[h, rows_at(index, size), :] += half(value, h)


def line(ref, index, size, k):
    return both(lambda h: ref[h, pl.ds(index * size + k, 1), :])


def listed_planes(listed, e, ids, size):
    step = SLOTS * size
    return [
        both(lambda h: listed[e, pl.ds(h * step + k, SLOTS, stride=size), :]) for k in ids
    ]


def listed_support(listed, slot):
    at = (slot % SLOTS) * ROWS + 3
    return both(lambda h: listed[slot // SLOTS, pl.ds(h * SLOTS * ROWS + at, 1), :])


def first_operand(rows):
    a1, a2, a3 = split3(rows)
    return jnp.concatenate([a1, a1, a2, a2, a1, a3, jnp.zeros((80, WIDTH), F32)], 0).T.astype(BF)


def second_operands(rows, both):
    b1, b2, b3 = split3(rows)
    stacked = jnp.concatenate([b1, b2, b1, b2, b3, b1, jnp.zeros((80, WIDTH), F32)], 0)
    part = lax.broadcasted_iota(jnp.int32, stacked.shape, 0) % 8
    near = jnp.where(part < 5, stacked, 0.0).astype(BF)
    if not both:
        return near
    return near, jnp.where(part >= 5, stacked, 0.0).astype(BF)


def support_columns(row):
    return jnp.broadcast_to(row, (128, WIDTH)).T


def density_products(left, operands, count, s_ref, mix_ref):
    part = left[:count]
    s_ref[0:count] = jnp.dot(part, operands[0], preferred_element_type=F32)
    mix_ref[0:count] = jnp.dot(part, operands[1], preferred_element_type=F32)


def density_weights(count, s_ref, mix_ref, columns, row, one_sided):
    second = jnp.zeros((8, WIDTH), F32)
    firsts = []
    for start in range(0, count, CHUNK):
        s = jnp.maximum(s_ref[start : start + CHUNK], TINY)
        dist = s * lax.rsqrt(s)
        wide = columns[start : start + CHUNK]
        support = jnp.concatenate([wide, wide], 1) + row
        d = jnp.maximum(support - dist, 0.0)
        x = pl.reciprocal(mix_ref[start : start + CHUNK], approx=True) * d
        x = x * x
        x = x * x
        w = x * (support + 4.0 * dist)
        for k in range(CHUNK // 8):
            second = second + w[8 * k : 8 * k + 8]
        if not one_sided:
            firsts.append(w[:, :128] + w[:, 128:])
    if one_sided:
        return second
    if count < WIDTH:
        firsts.append(jnp.zeros((WIDTH - count, 128), F32))
    turned = jnp.concatenate(firsts, 0).T
    first = turned[:8]
    for k in range(1, 16):
        first = first + turned[8 * k : 8 * k + 8]
    return second, first


def inverse_mass(m):
    return jnp.where(m > 0.0, W_SCALE / jnp.where(m > 0.0, m, 1.0), 0.0)


def plan_kernel(occ, fill, cells, _, plan):
    classes = len(LOCAL_ROWS)
    for kind in range(2 * classes):
        plan[kind] = 0
        for k in range(2):
            plan[LOCAL_AT + kind * LOCAL_LIST + k] = CELLS

    def local_step(c, _):
        size = occ[c]
        kind = sum((size > rows).astype(jnp.int32) for rows in LOCAL_ROWS[:-1])
        kind = kind + jnp.where(c >= SPLIT, classes, 0)
        count = plan[kind]
        plan[LOCAL_AT + kind * LOCAL_LIST + 2 + count] = c
        plan[kind] = count + 1
        return 0

    lax.fori_loop(0, CELLS, local_step, 0)
    for kind in range(2 * classes):
        count = plan[kind]
        for k in range(2):
            plan[LOCAL_AT + kind * LOCAL_LIST + 2 + count + k] = CELLS
        plan[kind] = (count + 1) // 2

    base = 2 * classes

    unused = jnp.int32(0)
    for e in range(PEERS):
        unused = jnp.where(fill[0, e] == 0, e * SLOTS, unused)

    def blank(at):
        plan[at] = unused
        plan[at + CROSS_LIST] = CELLS

    for kind in range(len(CROSS_ROWS)):
        for k in range(LEAD):
            blank(CROSS_AT + 2 * kind * CROSS_LIST + k)

    def peer_step(e, counts):
        def slot_step(s, counts):
            cell = cells[e, s]
            wide = (occ[cell] > CROSS_ROWS[0]).astype(jnp.int32)
            at = CROSS_AT + LEAD + jnp.where(
                wide > 0, 2 * CROSS_LIST + counts[1], counts[0]
            )
            plan[at] = e * SLOTS + s
            plan[at + CROSS_LIST] = cell
            return (counts[0] + 1 - wide, counts[1] + wide)

        return lax.fori_loop(0, fill[0, e], slot_step, counts)

    counts = lax.fori_loop(0, PEERS, peer_step, (jnp.int32(0), jnp.int32(0)))
    for kind in range(len(CROSS_ROWS)):
        trips = (counts[kind] + UNIT - 1) // UNIT
        plan[base + 2 * kind] = trips
        plan[base + 2 * kind + 1] = LEAD + counts[kind] - UNIT * trips
        for k in range(2):
            blank(CROSS_AT + 2 * kind * CROSS_LIST + LEAD + counts[kind] + k)


def make_plan(occ, fill, cells, own):
    return pl.pallas_call(
        plan_kernel,
        in_specs=[SM] * 3 + [ANYWHERE],
        out_specs=SM,
        out_shape=jax.ShapeDtypeStruct((PLAN,), jnp.int32),
    )(occ, fill, cells, own)


def fetch(pairs, sem):
    copies = [
        pltpu.make_async_copy(source, target, sem.at[k])
        for k, (source, target) in enumerate(pairs)
    ]
    for copy in copies:
        copy.start()
    return copies


def prepare_kernel(
    occ, pair, pos_in, vel_in, smooth_in, mass_in, own, first, second, out,
    pos, vel, smooth, mass, full, cells, sem,
):
    copies = fetch(
        [(pos_in, pos), (vel_in, vel), (smooth_in, smooth), (mass_in, mass)], sem
    )
    lane = lax.broadcasted_iota(jnp.int32, (1, WIDTH), 1)
    for c in range(CELLS):
        full[c : c + 1, :] = (lane < occ[c]).astype(F32)
    for copy in copies:
        copy.wait()
    place = [pos[k] - 0.5 for k in range(3)]
    m = jnp.where(full[...] > 0.0, mass[...], 0.0)
    h = smooth[...]
    put(own, place + [h, m] + [vel[k] for k in range(3)], 0, CELLS, CELL)
    blank = jnp.zeros((CELL, WIDTH), F32)
    wide = jnp.full((1, WIDTH), 0.5, F32)
    set_block(own, CELLS, CELL, jnp.concatenate([blank[:3], wide, blank[:4]], 0))
    before, after = pair_terms(*place, h, m)
    put(first, before, 0, CELLS, CELL)
    put(second, after, 0, CELLS, CELL)
    before, after = pair_terms(*[blank[:1]] * 3, wide, blank[:1])
    set_block(first, CELLS, CELL, jnp.concatenate(before, 0))
    set_block(second, CELLS, CELL, jnp.concatenate(after, 0))

    def cell_step(c, _):
        cells[c] = block(own, c, CELL)
        return 0

    lax.fori_loop(0, CELLS, cell_step, 0, unroll=8)

    def peer_step(e, _):
        for s in range(SLOTS):
            cell = cells[pair[e, s], 0:ROWS]
            for h in range(2):
                at = (h * SLOTS + s) * ROWS
                out[e, at : at + ROWS] = half(cell, h)
        return 0

    lax.fori_loop(0, PEERS, peer_step, 0)


def prepare(occ, pair, pos, vel, smooth, mass):
    rows = jax.ShapeDtypeStruct((2, (CELLS + 1) * CELL, 128), F32)
    plane = pltpu.VMEM((CELLS, WIDTH), F32)
    return pl.pallas_call(
        prepare_kernel,
        in_specs=[SM] * 2 + [ANYWHERE] * 4,
        out_specs=[VM] * 4,
        out_shape=[rows] * 3 + [jax.ShapeDtypeStruct((PEERS, 2 * SLOTS * ROWS, 128), F32)],
        scratch_shapes=[
            pltpu.VMEM((3, CELLS, WIDTH), F32),
            pltpu.VMEM((3, CELLS, WIDTH), F32),
            plane,
            plane,
            plane,
            pltpu.VMEM((CELLS, CELL, WIDTH), F32),
            pltpu.SemaphoreType.DMA((4,)),
        ],
        compiler_params=pltpu.CompilerParams(vmem_limit_bytes=60 * 2**20),
    )(occ, pair, pos, vel, smooth, mass)


def fold(total, own, out, carried):
    mine = sum(planes_of(total, range(CELL), 0, CELLS, CELL))
    mass = planes_of(own, [4], 0, CELLS, CELL)[0]
    mine = mine * inverse_mass(mass)
    out[...] = mine if carried is None else carried[...] + mine


def make_face_first(faces, face_first):
    planes = planes_of(faces, range(ROWS), 0, 2 * FACE, CELL)
    put(face_first, pair_terms(*planes)[0], 0, 2 * FACE, CELL)


def face_cell(n):
    return jnp.where(n < FACE, n, CELLS - 2 * FACE + n)


def in_turns(trips, item, last, products, weights, slot_a, slot_b):
    products(item(0), slot_a)

    def step(i, _):
        products(item(2 * i + 1), slot_b)
        weights(item(2 * i), slot_a)
        after = 2 * i + 2
        products(item(after if last is None else jnp.minimum(after, last - 1)), slot_a)
        weights(item(2 * i + 1), slot_b)
        return 0

    lax.fori_loop(0, trips, step, 0)


def cell_list(plan, part, kind):
    at = kind + part * len(LOCAL_ROWS)
    start = LOCAL_AT + at * LOCAL_LIST + 2
    return plan[at], lambda n: plan[start + n]


def local_density_kernel(part, plan, own, first, second, *rest):
    if part:
        faces, carried, rho, total, face_first, *slots = rest
    else:
        carried = None
        rho, total, *slots = rest
    slot_a, slot_b = slots[:6], slots[6:]
    total[...] = jnp.zeros_like(total)

    def products(count, c, held):
        left = first_operand(block(first, c, CELL))
        after = jnp.minimum(c + 1, CELLS)
        held[4][...] = support_columns(line(own, c, CELL, 3))
        density_products(left, second_operands(block(second, c, CELL), True), count, *held[0:2])
        density_products(
            left, second_operands(block(second, after, CELL), True), count, *held[2:4]
        )

    def weights(count, c, held):
        after = jnp.minimum(c + 1, CELLS)
        row, other = line(own, c, CELL, 3), line(own, after, CELL, 3)
        own_sum = density_weights(count, *held[0:2], held[4], row, True)
        there, here = density_weights(count, *held[2:4], held[4], other, False)
        add_block(total, c, CELL, own_sum + here)
        add_block(total, after, CELL, there)

    for kind, count in enumerate(LOCAL_ROWS):
        trips, item = cell_list(plan, part, kind)
        in_turns(
            trips, item, None, functools.partial(products, count),
            functools.partial(weights, count), slot_a, slot_b,
        )

    if part:
        make_face_first(faces, face_first)

        def face_products(i, held):
            for k in range(2):
                n = 2 * i + k
                left = first_operand(block(face_first, n, CELL))
                operands = second_operands(block(second, face_cell(n), CELL), True)
                held[4 + k][...] = support_columns(line(faces, n, CELL, 3))
                density_products(left, operands, WIDTH, *held[2 * k : 2 * k + 2])

        def face_weights(i, held):
            for k in range(2):
                c = face_cell(2 * i + k)
                added = density_weights(
                    WIDTH, *held[2 * k : 2 * k + 2], held[4 + k], line(own, c, CELL, 3), True
                )
                add_block(total, c, CELL, added)

        in_turns(FACE // 2, lambda i: i, FACE, face_products, face_weights, slot_a, slot_b)

    fold(total, own, rho, carried)


DENSITY_SLOT = [pltpu.VMEM((WIDTH, WIDTH), F32)] * 4 + [pltpu.VMEM((WIDTH, 128), F32)] * 2


def local_density(part, plan, own, first, second, *rest):
    return pl.pallas_call(
        functools.partial(local_density_kernel, part),
        in_specs=[SM] + [VM] * (3 + len(rest)),
        out_specs=VM,
        out_shape=jax.ShapeDtypeStruct((CELLS, WIDTH), F32),
        scratch_shapes=[pltpu.VMEM((2, (CELLS + 1) * CELL, 128), F32)]
        + [pltpu.VMEM((2, 2 * FACE * CELL, 128), F32)] * part
        + DENSITY_SLOT * 2,
        cost_estimate=pl.CostEstimate(
            flops=64 * 65536 * 60, bytes_accessed=2 * 2**20, transcendentals=0
        ),
        compiler_params=params(),
    )(plan, own, first, second, *rest)


def pair_list(plan, kind):
    base = 2 * len(LOCAL_ROWS) + 2 * kind
    at = CROSS_AT + 2 * kind * CROSS_LIST + plan[base + 1]

    def item(n):
        return [(plan[at + 2 * n + k], plan[at + CROSS_LIST + 2 * n + k]) for k in range(2)]

    return plan[base], item


def live_rows(fill, e):
    row = lax.broadcasted_iota(jnp.int32, (SLOTS, WIDTH), 0)
    return row < fill[0, e]


def cross_density_kernel(
    fill, plan, own, first, listed, carried, rho, back, total, theirs, there_of, *slots
):
    slot_a, slot_b = slots[:6], slots[6:]
    total[...] = jnp.zeros_like(total)

    def peer_step(e, _):
        after = pair_terms(*listed_planes(listed, e, range(ROWS), ROWS))[1]
        put(theirs, after, e * SLOTS * CELL, SLOTS, CELL)
        return 0

    lax.fori_loop(0, PEERS, peer_step, 0, unroll=2)

    def products(count, pairs, held):
        for k, (slot, c) in enumerate(pairs):
            left = first_operand(block(first, c, CELL))
            held[4 + k][...] = support_columns(line(own, c, CELL, 3))
            operands = second_operands(block(theirs, slot, CELL), True)
            density_products(left, operands, count, *held[2 * k : 2 * k + 2])

    def weights(count, pairs, held):
        for k, (slot, c) in enumerate(pairs):
            support = listed_support(listed, slot)
            there, here = density_weights(
                count, *held[2 * k : 2 * k + 2], held[4 + k], support, False
            )
            add_block(total, c, CELL, here)
            set_block(there_of, slot, CELL, there)

    for kind, count in enumerate(CROSS_ROWS):
        trips, item = pair_list(plan, kind)
        in_turns(
            trips, item, None, functools.partial(products, count),
            functools.partial(weights, count), slot_a, slot_b,
        )

    def back_step(e, _):
        summed = sum(planes_of(there_of, range(CELL), e * SLOTS * CELL, SLOTS, CELL))
        mass = listed_planes(listed, e, [4], ROWS)[0]
        back[e] = jnp.where(live_rows(fill, e), summed * inverse_mass(mass), 0.0)
        return 0

    lax.fori_loop(0, PEERS, back_step, 0, unroll=2)
    fold(total, own, rho, carried)


def cross_density(fill, plan, own, first, listed, carried):
    return pl.pallas_call(
        cross_density_kernel,
        in_specs=[SM, SM] + [VM] * 4,
        out_specs=[VM, VM],
        out_shape=[
            jax.ShapeDtypeStruct((CELLS, WIDTH), F32),
            jax.ShapeDtypeStruct((PEERS, SLOTS, WIDTH), F32),
        ],
        scratch_shapes=[
            pltpu.VMEM((2, (CELLS + 1) * CELL, 128), F32),
            pltpu.VMEM((2, LISTED * CELL, 128), F32),
            pltpu.VMEM((2, LISTED * CELL, 128), F32),
        ]
        + DENSITY_SLOT * 2,
        cost_estimate=pl.CostEstimate(
            flops=80 * 65536 * 60, bytes_accessed=2 * 2**20, transcendentals=0
        ),
        compiler_params=params(),
    )(fill, plan, own, first, listed, carried)


def pressure_kernel(
    pair, near, returned, energy_in, own, density, term, out, energy, sum_of, moving, sem
):
    copies = fetch([(energy_in, energy)], sem)
    sum_of[...] = near[...]

    def peer_step(e, _):
        for s in range(SLOTS):
            sum_of[pl.ds(pair[e, s], 1), :] += returned[e, s : s + 1]
        return 0

    lax.fori_loop(0, PEERS, peer_step, 0)
    copies[0].wait()
    full = planes_of(own, [4], 0, CELLS, CELL)[0] > 0.0
    rho = jnp.where(full, sum_of[...], 0.0)
    density[...] = rho
    term[...] = jnp.where(full, GAMMA_LESS * energy[...] / jnp.where(full, rho, 1.0), 0.0)

    def cell_step(c, _):
        moving[c] = jnp.concatenate(
            [line(own, c, CELL, k) for k in (5, 6, 7)] + [term[pl.ds(c, 1), :]], 0
        )
        return 0

    lax.fori_loop(0, CELLS, cell_step, 0, unroll=8)

    def send_step(e, _):
        for s in range(SLOTS):
            cell = moving[pair[e, s]]
            for h in range(2):
                at = (h * SLOTS + s) * MOVING
                out[e, at : at + MOVING] = half(cell, h)
        return 0

    lax.fori_loop(0, PEERS, send_step, 0)


def pressure(pair, near, returned, energy, own):
    plane = jax.ShapeDtypeStruct((CELLS, WIDTH), F32)
    return pl.pallas_call(
        pressure_kernel,
        in_specs=[SM, VM, VM, ANYWHERE, VM],
        out_specs=[VM, VM, VM],
        out_shape=[
            plane,
            plane,
            jax.ShapeDtypeStruct((PEERS, 2 * SLOTS * MOVING, 128), F32),
        ],
        scratch_shapes=[
            pltpu.VMEM((CELLS, WIDTH), F32),
            pltpu.VMEM((CELLS, WIDTH), F32),
            pltpu.VMEM((CELLS, MOVING, WIDTH), F32),
            pltpu.SemaphoreType.DMA((1,)),
        ],
        compiler_params=params(),
    )(pair, near, returned, energy, own)


def force_terms(place, m, speed, term):
    mp = m * term
    turned = sum(a * b for a, b in zip(place, speed))
    return (
        [m] + [m * a for a in place] + [mp] + [mp * a for a in place]
        + [m * a for a in speed] + [m * turned]
    )


def forces_of(sums, place, speed, term):
    lean = [a * sums[0] - b for a, b in zip(place, sums[1:4])]
    acc = [term * a + (b * sums[4] - c) for a, b, c in zip(lean, place, sums[5:8])]
    mixed = sum(a * b - c * d for a, b, c, d in zip(speed, lean, place, sums[8:11]))
    return [G_SCALE * a for a in acc] + [-G_SCALE * term * (mixed + sums[11])]


def force_operand(ref, index):
    high, low = split2(block(ref, index, SUMS))
    return jnp.concatenate([high, low], 0)


def own_terms(own, term, rows):
    planes = planes_of(own, range(CELL), 0, CELLS, CELL)
    terms = force_terms(planes[0:3], planes[4], planes[5:8], term[...])
    put(rows, terms, 0, CELLS, SUMS)
    put(rows, [jnp.zeros((CELLS, WIDTH), F32)] * 4, 12, CELLS, SUMS)
    set_block(rows, CELLS, SUMS, jnp.zeros((SUMS, WIDTH), F32))


def slopes(s_ref, high, low, columns, row, count):
    for start in range(0, count, CHUNK):
        s = jnp.maximum(s_ref[start : start + CHUNK], TINY)
        dist = s * lax.rsqrt(s)
        wide = columns[start : start + CHUNK]
        support = jnp.concatenate([wide, wide], 1) + row
        d = jnp.maximum(support - dist, 0.0)
        e = pl.reciprocal(support * support, approx=True)
        x = e * d
        g = (x * x) * (x * e)
        top = g.astype(BF)
        high[start : start + CHUNK] = top
        low[start : start + CHUNK] = (g - top.astype(F32)).astype(BF)


def distances(left, rows, count, s_ref):
    s_ref[0:count] = jnp.dot(
        left[:count], second_operands(rows, False), preferred_element_type=F32
    )


def to_seconds(rows, count, high, low):
    part = rows[:, :count]
    top = lax.dot_general(part, high[0:count], NN, preferred_element_type=F32)
    both = top + lax.dot_general(part, low[0:count], NN, preferred_element_type=F32)
    return both[:SUMS] + both[SUMS:]


def to_firsts(rows, count, high, low):
    top = lax.dot_general(rows, high[0:count], NT, preferred_element_type=F32)
    both = top + lax.dot_general(rows, low[0:count], NT, preferred_element_type=F32)
    return both[:SUMS] + both[SUMS:]


def in_three_turns(trips, item, last, products, tiles, sums, slot_a, slot_b):
    products(item(0), slot_a)

    def step(i, _):
        products(item(2 * i + 1), slot_b)
        sums(item(2 * i - 2), slot_a)
        tiles(item(2 * i), slot_a)
        after = 2 * i + 2
        products(item(after if last is None else jnp.minimum(after, last - 1)), slot_a)
        sums(item(2 * i - 1), slot_b)
        tiles(item(2 * i + 1), slot_b)
        return 0

    lax.fori_loop(0, trips, step, 0)
    sums(item(2 * trips - 2), slot_a)
    sums(item(2 * trips - 1), slot_b)


def clear(slots):
    for held in slots:
        held[...] = jnp.zeros_like(held)


def add_forces(total, own, term, out, carried):
    planes = planes_of(own, range(CELL), 0, CELLS, CELL)
    sums = planes_of(total, range(12), 0, CELLS, SUMS)
    for k, force in enumerate(forces_of(sums, planes[0:3], planes[5:8], term[...])):
        out[k] = force if carried is None else carried[k] + force


def local_force_kernel(part, plan, own, first, second, term, *rest):
    if part:
        faces, face_terms, carried, out, rows, total, face_rows, face_first, *slots = rest
    else:
        carried = None
        out, rows, total, *slots = rest
    slot_a, slot_b = slots[:7], slots[7:]
    own_terms(own, term, rows)
    total[...] = jnp.zeros_like(total)
    clear([held[k] for held in (slot_a, slot_b) for k in (2, 3, 5, 6)])

    def products(count, c, held):
        left = first_operand(block(first, c, CELL))
        held[0][...] = support_columns(line(own, c, CELL, 3))
        distances(left, block(second, c, CELL), count, held[1])
        distances(left, block(second, jnp.minimum(c + 1, CELLS), CELL), count, held[4])

    def tiles(count, c, held):
        other = line(own, jnp.minimum(c + 1, CELLS), CELL, 3)
        slopes(*held[1:4], held[0], line(own, c, CELL, 3), count)
        slopes(*held[4:7], held[0], other, count)

    def sums(count, c, held):
        after = jnp.minimum(c + 1, CELLS)
        mine, other = force_operand(rows, c), force_operand(rows, after)
        added = to_firsts(other, count, *held[5:7])
        if count < WIDTH:
            added = jnp.concatenate([added, jnp.zeros((SUMS, WIDTH - count), F32)], 1)
        add_block(total, c, SUMS, to_seconds(mine, count, *held[2:4]) + added)
        add_block(total, after, SUMS, to_seconds(mine, count, *held[5:7]))

    for kind, count in enumerate(LOCAL_ROWS):
        trips, item = cell_list(plan, part, kind)
        in_three_turns(
            trips, item, None, functools.partial(products, count),
            functools.partial(tiles, count), functools.partial(sums, count), slot_a, slot_b,
        )

    if part:
        make_face_first(faces, face_first)
        planes = planes_of(faces, range(CELL), 0, 2 * FACE, CELL)
        terms = force_terms(planes[0:3], planes[4], planes[5:8], face_terms[...])
        blank = jnp.zeros((2 * FACE, WIDTH), F32)
        put(face_rows, terms + [blank] * 4, 0, 2 * FACE, SUMS)

        def face_products(i, held):
            for k in range(2):
                n = 2 * i + k
                left = first_operand(block(face_first, n, CELL))
                distances(left, block(second, face_cell(n), CELL), WIDTH, held[1 + 3 * k])

        def face_tiles(i, held):
            for k in range(2):
                n = 2 * i + k
                columns = support_columns(line(faces, n, CELL, 3))
                slopes(
                    *held[1 + 3 * k : 4 + 3 * k], columns, line(own, face_cell(n), CELL, 3), WIDTH
                )

        def face_sums(i, held):
            for k in range(2):
                n = jnp.maximum(2 * i, 0) + k
                c = jnp.where(i < 0, CELLS, face_cell(n))
                theirs = force_operand(face_rows, n)
                add_block(
                    total, c, SUMS, to_seconds(theirs, WIDTH, *held[2 + 3 * k : 4 + 3 * k])
                )

        in_three_turns(
            FACE // 2, lambda i: i, FACE, face_products, face_tiles, face_sums, slot_a, slot_b
        )

    add_forces(total, own, term, out, carried)


FORCE_PAIR = [
    pltpu.VMEM((WIDTH, WIDTH), F32),
    pltpu.VMEM((WIDTH, WIDTH), BF),
    pltpu.VMEM((WIDTH, WIDTH), BF),
]
FORCE_SLOT = [pltpu.VMEM((WIDTH, 128), F32)] + FORCE_PAIR * 2


def local_force(part, plan, own, first, second, term, *rest):
    scratch = [
        pltpu.VMEM((2, (CELLS + 1) * SUMS, 128), F32),
        pltpu.VMEM((2, (CELLS + 1) * SUMS, 128), F32),
    ]
    if part:
        scratch.append(pltpu.VMEM((2, 2 * FACE * SUMS, 128), F32))
        scratch.append(pltpu.VMEM((2, 2 * FACE * CELL, 128), F32))
    return pl.pallas_call(
        functools.partial(local_force_kernel, part),
        in_specs=[SM] + [VM] * (4 + len(rest)),
        out_specs=VM,
        out_shape=jax.ShapeDtypeStruct((4, CELLS, WIDTH), F32),
        scratch_shapes=scratch + FORCE_SLOT * 2,
        cost_estimate=pl.CostEstimate(
            flops=64 * 65536 * 80, bytes_accessed=2 * 2**20, transcendentals=0
        ),
        compiler_params=params(),
    )(plan, own, first, second, term, *rest)


def cross_force_kernel(
    fill, plan, own, first, term, listed, arrived, carried, out, back,
    rows, total, theirs, their_rows, sums_of, *slots
):
    slot_a, slot_b = slots[:8], slots[8:]
    own_terms(own, term, rows)
    total[...] = jnp.zeros_like(total)
    clear([held[k] for held in (slot_a, slot_b) for k in (3, 4, 6, 7)])

    def peer_step(e, _):
        planes = listed_planes(listed, e, range(ROWS), ROWS)
        put(theirs, pair_terms(*planes)[1], e * SLOTS * CELL, SLOTS, CELL)
        *speed, pressed = listed_planes(arrived, e, range(MOVING), MOVING)
        terms = force_terms(planes[0:3], planes[4], speed, pressed)
        blank = jnp.zeros((SLOTS, WIDTH), F32)
        put(their_rows, terms + [blank] * 4, e * SLOTS * SUMS, SLOTS, SUMS)
        return 0

    lax.fori_loop(0, PEERS, peer_step, 0)

    def products(count, pairs, held):
        for k, (slot, c) in enumerate(pairs):
            held[k][...] = support_columns(line(own, c, CELL, 3))
            left = first_operand(block(first, c, CELL))
            distances(left, block(theirs, slot, CELL), count, held[2 + 3 * k])

    def tiles(count, pairs, held):
        for k, (slot, c) in enumerate(pairs):
            support = listed_support(listed, slot)
            slopes(*held[2 + 3 * k : 5 + 3 * k], held[k], support, count)

    def sums(count, pairs, held):
        for k, (slot, c) in enumerate(pairs):
            tile = held[3 + 3 * k : 5 + 3 * k]
            set_block(sums_of, slot, SUMS, to_seconds(force_operand(rows, c), count, *tile))
            added = to_firsts(force_operand(their_rows, slot), count, *tile)
            if count < WIDTH:
                added = jnp.concatenate([added, jnp.zeros((SUMS, WIDTH - count), F32)], 1)
            add_block(total, c, SUMS, added)

    for kind, count in enumerate(CROSS_ROWS):
        trips, item = pair_list(plan, kind)
        in_three_turns(
            trips, item, None, functools.partial(products, count),
            functools.partial(tiles, count), functools.partial(sums, count), slot_a, slot_b,
        )

    def back_step(e, _):
        planes = listed_planes(listed, e, range(3), ROWS)
        *speed, pressed = listed_planes(arrived, e, range(MOVING), MOVING)
        summed = planes_of(sums_of, range(12), e * SLOTS * SUMS, SLOTS, SUMS)
        live = live_rows(fill, e)
        for k, force in enumerate(forces_of(summed, planes, speed, pressed)):
            force = jnp.where(live, force, 0.0)
            for h in range(2):
                at = pl.ds(h * SLOTS * MOVING + k, SLOTS, stride=MOVING)
                back[e, at, :] = half(force, h)
        return 0

    lax.fori_loop(0, PEERS, back_step, 0)
    add_forces(total, own, term, out, carried)


def cross_force(fill, plan, own, first, term, listed, arrived, carried):
    return pl.pallas_call(
        cross_force_kernel,
        in_specs=[SM, SM] + [VM] * 6,
        out_specs=[VM, VM],
        out_shape=[
            jax.ShapeDtypeStruct((4, CELLS, WIDTH), F32),
            jax.ShapeDtypeStruct((PEERS, 2 * SLOTS * MOVING, 128), F32),
        ],
        scratch_shapes=[
            pltpu.VMEM((2, (CELLS + 1) * SUMS, 128), F32),
            pltpu.VMEM((2, (CELLS + 1) * SUMS, 128), F32),
            pltpu.VMEM((2, LISTED * CELL, 128), F32),
            pltpu.VMEM((2, LISTED * SUMS, 128), F32),
            pltpu.VMEM((2, LISTED * SUMS, 128), F32),
        ]
        + (FORCE_SLOT[:1] * 2 + FORCE_PAIR * 2) * 2,
        cost_estimate=pl.CostEstimate(
            flops=80 * 65536 * 80, bytes_accessed=2 * 2**20, transcendentals=0
        ),
        compiler_params=params(),
    )(fill, plan, own, first, term, listed, arrived, carried)


def finish_kernel(pair, near, returned, active_in, own, out, total, active, gate, sem):
    copies = fetch([(active_in, active)], sem)
    total[...] = jnp.zeros_like(total)

    def peer_step(e, _):
        for s in range(SLOTS):
            at = s * MOVING
            total[pair[e, s]] += both(
                lambda h: returned[
                    e, h * SLOTS * MOVING + at : h * SLOTS * MOVING + at + MOVING
                ]
            )
        return 0

    lax.fori_loop(0, PEERS, peer_step, 0)
    copies[0].wait()
    full = planes_of(own, [4], 0, CELLS, CELL)[0] > 0.0
    gate[...] = jnp.where(full, active[...].astype(F32), 0.0)

    def cell_step(c, _):
        one = pl.ds(c, 1)
        open_to = gate[one, :]
        for k in range(4):
            out[k, one, :] = (near[k, one, :] + total[c, k : k + 1]) * open_to
        return 0

    lax.fori_loop(0, CELLS, cell_step, 0, unroll=8)


def finish(pair, near, returned, active, own):
    return pl.pallas_call(
        finish_kernel,
        in_specs=[SM, VM, VM, ANYWHERE, VM],
        out_specs=VM,
        out_shape=jax.ShapeDtypeStruct((4, CELLS, WIDTH), F32),
        scratch_shapes=[
            pltpu.VMEM((CELLS, 4, WIDTH), F32),
            pltpu.VMEM((CELLS, WIDTH), jnp.int32),
            pltpu.VMEM((CELLS, WIDTH), F32),
            pltpu.SemaphoreType.DMA((1,)),
        ],
        compiler_params=params(),
    )(pair, near, returned, active, own)


def to_peers(block):
    return lax.all_to_all(block, "dev", split_axis=0, concat_axis=0, tiled=True)


def with_neighbours(rows, size):
    count = lax.axis_size("region")
    up = [(i, (i + 1) % count) for i in range(count)]
    down = [(i, (i - 1) % count) for i in range(count)]
    return jnp.concatenate(
        [
            lax.ppermute(rows[..., (CELLS - FACE) * size : CELLS * size, :], "region", up),
            lax.ppermute(rows[..., : FACE * size, :], "region", down),
        ],
        -2,
    )


def local(
    positions, velocity, smoothing, masses, energy, occupancy, active, send_cells, send_fill,
    pair_cell,
):
    pair = pair_cell[0]
    own, first, second, listed = prepare(
        occupancy, pair, positions, velocity, smoothing, masses
    )
    arrived = to_peers(listed)
    plan = make_plan(occupancy, send_fill, send_cells[0], own)
    faces = with_neighbours(own, CELL)
    rho = local_density(0, plan, own, first, second)
    rho, back = cross_density(send_fill, plan, own, first, arrived, rho)
    returned = to_peers(back)
    rho = local_density(1, plan, own, first, second, faces, rho)
    density, term, leaving = pressure(pair, rho, returned, energy, own)
    arrived_moving = to_peers(leaving)
    face_terms = with_neighbours(term, 1)
    sums = local_force(0, plan, own, first, second, term)
    sums, force_back = cross_force(
        send_fill, plan, own, first, term, arrived, arrived_moving, sums
    )
    returned_force = to_peers(force_back)
    sums = local_force(1, plan, own, first, second, term, faces, face_terms, sums)
    forces = finish(pair, sums, returned_force, active, own)
    return (density, forces)


def solution(mesh):
    cells = P(("region", "dev"), None)
    vectors = P(None, ("region", "dev"), None)
    lists = P(("region", "dev"), None, None)
    in_specs = (
        vectors, vectors, cells, cells, cells, P(("region", "dev")), cells, lists, cells, lists,
    )
    return jax.shard_map(
        local, mesh=mesh, in_specs=in_specs, out_specs=(cells, vectors), check_vma=False
    )
```

```python
import functools
import math

import jax
import jax.numpy as jnp
from jax import lax
from jax.experimental import pallas as pl
from jax.experimental.pallas import tpu as pltpu
from jax.sharding import PartitionSpec as P

BF = jnp.bfloat16
F32 = jnp.float32
FACE = 4
CELLS = 64
WIDTH = 256
PEERS = 16
SLOTS = 16
LISTED = PEERS * SLOTS
GAMMA_LESS = 2.0 / 3.0
W_SCALE = 84.0 / math.pi
G_SCALE = 6720.0 / math.pi
TINY = 1e-14
EMPTY = 1e8
CHUNK = 32
CELL = 8
SUMS = 16
NN = (((1,), (0,)), ((), ()))
NT = (((1,), (1,)), ((), ()))
VM = pl.BlockSpec(memory_space=pltpu.VMEM)
SM = pl.BlockSpec(memory_space=pltpu.SMEM)
ROWS = 5
MOVING = 4
SPLIT = 40
SIZES = (160, 192, 224, 256)
KINDS = len(SIZES)
UNIT = 4
LOCAL_AT = 16
LOCAL_LEAD = 2
LOCAL_LIST = CELLS + 8
CROSS_AT = LOCAL_AT + 2 * LOCAL_LIST
CROSS_LEAD = 4
CROSS_LIST = LISTED + 16
PLAN = CROSS_AT + CROSS_LIST
PACK = 128
ANYWHERE = pl.BlockSpec(memory_space=pl.ANY)


def params():
    return pltpu.CompilerParams(vmem_limit_bytes=50 * 2**20)


def split2(x):
    a = x.astype(BF)
    return a, (x - a.astype(F32)).astype(BF)


def split3(x):
    a = x.astype(BF).astype(F32)
    rest = x - a
    b = rest.astype(BF).astype(F32)
    return a, b, rest - b


def pair_terms(x, y, z, h, m):
    norm = 4.0 * (x * x + y * y + z * z)
    root = lax.rsqrt(jnp.where(m > 0.0, m, 1.0))
    mu = jnp.where(m > 0.0, root * lax.rsqrt(root), EMPTY)
    one = jnp.ones_like(x)
    first = [-8.0 * x, -8.0 * y, -8.0 * z, norm, one, h * h * mu, 2.0 * h * mu, mu]
    second = [x, y, z, one, norm, mu, h * mu, h * h * mu]
    return first, second


def both(read):
    return jnp.concatenate([read(0), read(1)], -1)


def half(value, h):
    return value[..., 128 * h : 128 * (h + 1)]


def put(ref, planes, start, count, stride):
    for k, plane in enumerate(planes):
        for h in range(2):
            ref[h, pl.ds(start + k, count, stride=stride), :] = half(plane, h)


def planes_of(ref, ids, start, count, stride):
    return [both(lambda h: ref[h, pl.ds(start + k, count, stride=stride), :]) for k in ids]


def rows_at(index, size):
    return pl.ds(pl.multiple_of(index * size, size), size)


def block(ref, index, size):
    return both(lambda h: ref[h, rows_at(index, size), :])


def set_block(ref, index, size, value):
    for h in range(2):
        ref[h, rows_at(index, size), :] = half(value, h)


def add_block(ref, index, size, value):
    for h in range(2):
        ref[h, rows_at(index, size), :] += half(value, h)


def line(ref, index, size, k):
    return both(lambda h: ref[h, pl.ds(index * size + k, 1), :])


def listed_planes(listed, e, part, ids, size):
    step = SLOTS * size
    start = 8 * part * size
    return [
        both(lambda h: listed[e, pl.ds(h * step + start + k, 8, stride=size), :]) for k in ids
    ]


def listed_support(listed, slot):
    at = (slot % SLOTS) * ROWS + 3
    return both(lambda h: listed[slot // SLOTS, pl.ds(h * SLOTS * ROWS + at, 1), :])


def first_operand(rows):
    a1, a2, a3 = split3(rows)
    return jnp.concatenate([a1, a1, a2, a2, a1, a3, jnp.zeros((80, WIDTH), F32)], 0).T.astype(BF)


def second_operands(rows, both):
    b1, b2, b3 = split3(rows)
    stacked = jnp.concatenate([b1, b2, b1, b2, b3, b1, jnp.zeros((80, WIDTH), F32)], 0)
    part = lax.broadcasted_iota(jnp.int32, stacked.shape, 0) % 8
    near = jnp.where(part < 5, stacked, 0.0).astype(BF)
    if not both:
        return near
    return near, jnp.where(part >= 5, stacked, 0.0).astype(BF)


def support_columns(row):
    return jnp.broadcast_to(row, (128, WIDTH)).T


def density_products(left, operands, s_ref, mix_ref):
    s_ref[...] = jnp.dot(left, operands[0], preferred_element_type=F32)
    mix_ref[...] = jnp.dot(left, operands[1], preferred_element_type=F32)


def density_weights(count, s_ref, mix_ref, columns, row, one_sided):
    second = jnp.zeros((8, WIDTH), F32)
    firsts = []
    for start in range(0, count, CHUNK):
        s = jnp.maximum(s_ref[start : start + CHUNK], TINY)
        dist = s * lax.rsqrt(s)
        wide = columns[start : start + CHUNK]
        support = jnp.concatenate([wide, wide], 1) + row
        d = jnp.maximum(support - dist, 0.0)
        x = pl.reciprocal(mix_ref[start : start + CHUNK], approx=True) * d
        x = x * x
        x = x * x
        w = x * (support + 4.0 * dist)
        for k in range(CHUNK // 8):
            second = second + w[8 * k : 8 * k + 8]
        if not one_sided:
            firsts.append(w[:, :128] + w[:, 128:])
    if one_sided:
        return second
    if count < WIDTH:
        firsts.append(jnp.zeros((WIDTH - count, 128), F32))
    turned = jnp.concatenate(firsts, 0).T
    first = turned[:8]
    for k in range(1, 16):
        first = first + turned[8 * k : 8 * k + 8]
    return second, first


def inverse_mass(m):
    return jnp.where(m > 0.0, W_SCALE / jnp.where(m > 0.0, m, 1.0), 0.0)


def kind_of(size):
    return sum((size > rows).astype(jnp.int32) for rows in SIZES[:-1])


def plan_kernel(occ, fill, cells, _, plan, next_at):
    for k in range(3 * KINDS):
        next_at[k] = 0

    def local_count(c, _):
        kind = kind_of(occ[c]) + jnp.where(c >= SPLIT, KINDS, 0)
        next_at[kind] = next_at[kind] + 1
        return 0

    lax.fori_loop(0, CELLS, local_count, 0)

    def over_pairs(visit):
        def peer_step(e, _):
            def slot_step(s, _):
                cell = cells[e, s]
                visit(2 * KINDS + kind_of(occ[cell]), (e * SLOTS + s) * PACK + cell)
                return 0

            return lax.fori_loop(0, fill[0, e], slot_step, 0)

        lax.fori_loop(0, PEERS, peer_step, 0)

    def pair_count(kind, _):
        next_at[kind] = next_at[kind] + 1

    over_pairs(pair_count)

    unused = jnp.int32(0)
    for e in range(PEERS):
        unused = jnp.where(fill[0, e] == 0, e * SLOTS, unused)

    for group, (start, lead, unit, blank) in enumerate(
        [
            (LOCAL_AT, LOCAL_LEAD, 2, CELLS),
            (LOCAL_AT + LOCAL_LIST, LOCAL_LEAD, 2, CELLS),
            (CROSS_AT, CROSS_LEAD, UNIT, unused * PACK + CELLS),
        ]
    ):
        total = jnp.int32(0)
        done = jnp.int32(0)
        for k in range(KINDS):
            at = group * KINDS + k
            count = next_at[at]
            next_at[at] = start + lead + total
            total = total + count
            upto = (total + (unit - 1 if k == KINDS - 1 else 0)) // unit
            plan[at] = upto - done
            done = upto
        for k in range(lead):
            plan[start + k] = blank
        for k in range(unit + 1):
            plan[start + lead + total + k] = blank

    def place(kind, value):
        at = next_at[kind]
        plan[at] = value
        next_at[kind] = at + 1

    def local_place(c, _):
        place(kind_of(occ[c]) + jnp.where(c >= SPLIT, KINDS, 0), c)
        return 0

    lax.fori_loop(0, CELLS, local_place, 0)
    over_pairs(place)


def make_plan(occ, fill, cells, own):
    return pl.pallas_call(
        plan_kernel,
        in_specs=[SM] * 3 + [ANYWHERE],
        out_specs=SM,
        out_shape=jax.ShapeDtypeStruct((PLAN,), jnp.int32),
        scratch_shapes=[pltpu.SMEM((3 * KINDS,), jnp.int32)],
    )(occ, fill, cells, own)


def fetch(pairs, sem):
    copies = [
        pltpu.make_async_copy(source, target, sem.at[k])
        for k, (source, target) in enumerate(pairs)
    ]
    for copy in copies:
        copy.start()
    return copies


def prepare_kernel(
    occ, pair, pos_in, vel_in, smooth_in, mass_in, own, first, second, out,
    pos, vel, smooth, mass, full, cells, sem,
):
    copies = fetch(
        [(pos_in, pos), (vel_in, vel), (smooth_in, smooth), (mass_in, mass)], sem
    )
    lane = lax.broadcasted_iota(jnp.int32, (1, WIDTH), 1)
    for c in range(CELLS):
        full[c : c + 1, :] = (lane < occ[c]).astype(F32)
    for copy in copies:
        copy.wait()
    place = [pos[k] - 0.5 for k in range(3)]
    m = jnp.where(full[...] > 0.0, mass[...], 0.0)
    h = smooth[...]
    put(own, place + [h, m] + [vel[k] for k in range(3)], 0, CELLS, CELL)
    blank = jnp.zeros((CELL, WIDTH), F32)
    wide = jnp.full((1, WIDTH), 0.5, F32)
    set_block(own, CELLS, CELL, jnp.concatenate([blank[:3], wide, blank[:4]], 0))
    before, after = pair_terms(*place, h, m)
    put(first, before, 0, CELLS, CELL)
    put(second, after, 0, CELLS, CELL)
    before, after = pair_terms(*[blank[:1]] * 3, wide, blank[:1])
    set_block(first, CELLS, CELL, jnp.concatenate(before, 0))
    set_block(second, CELLS, CELL, jnp.concatenate(after, 0))

    def cell_step(c, _):
        cells[c] = block(own, c, CELL)
        return 0

    lax.fori_loop(0, CELLS, cell_step, 0, unroll=8)

    def peer_step(e, _):
        for s in range(SLOTS):
            cell = cells[pair[e, s], 0:ROWS]
            for h in range(2):
                at = (h * SLOTS + s) * ROWS
                out[e, at : at + ROWS] = half(cell, h)
        return 0

    lax.fori_loop(0, PEERS, peer_step, 0)


def prepare(occ, pair, pos, vel, smooth, mass):
    rows = jax.ShapeDtypeStruct((2, (CELLS + 1) * CELL, 128), F32)
    plane = pltpu.VMEM((CELLS, WIDTH), F32)
    return pl.pallas_call(
        prepare_kernel,
        in_specs=[SM] * 2 + [ANYWHERE] * 4,
        out_specs=[VM] * 4,
        out_shape=[rows] * 3 + [jax.ShapeDtypeStruct((PEERS, 2 * SLOTS * ROWS, 128), F32)],
        scratch_shapes=[
            pltpu.VMEM((3, CELLS, WIDTH), F32),
            pltpu.VMEM((3, CELLS, WIDTH), F32),
            plane,
            plane,
            plane,
            pltpu.VMEM((CELLS, CELL, WIDTH), F32),
            pltpu.SemaphoreType.DMA((4,)),
        ],
        compiler_params=pltpu.CompilerParams(vmem_limit_bytes=60 * 2**20),
    )(occ, pair, pos, vel, smooth, mass)


def fold(total, own, out, carried):
    mine = sum(planes_of(total, range(CELL), 0, CELLS, CELL))
    mass = planes_of(own, [4], 0, CELLS, CELL)[0]
    mine = mine * inverse_mass(mass)
    out[...] = mine if carried is None else carried[...] + mine


def make_face_first(faces, face_first):
    planes = planes_of(faces, range(ROWS), 0, 2 * FACE, CELL)
    put(face_first, pair_terms(*planes)[0], 0, 2 * FACE, CELL)


def face_cell(n):
    return jnp.where(n < FACE, n, CELLS - 2 * FACE + n)


def in_turns(trips, sizes, item, last, products, weights, slot_a, slot_b):
    products(item(0), slot_a)
    base = 0
    for count, size in zip(trips, sizes):

        def step(i, _, size=size):
            products(item(2 * i + 1), slot_b)
            weights(size, item(2 * i), slot_a)
            after = 2 * i + 2
            products(item(after if last is None else jnp.minimum(after, last - 1)), slot_a)
            weights(size, item(2 * i + 1), slot_b)
            return 0

        lax.fori_loop(base, base + count, step, 0)
        base = base + count


def cell_list(plan, part):
    start = LOCAL_AT + part * LOCAL_LIST + LOCAL_LEAD
    return [plan[part * KINDS + k] for k in range(KINDS)], lambda n: plan[start + n]


def pair_list(plan):
    start = CROSS_AT + CROSS_LEAD

    def item(n):
        entries = [plan[start + 2 * n + k] for k in range(2)]
        return [(entry // PACK, entry % PACK) for entry in entries]

    return [plan[2 * KINDS + k] for k in range(KINDS)], item


def live_parts(fill, visit, other):
    def step(n, _):
        e, part = n // 2, n % 2
        live = fill[0, e] > 8 * part

        @pl.when(live)
        def _():
            visit(e, part)

        if other is not None:

            @pl.when(jnp.logical_not(live))
            def _():
                other(e, part)

        return 0

    lax.fori_loop(0, 2 * PEERS, step, 0)


def local_density_kernel(part, plan, own, first, second, *rest):
    if part:
        faces, carried, rho, total, face_first, *slots = rest
    else:
        carried = None
        rho, total, *slots = rest
    slot_a, slot_b = slots[:6], slots[6:]
    total[...] = jnp.zeros_like(total)

    def products(c, held):
        left = first_operand(block(first, c, CELL))
        after = jnp.minimum(c + 1, CELLS)
        held[4][...] = support_columns(line(own, c, CELL, 3))
        density_products(left, second_operands(block(second, c, CELL), True), *held[0:2])
        density_products(left, second_operands(block(second, after, CELL), True), *held[2:4])

    def weights(count, c, held):
        after = jnp.minimum(c + 1, CELLS)
        row, other = line(own, c, CELL, 3), line(own, after, CELL, 3)
        own_sum = density_weights(count, *held[0:2], held[4], row, True)
        there, here = density_weights(count, *held[2:4], held[4], other, False)
        add_block(total, c, CELL, own_sum + here)
        add_block(total, after, CELL, there)

    trips, item = cell_list(plan, part)
    in_turns(trips, SIZES, item, None, products, weights, slot_a, slot_b)

    if part:
        make_face_first(faces, face_first)

        def face_products(i, held):
            for k in range(2):
                n = 2 * i + k
                left = first_operand(block(face_first, n, CELL))
                operands = second_operands(block(second, face_cell(n), CELL), True)
                held[4 + k][...] = support_columns(line(faces, n, CELL, 3))
                density_products(left, operands, *held[2 * k : 2 * k + 2])

        def face_weights(size, i, held):
            for k in range(2):
                c = face_cell(2 * i + k)
                added = density_weights(
                    size, *held[2 * k : 2 * k + 2], held[4 + k], line(own, c, CELL, 3), True
                )
                add_block(total, c, CELL, added)

        in_turns(
            [FACE // 2], [WIDTH], lambda i: i, FACE, face_products, face_weights, slot_a, slot_b
        )

    fold(total, own, rho, carried)


DENSITY_SLOT = [pltpu.VMEM((WIDTH, WIDTH), F32)] * 4 + [pltpu.VMEM((WIDTH, 128), F32)] * 2


def local_density(part, plan, own, first, second, *rest):
    return pl.pallas_call(
        functools.partial(local_density_kernel, part),
        in_specs=[SM] + [VM] * (3 + len(rest)),
        out_specs=VM,
        out_shape=jax.ShapeDtypeStruct((CELLS, WIDTH), F32),
        scratch_shapes=[pltpu.VMEM((2, (CELLS + 1) * CELL, 128), F32)]
        + [pltpu.VMEM((2, 2 * FACE * CELL, 128), F32)] * part
        + DENSITY_SLOT * 2,
        cost_estimate=pl.CostEstimate(
            flops=64 * 65536 * 60, bytes_accessed=2 * 2**20, transcendentals=0
        ),
        compiler_params=params(),
    )(plan, own, first, second, *rest)


def live_rows(fill, e, part):
    row = lax.broadcasted_iota(jnp.int32, (8, WIDTH), 0)
    return row < fill[0, e] - 8 * part


def cross_density_kernel(
    fill, plan, own, first, listed, carried, rho, back, total, theirs, there_of, *slots
):
    slot_a, slot_b = slots[:6], slots[6:]
    total[...] = jnp.zeros_like(total)

    def make(e, part):
        after = pair_terms(*listed_planes(listed, e, part, range(ROWS), ROWS))[1]
        put(theirs, after, (e * SLOTS + 8 * part) * CELL, 8, CELL)

    live_parts(fill, make, None)

    def products(pairs, held):
        for k, (slot, c) in enumerate(pairs):
            left = first_operand(block(first, c, CELL))
            held[4 + k][...] = support_columns(line(own, c, CELL, 3))
            operands = second_operands(block(theirs, slot, CELL), True)
            density_products(left, operands, *held[2 * k : 2 * k + 2])

    def weights(count, pairs, held):
        for k, (slot, c) in enumerate(pairs):
            support = listed_support(listed, slot)
            there, here = density_weights(
                count, *held[2 * k : 2 * k + 2], held[4 + k], support, False
            )
            add_block(total, c, CELL, here)
            set_block(there_of, slot, CELL, there)

    trips, item = pair_list(plan)
    in_turns(trips, SIZES, item, None, products, weights, slot_a, slot_b)

    def send(e, part):
        start = (e * SLOTS + 8 * part) * CELL
        summed = sum(planes_of(there_of, range(CELL), start, 8, CELL))
        mass = listed_planes(listed, e, part, [4], ROWS)[0]
        value = jnp.where(live_rows(fill, e, part), summed * inverse_mass(mass), 0.0)
        back[e, rows_at(part, 8), :] = value

    def send_none(e, part):
        back[e, rows_at(part, 8), :] = jnp.zeros((8, WIDTH), F32)

    live_parts(fill, send, send_none)
    fold(total, own, rho, carried)


def cross_density(fill, plan, own, first, listed, carried):
    return pl.pallas_call(
        cross_density_kernel,
        in_specs=[SM, SM] + [VM] * 4,
        out_specs=[VM, VM],
        out_shape=[
            jax.ShapeDtypeStruct((CELLS, WIDTH), F32),
            jax.ShapeDtypeStruct((PEERS, SLOTS, WIDTH), F32),
        ],
        scratch_shapes=[
            pltpu.VMEM((2, (CELLS + 1) * CELL, 128), F32),
            pltpu.VMEM((2, LISTED * CELL, 128), F32),
            pltpu.VMEM((2, LISTED * CELL, 128), F32),
        ]
        + DENSITY_SLOT * 2,
        cost_estimate=pl.CostEstimate(
            flops=80 * 65536 * 60, bytes_accessed=2 * 2**20, transcendentals=0
        ),
        compiler_params=params(),
    )(fill, plan, own, first, listed, carried)


def pressure_kernel(
    pair, near, returned, energy_in, own, density, term, out, energy, sum_of, moving, sem
):
    copies = fetch([(energy_in, energy)], sem)
    sum_of[...] = near[...]

    def peer_step(e, _):
        for s in range(SLOTS):
            sum_of[pl.ds(pair[e, s], 1), :] += returned[e, s : s + 1]
        return 0

    lax.fori_loop(0, PEERS, peer_step, 0)
    copies[0].wait()
    full = planes_of(own, [4], 0, CELLS, CELL)[0] > 0.0
    rho = jnp.where(full, sum_of[...], 0.0)
    density[...] = rho
    term[...] = jnp.where(full, GAMMA_LESS * energy[...] / jnp.where(full, rho, 1.0), 0.0)

    def cell_step(c, _):
        moving[c] = jnp.concatenate(
            [line(own, c, CELL, k) for k in (5, 6, 7)] + [term[pl.ds(c, 1), :]], 0
        )
        return 0

    lax.fori_loop(0, CELLS, cell_step, 0, unroll=8)

    def send_step(e, _):
        for s in range(SLOTS):
            cell = moving[pair[e, s]]
            for h in range(2):
                at = (h * SLOTS + s) * MOVING
                out[e, at : at + MOVING] = half(cell, h)
        return 0

    lax.fori_loop(0, PEERS, send_step, 0)


def pressure(pair, near, returned, energy, own):
    plane = jax.ShapeDtypeStruct((CELLS, WIDTH), F32)
    return pl.pallas_call(
        pressure_kernel,
        in_specs=[SM, VM, VM, ANYWHERE, VM],
        out_specs=[VM, VM, VM],
        out_shape=[
            plane,
            plane,
            jax.ShapeDtypeStruct((PEERS, 2 * SLOTS * MOVING, 128), F32),
        ],
        scratch_shapes=[
            pltpu.VMEM((CELLS, WIDTH), F32),
            pltpu.VMEM((CELLS, WIDTH), F32),
            pltpu.VMEM((CELLS, MOVING, WIDTH), F32),
            pltpu.SemaphoreType.DMA((1,)),
        ],
        compiler_params=params(),
    )(pair, near, returned, energy, own)


def force_terms(place, m, speed, term):
    mp = m * term
    turned = sum(a * b for a, b in zip(place, speed))
    return (
        [m] + [m * a for a in place] + [mp] + [mp * a for a in place]
        + [m * a for a in speed] + [m * turned]
    )


def forces_of(sums, place, speed, term):
    lean = [a * sums[0] - b for a, b in zip(place, sums[1:4])]
    acc = [term * a + (b * sums[4] - c) for a, b, c in zip(lean, place, sums[5:8])]
    mixed = sum(a * b - c * d for a, b, c, d in zip(speed, lean, place, sums[8:11]))
    return [G_SCALE * a for a in acc] + [-G_SCALE * term * (mixed + sums[11])]


def force_operand(ref, index):
    high, low = split2(block(ref, index, SUMS))
    return jnp.concatenate([high, low], 0)


def own_terms(own, term, rows):
    planes = planes_of(own, range(CELL), 0, CELLS, CELL)
    terms = force_terms(planes[0:3], planes[4], planes[5:8], term[...])
    put(rows, terms, 0, CELLS, SUMS)
    put(rows, [jnp.zeros((CELLS, WIDTH), F32)] * 4, 12, CELLS, SUMS)
    set_block(rows, CELLS, SUMS, jnp.zeros((SUMS, WIDTH), F32))


def slopes(s_ref, high, low, columns, row, count):
    for start in range(0, count, CHUNK):
        s = jnp.maximum(s_ref[start : start + CHUNK], TINY)
        dist = s * lax.rsqrt(s)
        wide = columns[start : start + CHUNK]
        support = jnp.concatenate([wide, wide], 1) + row
        d = jnp.maximum(support - dist, 0.0)
        e = pl.reciprocal(support * support, approx=True)
        x = e * d
        g = (x * x) * (x * e)
        top = g.astype(BF)
        high[start : start + CHUNK] = top
        low[start : start + CHUNK] = (g - top.astype(F32)).astype(BF)


def distances(left, rows, s_ref):
    s_ref[...] = jnp.dot(left, second_operands(rows, False), preferred_element_type=F32)


def to_seconds(rows, count, high, low):
    part = rows[:, :count]
    top = lax.dot_general(part, high[0:count], NN, preferred_element_type=F32)
    both = top + lax.dot_general(part, low[0:count], NN, preferred_element_type=F32)
    return both[:SUMS] + both[SUMS:]


def to_firsts(rows, count, high, low):
    top = lax.dot_general(rows, high[0:count], NT, preferred_element_type=F32)
    both = top + lax.dot_general(rows, low[0:count], NT, preferred_element_type=F32)
    return both[:SUMS] + both[SUMS:]


def in_three_turns(trips, sizes, item, last, products, tiles, sums, slot_a, slot_b):
    products(item(0), slot_a)
    base = 0
    for count, size in zip(trips, sizes):

        def step(i, _, size=size):
            products(item(2 * i + 1), slot_b)
            sums(size, item(2 * i - 2), slot_a)
            tiles(size, item(2 * i), slot_a)
            after = 2 * i + 2
            products(item(after if last is None else jnp.minimum(after, last - 1)), slot_a)
            sums(size, item(2 * i - 1), slot_b)
            tiles(size, item(2 * i + 1), slot_b)
            return 0

        lax.fori_loop(base, base + count, step, 0)
        base = base + count
    sums(sizes[-1], item(2 * base - 2), slot_a)
    sums(sizes[-1], item(2 * base - 1), slot_b)


def clear(slots):
    for held in slots:
        held[...] = jnp.zeros_like(held)


def add_forces(total, own, term, out, carried):
    planes = planes_of(own, range(CELL), 0, CELLS, CELL)
    sums = planes_of(total, range(12), 0, CELLS, SUMS)
    for k, force in enumerate(forces_of(sums, planes[0:3], planes[5:8], term[...])):
        out[k] = force if carried is None else carried[k] + force


def local_force_kernel(part, plan, own, first, second, term, *rest):
    if part:
        faces, face_terms, carried, out, rows, total, face_rows, face_first, *slots = rest
    else:
        carried = None
        out, rows, total, *slots = rest
    slot_a, slot_b = slots[:7], slots[7:]
    own_terms(own, term, rows)
    total[...] = jnp.zeros_like(total)
    clear([held[k] for held in (slot_a, slot_b) for k in (2, 3, 5, 6)])

    def products(c, held):
        left = first_operand(block(first, c, CELL))
        held[0][...] = support_columns(line(own, c, CELL, 3))
        distances(left, block(second, c, CELL), held[1])
        distances(left, block(second, jnp.minimum(c + 1, CELLS), CELL), held[4])

    def tiles(count, c, held):
        other = line(own, jnp.minimum(c + 1, CELLS), CELL, 3)
        slopes(*held[1:4], held[0], line(own, c, CELL, 3), count)
        slopes(*held[4:7], held[0], other, count)

    def sums(count, c, held):
        after = jnp.minimum(c + 1, CELLS)
        mine, other = force_operand(rows, c), force_operand(rows, after)
        added = to_firsts(other, count, *held[5:7])
        if count < WIDTH:
            added = jnp.concatenate([added, jnp.zeros((SUMS, WIDTH - count), F32)], 1)
        add_block(total, c, SUMS, to_seconds(mine, count, *held[2:4]) + added)
        add_block(total, after, SUMS, to_seconds(mine, count, *held[5:7]))

    trips, item = cell_list(plan, part)
    in_three_turns(trips, SIZES, item, None, products, tiles, sums, slot_a, slot_b)

    if part:
        make_face_first(faces, face_first)
        planes = planes_of(faces, range(CELL), 0, 2 * FACE, CELL)
        terms = force_terms(planes[0:3], planes[4], planes[5:8], face_terms[...])
        blank = jnp.zeros((2 * FACE, WIDTH), F32)
        put(face_rows, terms + [blank] * 4, 0, 2 * FACE, SUMS)

        def face_products(i, held):
            for k in range(2):
                n = 2 * i + k
                left = first_operand(block(face_first, n, CELL))
                distances(left, block(second, face_cell(n), CELL), held[1 + 3 * k])

        def face_tiles(size, i, held):
            for k in range(2):
                n = 2 * i + k
                columns = support_columns(line(faces, n, CELL, 3))
                slopes(
                    *held[1 + 3 * k : 4 + 3 * k], columns, line(own, face_cell(n), CELL, 3), size
                )

        def face_sums(size, i, held):
            for k in range(2):
                n = jnp.maximum(2 * i, 0) + k
                c = jnp.where(i < 0, CELLS, face_cell(n))
                theirs = force_operand(face_rows, n)
                add_block(
                    total, c, SUMS, to_seconds(theirs, size, *held[2 + 3 * k : 4 + 3 * k])
                )

        in_three_turns(
            [FACE // 2], [WIDTH], lambda i: i, FACE, face_products, face_tiles, face_sums,
            slot_a, slot_b,
        )

    add_forces(total, own, term, out, carried)


FORCE_PAIR = [
    pltpu.VMEM((WIDTH, WIDTH), F32),
    pltpu.VMEM((WIDTH, WIDTH), BF),
    pltpu.VMEM((WIDTH, WIDTH), BF),
]
FORCE_SLOT = [pltpu.VMEM((WIDTH, 128), F32)] + FORCE_PAIR * 2


def local_force(part, plan, own, first, second, term, *rest):
    scratch = [
        pltpu.VMEM((2, (CELLS + 1) * SUMS, 128), F32),
        pltpu.VMEM((2, (CELLS + 1) * SUMS, 128), F32),
    ]
    if part:
        scratch.append(pltpu.VMEM((2, 2 * FACE * SUMS, 128), F32))
        scratch.append(pltpu.VMEM((2, 2 * FACE * CELL, 128), F32))
    return pl.pallas_call(
        functools.partial(local_force_kernel, part),
        in_specs=[SM] + [VM] * (4 + len(rest)),
        out_specs=VM,
        out_shape=jax.ShapeDtypeStruct((4, CELLS, WIDTH), F32),
        scratch_shapes=scratch + FORCE_SLOT * 2,
        cost_estimate=pl.CostEstimate(
            flops=64 * 65536 * 80, bytes_accessed=2 * 2**20, transcendentals=0
        ),
        compiler_params=params(),
    )(plan, own, first, second, term, *rest)


def cross_force_kernel(
    fill, plan, own, first, term, listed, arrived, carried, out, back,
    rows, total, theirs, their_rows, sums_of, *slots
):
    slot_a, slot_b = slots[:8], slots[8:]
    own_terms(own, term, rows)
    total[...] = jnp.zeros_like(total)
    clear([held[k] for held in (slot_a, slot_b) for k in (3, 4, 6, 7)])

    def make(e, part):
        planes = listed_planes(listed, e, part, range(ROWS), ROWS)
        at = e * SLOTS + 8 * part
        put(theirs, pair_terms(*planes)[1], at * CELL, 8, CELL)
        *speed, pressed = listed_planes(arrived, e, part, range(MOVING), MOVING)
        terms = force_terms(planes[0:3], planes[4], speed, pressed)
        blank = jnp.zeros((8, WIDTH), F32)
        put(their_rows, terms + [blank] * 4, at * SUMS, 8, SUMS)

    live_parts(fill, make, None)

    def products(pairs, held):
        for k, (slot, c) in enumerate(pairs):
            held[k][...] = support_columns(line(own, c, CELL, 3))
            left = first_operand(block(first, c, CELL))
            distances(left, block(theirs, slot, CELL), held[2 + 3 * k])

    def tiles(count, pairs, held):
        for k, (slot, c) in enumerate(pairs):
            support = listed_support(listed, slot)
            slopes(*held[2 + 3 * k : 5 + 3 * k], held[k], support, count)

    def sums(count, pairs, held):
        for k, (slot, c) in enumerate(pairs):
            tile = held[3 + 3 * k : 5 + 3 * k]
            set_block(sums_of, slot, SUMS, to_seconds(force_operand(rows, c), count, *tile))
            added = to_firsts(force_operand(their_rows, slot), count, *tile)
            if count < WIDTH:
                added = jnp.concatenate([added, jnp.zeros((SUMS, WIDTH - count), F32)], 1)
            add_block(total, c, SUMS, added)

    trips, item = pair_list(plan)
    in_three_turns(trips, SIZES, item, None, products, tiles, sums, slot_a, slot_b)

    def send(e, part):
        planes = listed_planes(listed, e, part, range(3), ROWS)
        *speed, pressed = listed_planes(arrived, e, part, range(MOVING), MOVING)
        summed = planes_of(sums_of, range(12), (e * SLOTS + 8 * part) * SUMS, 8, SUMS)
        live = live_rows(fill, e, part)
        send_rows(e, part, [jnp.where(live, f, 0.0) for f in forces_of(summed, planes, speed, pressed)])

    def send_none(e, part):
        send_rows(e, part, [jnp.zeros((8, WIDTH), F32)] * MOVING)

    def send_rows(e, part, forces):
        for k, force in enumerate(forces):
            for h in range(2):
                start = (h * SLOTS + 8 * part) * MOVING + k
                back[e, pl.ds(start, 8, stride=MOVING), :] = half(force, h)

    live_parts(fill, send, send_none)
    add_forces(total, own, term, out, carried)


def cross_force(fill, plan, own, first, term, listed, arrived, carried):
    return pl.pallas_call(
        cross_force_kernel,
        in_specs=[SM, SM] + [VM] * 6,
        out_specs=[VM, VM],
        out_shape=[
            jax.ShapeDtypeStruct((4, CELLS, WIDTH), F32),
            jax.ShapeDtypeStruct((PEERS, 2 * SLOTS * MOVING, 128), F32),
        ],
        scratch_shapes=[
            pltpu.VMEM((2, (CELLS + 1) * SUMS, 128), F32),
            pltpu.VMEM((2, (CELLS + 1) * SUMS, 128), F32),
            pltpu.VMEM((2, LISTED * CELL, 128), F32),
            pltpu.VMEM((2, LISTED * SUMS, 128), F32),
            pltpu.VMEM((2, LISTED * SUMS, 128), F32),
        ]
        + (FORCE_SLOT[:1] * 2 + FORCE_PAIR * 2) * 2,
        cost_estimate=pl.CostEstimate(
            flops=80 * 65536 * 80, bytes_accessed=2 * 2**20, transcendentals=0
        ),
        compiler_params=params(),
    )(fill, plan, own, first, term, listed, arrived, carried)


def finish_kernel(pair, near, returned, active_in, own, out, total, active, gate, sem):
    copies = fetch([(active_in, active)], sem)
    total[...] = jnp.zeros_like(total)

    def peer_step(e, _):
        for s in range(SLOTS):
            at = s * MOVING
            total[pair[e, s]] += both(
                lambda h: returned[
                    e, h * SLOTS * MOVING + at : h * SLOTS * MOVING + at + MOVING
                ]
            )
        return 0

    lax.fori_loop(0, PEERS, peer_step, 0)
    copies[0].wait()
    full = planes_of(own, [4], 0, CELLS, CELL)[0] > 0.0
    gate[...] = jnp.where(full, active[...].astype(F32), 0.0)

    def cell_step(c, _):
        one = pl.ds(c, 1)
        open_to = gate[one, :]
        for k in range(4):
            out[k, one, :] = (near[k, one, :] + total[c, k : k + 1]) * open_to
        return 0

    lax.fori_loop(0, CELLS, cell_step, 0, unroll=8)


def finish(pair, near, returned, active, own):
    return pl.pallas_call(
        finish_kernel,
        in_specs=[SM, VM, VM, ANYWHERE, VM],
        out_specs=VM,
        out_shape=jax.ShapeDtypeStruct((4, CELLS, WIDTH), F32),
        scratch_shapes=[
            pltpu.VMEM((CELLS, 4, WIDTH), F32),
            pltpu.VMEM((CELLS, WIDTH), jnp.int32),
            pltpu.VMEM((CELLS, WIDTH), F32),
            pltpu.SemaphoreType.DMA((1,)),
        ],
        compiler_params=params(),
    )(pair, near, returned, active, own)


def to_peers(block):
    return lax.all_to_all(block, "dev", split_axis=0, concat_axis=0, tiled=True)


def with_neighbours(rows, size):
    count = lax.axis_size("region")
    up = [(i, (i + 1) % count) for i in range(count)]
    down = [(i, (i - 1) % count) for i in range(count)]
    return jnp.concatenate(
        [
            lax.ppermute(rows[..., (CELLS - FACE) * size : CELLS * size, :], "region", up),
            lax.ppermute(rows[..., : FACE * size, :], "region", down),
        ],
        -2,
    )


def local(
    positions, velocity, smoothing, masses, energy, occupancy, active, send_cells, send_fill,
    pair_cell,
):
    pair = pair_cell[0]
    own, first, second, listed = prepare(
        occupancy, pair, positions, velocity, smoothing, masses
    )
    arrived = to_peers(listed)
    plan = make_plan(occupancy, send_fill, send_cells[0], own)
    faces = with_neighbours(own, CELL)
    rho = local_density(0, plan, own, first, second)
    rho, back = cross_density(send_fill, plan, own, first, arrived, rho)
    returned = to_peers(back)
    rho = local_density(1, plan, own, first, second, faces, rho)
    density, term, leaving = pressure(pair, rho, returned, energy, own)
    arrived_moving = to_peers(leaving)
    face_terms = with_neighbours(term, 1)
    sums = local_force(0, plan, own, first, second, term)
    sums, force_back = cross_force(
        send_fill, plan, own, first, term, arrived, arrived_moving, sums
    )
    returned_force = to_peers(force_back)
    sums = local_force(1, plan, own, first, second, term, faces, face_terms, sums)
    forces = finish(pair, sums, returned_force, active, own)
    return (density, forces)


def solution(mesh):
    cells = P(("region", "dev"), None)
    vectors = P(None, ("region", "dev"), None)
    lists = P(("region", "dev"), None, None)
    in_specs = (
        vectors, vectors, cells, cells, cells, P(("region", "dev")), cells, lists, cells, lists,
    )
    return jax.shard_map(
        local, mesh=mesh, in_specs=in_specs, out_specs=(cells, vectors), check_vma=False
    )
```

```python
import functools
import math

import jax
import jax.numpy as jnp
from jax import lax
from jax.experimental import pallas as pl
from jax.experimental.pallas import tpu as pltpu
from jax.sharding import PartitionSpec as P

BF = jnp.bfloat16
F32 = jnp.float32
FACE = 4
CELLS = 64
WIDTH = 256
PEERS = 16
SLOTS = 16
LISTED = PEERS * SLOTS
GAMMA_LESS = 2.0 / 3.0
W_SCALE = 84.0 / math.pi
G_SCALE = 6720.0 / math.pi
TINY = 1e-14
EMPTY = 1e8
CHUNK = 32
CELL = 8
SUMS = 16
NN = (((1,), (0,)), ((), ()))
NT = (((1,), (1,)), ((), ()))
VM = pl.BlockSpec(memory_space=pltpu.VMEM)
SM = pl.BlockSpec(memory_space=pltpu.SMEM)
ROWS = 5
MOVING = 4
SPLIT = 40
SIZES = (160, 192, 224, 256)
KINDS = len(SIZES)
UNIT = 4
LOCAL_AT = 16
LOCAL_LEAD = 2
LOCAL_LIST = CELLS + 8
CROSS_AT = LOCAL_AT + 2 * LOCAL_LIST
CROSS_LEAD = 4
CROSS_LIST = LISTED + 16
PLAN = CROSS_AT + CROSS_LIST
PACK = 128
ANYWHERE = pl.BlockSpec(memory_space=pl.ANY)
OWN_ROWS = jax.ShapeDtypeStruct((2, (CELLS + 1) * CELL, 128), F32)


def params(mib=50):
    return pltpu.CompilerParams(vmem_limit_bytes=int(mib * 2**20))


def split2(x):
    a = x.astype(BF)
    return a, (x - a.astype(F32)).astype(BF)


def split3(x):
    a = x.astype(BF).astype(F32)
    rest = x - a
    b = rest.astype(BF).astype(F32)
    return a, b, rest - b


def pair_terms(x, y, z, h, m):
    norm = 4.0 * (x * x + y * y + z * z)
    root = lax.rsqrt(jnp.where(m > 0.0, m, 1.0))
    mu = jnp.where(m > 0.0, root * lax.rsqrt(root), EMPTY)
    one = jnp.ones_like(x)
    first = [-8.0 * x, -8.0 * y, -8.0 * z, norm, one, h * h * mu, 2.0 * h * mu, mu]
    second = [x, y, z, one, norm, mu, h * mu, h * h * mu]
    return first, second


def both(read):
    return jnp.concatenate([read(0), read(1)], -1)


def half(value, h):
    return value[..., 128 * h : 128 * (h + 1)]


def put(ref, planes, start, count, stride):
    for k, plane in enumerate(planes):
        for h in range(2):
            ref[h, pl.ds(start + k, count, stride=stride), :] = half(plane, h)


def planes_of(ref, ids, start, count, stride):
    return [both(lambda h: ref[h, pl.ds(start + k, count, stride=stride), :]) for k in ids]


def rows_at(index, size):
    return pl.ds(pl.multiple_of(index * size, size), size)


def block(ref, index, size):
    return both(lambda h: ref[h, rows_at(index, size), :])


def set_block(ref, index, size, value):
    for h in range(2):
        ref[h, rows_at(index, size), :] = half(value, h)


def add_block(ref, index, size, value):
    for h in range(2):
        ref[h, rows_at(index, size), :] += half(value, h)


def line(ref, index, size, k):
    return both(lambda h: ref[h, pl.ds(index * size + k, 1), :])


def listed_planes(listed, e, part, ids, size):
    step = SLOTS * size
    start = 8 * part * size
    return [
        both(lambda h: listed[e, pl.ds(h * step + start + k, 8, stride=size), :]) for k in ids
    ]


def listed_support(listed, slot):
    at = (slot % SLOTS) * ROWS + 3
    return both(lambda h: listed[slot // SLOTS, pl.ds(h * SLOTS * ROWS + at, 1), :])


def first_operand(rows):
    a1, a2, a3 = split3(rows)
    return jnp.concatenate([a1, a1, a2, a2, a1, a3, jnp.zeros((80, WIDTH), F32)], 0).T.astype(BF)


def second_operands(rows, both):
    b1, b2, b3 = split3(rows)
    stacked = jnp.concatenate([b1, b2, b1, b2, b3, b1, jnp.zeros((80, WIDTH), F32)], 0)
    part = lax.broadcasted_iota(jnp.int32, stacked.shape, 0) % 8
    near = jnp.where(part < 5, stacked, 0.0).astype(BF)
    if not both:
        return near
    return near, jnp.where(part >= 5, stacked, 0.0).astype(BF)


def support_columns(row):
    return jnp.broadcast_to(row, (128, WIDTH)).T


def density_products(left, operands, s_ref, mix_ref):
    s_ref[...] = jnp.dot(left, operands[0], preferred_element_type=F32)
    mix_ref[...] = jnp.dot(left, operands[1], preferred_element_type=F32)


def weights_of(s, mix, columns, row):
    s = jnp.maximum(s, TINY)
    dist = s * lax.rsqrt(s)
    support = columns + row
    d = jnp.maximum(support - dist, 0.0)
    x = pl.reciprocal(mix, approx=True) * d
    x = x * x
    x = x * x
    return x * (support + 4.0 * dist)


def density_weights(count, s_ref, mix_ref, columns, row, one_sided):
    second = jnp.zeros((8, WIDTH), F32)
    firsts = []
    for start in range(0, count, CHUNK):
        part = slice(start, start + CHUNK)
        wide = columns[part]
        w = weights_of(s_ref[part], mix_ref[part], jnp.concatenate([wide, wide], 1), row)
        for k in range(CHUNK // 8):
            second = second + w[8 * k : 8 * k + 8]
        if not one_sided:
            firsts.append(w[:, :128] + w[:, 128:])
    if one_sided:
        return second
    if count < WIDTH:
        firsts.append(jnp.zeros((WIDTH - count, 128), F32))
    turned = jnp.concatenate(firsts, 0).T
    first = turned[:8]
    for k in range(1, 16):
        first = first + turned[8 * k : 8 * k + 8]
    return second, first


def inverse_mass(m):
    return jnp.where(m > 0.0, W_SCALE / jnp.where(m > 0.0, m, 1.0), 0.0)


def self_weights(count, s_ref, mix_ref, columns, row):
    sums = [jnp.zeros((8, 128), F32)] * 2
    crossing = []
    for start in range(0, count, CHUNK):
        part = slice(start, start + CHUNK)
        for h in range(0 if start < 128 else 1, 2):
            lanes = slice(128 * h, 128 * (h + 1))
            w = weights_of(s_ref[part, lanes], mix_ref[part, lanes], columns[part], half(row, h))
            for k in range(CHUNK // 8):
                sums[h] = sums[h] + w[8 * k : 8 * k + 8]
            if h and start < 128:
                crossing.append(w)
    turned = jnp.concatenate(crossing, 0).T
    for k in range(16):
        sums[0] = sums[0] + turned[8 * k : 8 * k + 8]
    return jnp.concatenate(sums, 1)


def fetch(pairs, sem):
    copies = [
        pltpu.make_async_copy(source, target, sem.at[k])
        for k, (source, target) in enumerate(pairs)
    ]
    for copy in copies:
        copy.start()
    return copies


def prepare_kernel(
    occ, pair, pos_in, vel_in, smooth_in, mass_in, own, out, pos, vel, smooth, mass, full, sem
):
    copies = fetch(
        [(pos_in, pos), (vel_in, vel), (smooth_in, smooth), (mass_in, mass)], sem
    )
    lane = lax.broadcasted_iota(jnp.int32, (1, WIDTH), 1)
    for c in range(CELLS):
        full[c : c + 1, :] = (lane < occ[c]).astype(F32)
    for copy in copies:
        copy.wait()
    place = [pos[k] - 0.5 for k in range(3)]
    m = jnp.where(full[...] > 0.0, mass[...], 0.0)
    put(own, place + [smooth[...], m] + [vel[k] for k in range(3)], 0, CELLS, CELL)
    blank = jnp.zeros((CELL, WIDTH), F32)
    wide = jnp.full((1, WIDTH), 0.5, F32)
    set_block(own, CELLS, CELL, jnp.concatenate([blank[:3], wide, blank[:4]], 0))

    def peer_step(e, _):
        for s in range(SLOTS):
            c = pair[e, s]
            for h in range(2):
                at = (h * SLOTS + s) * ROWS
                out[e, at : at + ROWS] = own[h, rows_at(c, CELL), :][:ROWS]
        return 0

    lax.fori_loop(0, PEERS, peer_step, 0)


def prepare(occ, pair, pos, vel, smooth, mass):
    plane = pltpu.VMEM((CELLS, WIDTH), F32)
    return pl.pallas_call(
        prepare_kernel,
        in_specs=[SM] * 2 + [ANYWHERE] * 4,
        out_specs=[VM] * 2,
        out_shape=[
            OWN_ROWS,
            jax.ShapeDtypeStruct((PEERS, 2 * SLOTS * ROWS, 128), F32),
        ],
        scratch_shapes=[
            pltpu.VMEM((3, CELLS, WIDTH), F32),
            pltpu.VMEM((3, CELLS, WIDTH), F32),
            plane,
            plane,
            plane,
            pltpu.SemaphoreType.DMA((4,)),
        ],
        compiler_params=params(60),
    )(occ, pair, pos, vel, smooth, mass)


def kind_of(size):
    return jnp.maximum(size - SIZES[0] + 31, 0) >> 5


def make_plan(occ, fill, cells, plan):
    def over_local(visit, part, carry):
        low, high = (SPLIT, CELLS) if part else (0, SPLIT)
        step = lambda c, carry: visit(kind_of(occ[c]), c, carry)
        return lax.fori_loop(low, high, step, carry, unroll=8)

    def over_pairs(visit, carry):
        def peer_step(e, carry):
            def slot_step(s, carry):
                cell = cells[e, s]
                return visit(kind_of(occ[cell]), (e * SLOTS + s) * PACK + cell, carry)

            return lax.fori_loop(0, fill[0, e], slot_step, carry)

        return lax.fori_loop(0, PEERS, peer_step, carry)

    unused = jnp.int32(0)
    for e in range(PEERS):
        unused = jnp.where(fill[0, e] == 0, e * SLOTS, unused)

    def one_of(kind):
        return jnp.left_shift(jnp.int32(1), 8 * kind)

    for group, (walk, start, lead, unit, blank) in enumerate(
        [
            (lambda v, x: over_local(v, 0, x), LOCAL_AT, LOCAL_LEAD, 2, CELLS),
            (lambda v, x: over_local(v, 1, x), LOCAL_AT + LOCAL_LIST, LOCAL_LEAD, 2, CELLS),
            (over_pairs, CROSS_AT, CROSS_LEAD, UNIT, unused * PACK + CELLS),
        ]
    ):
        counts = walk(lambda kind, value, packed: packed + one_of(kind), jnp.int32(0))
        total = jnp.int32(0)
        done = jnp.int32(0)
        places = jnp.int32(0)
        for k in range(KINDS):
            places = places + jnp.left_shift(total, 8 * k)
            total = total + ((counts >> (8 * k)) & 255)
            upto = (total + (unit - 1 if k == KINDS - 1 else 0)) // unit
            plan[group * KINDS + k] = upto - done
            done = upto
        for k in range(lead):
            plan[start + k] = blank
        for k in range(unit + 1):
            plan[start + lead + total + k] = blank

        def place(kind, value, packed, start=start + lead):
            plan[start + ((packed >> (8 * kind)) & 255)] = value
            return packed + one_of(kind)

        walk(place, places)


def fold(total, own, out, carried):
    mine = sum(planes_of(total, range(CELL), 0, CELLS, CELL))
    mass = planes_of(own, [4], 0, CELLS, CELL)[0]
    mine = mine * inverse_mass(mass)
    out[...] = mine if carried is None else carried[...] + mine


def make_face_first(faces, face_first):
    planes = planes_of(faces, range(ROWS), 0, 2 * FACE, CELL)
    put(face_first, pair_terms(*planes)[0], 0, 2 * FACE, CELL)


def face_cell(n):
    return jnp.where(n < FACE, n, CELLS - 2 * FACE + n)


def in_turns(trips, sizes, item, last, products, weights, slot_a, slot_b):
    products(item(0), slot_a)
    base = 0
    for count, size in zip(trips, sizes):

        def step(i, _, size=size):
            products(item(2 * i + 1), slot_b)
            weights(size, item(2 * i), slot_a)
            after = 2 * i + 2
            products(item(after if last is None else jnp.minimum(after, last - 1)), slot_a)
            weights(size, item(2 * i + 1), slot_b)
            return 0

        lax.fori_loop(base, base + count, step, 0)
        base = base + count


def cell_list(plan, part):
    start = LOCAL_AT + part * LOCAL_LIST + LOCAL_LEAD
    return [plan[part * KINDS + k] for k in range(KINDS)], lambda n: plan[start + n]


def pair_list(plan):
    start = CROSS_AT + CROSS_LEAD

    def item(n):
        entries = [plan[start + 2 * n + k] for k in range(2)]
        return [(entry // PACK, entry % PACK) for entry in entries]

    return [plan[2 * KINDS + k] for k in range(KINDS)], item


def live_parts(fill, visit, other):
    def step(n, _):
        e, part = n // 2, n % 2
        live = fill[0, e] > 8 * part

        @pl.when(live)
        def _():
            visit(e, part)

        if other is not None:

            @pl.when(jnp.logical_not(live))
            def _():
                other(e, part)

        return 0

    lax.fori_loop(0, 2 * PEERS, step, 0)


def local_density_kernel(part, *refs):
    if part:
        plan, own, first, second, faces, carried, rho, total, face_first, *slots = refs
    else:
        carried = None
        occ, fill, cells, own, rho, first, second, plan, total, *slots = refs
        make_plan(occ, fill, cells, plan)
        planes = planes_of(own, range(ROWS), 0, CELLS, CELL)
        blank = [jnp.zeros((1, WIDTH), F32)] * 3 + [jnp.full((1, WIDTH), 0.5, F32)]
        for ref, some, none in zip(
            (first, second), pair_terms(*planes), pair_terms(*blank, blank[0])
        ):
            put(ref, some, 0, CELLS, CELL)
            set_block(ref, CELLS, CELL, jnp.concatenate(none, 0))
    slot_a, slot_b = slots[:6], slots[6:]
    total[...] = jnp.zeros_like(total)

    def products(c, held):
        left = first_operand(block(first, c, CELL))
        after = jnp.minimum(c + 1, CELLS)
        held[4][...] = support_columns(line(own, c, CELL, 3))
        density_products(left, second_operands(block(second, c, CELL), True), *held[0:2])
        density_products(left, second_operands(block(second, after, CELL), True), *held[2:4])

    def weights(count, c, held):
        after = jnp.minimum(c + 1, CELLS)
        row, other = line(own, c, CELL, 3), line(own, after, CELL, 3)
        own_sum = self_weights(count, *held[0:2], held[4], row)
        there, here = density_weights(count, *held[2:4], held[4], other, False)
        add_block(total, c, CELL, own_sum + here)
        add_block(total, after, CELL, there)

    trips, item = cell_list(plan, part)
    in_turns(trips, SIZES, item, None, products, weights, slot_a, slot_b)

    if part:
        make_face_first(faces, face_first)

        def face_products(i, held):
            for k in range(2):
                n = 2 * i + k
                left = first_operand(block(face_first, n, CELL))
                operands = second_operands(block(second, face_cell(n), CELL), True)
                held[4 + k][...] = support_columns(line(faces, n, CELL, 3))
                density_products(left, operands, *held[2 * k : 2 * k + 2])

        def face_weights(size, i, held):
            for k in range(2):
                c = face_cell(2 * i + k)
                added = density_weights(
                    size, *held[2 * k : 2 * k + 2], held[4 + k], line(own, c, CELL, 3), True
                )
                add_block(total, c, CELL, added)

        in_turns(
            [FACE // 2], [WIDTH], lambda i: i, FACE, face_products, face_weights, slot_a, slot_b
        )

    fold(total, own, rho, carried)


DENSITY_SLOT = [pltpu.VMEM((WIDTH, WIDTH), F32)] * 4 + [pltpu.VMEM((WIDTH, 128), F32)] * 2


def local_density(part, *operands):
    plane = jax.ShapeDtypeStruct((CELLS, WIDTH), F32)
    if part:
        in_specs, out_specs, out_shape = [SM] + [VM] * 5, VM, plane
    else:
        in_specs, out_specs = [SM] * 3 + [VM], [VM] * 3 + [SM]
        out_shape = [plane, OWN_ROWS, OWN_ROWS, jax.ShapeDtypeStruct((PLAN,), jnp.int32)]
    return pl.pallas_call(
        functools.partial(local_density_kernel, part),
        in_specs=in_specs,
        out_specs=out_specs,
        out_shape=out_shape,
        scratch_shapes=[pltpu.VMEM((2, (CELLS + 1) * CELL, 128), F32)]
        + [pltpu.VMEM((2, 2 * FACE * CELL, 128), F32)] * part
        + DENSITY_SLOT * 2,
        cost_estimate=pl.CostEstimate(
            flops=64 * 65536 * 60, bytes_accessed=2 * 2**20, transcendentals=0
        ),
        compiler_params=params(),
    )(*operands)


def live_rows(fill, e, part):
    row = lax.broadcasted_iota(jnp.int32, (8, WIDTH), 0)
    return row < fill[0, e] - 8 * part


def cross_density_kernel(
    fill, plan, own, first, listed, carried, rho, back, total, theirs, there_of, *slots
):
    slot_a, slot_b = slots[:6], slots[6:]
    total[...] = jnp.zeros_like(total)

    def make(e, part):
        after = pair_terms(*listed_planes(listed, e, part, range(ROWS), ROWS))[1]
        put(theirs, after, (e * SLOTS + 8 * part) * CELL, 8, CELL)

    live_parts(fill, make, None)

    def products(pairs, held):
        for k, (slot, c) in enumerate(pairs):
            left = first_operand(block(first, c, CELL))
            held[4 + k][...] = support_columns(line(own, c, CELL, 3))
            operands = second_operands(block(theirs, slot, CELL), True)
            density_products(left, operands, *held[2 * k : 2 * k + 2])

    def weights(count, pairs, held):
        for k, (slot, c) in enumerate(pairs):
            support = listed_support(listed, slot)
            there, here = density_weights(
                count, *held[2 * k : 2 * k + 2], held[4 + k], support, False
            )
            add_block(total, c, CELL, here)
            set_block(there_of, slot, CELL, there)

    trips, item = pair_list(plan)
    in_turns(trips, SIZES, item, None, products, weights, slot_a, slot_b)

    def send(e, part):
        start = (e * SLOTS + 8 * part) * CELL
        summed = sum(planes_of(there_of, range(CELL), start, 8, CELL))
        mass = listed_planes(listed, e, part, [4], ROWS)[0]
        value = jnp.where(live_rows(fill, e, part), summed * inverse_mass(mass), 0.0)
        back[e, rows_at(part, 8), :] = value

    def send_none(e, part):
        back[e, rows_at(part, 8), :] = jnp.zeros((8, WIDTH), F32)

    live_parts(fill, send, send_none)
    fold(total, own, rho, carried)


def cross_density(fill, plan, own, first, listed, carried):
    return pl.pallas_call(
        cross_density_kernel,
        in_specs=[SM, SM] + [VM] * 4,
        out_specs=[VM, VM],
        out_shape=[
            jax.ShapeDtypeStruct((CELLS, WIDTH), F32),
            jax.ShapeDtypeStruct((PEERS, SLOTS, WIDTH), F32),
        ],
        scratch_shapes=[
            pltpu.VMEM((2, (CELLS + 1) * CELL, 128), F32),
            pltpu.VMEM((2, LISTED * CELL, 128), F32),
            pltpu.VMEM((2, LISTED * CELL, 128), F32),
        ]
        + DENSITY_SLOT * 2,
        cost_estimate=pl.CostEstimate(
            flops=80 * 65536 * 60, bytes_accessed=2 * 2**20, transcendentals=0
        ),
        compiler_params=params(),
    )(fill, plan, own, first, listed, carried)


def pressure_kernel(
    pair, near, returned, energy_in, own, density, term, out, energy, sum_of, moving, sem
):
    copies = fetch([(energy_in, energy)], sem)
    sum_of[...] = near[...]

    def peer_step(e, _):
        for s in range(SLOTS):
            sum_of[pl.ds(pair[e, s], 1), :] += returned[e, s : s + 1]
        return 0

    lax.fori_loop(0, PEERS, peer_step, 0)
    copies[0].wait()
    full = planes_of(own, [4], 0, CELLS, CELL)[0] > 0.0
    rho = jnp.where(full, sum_of[...], 0.0)
    density[...] = rho
    term[...] = jnp.where(full, GAMMA_LESS * energy[...] / jnp.where(full, rho, 1.0), 0.0)

    def cell_step(c, _):
        moving[c] = jnp.concatenate(
            [line(own, c, CELL, k) for k in (5, 6, 7)] + [term[pl.ds(c, 1), :]], 0
        )
        return 0

    lax.fori_loop(0, CELLS, cell_step, 0, unroll=8)

    def send_step(e, _):
        for s in range(SLOTS):
            cell = moving[pair[e, s]]
            for h in range(2):
                at = (h * SLOTS + s) * MOVING
                out[e, at : at + MOVING] = half(cell, h)
        return 0

    lax.fori_loop(0, PEERS, send_step, 0)


def pressure(pair, near, returned, energy, own):
    plane = jax.ShapeDtypeStruct((CELLS, WIDTH), F32)
    return pl.pallas_call(
        pressure_kernel,
        in_specs=[SM, VM, VM, ANYWHERE, VM],
        out_specs=[VM, VM, VM],
        out_shape=[
            plane,
            plane,
            jax.ShapeDtypeStruct((PEERS, 2 * SLOTS * MOVING, 128), F32),
        ],
        scratch_shapes=[
            pltpu.VMEM((CELLS, WIDTH), F32),
            pltpu.VMEM((CELLS, WIDTH), F32),
            pltpu.VMEM((CELLS, MOVING, WIDTH), F32),
            pltpu.SemaphoreType.DMA((1,)),
        ],
        compiler_params=params(),
    )(pair, near, returned, energy, own)


def force_terms(place, m, speed, term):
    mp = m * term
    turned = sum(a * b for a, b in zip(place, speed))
    return (
        [m] + [m * a for a in place] + [mp] + [mp * a for a in place]
        + [m * a for a in speed] + [m * turned]
    )


def forces_of(sums, place, speed, term):
    lean = [a * sums[0] - b for a, b in zip(place, sums[1:4])]
    acc = [term * a + (b * sums[4] - c) for a, b, c in zip(lean, place, sums[5:8])]
    mixed = sum(a * b - c * d for a, b, c, d in zip(speed, lean, place, sums[8:11]))
    return [G_SCALE * a for a in acc] + [-G_SCALE * term * (mixed + sums[11])]


def force_operand(ref, index):
    high, low = split2(block(ref, index, SUMS))
    return jnp.concatenate([high, low], 0)


def own_terms(own, term, rows):
    planes = planes_of(own, range(CELL), 0, CELLS, CELL)
    terms = force_terms(planes[0:3], planes[4], planes[5:8], term[...])
    put(rows, terms, 0, CELLS, SUMS)
    put(rows, [jnp.zeros((CELLS, WIDTH), F32)] * 4, 12, CELLS, SUMS)
    set_block(rows, CELLS, SUMS, jnp.zeros((SUMS, WIDTH), F32))


def slopes(s_ref, high, low, columns, row, count):
    for start in range(0, count, CHUNK):
        s = jnp.maximum(s_ref[start : start + CHUNK], TINY)
        dist = s * lax.rsqrt(s)
        wide = columns[start : start + CHUNK]
        support = jnp.concatenate([wide, wide], 1) + row
        d = jnp.maximum(support - dist, 0.0)
        e = pl.reciprocal(support * support, approx=True)
        x = e * d
        g = (x * x) * (x * e)
        top = g.astype(BF)
        high[start : start + CHUNK] = top
        low[start : start + CHUNK] = (g - top.astype(F32)).astype(BF)


def distances(left, rows, s_ref):
    s_ref[...] = jnp.dot(left, second_operands(rows, False), preferred_element_type=F32)


def to_seconds(rows, count, high, low):
    part = rows[:, :count]
    top = lax.dot_general(part, high[0:count], NN, preferred_element_type=F32)
    both = top + lax.dot_general(part, low[0:count], NN, preferred_element_type=F32)
    return both[:SUMS] + both[SUMS:]


def to_firsts(rows, count, high, low):
    top = lax.dot_general(rows, high[0:count], NT, preferred_element_type=F32)
    both = top + lax.dot_general(rows, low[0:count], NT, preferred_element_type=F32)
    return both[:SUMS] + both[SUMS:]


def in_three_turns(trips, sizes, item, last, products, tiles, sums, slot_a, slot_b):
    products(item(0), slot_a)
    base = 0
    for count, size in zip(trips, sizes):

        def step(i, _, size=size):
            products(item(2 * i + 1), slot_b)
            sums(size, item(2 * i - 2), slot_a)
            tiles(size, item(2 * i), slot_a)
            after = 2 * i + 2
            products(item(after if last is None else jnp.minimum(after, last - 1)), slot_a)
            sums(size, item(2 * i - 1), slot_b)
            tiles(size, item(2 * i + 1), slot_b)
            return 0

        lax.fori_loop(base, base + count, step, 0)
        base = base + count
    sums(sizes[-1], item(2 * base - 2), slot_a)
    sums(sizes[-1], item(2 * base - 1), slot_b)


def clear(slots):
    for held in slots:
        held[...] = jnp.zeros_like(held)


def add_forces(total, own, term, out, carried):
    planes = planes_of(own, range(CELL), 0, CELLS, CELL)
    sums = planes_of(total, range(12), 0, CELLS, SUMS)
    for k, force in enumerate(forces_of(sums, planes[0:3], planes[5:8], term[...])):
        out[k] = force if carried is None else carried[k] + force


def local_force_kernel(part, plan, own, first, second, term, *rest):
    if part:
        faces, face_terms, carried, out, rows, total, face_rows, face_first, *slots = rest
    else:
        carried = None
        out, rows, total, *slots = rest
    slot_a, slot_b = slots[:7], slots[7:]
    own_terms(own, term, rows)
    total[...] = jnp.zeros_like(total)
    clear([held[k] for held in (slot_a, slot_b) for k in (2, 3, 5, 6)])

    def products(c, held):
        left = first_operand(block(first, c, CELL))
        held[0][...] = support_columns(line(own, c, CELL, 3))
        distances(left, block(second, c, CELL), held[1])
        distances(left, block(second, jnp.minimum(c + 1, CELLS), CELL), held[4])

    def tiles(count, c, held):
        other = line(own, jnp.minimum(c + 1, CELLS), CELL, 3)
        slopes(*held[1:4], held[0], line(own, c, CELL, 3), count)
        slopes(*held[4:7], held[0], other, count)

    def sums(count, c, held):
        after = jnp.minimum(c + 1, CELLS)
        mine, other = force_operand(rows, c), force_operand(rows, after)
        added = to_firsts(other, count, *held[5:7])
        if count < WIDTH:
            added = jnp.concatenate([added, jnp.zeros((SUMS, WIDTH - count), F32)], 1)
        add_block(total, c, SUMS, to_seconds(mine, count, *held[2:4]) + added)
        add_block(total, after, SUMS, to_seconds(mine, count, *held[5:7]))

    trips, item = cell_list(plan, part)
    in_three_turns(trips, SIZES, item, None, products, tiles, sums, slot_a, slot_b)

    if part:
        make_face_first(faces, face_first)
        planes = planes_of(faces, range(CELL), 0, 2 * FACE, CELL)
        terms = force_terms(planes[0:3], planes[4], planes[5:8], face_terms[...])
        blank = jnp.zeros((2 * FACE, WIDTH), F32)
        put(face_rows, terms + [blank] * 4, 0, 2 * FACE, SUMS)

        def face_products(i, held):
            for k in range(2):
                n = 2 * i + k
                left = first_operand(block(face_first, n, CELL))
                distances(left, block(second, face_cell(n), CELL), held[1 + 3 * k])

        def face_tiles(size, i, held):
            for k in range(2):
                n = 2 * i + k
                columns = support_columns(line(faces, n, CELL, 3))
                slopes(
                    *held[1 + 3 * k : 4 + 3 * k], columns, line(own, face_cell(n), CELL, 3), size
                )

        def face_sums(size, i, held):
            for k in range(2):
                n = jnp.maximum(2 * i, 0) + k
                c = jnp.where(i < 0, CELLS, face_cell(n))
                theirs = force_operand(face_rows, n)
                add_block(
                    total, c, SUMS, to_seconds(theirs, size, *held[2 + 3 * k : 4 + 3 * k])
                )

        in_three_turns(
            [FACE // 2], [WIDTH], lambda i: i, FACE, face_products, face_tiles, face_sums,
            slot_a, slot_b,
        )

    add_forces(total, own, term, out, carried)


FORCE_PAIR = [
    pltpu.VMEM((WIDTH, WIDTH), F32),
    pltpu.VMEM((WIDTH, WIDTH), BF),
    pltpu.VMEM((WIDTH, WIDTH), BF),
]
FORCE_SLOT = [pltpu.VMEM((WIDTH, 128), F32)] + FORCE_PAIR * 2


def local_force(part, plan, own, first, second, term, *rest):
    scratch = [
        pltpu.VMEM((2, (CELLS + 1) * SUMS, 128), F32),
        pltpu.VMEM((2, (CELLS + 1) * SUMS, 128), F32),
    ]
    if part:
        scratch.append(pltpu.VMEM((2, 2 * FACE * SUMS, 128), F32))
        scratch.append(pltpu.VMEM((2, 2 * FACE * CELL, 128), F32))
    return pl.pallas_call(
        functools.partial(local_force_kernel, part),
        in_specs=[SM] + [VM] * (4 + len(rest)),
        out_specs=VM,
        out_shape=jax.ShapeDtypeStruct((4, CELLS, WIDTH), F32),
        scratch_shapes=scratch + FORCE_SLOT * 2,
        cost_estimate=pl.CostEstimate(
            flops=64 * 65536 * 80, bytes_accessed=2 * 2**20, transcendentals=0
        ),
        compiler_params=params(),
    )(plan, own, first, second, term, *rest)


def cross_force_kernel(
    fill, plan, own, first, term, listed, arrived, carried, _, out, back,
    rows, total, theirs, their_rows, sums_of, *slots
):
    slot_a, slot_b = slots[:8], slots[8:]
    own_terms(own, term, rows)
    total[...] = jnp.zeros_like(total)
    clear([held[k] for held in (slot_a, slot_b) for k in (3, 4, 6, 7)])

    def make(e, part):
        planes = listed_planes(listed, e, part, range(ROWS), ROWS)
        at = e * SLOTS + 8 * part
        put(theirs, pair_terms(*planes)[1], at * CELL, 8, CELL)
        *speed, pressed = listed_planes(arrived, e, part, range(MOVING), MOVING)
        terms = force_terms(planes[0:3], planes[4], speed, pressed)
        blank = jnp.zeros((8, WIDTH), F32)
        put(their_rows, terms + [blank] * 4, at * SUMS, 8, SUMS)

    live_parts(fill, make, None)

    def products(pairs, held):
        for k, (slot, c) in enumerate(pairs):
            held[k][...] = support_columns(line(own, c, CELL, 3))
            left = first_operand(block(first, c, CELL))
            distances(left, block(theirs, slot, CELL), held[2 + 3 * k])

    def tiles(count, pairs, held):
        for k, (slot, c) in enumerate(pairs):
            support = listed_support(listed, slot)
            slopes(*held[2 + 3 * k : 5 + 3 * k], held[k], support, count)

    def sums(count, pairs, held):
        for k, (slot, c) in enumerate(pairs):
            tile = held[3 + 3 * k : 5 + 3 * k]
            set_block(sums_of, slot, SUMS, to_seconds(force_operand(rows, c), count, *tile))
            added = to_firsts(force_operand(their_rows, slot), count, *tile)
            if count < WIDTH:
                added = jnp.concatenate([added, jnp.zeros((SUMS, WIDTH - count), F32)], 1)
            add_block(total, c, SUMS, added)

    trips, item = pair_list(plan)
    in_three_turns(trips, SIZES, item, None, products, tiles, sums, slot_a, slot_b)

    def send(e, part):
        planes = listed_planes(listed, e, part, range(3), ROWS)
        *speed, pressed = listed_planes(arrived, e, part, range(MOVING), MOVING)
        summed = planes_of(sums_of, range(12), (e * SLOTS + 8 * part) * SUMS, 8, SUMS)
        live = live_rows(fill, e, part)
        send_rows(e, part, [jnp.where(live, f, 0.0) for f in forces_of(summed, planes, speed, pressed)])

    def send_none(e, part):
        send_rows(e, part, [jnp.zeros((8, WIDTH), F32)] * MOVING)

    def send_rows(e, part, forces):
        for k, force in enumerate(forces):
            for h in range(2):
                start = (h * SLOTS + 8 * part) * MOVING + k
                back[e, pl.ds(start, 8, stride=MOVING), :] = half(force, h)

    live_parts(fill, send, send_none)
    add_forces(total, own, term, out, carried)


def cross_force(fill, plan, own, first, term, listed, arrived, carried, after):
    return pl.pallas_call(
        cross_force_kernel,
        in_specs=[SM, SM] + [VM] * 6 + [ANYWHERE],
        out_specs=[VM, VM],
        out_shape=[
            jax.ShapeDtypeStruct((4, CELLS, WIDTH), F32),
            jax.ShapeDtypeStruct((PEERS, 2 * SLOTS * MOVING, 128), F32),
        ],
        scratch_shapes=[
            pltpu.VMEM((2, (CELLS + 1) * SUMS, 128), F32),
            pltpu.VMEM((2, (CELLS + 1) * SUMS, 128), F32),
            pltpu.VMEM((2, LISTED * CELL, 128), F32),
            pltpu.VMEM((2, LISTED * SUMS, 128), F32),
            pltpu.VMEM((2, LISTED * SUMS, 128), F32),
        ]
        + (FORCE_SLOT[:1] * 2 + FORCE_PAIR * 2) * 2,
        cost_estimate=pl.CostEstimate(
            flops=80 * 65536 * 80, bytes_accessed=2 * 2**20, transcendentals=0
        ),
        compiler_params=params(),
    )(fill, plan, own, first, term, listed, arrived, carried, after)


def finish_kernel(pair, near, returned, active_in, own, out, total, active, gate, sem):
    copies = fetch([(active_in, active)], sem)
    total[...] = jnp.zeros_like(total)

    def peer_step(e, _):
        for s in range(SLOTS):
            at = s * MOVING
            total[pair[e, s]] += both(
                lambda h: returned[
                    e, h * SLOTS * MOVING + at : h * SLOTS * MOVING + at + MOVING
                ]
            )
        return 0

    lax.fori_loop(0, PEERS, peer_step, 0)
    copies[0].wait()
    full = planes_of(own, [4], 0, CELLS, CELL)[0] > 0.0
    gate[...] = jnp.where(full, active[...].astype(F32), 0.0)

    def cell_step(c, _):
        one = pl.ds(c, 1)
        open_to = gate[one, :]
        for k in range(4):
            out[k, one, :] = (near[k, one, :] + total[c, k : k + 1]) * open_to
        return 0

    lax.fori_loop(0, CELLS, cell_step, 0, unroll=8)


def finish(pair, near, returned, active, own):
    return pl.pallas_call(
        finish_kernel,
        in_specs=[SM, VM, VM, ANYWHERE, VM],
        out_specs=VM,
        out_shape=jax.ShapeDtypeStruct((4, CELLS, WIDTH), F32),
        scratch_shapes=[
            pltpu.VMEM((CELLS, 4, WIDTH), F32),
            pltpu.VMEM((CELLS, WIDTH), jnp.int32),
            pltpu.VMEM((CELLS, WIDTH), F32),
            pltpu.SemaphoreType.DMA((1,)),
        ],
        compiler_params=params(),
    )(pair, near, returned, active, own)


def to_peers(block):
    return lax.all_to_all(block, "dev", split_axis=0, concat_axis=0, tiled=True)


def with_neighbours(rows, size):
    count = lax.axis_size("region")
    up = [(i, (i + 1) % count) for i in range(count)]
    down = [(i, (i - 1) % count) for i in range(count)]
    return jnp.concatenate(
        [
            lax.ppermute(rows[..., (CELLS - FACE) * size : CELLS * size, :], "region", up),
            lax.ppermute(rows[..., : FACE * size, :], "region", down),
        ],
        -2,
    )


def local(
    positions, velocity, smoothing, masses, energy, occupancy, active, send_cells, send_fill,
    pair_cell,
):
    pair = pair_cell[0]
    own, listed = prepare(occupancy, pair, positions, velocity, smoothing, masses)
    arrived = to_peers(listed)
    faces = with_neighbours(own, CELL)
    rho, first, second, plan = local_density(0, occupancy, send_fill, send_cells[0], own)
    rho, back = cross_density(send_fill, plan, own, first, arrived, rho)
    returned = to_peers(back)
    rho = local_density(1, plan, own, first, second, faces, rho)
    density, term, leaving = pressure(pair, rho, returned, energy, own)
    arrived_moving = to_peers(leaving)
    face_terms = with_neighbours(term, 1)
    sums = local_force(0, plan, own, first, second, term)
    sums, force_back = cross_force(
        send_fill, plan, own, first, term, arrived, arrived_moving, sums, face_terms
    )
    returned_force = to_peers(force_back)
    sums = local_force(1, plan, own, first, second, term, faces, face_terms, sums)
    forces = finish(pair, sums, returned_force, active, own)
    return (density, forces)


def solution(mesh):
    cells = P(("region", "dev"), None)
    vectors = P(None, ("region", "dev"), None)
    lists = P(("region", "dev"), None, None)
    in_specs = (
        vectors, vectors, cells, cells, cells, P(("region", "dev")), cells, lists, cells, lists,
    )
    return jax.shard_map(
        local, mesh=mesh, in_specs=in_specs, out_specs=(cells, vectors), check_vma=False
    )
```

```python
import functools
import math

import jax
import jax.numpy as jnp
from jax import lax
from jax.experimental import pallas as pl
from jax.experimental.pallas import tpu as pltpu
from jax.sharding import PartitionSpec as P

BF = jnp.bfloat16
F32 = jnp.float32
FACE = 4
CELLS = 64
WIDTH = 256
PEERS = 16
SLOTS = 16
LISTED = PEERS * SLOTS
GAMMA_LESS = 2.0 / 3.0
W_SCALE = 84.0 / math.pi
G_SCALE = 6720.0 / math.pi
TINY = 1e-14
EMPTY = 1e8
CHUNK = 32
CELL = 8
SUMS = 16
NN = (((1,), (0,)), ((), ()))
NT = (((1,), (1,)), ((), ()))
VM = pl.BlockSpec(memory_space=pltpu.VMEM)
SM = pl.BlockSpec(memory_space=pltpu.SMEM)
ROWS = 5
MOVING = 4
SPLIT = 40
SIZES = (144, 160, 176, 192, 208, 224, 240, 256)
STEP = 16
KINDS = len(SIZES)
UNIT = 4
LOCAL_AT = 3 * KINDS
LOCAL_LEAD = 2
LOCAL_LIST = CELLS + 8
CROSS_AT = LOCAL_AT + 2 * LOCAL_LIST
CROSS_LEAD = 4
CROSS_LIST = LISTED + 16
PLAN = CROSS_AT + CROSS_LIST
PACK = 128
ANYWHERE = pl.BlockSpec(memory_space=pl.ANY)
OWN_ROWS = jax.ShapeDtypeStruct((2, (CELLS + 1) * CELL, 128), F32)


def params(mib=50):
    return pltpu.CompilerParams(vmem_limit_bytes=int(mib * 2**20))


def split2(x):
    a = x.astype(BF)
    return a, (x - a.astype(F32)).astype(BF)


def split3(x):
    a = x.astype(BF).astype(F32)
    rest = x - a
    b = rest.astype(BF).astype(F32)
    return a, b, rest - b


def pair_terms(x, y, z, h, m):
    norm = 4.0 * (x * x + y * y + z * z)
    root = lax.rsqrt(jnp.where(m > 0.0, m, 1.0))
    mu = jnp.where(m > 0.0, root * lax.rsqrt(root), EMPTY)
    one = jnp.ones_like(x)
    first = [-8.0 * x, -8.0 * y, -8.0 * z, norm, one, h * h * mu, 2.0 * h * mu, mu]
    second = [x, y, z, one, norm, mu, h * mu, h * h * mu]
    return first, second


def both(read):
    return jnp.concatenate([read(0), read(1)], -1)


def half(value, h):
    return value[..., 128 * h : 128 * (h + 1)]


def put(ref, planes, start, count, stride):
    for k, plane in enumerate(planes):
        for h in range(2):
            ref[h, pl.ds(start + k, count, stride=stride), :] = half(plane, h)


def planes_of(ref, ids, start, count, stride):
    return [both(lambda h: ref[h, pl.ds(start + k, count, stride=stride), :]) for k in ids]


def rows_at(index, size):
    return pl.ds(pl.multiple_of(index * size, size), size)


def block(ref, index, size):
    return both(lambda h: ref[h, rows_at(index, size), :])


def set_block(ref, index, size, value):
    for h in range(2):
        ref[h, rows_at(index, size), :] = half(value, h)


def add_block(ref, index, size, value):
    for h in range(2):
        ref[h, rows_at(index, size), :] += half(value, h)


def line(ref, index, size, k):
    return both(lambda h: ref[h, pl.ds(index * size + k, 1), :])


def listed_planes(listed, e, part, ids, size):
    step = SLOTS * size
    start = 8 * part * size
    return [
        both(lambda h: listed[e, pl.ds(h * step + start + k, 8, stride=size), :]) for k in ids
    ]


def listed_support(listed, slot):
    at = (slot % SLOTS) * ROWS + 3
    return both(lambda h: listed[slot // SLOTS, pl.ds(h * SLOTS * ROWS + at, 1), :])


def first_operand(rows):
    a1, a2, a3 = split3(rows)
    return jnp.concatenate([a1, a1, a2, a2, a1, a3, jnp.zeros((80, WIDTH), F32)], 0).T.astype(BF)


def second_operands(rows, both):
    b1, b2, b3 = split3(rows)
    stacked = jnp.concatenate([b1, b2, b1, b2, b3, b1, jnp.zeros((80, WIDTH), F32)], 0)
    part = lax.broadcasted_iota(jnp.int32, stacked.shape, 0) % 8
    near = jnp.where(part < 5, stacked, 0.0).astype(BF)
    if not both:
        return near
    return near, jnp.where(part >= 5, stacked, 0.0).astype(BF)


def support_columns(row):
    return jnp.broadcast_to(row, (128, WIDTH)).T


def density_products(left, operands, s_ref, mix_ref):
    s_ref[...] = jnp.dot(left, operands[0], preferred_element_type=F32)
    mix_ref[...] = jnp.dot(left, operands[1], preferred_element_type=F32)


def weights_of(s, mix, columns, row):
    s = jnp.maximum(s, TINY)
    dist = s * lax.rsqrt(s)
    support = columns + row
    d = jnp.maximum(support - dist, 0.0)
    x = pl.reciprocal(mix, approx=True) * d
    x = x * x
    x = x * x
    return x * (support + 4.0 * dist)


def density_weights(count, s_ref, mix_ref, columns, row, one_sided):
    second = jnp.zeros((8, WIDTH), F32)
    firsts = []
    for start in range(0, count, CHUNK):
        part = slice(start, min(start + CHUNK, count))
        wide = columns[part]
        w = weights_of(s_ref[part], mix_ref[part], jnp.concatenate([wide, wide], 1), row)
        for k in range(w.shape[0] // 8):
            second = second + w[8 * k : 8 * k + 8]
        if not one_sided:
            firsts.append(w[:, :128] + w[:, 128:])
    if one_sided:
        return second
    if count < WIDTH:
        firsts.append(jnp.zeros((WIDTH - count, 128), F32))
    turned = jnp.concatenate(firsts, 0).T
    first = turned[:8]
    for k in range(1, 16):
        first = first + turned[8 * k : 8 * k + 8]
    return second, first


def inverse_mass(m):
    return jnp.where(m > 0.0, W_SCALE / jnp.where(m > 0.0, m, 1.0), 0.0)


def self_weights(count, s_ref, mix_ref, columns, row):
    sums = [jnp.zeros((8, 128), F32)] * 2
    crossing = []
    for start in range(0, count, CHUNK):
        part = slice(start, min(start + CHUNK, count))
        for h in range(0 if start < 128 else 1, 2):
            lanes = slice(128 * h, 128 * (h + 1))
            w = weights_of(s_ref[part, lanes], mix_ref[part, lanes], columns[part], half(row, h))
            for k in range(w.shape[0] // 8):
                sums[h] = sums[h] + w[8 * k : 8 * k + 8]
            if h and start < 128:
                crossing.append(w)
    turned = jnp.concatenate(crossing, 0).T
    for k in range(16):
        sums[0] = sums[0] + turned[8 * k : 8 * k + 8]
    return jnp.concatenate(sums, 1)


def fetch(pairs, sem):
    copies = [
        pltpu.make_async_copy(source, target, sem.at[k])
        for k, (source, target) in enumerate(pairs)
    ]
    for copy in copies:
        copy.start()
    return copies


def prepare_kernel(
    occ, pair, pos_in, vel_in, smooth_in, mass_in, own, out, pos, vel, smooth, mass, full, sem
):
    copies = fetch(
        [(pos_in, pos), (vel_in, vel), (smooth_in, smooth), (mass_in, mass)], sem
    )
    lane = lax.broadcasted_iota(jnp.int32, (1, WIDTH), 1)
    for c in range(CELLS):
        full[c : c + 1, :] = (lane < occ[c]).astype(F32)
    for copy in copies:
        copy.wait()
    place = [pos[k] - 0.5 for k in range(3)]
    m = jnp.where(full[...] > 0.0, mass[...], 0.0)
    put(own, place + [smooth[...], m] + [vel[k] for k in range(3)], 0, CELLS, CELL)
    blank = jnp.zeros((CELL, WIDTH), F32)
    wide = jnp.full((1, WIDTH), 0.5, F32)
    set_block(own, CELLS, CELL, jnp.concatenate([blank[:3], wide, blank[:4]], 0))

    def peer_step(e, _):
        for s in range(SLOTS):
            c = pair[e, s]
            for h in range(2):
                at = (h * SLOTS + s) * ROWS
                out[e, at : at + ROWS] = own[h, rows_at(c, CELL), :][:ROWS]
        return 0

    lax.fori_loop(0, PEERS, peer_step, 0)


def prepare(occ, pair, pos, vel, smooth, mass):
    plane = pltpu.VMEM((CELLS, WIDTH), F32)
    return pl.pallas_call(
        prepare_kernel,
        in_specs=[SM] * 2 + [ANYWHERE] * 4,
        out_specs=[VM] * 2,
        out_shape=[
            OWN_ROWS,
            jax.ShapeDtypeStruct((PEERS, 2 * SLOTS * ROWS, 128), F32),
        ],
        scratch_shapes=[
            pltpu.VMEM((3, CELLS, WIDTH), F32),
            pltpu.VMEM((3, CELLS, WIDTH), F32),
            plane,
            plane,
            plane,
            pltpu.SemaphoreType.DMA((4,)),
        ],
        compiler_params=params(60),
    )(occ, pair, pos, vel, smooth, mass)


def kind_of(size):
    return jnp.maximum(size - SIZES[0] + STEP - 1, 0) // STEP


def byte_of(kind):
    one = jnp.left_shift(jnp.int32(1), 8 * (kind % 4))
    return jnp.where(kind < 4, one, 0), jnp.where(kind < 4, 0, one)


def read_byte(pair, kind):
    return (jnp.where(kind < 4, pair[0], pair[1]) >> (8 * (kind % 4))) & 255


def add_byte(pair, kind):
    low, high = byte_of(kind)
    return pair[0] + low, pair[1] + high


def make_plan(occ, fill, cells, plan):
    def over_local(visit, part, carry):
        low, high = (SPLIT, CELLS) if part else (0, SPLIT)
        step = lambda c, carry: visit(kind_of(occ[c]), c, carry)
        return lax.fori_loop(low, high, step, carry, unroll=8)

    def over_pairs(visit, carry):
        def peer_step(e, carry):
            def slot_step(s, carry):
                cell = cells[e, s]
                return visit(kind_of(occ[cell]), (e * SLOTS + s) * PACK + cell, carry)

            return lax.fori_loop(0, fill[0, e], slot_step, carry)

        return lax.fori_loop(0, PEERS, peer_step, carry)

    unused = jnp.int32(0)
    for e in range(PEERS):
        unused = jnp.where(fill[0, e] == 0, e * SLOTS, unused)

    for group, (walk, start, lead, unit, blank) in enumerate(
        [
            (lambda v, x: over_local(v, 0, x), LOCAL_AT, LOCAL_LEAD, 2, CELLS),
            (lambda v, x: over_local(v, 1, x), LOCAL_AT + LOCAL_LIST, LOCAL_LEAD, 2, CELLS),
            (over_pairs, CROSS_AT, CROSS_LEAD, UNIT, unused * PACK + CELLS),
        ]
    ):
        none = (jnp.int32(0), jnp.int32(0))
        counts = walk(lambda kind, value, packed: add_byte(packed, kind), none)
        total = jnp.int32(0)
        done = jnp.int32(0)
        places = [jnp.int32(0)] * 2
        for k in range(KINDS):
            places[k // 4] = places[k // 4] + jnp.left_shift(total, 8 * (k % 4))
            total = total + ((counts[k // 4] >> (8 * (k % 4))) & 255)
            upto = (total + (unit - 1 if k == KINDS - 1 else 0)) // unit
            plan[group * KINDS + k] = upto - done
            done = upto
        for k in range(lead):
            plan[start + k] = blank
        for k in range(unit + 1):
            plan[start + lead + total + k] = blank

        def place(kind, value, packed, start=start + lead):
            plan[start + read_byte(packed, kind)] = value
            return add_byte(packed, kind)

        walk(place, tuple(places))


def fold(total, own, out, carried):
    mine = sum(planes_of(total, range(CELL), 0, CELLS, CELL))
    mass = planes_of(own, [4], 0, CELLS, CELL)[0]
    mine = mine * inverse_mass(mass)
    out[...] = mine if carried is None else carried[...] + mine


def make_face_first(faces, face_first):
    planes = planes_of(faces, range(ROWS), 0, 2 * FACE, CELL)
    put(face_first, pair_terms(*planes)[0], 0, 2 * FACE, CELL)


def face_cell(n):
    return jnp.where(n < FACE, n, CELLS - 2 * FACE + n)


def in_turns(trips, sizes, item, last, products, weights, slot_a, slot_b):
    products(item(0), slot_a)
    base = 0
    for count, size in zip(trips, sizes):

        def step(i, _, size=size):
            products(item(2 * i + 1), slot_b)
            weights(size, item(2 * i), slot_a)
            after = 2 * i + 2
            products(item(after if last is None else jnp.minimum(after, last - 1)), slot_a)
            weights(size, item(2 * i + 1), slot_b)
            return 0

        lax.fori_loop(base, base + count, step, 0)
        base = base + count


def cell_list(plan, part):
    start = LOCAL_AT + part * LOCAL_LIST + LOCAL_LEAD
    return [plan[part * KINDS + k] for k in range(KINDS)], lambda n: plan[start + n]


def pair_list(plan):
    start = CROSS_AT + CROSS_LEAD

    def item(n):
        entries = [plan[start + 2 * n + k] for k in range(2)]
        return [(entry // PACK, entry % PACK) for entry in entries]

    return [plan[2 * KINDS + k] for k in range(KINDS)], item


def live_parts(fill, visit, other):
    def step(n, _):
        e, part = n // 2, n % 2
        live = fill[0, e] > 8 * part

        @pl.when(live)
        def _():
            visit(e, part)

        if other is not None:

            @pl.when(jnp.logical_not(live))
            def _():
                other(e, part)

        return 0

    lax.fori_loop(0, 2 * PEERS, step, 0)


def local_density_kernel(part, *refs):
    if part:
        plan, own, first, second, faces, carried, rho, total, face_first, *slots = refs
    else:
        carried = None
        occ, fill, cells, own, rho, first, second, plan, total, *slots = refs
        make_plan(occ, fill, cells, plan)
        planes = planes_of(own, range(ROWS), 0, CELLS, CELL)
        blank = [jnp.zeros((1, WIDTH), F32)] * 3 + [jnp.full((1, WIDTH), 0.5, F32)]
        for ref, some, none in zip(
            (first, second), pair_terms(*planes), pair_terms(*blank, blank[0])
        ):
            put(ref, some, 0, CELLS, CELL)
            set_block(ref, CELLS, CELL, jnp.concatenate(none, 0))
    slot_a, slot_b = slots[:6], slots[6:]
    total[...] = jnp.zeros_like(total)

    def products(c, held):
        left = first_operand(block(first, c, CELL))
        after = jnp.minimum(c + 1, CELLS)
        held[4][...] = support_columns(line(own, c, CELL, 3))
        density_products(left, second_operands(block(second, c, CELL), True), *held[0:2])
        density_products(left, second_operands(block(second, after, CELL), True), *held[2:4])

    def weights(count, c, held):
        after = jnp.minimum(c + 1, CELLS)
        row, other = line(own, c, CELL, 3), line(own, after, CELL, 3)
        own_sum = self_weights(count, *held[0:2], held[4], row)
        there, here = density_weights(count, *held[2:4], held[4], other, False)
        add_block(total, c, CELL, own_sum + here)
        add_block(total, after, CELL, there)

    trips, item = cell_list(plan, part)
    in_turns(trips, SIZES, item, None, products, weights, slot_a, slot_b)

    if part:
        make_face_first(faces, face_first)

        def face_products(i, held):
            for k in range(2):
                n = 2 * i + k
                left = first_operand(block(face_first, n, CELL))
                operands = second_operands(block(second, face_cell(n), CELL), True)
                held[4 + k][...] = support_columns(line(faces, n, CELL, 3))
                density_products(left, operands, *held[2 * k : 2 * k + 2])

        def face_weights(size, i, held):
            for k in range(2):
                c = face_cell(2 * i + k)
                added = density_weights(
                    size, *held[2 * k : 2 * k + 2], held[4 + k], line(own, c, CELL, 3), True
                )
                add_block(total, c, CELL, added)

        in_turns(
            [FACE // 2], [WIDTH], lambda i: i, FACE, face_products, face_weights, slot_a, slot_b
        )

    fold(total, own, rho, carried)


DENSITY_SLOT = [pltpu.VMEM((WIDTH, WIDTH), F32)] * 4 + [pltpu.VMEM((WIDTH, 128), F32)] * 2


def local_density(part, *operands):
    plane = jax.ShapeDtypeStruct((CELLS, WIDTH), F32)
    if part:
        in_specs, out_specs, out_shape = [SM] + [VM] * 5, VM, plane
    else:
        in_specs, out_specs = [SM] * 3 + [VM], [VM] * 3 + [SM]
        out_shape = [plane, OWN_ROWS, OWN_ROWS, jax.ShapeDtypeStruct((PLAN,), jnp.int32)]
    return pl.pallas_call(
        functools.partial(local_density_kernel, part),
        in_specs=in_specs,
        out_specs=out_specs,
        out_shape=out_shape,
        scratch_shapes=[pltpu.VMEM((2, (CELLS + 1) * CELL, 128), F32)]
        + [pltpu.VMEM((2, 2 * FACE * CELL, 128), F32)] * part
        + DENSITY_SLOT * 2,
        cost_estimate=pl.CostEstimate(
            flops=64 * 65536 * 60, bytes_accessed=2 * 2**20, transcendentals=0
        ),
        compiler_params=params(),
    )(*operands)


def live_rows(fill, e, part):
    row = lax.broadcasted_iota(jnp.int32, (8, WIDTH), 0)
    return row < fill[0, e] - 8 * part


def cross_density_kernel(
    fill, plan, own, first, listed, carried, rho, back, total, theirs, there_of, *slots
):
    slot_a, slot_b = slots[:6], slots[6:]
    total[...] = jnp.zeros_like(total)

    def make(e, part):
        after = pair_terms(*listed_planes(listed, e, part, range(ROWS), ROWS))[1]
        put(theirs, after, (e * SLOTS + 8 * part) * CELL, 8, CELL)

    live_parts(fill, make, None)

    def products(pairs, held):
        for k, (slot, c) in enumerate(pairs):
            left = first_operand(block(first, c, CELL))
            held[4 + k][...] = support_columns(line(own, c, CELL, 3))
            operands = second_operands(block(theirs, slot, CELL), True)
            density_products(left, operands, *held[2 * k : 2 * k + 2])

    def weights(count, pairs, held):
        for k, (slot, c) in enumerate(pairs):
            support = listed_support(listed, slot)
            there, here = density_weights(
                count, *held[2 * k : 2 * k + 2], held[4 + k], support, False
            )
            add_block(total, c, CELL, here)
            set_block(there_of, slot, CELL, there)

    trips, item = pair_list(plan)
    in_turns(trips, SIZES, item, None, products, weights, slot_a, slot_b)

    def send(e, part):
        start = (e * SLOTS + 8 * part) * CELL
        summed = sum(planes_of(there_of, range(CELL), start, 8, CELL))
        mass = listed_planes(listed, e, part, [4], ROWS)[0]
        value = jnp.where(live_rows(fill, e, part), summed * inverse_mass(mass), 0.0)
        back[e, rows_at(part, 8), :] = value

    def send_none(e, part):
        back[e, rows_at(part, 8), :] = jnp.zeros((8, WIDTH), F32)

    live_parts(fill, send, send_none)
    fold(total, own, rho, carried)


def cross_density(fill, plan, own, first, listed, carried):
    return pl.pallas_call(
        cross_density_kernel,
        in_specs=[SM, SM] + [VM] * 4,
        out_specs=[VM, VM],
        out_shape=[
            jax.ShapeDtypeStruct((CELLS, WIDTH), F32),
            jax.ShapeDtypeStruct((PEERS, SLOTS, WIDTH), F32),
        ],
        scratch_shapes=[
            pltpu.VMEM((2, (CELLS + 1) * CELL, 128), F32),
            pltpu.VMEM((2, LISTED * CELL, 128), F32),
            pltpu.VMEM((2, LISTED * CELL, 128), F32),
        ]
        + DENSITY_SLOT * 2,
        cost_estimate=pl.CostEstimate(
            flops=80 * 65536 * 60, bytes_accessed=2 * 2**20, transcendentals=0
        ),
        compiler_params=params(),
    )(fill, plan, own, first, listed, carried)


def pressure_kernel(
    pair, near, returned, energy_in, own, density, term, out, energy, sum_of, moving, sem
):
    copies = fetch([(energy_in, energy)], sem)
    sum_of[...] = near[...]

    def peer_step(e, _):
        for s in range(SLOTS):
            sum_of[pl.ds(pair[e, s], 1), :] += returned[e, s : s + 1]
        return 0

    lax.fori_loop(0, PEERS, peer_step, 0)
    copies[0].wait()
    full = planes_of(own, [4], 0, CELLS, CELL)[0] > 0.0
    rho = jnp.where(full, sum_of[...], 0.0)
    density[...] = rho
    term[...] = jnp.where(full, GAMMA_LESS * energy[...] / jnp.where(full, rho, 1.0), 0.0)

    def cell_step(c, _):
        moving[c] = jnp.concatenate(
            [line(own, c, CELL, k) for k in (5, 6, 7)] + [term[pl.ds(c, 1), :]], 0
        )
        return 0

    lax.fori_loop(0, CELLS, cell_step, 0, unroll=8)

    def send_step(e, _):
        for s in range(SLOTS):
            cell = moving[pair[e, s]]
            for h in range(2):
                at = (h * SLOTS + s) * MOVING
                out[e, at : at + MOVING] = half(cell, h)
        return 0

    lax.fori_loop(0, PEERS, send_step, 0)


def pressure(pair, near, returned, energy, own):
    plane = jax.ShapeDtypeStruct((CELLS, WIDTH), F32)
    return pl.pallas_call(
        pressure_kernel,
        in_specs=[SM, VM, VM, ANYWHERE, VM],
        out_specs=[VM, VM, VM],
        out_shape=[
            plane,
            plane,
            jax.ShapeDtypeStruct((PEERS, 2 * SLOTS * MOVING, 128), F32),
        ],
        scratch_shapes=[
            pltpu.VMEM((CELLS, WIDTH), F32),
            pltpu.VMEM((CELLS, WIDTH), F32),
            pltpu.VMEM((CELLS, MOVING, WIDTH), F32),
            pltpu.SemaphoreType.DMA((1,)),
        ],
        compiler_params=params(),
    )(pair, near, returned, energy, own)


def force_terms(place, m, speed, term):
    mp = m * term
    turned = sum(a * b for a, b in zip(place, speed))
    return (
        [m] + [m * a for a in place] + [mp] + [mp * a for a in place]
        + [m * a for a in speed] + [m * turned]
    )


def forces_of(sums, place, speed, term):
    lean = [a * sums[0] - b for a, b in zip(place, sums[1:4])]
    acc = [term * a + (b * sums[4] - c) for a, b, c in zip(lean, place, sums[5:8])]
    mixed = sum(a * b - c * d for a, b, c, d in zip(speed, lean, place, sums[8:11]))
    return [G_SCALE * a for a in acc] + [-G_SCALE * term * (mixed + sums[11])]


def force_operand(ref, index):
    high, low = split2(block(ref, index, SUMS))
    return jnp.concatenate([high, low], 0)


def own_terms(own, term, rows):
    planes = planes_of(own, range(CELL), 0, CELLS, CELL)
    terms = force_terms(planes[0:3], planes[4], planes[5:8], term[...])
    put(rows, terms, 0, CELLS, SUMS)
    put(rows, [jnp.zeros((CELLS, WIDTH), F32)] * 4, 12, CELLS, SUMS)
    set_block(rows, CELLS, SUMS, jnp.zeros((SUMS, WIDTH), F32))


def slopes(s_ref, high, low, columns, row, count):
    for start in range(0, count, CHUNK):
        part = slice(start, min(start + CHUNK, count))
        s = jnp.maximum(s_ref[part], TINY)
        dist = s * lax.rsqrt(s)
        wide = columns[part]
        support = jnp.concatenate([wide, wide], 1) + row
        d = jnp.maximum(support - dist, 0.0)
        e = pl.reciprocal(support * support, approx=True)
        x = e * d
        g = (x * x) * (x * e)
        top = g.astype(BF)
        high[part] = top
        low[part] = (g - top.astype(F32)).astype(BF)


def distances(left, rows, s_ref):
    s_ref[...] = jnp.dot(left, second_operands(rows, False), preferred_element_type=F32)


def to_seconds(rows, count, high, low):
    part = rows[:, :count]
    top = lax.dot_general(part, high[0:count], NN, preferred_element_type=F32)
    both = top + lax.dot_general(part, low[0:count], NN, preferred_element_type=F32)
    return both[:SUMS] + both[SUMS:]


def to_firsts(rows, count, high, low):
    top = lax.dot_general(rows, high[0:count], NT, preferred_element_type=F32)
    both = top + lax.dot_general(rows, low[0:count], NT, preferred_element_type=F32)
    return both[:SUMS] + both[SUMS:]


def in_three_turns(trips, sizes, item, last, products, tiles, sums, slot_a, slot_b):
    products(item(0), slot_a)
    base = 0
    for count, size in zip(trips, sizes):

        def step(i, _, size=size):
            products(item(2 * i + 1), slot_b)
            sums(size, item(2 * i - 2), slot_a)
            tiles(size, item(2 * i), slot_a)
            after = 2 * i + 2
            products(item(after if last is None else jnp.minimum(after, last - 1)), slot_a)
            sums(size, item(2 * i - 1), slot_b)
            tiles(size, item(2 * i + 1), slot_b)
            return 0

        lax.fori_loop(base, base + count, step, 0)
        base = base + count
    sums(sizes[-1], item(2 * base - 2), slot_a)
    sums(sizes[-1], item(2 * base - 1), slot_b)


def clear(slots):
    for held in slots:
        held[SIZES[0] :, :] = jnp.zeros((WIDTH - SIZES[0], WIDTH), BF)


def add_forces(total, own, term, out):
    planes = planes_of(own, range(CELL), 0, CELLS, CELL)
    sums = planes_of(total, range(12), 0, CELLS, SUMS)
    for k, force in enumerate(forces_of(sums, planes[0:3], planes[5:8], term[...])):
        out[k] = force


def local_force_kernel(part, plan, own, first, second, term, *rest):
    if part:
        faces, face_terms, rows, carried, out, total, face_rows, face_first, *slots = rest
        total[...] = carried[...]
    else:
        rows, total, *slots = rest
        own_terms(own, term, rows)
        total[...] = jnp.zeros_like(total)
    slot_a, slot_b = slots[:7], slots[7:]
    clear([held[k] for held in (slot_a, slot_b) for k in (2, 3, 5, 6)])

    def products(c, held):
        left = first_operand(block(first, c, CELL))
        held[0][...] = support_columns(line(own, c, CELL, 3))
        distances(left, block(second, c, CELL), held[1])
        distances(left, block(second, jnp.minimum(c + 1, CELLS), CELL), held[4])

    def tiles(count, c, held):
        other = line(own, jnp.minimum(c + 1, CELLS), CELL, 3)
        slopes(*held[1:4], held[0], line(own, c, CELL, 3), count)
        slopes(*held[4:7], held[0], other, count)

    def sums(count, c, held):
        after = jnp.minimum(c + 1, CELLS)
        mine, other = force_operand(rows, c), force_operand(rows, after)
        added = to_firsts(other, count, *held[5:7])
        if count < WIDTH:
            added = jnp.concatenate([added, jnp.zeros((SUMS, WIDTH - count), F32)], 1)
        add_block(total, c, SUMS, to_seconds(mine, count, *held[2:4]) + added)
        add_block(total, after, SUMS, to_seconds(mine, count, *held[5:7]))

    trips, item = cell_list(plan, part)
    in_three_turns(trips, SIZES, item, None, products, tiles, sums, slot_a, slot_b)

    if part:
        make_face_first(faces, face_first)
        planes = planes_of(faces, range(CELL), 0, 2 * FACE, CELL)
        terms = force_terms(planes[0:3], planes[4], planes[5:8], face_terms[...])
        blank = jnp.zeros((2 * FACE, WIDTH), F32)
        put(face_rows, terms + [blank] * 4, 0, 2 * FACE, SUMS)

        def face_products(i, held):
            for k in range(2):
                n = 2 * i + k
                left = first_operand(block(face_first, n, CELL))
                distances(left, block(second, face_cell(n), CELL), held[1 + 3 * k])

        def face_tiles(size, i, held):
            for k in range(2):
                n = 2 * i + k
                columns = support_columns(line(faces, n, CELL, 3))
                slopes(
                    *held[1 + 3 * k : 4 + 3 * k], columns, line(own, face_cell(n), CELL, 3), size
                )

        def face_sums(size, i, held):
            for k in range(2):
                n = jnp.maximum(2 * i, 0) + k
                c = jnp.where(i < 0, CELLS, face_cell(n))
                theirs = force_operand(face_rows, n)
                add_block(
                    total, c, SUMS, to_seconds(theirs, size, *held[2 + 3 * k : 4 + 3 * k])
                )

        in_three_turns(
            [FACE // 2], [WIDTH], lambda i: i, FACE, face_products, face_tiles, face_sums,
            slot_a, slot_b,
        )

        add_forces(total, own, term, out)


FORCE_PAIR = [
    pltpu.VMEM((WIDTH, WIDTH), F32),
    pltpu.VMEM((WIDTH, WIDTH), BF),
    pltpu.VMEM((WIDTH, WIDTH), BF),
]
FORCE_SLOT = [pltpu.VMEM((WIDTH, 128), F32)] + FORCE_PAIR * 2


SUM_ROWS = jax.ShapeDtypeStruct((2, (CELLS + 1) * SUMS, 128), F32)


def local_force(part, plan, own, first, second, term, *rest):
    if part:
        out_shape = jax.ShapeDtypeStruct((4, CELLS, WIDTH), F32)
        scratch = [
            pltpu.VMEM(SUM_ROWS.shape, F32),
            pltpu.VMEM((2, 2 * FACE * SUMS, 128), F32),
            pltpu.VMEM((2, 2 * FACE * CELL, 128), F32),
        ]
    else:
        out_shape = [SUM_ROWS] * 2
        scratch = []
    return pl.pallas_call(
        functools.partial(local_force_kernel, part),
        in_specs=[SM] + [VM] * (4 + len(rest)),
        out_specs=VM if part else [VM, VM],
        out_shape=out_shape,
        scratch_shapes=scratch + FORCE_SLOT * 2,
        cost_estimate=pl.CostEstimate(
            flops=64 * 65536 * 80, bytes_accessed=2 * 2**20, transcendentals=0
        ),
        compiler_params=params(),
    )(plan, own, first, second, term, *rest)


def cross_force_kernel(
    fill, plan, own, first, rows, listed, arrived, carried, _, total, back,
    theirs, their_rows, sums_of, *slots
):
    slot_a, slot_b = slots[:8], slots[8:]
    total[...] = carried[...]
    clear([held[k] for held in (slot_a, slot_b) for k in (3, 4, 6, 7)])

    def make(e, part):
        planes = listed_planes(listed, e, part, range(ROWS), ROWS)
        at = e * SLOTS + 8 * part
        put(theirs, pair_terms(*planes)[1], at * CELL, 8, CELL)
        *speed, pressed = listed_planes(arrived, e, part, range(MOVING), MOVING)
        terms = force_terms(planes[0:3], planes[4], speed, pressed)
        blank = jnp.zeros((8, WIDTH), F32)
        put(their_rows, terms + [blank] * 4, at * SUMS, 8, SUMS)

    live_parts(fill, make, None)

    def products(pairs, held):
        for k, (slot, c) in enumerate(pairs):
            held[k][...] = support_columns(line(own, c, CELL, 3))
            left = first_operand(block(first, c, CELL))
            distances(left, block(theirs, slot, CELL), held[2 + 3 * k])

    def tiles(count, pairs, held):
        for k, (slot, c) in enumerate(pairs):
            support = listed_support(listed, slot)
            slopes(*held[2 + 3 * k : 5 + 3 * k], held[k], support, count)

    def sums(count, pairs, held):
        for k, (slot, c) in enumerate(pairs):
            tile = held[3 + 3 * k : 5 + 3 * k]
            set_block(sums_of, slot, SUMS, to_seconds(force_operand(rows, c), count, *tile))
            added = to_firsts(force_operand(their_rows, slot), count, *tile)
            if count < WIDTH:
                added = jnp.concatenate([added, jnp.zeros((SUMS, WIDTH - count), F32)], 1)
            add_block(total, c, SUMS, added)

    trips, item = pair_list(plan)
    in_three_turns(trips, SIZES, item, None, products, tiles, sums, slot_a, slot_b)

    def send(e, part):
        planes = listed_planes(listed, e, part, range(3), ROWS)
        *speed, pressed = listed_planes(arrived, e, part, range(MOVING), MOVING)
        summed = planes_of(sums_of, range(12), (e * SLOTS + 8 * part) * SUMS, 8, SUMS)
        live = live_rows(fill, e, part)
        send_rows(e, part, [jnp.where(live, f, 0.0) for f in forces_of(summed, planes, speed, pressed)])

    def send_none(e, part):
        send_rows(e, part, [jnp.zeros((8, WIDTH), F32)] * MOVING)

    def send_rows(e, part, forces):
        for k, force in enumerate(forces):
            for h in range(2):
                start = (h * SLOTS + 8 * part) * MOVING + k
                back[e, pl.ds(start, 8, stride=MOVING), :] = half(force, h)

    live_parts(fill, send, send_none)


def cross_force(fill, plan, own, first, rows, listed, arrived, carried, after):
    return pl.pallas_call(
        cross_force_kernel,
        in_specs=[SM, SM] + [VM] * 6 + [ANYWHERE],
        out_specs=[VM, VM],
        out_shape=[
            SUM_ROWS,
            jax.ShapeDtypeStruct((PEERS, 2 * SLOTS * MOVING, 128), F32),
        ],
        scratch_shapes=[
            pltpu.VMEM((2, LISTED * CELL, 128), F32),
            pltpu.VMEM((2, LISTED * SUMS, 128), F32),
            pltpu.VMEM((2, LISTED * SUMS, 128), F32),
        ]
        + (FORCE_SLOT[:1] * 2 + FORCE_PAIR * 2) * 2,
        cost_estimate=pl.CostEstimate(
            flops=80 * 65536 * 80, bytes_accessed=2 * 2**20, transcendentals=0
        ),
        compiler_params=params(),
    )(fill, plan, own, first, rows, listed, arrived, carried, after)


def finish_kernel(pair, near, returned, active_in, own, out, total, active, gate, sem):
    copies = fetch([(active_in, active)], sem)
    total[...] = jnp.zeros_like(total)

    def peer_step(e, _):
        for s in range(SLOTS):
            at = s * MOVING
            total[pair[e, s]] += both(
                lambda h: returned[
                    e, h * SLOTS * MOVING + at : h * SLOTS * MOVING + at + MOVING
                ]
            )
        return 0

    lax.fori_loop(0, PEERS, peer_step, 0)
    copies[0].wait()
    full = planes_of(own, [4], 0, CELLS, CELL)[0] > 0.0
    gate[...] = jnp.where(full, active[...].astype(F32), 0.0)

    def cell_step(c, _):
        one = pl.ds(c, 1)
        open_to = gate[one, :]
        for k in range(4):
            out[k, one, :] = (near[k, one, :] + total[c, k : k + 1]) * open_to
        return 0

    lax.fori_loop(0, CELLS, cell_step, 0, unroll=8)


def finish(pair, near, returned, active, own):
    return pl.pallas_call(
        finish_kernel,
        in_specs=[SM, VM, VM, ANYWHERE, VM],
        out_specs=VM,
        out_shape=jax.ShapeDtypeStruct((4, CELLS, WIDTH), F32),
        scratch_shapes=[
            pltpu.VMEM((CELLS, 4, WIDTH), F32),
            pltpu.VMEM((CELLS, WIDTH), jnp.int32),
            pltpu.VMEM((CELLS, WIDTH), F32),
            pltpu.SemaphoreType.DMA((1,)),
        ],
        compiler_params=params(),
    )(pair, near, returned, active, own)


def to_peers(block):
    return lax.all_to_all(block, "dev", split_axis=0, concat_axis=0, tiled=True)


def with_neighbours(rows, size):
    count = lax.axis_size("region")
    up = [(i, (i + 1) % count) for i in range(count)]
    down = [(i, (i - 1) % count) for i in range(count)]
    return jnp.concatenate(
        [
            lax.ppermute(rows[..., (CELLS - FACE) * size : CELLS * size, :], "region", up),
            lax.ppermute(rows[..., : FACE * size, :], "region", down),
        ],
        -2,
    )


def local(
    positions, velocity, smoothing, masses, energy, occupancy, active, send_cells, send_fill,
    pair_cell,
):
    pair = pair_cell[0]
    own, listed = prepare(occupancy, pair, positions, velocity, smoothing, masses)
    arrived = to_peers(listed)
    faces = with_neighbours(own, CELL)
    rho, first, second, plan = local_density(0, occupancy, send_fill, send_cells[0], own)
    rho, back = cross_density(send_fill, plan, own, first, arrived, rho)
    returned = to_peers(back)
    rho = local_density(1, plan, own, first, second, faces, rho)
    density, term, leaving = pressure(pair, rho, returned, energy, own)
    arrived_moving = to_peers(leaving)
    face_terms = with_neighbours(term, 1)
    rows, sums = local_force(0, plan, own, first, second, term)
    sums, force_back = cross_force(
        send_fill, plan, own, first, rows, arrived, arrived_moving, sums, face_terms
    )
    returned_force = to_peers(force_back)
    sums = local_force(1, plan, own, first, second, term, faces, face_terms, rows, sums)
    forces = finish(pair, sums, returned_force, active, own)
    return (density, forces)


def solution(mesh):
    cells = P(("region", "dev"), None)
    vectors = P(None, ("region", "dev"), None)
    lists = P(("region", "dev"), None, None)
    in_specs = (
        vectors, vectors, cells, cells, cells, P(("region", "dev")), cells, lists, cells, lists,
    )
    return jax.shard_map(
        local, mesh=mesh, in_specs=in_specs, out_specs=(cells, vectors), check_vma=False
    )
```

```python
import functools
import math

import jax
import jax.numpy as jnp
from jax import lax
from jax.experimental import pallas as pl
from jax.experimental.pallas import tpu as pltpu
from jax.sharding import PartitionSpec as P

BF = jnp.bfloat16
F32 = jnp.float32
FACE = 4
CELLS = 64
WIDTH = 256
PEERS = 16
SLOTS = 16
LISTED = PEERS * SLOTS
GAMMA_LESS = 2.0 / 3.0
W_SCALE = 84.0 / math.pi
G_SCALE = 6720.0 / math.pi
TINY = 1e-14
EMPTY = 1e8
CHUNK = 32
CELL = 8
SUMS = 16
NN = (((1,), (0,)), ((), ()))
NT = (((1,), (1,)), ((), ()))
VM = pl.BlockSpec(memory_space=pltpu.VMEM)
SM = pl.BlockSpec(memory_space=pltpu.SMEM)
ROWS = 5
MOVING = 4
SPLIT = 40
SIZES = (160, 192, 224, 256)
STEP = 32
KINDS = len(SIZES)
UNIT = 4
LOCAL_AT = 3 * KINDS
LOCAL_LEAD = 2
LOCAL_LIST = CELLS + 8
CROSS_AT = LOCAL_AT + 2 * LOCAL_LIST
CROSS_LEAD = 4
CROSS_LIST = LISTED + 16
PLAN = CROSS_AT + CROSS_LIST
PACK = 128
ANYWHERE = pl.BlockSpec(memory_space=pl.ANY)
OWN_ROWS = jax.ShapeDtypeStruct((2, (CELLS + 1) * CELL, 128), F32)


def params(mib=32):
    return pltpu.CompilerParams(vmem_limit_bytes=int(mib * 2**20))


def split2(x):
    a = x.astype(BF)
    return a, (x - a.astype(F32)).astype(BF)


def split3(x):
    a = x.astype(BF).astype(F32)
    rest = x - a
    b = rest.astype(BF).astype(F32)
    return a, b, rest - b


def pair_terms(x, y, z, h, m):
    norm = 4.0 * (x * x + y * y + z * z)
    root = lax.rsqrt(jnp.where(m > 0.0, m, 1.0))
    mu = jnp.where(m > 0.0, root * lax.rsqrt(root), EMPTY)
    one = jnp.ones_like(x)
    first = [-8.0 * x, -8.0 * y, -8.0 * z, norm, one, h * h * mu, 2.0 * h * mu, mu]
    second = [x, y, z, one, norm, mu, h * mu, h * h * mu]
    return first, second


def both(read):
    return jnp.concatenate([read(0), read(1)], -1)


def half(value, h):
    return value[..., 128 * h : 128 * (h + 1)]


def put(ref, planes, start, count, stride):
    for k, plane in enumerate(planes):
        for h in range(2):
            ref[h, pl.ds(start + k, count, stride=stride), :] = half(plane, h)


def planes_of(ref, ids, start, count, stride):
    return [both(lambda h: ref[h, pl.ds(start + k, count, stride=stride), :]) for k in ids]


def rows_at(index, size):
    return pl.ds(pl.multiple_of(index * size, size), size)


def block(ref, index, size):
    return both(lambda h: ref[h, rows_at(index, size), :])


def set_block(ref, index, size, value):
    for h in range(2):
        ref[h, rows_at(index, size), :] = half(value, h)


def add_block(ref, index, size, value):
    for h in range(2):
        ref[h, rows_at(index, size), :] += half(value, h)


def line(ref, index, size, k):
    return both(lambda h: ref[h, pl.ds(index * size + k, 1), :])


def listed_planes(listed, e, part, ids, size):
    step = SLOTS * size
    start = 8 * part * size
    return [
        both(lambda h: listed[e, pl.ds(h * step + start + k, 8, stride=size), :]) for k in ids
    ]


def listed_support(listed, slot):
    at = (slot % SLOTS) * ROWS + 3
    return both(lambda h: listed[slot // SLOTS, pl.ds(h * SLOTS * ROWS + at, 1), :])


def first_operand(rows):
    a1, a2, a3 = split3(rows)
    return jnp.concatenate([a1, a1, a2, a2, a1, a3, jnp.zeros((80, WIDTH), F32)], 0).T.astype(BF)


def second_operands(rows, both):
    b1, b2, b3 = split3(rows)
    stacked = jnp.concatenate([b1, b2, b1, b2, b3, b1, jnp.zeros((80, WIDTH), F32)], 0)
    part = lax.broadcasted_iota(jnp.int32, stacked.shape, 0) % 8
    near = jnp.where(part < 5, stacked, 0.0).astype(BF)
    if not both:
        return near
    return near, jnp.where(part >= 5, stacked, 0.0).astype(BF)


def support_columns(row):
    return jnp.broadcast_to(row, (128, WIDTH)).T


def density_products(left, operands, s_ref, mix_ref):
    s_ref[...] = jnp.dot(left, operands[0], preferred_element_type=F32)
    mix_ref[...] = jnp.dot(left, operands[1], preferred_element_type=F32)


def weights_of(s, mix, columns, row):
    s = jnp.maximum(s, TINY)
    dist = s * lax.rsqrt(s)
    support = columns + row
    d = jnp.maximum(support - dist, 0.0)
    x = pl.reciprocal(mix, approx=True) * d
    x = x * x
    x = x * x
    return x * (support + 4.0 * dist)


def density_weights(count, s_ref, mix_ref, columns, row, one_sided):
    second = jnp.zeros((8, WIDTH), F32)
    firsts = []
    for start in range(0, count, CHUNK):
        part = slice(start, min(start + CHUNK, count))
        wide = columns[part]
        w = weights_of(s_ref[part], mix_ref[part], jnp.concatenate([wide, wide], 1), row)
        for k in range(w.shape[0] // 8):
            second = second + w[8 * k : 8 * k + 8]
        if not one_sided:
            firsts.append(w[:, :128] + w[:, 128:])
    if one_sided:
        return second
    if count < WIDTH:
        firsts.append(jnp.zeros((WIDTH - count, 128), F32))
    turned = jnp.concatenate(firsts, 0).T
    first = turned[:8]
    for k in range(1, 16):
        first = first + turned[8 * k : 8 * k + 8]
    return second, first


def inverse_mass(m):
    return jnp.where(m > 0.0, W_SCALE / jnp.where(m > 0.0, m, 1.0), 0.0)


def self_weights(count, s_ref, mix_ref, columns, row):
    sums = [jnp.zeros((8, 128), F32)] * 2
    crossing = []
    for start in range(0, count, CHUNK):
        part = slice(start, min(start + CHUNK, count))
        for h in range(0 if start < 128 else 1, 2):
            lanes = slice(128 * h, 128 * (h + 1))
            w = weights_of(s_ref[part, lanes], mix_ref[part, lanes], columns[part], half(row, h))
            for k in range(w.shape[0] // 8):
                sums[h] = sums[h] + w[8 * k : 8 * k + 8]
            if h and start < 128:
                crossing.append(w)
    turned = jnp.concatenate(crossing, 0).T
    for k in range(16):
        sums[0] = sums[0] + turned[8 * k : 8 * k + 8]
    return jnp.concatenate(sums, 1)


def fetch(pairs, sem):
    copies = [
        pltpu.make_async_copy(source, target, sem.at[k])
        for k, (source, target) in enumerate(pairs)
    ]
    for copy in copies:
        copy.start()
    return copies


def prepare_kernel(
    occ, pair, pos_in, vel_in, smooth_in, mass_in, own, out, pos, vel, smooth, mass, full, sem
):
    copies = fetch(
        [(pos_in, pos), (vel_in, vel), (smooth_in, smooth), (mass_in, mass)], sem
    )
    lane = lax.broadcasted_iota(jnp.int32, (1, WIDTH), 1)
    for c in range(CELLS):
        full[c : c + 1, :] = (lane < occ[c]).astype(F32)
    for copy in copies:
        copy.wait()
    place = [pos[k] - 0.5 for k in range(3)]
    m = jnp.where(full[...] > 0.0, mass[...], 0.0)
    put(own, place + [smooth[...], m] + [vel[k] for k in range(3)], 0, CELLS, CELL)
    blank = jnp.zeros((CELL, WIDTH), F32)
    wide = jnp.full((1, WIDTH), 0.5, F32)
    set_block(own, CELLS, CELL, jnp.concatenate([blank[:3], wide, blank[:4]], 0))

    def peer_step(e, _):
        for s in range(SLOTS):
            c = pair[e, s]
            for h in range(2):
                at = (h * SLOTS + s) * ROWS
                out[e, at : at + ROWS] = own[h, rows_at(c, CELL), :][:ROWS]
        return 0

    lax.fori_loop(0, PEERS, peer_step, 0)


def prepare(occ, pair, pos, vel, smooth, mass):
    plane = pltpu.VMEM((CELLS, WIDTH), F32)
    return pl.pallas_call(
        prepare_kernel,
        in_specs=[SM] * 2 + [ANYWHERE] * 4,
        out_specs=[VM] * 2,
        out_shape=[
            OWN_ROWS,
            jax.ShapeDtypeStruct((PEERS, 2 * SLOTS * ROWS, 128), F32),
        ],
        scratch_shapes=[
            pltpu.VMEM((3, CELLS, WIDTH), F32),
            pltpu.VMEM((3, CELLS, WIDTH), F32),
            plane,
            plane,
            plane,
            pltpu.SemaphoreType.DMA((4,)),
        ],
        compiler_params=params(60),
    )(occ, pair, pos, vel, smooth, mass)


def kind_of(size):
    return jnp.maximum(size - SIZES[0] + STEP - 1, 0) >> (STEP.bit_length() - 1)


def one_of(kind):
    return jnp.left_shift(jnp.int32(1), 8 * kind)


def make_plan(occ, fill, cells, plan):
    def over_local(visit, part, carry):
        low, high = (SPLIT, CELLS) if part else (0, SPLIT)
        step = lambda c, carry: visit(kind_of(occ[c]), c, carry)
        return lax.fori_loop(low, high, step, carry, unroll=8)

    def over_pairs(visit, carry):
        def peer_step(e, carry):
            def slot_step(s, carry):
                cell = cells[e, s]
                return visit(kind_of(occ[cell]), (e * SLOTS + s) * PACK + cell, carry)

            return lax.fori_loop(0, fill[0, e], slot_step, carry)

        return lax.fori_loop(0, PEERS, peer_step, carry)

    unused = jnp.int32(0)
    for e in range(PEERS):
        unused = jnp.where(fill[0, e] == 0, e * SLOTS, unused)

    for group, (walk, start, lead, unit, blank) in enumerate(
        [
            (lambda v, x: over_local(v, 0, x), LOCAL_AT, LOCAL_LEAD, 2, CELLS),
            (lambda v, x: over_local(v, 1, x), LOCAL_AT + LOCAL_LIST, LOCAL_LEAD, 2, CELLS),
            (over_pairs, CROSS_AT, CROSS_LEAD, UNIT, unused * PACK + CELLS),
        ]
    ):
        counts = walk(lambda kind, value, packed: packed + one_of(kind), jnp.int32(0))
        total = jnp.int32(0)
        done = jnp.int32(0)
        places = jnp.int32(0)
        for k in range(KINDS):
            places = places + jnp.left_shift(total, 8 * k)
            total = total + ((counts >> (8 * k)) & 255)
            upto = (total + (unit - 1 if k == KINDS - 1 else 0)) // unit
            plan[group * KINDS + k] = upto - done
            done = upto
        for k in range(lead):
            plan[start + k] = blank
        for k in range(unit + 1):
            plan[start + lead + total + k] = blank

        def place(kind, value, packed, start=start + lead):
            plan[start + ((packed >> (8 * kind)) & 255)] = value
            return packed + one_of(kind)

        walk(place, places)


def fold(total, own, out, carried):
    mine = sum(planes_of(total, range(CELL), 0, CELLS, CELL))
    mass = planes_of(own, [4], 0, CELLS, CELL)[0]
    mine = mine * inverse_mass(mass)
    out[...] = mine if carried is None else carried[...] + mine


def make_face_first(faces, face_first):
    planes = planes_of(faces, range(ROWS), 0, 2 * FACE, CELL)
    put(face_first, pair_terms(*planes)[0], 0, 2 * FACE, CELL)


def face_cell(n):
    return jnp.where(n < FACE, n, CELLS - 2 * FACE + n)


def in_turns(trips, sizes, item, last, products, weights, slot_a, slot_b):
    products(item(0), slot_a)
    base = 0
    for count, size in zip(trips, sizes):

        def step(i, _, size=size):
            products(item(2 * i + 1), slot_b)
            weights(size, item(2 * i), slot_a)
            after = 2 * i + 2
            products(item(after if last is None else jnp.minimum(after, last - 1)), slot_a)
            weights(size, item(2 * i + 1), slot_b)
            return 0

        lax.fori_loop(base, base + count, step, 0)
        base = base + count


def cell_list(plan, part):
    start = LOCAL_AT + part * LOCAL_LIST + LOCAL_LEAD
    return [plan[part * KINDS + k] for k in range(KINDS)], lambda n: plan[start + n]


def pair_list(plan):
    start = CROSS_AT + CROSS_LEAD

    def item(n):
        entries = [plan[start + 2 * n + k] for k in range(2)]
        return [(entry // PACK, entry % PACK) for entry in entries]

    return [plan[2 * KINDS + k] for k in range(KINDS)], item


def live_parts(fill, visit, other):
    def step(n, _):
        e, part = n // 2, n % 2
        live = fill[0, e] > 8 * part

        @pl.when(live)
        def _():
            visit(e, part)

        if other is not None:

            @pl.when(jnp.logical_not(live))
            def _():
                other(e, part)

        return 0

    lax.fori_loop(0, 2 * PEERS, step, 0)


def local_density_kernel(part, *refs):
    if part:
        plan, own, first, second, faces, carried, rho, total, face_first, *slots = refs
    else:
        carried = None
        occ, fill, cells, own, rho, first, second, plan, total, *slots = refs
        make_plan(occ, fill, cells, plan)
        planes = planes_of(own, range(ROWS), 0, CELLS, CELL)
        blank = [jnp.zeros((1, WIDTH), F32)] * 3 + [jnp.full((1, WIDTH), 0.5, F32)]
        for ref, some, none in zip(
            (first, second), pair_terms(*planes), pair_terms(*blank, blank[0])
        ):
            put(ref, some, 0, CELLS, CELL)
            set_block(ref, CELLS, CELL, jnp.concatenate(none, 0))
    slot_a, slot_b = slots[:6], slots[6:]
    total[...] = jnp.zeros_like(total)

    def products(c, held):
        left = first_operand(block(first, c, CELL))
        after = jnp.minimum(c + 1, CELLS)
        held[4][...] = support_columns(line(own, c, CELL, 3))
        density_products(left, second_operands(block(second, c, CELL), True), *held[0:2])
        density_products(left, second_operands(block(second, after, CELL), True), *held[2:4])

    def weights(count, c, held):
        after = jnp.minimum(c + 1, CELLS)
        row, other = line(own, c, CELL, 3), line(own, after, CELL, 3)
        own_sum = self_weights(count, *held[0:2], held[4], row)
        there, here = density_weights(count, *held[2:4], held[4], other, False)
        add_block(total, c, CELL, own_sum + here)
        add_block(total, after, CELL, there)

    trips, item = cell_list(plan, part)
    in_turns(trips, SIZES, item, None, products, weights, slot_a, slot_b)

    if part:
        make_face_first(faces, face_first)

        def face_products(i, held):
            for k in range(2):
                n = 2 * i + k
                left = first_operand(block(face_first, n, CELL))
                operands = second_operands(block(second, face_cell(n), CELL), True)
                held[4 + k][...] = support_columns(line(faces, n, CELL, 3))
                density_products(left, operands, *held[2 * k : 2 * k + 2])

        def face_weights(size, i, held):
            for k in range(2):
                c = face_cell(2 * i + k)
                added = density_weights(
                    size, *held[2 * k : 2 * k + 2], held[4 + k], line(own, c, CELL, 3), True
                )
                add_block(total, c, CELL, added)

        in_turns(
            [FACE // 2], [WIDTH], lambda i: i, FACE, face_products, face_weights, slot_a, slot_b
        )

    fold(total, own, rho, carried)


DENSITY_SLOT = [pltpu.VMEM((WIDTH, WIDTH), F32)] * 4 + [pltpu.VMEM((WIDTH, 128), F32)] * 2


def local_density(part, *operands):
    plane = jax.ShapeDtypeStruct((CELLS, WIDTH), F32)
    if part:
        in_specs, out_specs, out_shape = [SM] + [VM] * 5, VM, plane
    else:
        in_specs, out_specs = [SM] * 3 + [VM], [VM] * 3 + [SM]
        out_shape = [plane, OWN_ROWS, OWN_ROWS, jax.ShapeDtypeStruct((PLAN,), jnp.int32)]
    return pl.pallas_call(
        functools.partial(local_density_kernel, part),
        in_specs=in_specs,
        out_specs=out_specs,
        out_shape=out_shape,
        scratch_shapes=[pltpu.VMEM((2, (CELLS + 1) * CELL, 128), F32)]
        + [pltpu.VMEM((2, 2 * FACE * CELL, 128), F32)] * part
        + DENSITY_SLOT * 2,
        cost_estimate=pl.CostEstimate(
            flops=64 * 65536 * 60, bytes_accessed=2 * 2**20, transcendentals=0
        ),
        compiler_params=params(),
    )(*operands)


def live_rows(fill, e, part):
    row = lax.broadcasted_iota(jnp.int32, (8, WIDTH), 0)
    return row < fill[0, e] - 8 * part


def cross_density_kernel(
    fill, plan, own, first, listed, carried, rho, back, total, theirs, there_of, *slots
):
    slot_a, slot_b = slots[:6], slots[6:]
    total[...] = jnp.zeros_like(total)

    def make(e, part):
        after = pair_terms(*listed_planes(listed, e, part, range(ROWS), ROWS))[1]
        put(theirs, after, (e * SLOTS + 8 * part) * CELL, 8, CELL)

    live_parts(fill, make, None)

    def products(pairs, held):
        for k, (slot, c) in enumerate(pairs):
            left = first_operand(block(first, c, CELL))
            held[4 + k][...] = support_columns(line(own, c, CELL, 3))
            operands = second_operands(block(theirs, slot, CELL), True)
            density_products(left, operands, *held[2 * k : 2 * k + 2])

    def weights(count, pairs, held):
        for k, (slot, c) in enumerate(pairs):
            support = listed_support(listed, slot)
            there, here = density_weights(
                count, *held[2 * k : 2 * k + 2], held[4 + k], support, False
            )
            add_block(total, c, CELL, here)
            set_block(there_of, slot, CELL, there)

    trips, item = pair_list(plan)
    in_turns(trips, SIZES, item, None, products, weights, slot_a, slot_b)

    def send(e, part):
        start = (e * SLOTS + 8 * part) * CELL
        summed = sum(planes_of(there_of, range(CELL), start, 8, CELL))
        mass = listed_planes(listed, e, part, [4], ROWS)[0]
        value = jnp.where(live_rows(fill, e, part), summed * inverse_mass(mass), 0.0)
        back[e, rows_at(part, 8), :] = value

    def send_none(e, part):
        back[e, rows_at(part, 8), :] = jnp.zeros((8, WIDTH), F32)

    live_parts(fill, send, send_none)
    fold(total, own, rho, carried)


def cross_density(fill, plan, own, first, listed, carried):
    return pl.pallas_call(
        cross_density_kernel,
        in_specs=[SM, SM] + [VM] * 4,
        out_specs=[VM, VM],
        out_shape=[
            jax.ShapeDtypeStruct((CELLS, WIDTH), F32),
            jax.ShapeDtypeStruct((PEERS, SLOTS, WIDTH), F32),
        ],
        scratch_shapes=[
            pltpu.VMEM((2, (CELLS + 1) * CELL, 128), F32),
            pltpu.VMEM((2, LISTED * CELL, 128), F32),
            pltpu.VMEM((2, LISTED * CELL, 128), F32),
        ]
        + DENSITY_SLOT * 2,
        cost_estimate=pl.CostEstimate(
            flops=80 * 65536 * 60, bytes_accessed=2 * 2**20, transcendentals=0
        ),
        compiler_params=params(),
    )(fill, plan, own, first, listed, carried)


def pressure_kernel(
    pair, near, returned, energy_in, own, density, term, out, energy, sum_of, moving, sem
):
    copies = fetch([(energy_in, energy)], sem)
    sum_of[...] = near[...]

    def peer_step(e, _):
        for s in range(SLOTS):
            sum_of[pl.ds(pair[e, s], 1), :] += returned[e, s : s + 1]
        return 0

    lax.fori_loop(0, PEERS, peer_step, 0)
    copies[0].wait()
    full = planes_of(own, [4], 0, CELLS, CELL)[0] > 0.0
    rho = jnp.where(full, sum_of[...], 0.0)
    density[...] = rho
    term[...] = jnp.where(full, GAMMA_LESS * energy[...] / jnp.where(full, rho, 1.0), 0.0)

    def cell_step(c, _):
        moving[c] = jnp.concatenate(
            [line(own, c, CELL, k) for k in (5, 6, 7)] + [term[pl.ds(c, 1), :]], 0
        )
        return 0

    lax.fori_loop(0, CELLS, cell_step, 0, unroll=8)

    def send_step(e, _):
        for s in range(SLOTS):
            cell = moving[pair[e, s]]
            for h in range(2):
                at = (h * SLOTS + s) * MOVING
                out[e, at : at + MOVING] = half(cell, h)
        return 0

    lax.fori_loop(0, PEERS, send_step, 0)


def pressure(pair, near, returned, energy, own):
    plane = jax.ShapeDtypeStruct((CELLS, WIDTH), F32)
    return pl.pallas_call(
        pressure_kernel,
        in_specs=[SM, VM, VM, ANYWHERE, VM],
        out_specs=[VM, VM, VM],
        out_shape=[
            plane,
            plane,
            jax.ShapeDtypeStruct((PEERS, 2 * SLOTS * MOVING, 128), F32),
        ],
        scratch_shapes=[
            pltpu.VMEM((CELLS, WIDTH), F32),
            pltpu.VMEM((CELLS, WIDTH), F32),
            pltpu.VMEM((CELLS, MOVING, WIDTH), F32),
            pltpu.SemaphoreType.DMA((1,)),
        ],
        compiler_params=params(),
    )(pair, near, returned, energy, own)


def force_terms(place, m, speed, term):
    mp = m * term
    turned = sum(a * b for a, b in zip(place, speed))
    return (
        [m] + [m * a for a in place] + [mp] + [mp * a for a in place]
        + [m * a for a in speed] + [m * turned]
    )


def forces_of(sums, place, speed, term):
    lean = [a * sums[0] - b for a, b in zip(place, sums[1:4])]
    acc = [term * a + (b * sums[4] - c) for a, b, c in zip(lean, place, sums[5:8])]
    mixed = sum(a * b - c * d for a, b, c, d in zip(speed, lean, place, sums[8:11]))
    return [G_SCALE * a for a in acc] + [-G_SCALE * term * (mixed + sums[11])]


def force_operand(ref, index):
    high, low = split2(block(ref, index, SUMS))
    return jnp.concatenate([high, low], 0)


def own_terms(own, term, rows):
    planes = planes_of(own, range(CELL), 0, CELLS, CELL)
    terms = force_terms(planes[0:3], planes[4], planes[5:8], term[...])
    put(rows, terms, 0, CELLS, SUMS)
    put(rows, [jnp.zeros((CELLS, WIDTH), F32)] * 4, 12, CELLS, SUMS)
    set_block(rows, CELLS, SUMS, jnp.zeros((SUMS, WIDTH), F32))


def slopes(s_ref, high, low, columns, row, count):
    for start in range(0, count, CHUNK):
        part = slice(start, min(start + CHUNK, count))
        s = jnp.maximum(s_ref[part], TINY)
        dist = s * lax.rsqrt(s)
        wide = columns[part]
        support = jnp.concatenate([wide, wide], 1) + row
        d = jnp.maximum(support - dist, 0.0)
        e = pl.reciprocal(support * support, approx=True)
        x = e * d
        g = (x * x) * (x * e)
        top = g.astype(BF)
        high[part] = top
        low[part] = (g - top.astype(F32)).astype(BF)


def distances(left, rows, s_ref):
    s_ref[...] = jnp.dot(left, second_operands(rows, False), preferred_element_type=F32)


def to_seconds(rows, count, high, low):
    part = rows[:, :count]
    top = lax.dot_general(part, high[0:count], NN, preferred_element_type=F32)
    both = top + lax.dot_general(part, low[0:count], NN, preferred_element_type=F32)
    return both[:SUMS] + both[SUMS:]


def to_firsts(rows, count, high, low):
    top = lax.dot_general(rows, high[0:count], NT, preferred_element_type=F32)
    both = top + lax.dot_general(rows, low[0:count], NT, preferred_element_type=F32)
    return both[:SUMS] + both[SUMS:]


def in_three_turns(trips, sizes, item, last, products, tiles, sums, slot_a, slot_b):
    products(item(0), slot_a)
    base = 0
    for count, size in zip(trips, sizes):

        def step(i, _, size=size):
            products(item(2 * i + 1), slot_b)
            sums(size, item(2 * i - 2), slot_a)
            tiles(size, item(2 * i), slot_a)
            after = 2 * i + 2
            products(item(after if last is None else jnp.minimum(after, last - 1)), slot_a)
            sums(size, item(2 * i - 1), slot_b)
            tiles(size, item(2 * i + 1), slot_b)
            return 0

        lax.fori_loop(base, base + count, step, 0)
        base = base + count
    sums(sizes[-1], item(2 * base - 2), slot_a)
    sums(sizes[-1], item(2 * base - 1), slot_b)


def clear(slots):
    for held in slots:
        held[SIZES[0] :, :] = jnp.zeros((WIDTH - SIZES[0], WIDTH), BF)


def add_forces(total, own, term, out):
    planes = planes_of(own, range(CELL), 0, CELLS, CELL)
    sums = planes_of(total, range(12), 0, CELLS, SUMS)
    for k, force in enumerate(forces_of(sums, planes[0:3], planes[5:8], term[...])):
        out[k] = force


def local_force_kernel(part, plan, own, first, second, term, *rest):
    if part:
        faces, face_terms, rows, carried, out, total, face_rows, face_first, *slots = rest
        total[...] = carried[...]
    else:
        rows, total, *slots = rest
        own_terms(own, term, rows)
        total[...] = jnp.zeros_like(total)
    slot_a, slot_b = slots[:7], slots[7:]
    clear([held[k] for held in (slot_a, slot_b) for k in (2, 3, 5, 6)])

    def products(c, held):
        left = first_operand(block(first, c, CELL))
        held[0][...] = support_columns(line(own, c, CELL, 3))
        distances(left, block(second, c, CELL), held[1])
        distances(left, block(second, jnp.minimum(c + 1, CELLS), CELL), held[4])

    def tiles(count, c, held):
        other = line(own, jnp.minimum(c + 1, CELLS), CELL, 3)
        slopes(*held[1:4], held[0], line(own, c, CELL, 3), count)
        slopes(*held[4:7], held[0], other, count)

    def sums(count, c, held):
        after = jnp.minimum(c + 1, CELLS)
        mine, other = force_operand(rows, c), force_operand(rows, after)
        added = to_firsts(other, count, *held[5:7])
        if count < WIDTH:
            added = jnp.concatenate([added, jnp.zeros((SUMS, WIDTH - count), F32)], 1)
        add_block(total, c, SUMS, to_seconds(mine, count, *held[2:4]) + added)
        add_block(total, after, SUMS, to_seconds(mine, count, *held[5:7]))

    trips, item = cell_list(plan, part)
    in_three_turns(trips, SIZES, item, None, products, tiles, sums, slot_a, slot_b)

    if part:
        make_face_first(faces, face_first)
        planes = planes_of(faces, range(CELL), 0, 2 * FACE, CELL)
        terms = force_terms(planes[0:3], planes[4], planes[5:8], face_terms[...])
        blank = jnp.zeros((2 * FACE, WIDTH), F32)
        put(face_rows, terms + [blank] * 4, 0, 2 * FACE, SUMS)

        def face_products(i, held):
            for k in range(2):
                n = 2 * i + k
                left = first_operand(block(face_first, n, CELL))
                distances(left, block(second, face_cell(n), CELL), held[1 + 3 * k])

        def face_tiles(size, i, held):
            for k in range(2):
                n = 2 * i + k
                columns = support_columns(line(faces, n, CELL, 3))
                slopes(
                    *held[1 + 3 * k : 4 + 3 * k], columns, line(own, face_cell(n), CELL, 3), size
                )

        def face_sums(size, i, held):
            for k in range(2):
                n = jnp.maximum(2 * i, 0) + k
                c = jnp.where(i < 0, CELLS, face_cell(n))
                theirs = force_operand(face_rows, n)
                add_block(
                    total, c, SUMS, to_seconds(theirs, size, *held[2 + 3 * k : 4 + 3 * k])
                )

        in_three_turns(
            [FACE // 2], [WIDTH], lambda i: i, FACE, face_products, face_tiles, face_sums,
            slot_a, slot_b,
        )

        add_forces(total, own, term, out)


FORCE_PAIR = [
    pltpu.VMEM((WIDTH, WIDTH), F32),
    pltpu.VMEM((WIDTH, WIDTH), BF),
    pltpu.VMEM((WIDTH, WIDTH), BF),
]
FORCE_SLOT = [pltpu.VMEM((WIDTH, 128), F32)] + FORCE_PAIR * 2


SUM_ROWS = jax.ShapeDtypeStruct((2, (CELLS + 1) * SUMS, 128), F32)


def local_force(part, plan, own, first, second, term, *rest):
    if part:
        out_shape = jax.ShapeDtypeStruct((4, CELLS, WIDTH), F32)
        scratch = [
            pltpu.VMEM(SUM_ROWS.shape, F32),
            pltpu.VMEM((2, 2 * FACE * SUMS, 128), F32),
            pltpu.VMEM((2, 2 * FACE * CELL, 128), F32),
        ]
    else:
        out_shape = [SUM_ROWS] * 2
        scratch = []
    return pl.pallas_call(
        functools.partial(local_force_kernel, part),
        in_specs=[SM] + [VM] * (4 + len(rest)),
        out_specs=VM if part else [VM, VM],
        out_shape=out_shape,
        scratch_shapes=scratch + FORCE_SLOT * 2,
        cost_estimate=pl.CostEstimate(
            flops=64 * 65536 * 80, bytes_accessed=2 * 2**20, transcendentals=0
        ),
        compiler_params=params(),
    )(plan, own, first, second, term, *rest)


def cross_force_kernel(
    fill, plan, own, first, rows, listed, arrived, carried, _, total, back,
    theirs, their_rows, sums_of, *slots
):
    slot_a, slot_b = slots[:8], slots[8:]
    total[...] = carried[...]
    clear([held[k] for held in (slot_a, slot_b) for k in (3, 4, 6, 7)])

    def make(e, part):
        planes = listed_planes(listed, e, part, range(ROWS), ROWS)
        at = e * SLOTS + 8 * part
        put(theirs, pair_terms(*planes)[1], at * CELL, 8, CELL)
        *speed, pressed = listed_planes(arrived, e, part, range(MOVING), MOVING)
        terms = force_terms(planes[0:3], planes[4], speed, pressed)
        blank = jnp.zeros((8, WIDTH), F32)
        put(their_rows, terms + [blank] * 4, at * SUMS, 8, SUMS)

    live_parts(fill, make, None)

    def products(pairs, held):
        for k, (slot, c) in enumerate(pairs):
            held[k][...] = support_columns(line(own, c, CELL, 3))
            left = first_operand(block(first, c, CELL))
            distances(left, block(theirs, slot, CELL), held[2 + 3 * k])

    def tiles(count, pairs, held):
        for k, (slot, c) in enumerate(pairs):
            support = listed_support(listed, slot)
            slopes(*held[2 + 3 * k : 5 + 3 * k], held[k], support, count)

    def sums(count, pairs, held):
        for k, (slot, c) in enumerate(pairs):
            tile = held[3 + 3 * k : 5 + 3 * k]
            set_block(sums_of, slot, SUMS, to_seconds(force_operand(rows, c), count, *tile))
            added = to_firsts(force_operand(their_rows, slot), count, *tile)
            if count < WIDTH:
                added = jnp.concatenate([added, jnp.zeros((SUMS, WIDTH - count), F32)], 1)
            add_block(total, c, SUMS, added)

    trips, item = pair_list(plan)
    in_three_turns(trips, SIZES, item, None, products, tiles, sums, slot_a, slot_b)

    def send(e, part):
        planes = listed_planes(listed, e, part, range(3), ROWS)
        *speed, pressed = listed_planes(arrived, e, part, range(MOVING), MOVING)
        summed = planes_of(sums_of, range(12), (e * SLOTS + 8 * part) * SUMS, 8, SUMS)
        live = live_rows(fill, e, part)
        send_rows(e, part, [jnp.where(live, f, 0.0) for f in forces_of(summed, planes, speed, pressed)])

    def send_none(e, part):
        send_rows(e, part, [jnp.zeros((8, WIDTH), F32)] * MOVING)

    def send_rows(e, part, forces):
        for k, force in enumerate(forces):
            for h in range(2):
                start = (h * SLOTS + 8 * part) * MOVING + k
                back[e, pl.ds(start, 8, stride=MOVING), :] = half(force, h)

    live_parts(fill, send, send_none)


def cross_force(fill, plan, own, first, rows, listed, arrived, carried, after):
    return pl.pallas_call(
        cross_force_kernel,
        in_specs=[SM, SM] + [VM] * 6 + [ANYWHERE],
        out_specs=[VM, VM],
        out_shape=[
            SUM_ROWS,
            jax.ShapeDtypeStruct((PEERS, 2 * SLOTS * MOVING, 128), F32),
        ],
        scratch_shapes=[
            pltpu.VMEM((2, LISTED * CELL, 128), F32),
            pltpu.VMEM((2, LISTED * SUMS, 128), F32),
            pltpu.VMEM((2, LISTED * SUMS, 128), F32),
        ]
        + (FORCE_SLOT[:1] * 2 + FORCE_PAIR * 2) * 2,
        cost_estimate=pl.CostEstimate(
            flops=80 * 65536 * 80, bytes_accessed=2 * 2**20, transcendentals=0
        ),
        compiler_params=params(),
    )(fill, plan, own, first, rows, listed, arrived, carried, after)


def finish_kernel(pair, near, returned, active_in, own, out, total, active, gate, sem):
    copies = fetch([(active_in, active)], sem)
    total[...] = jnp.zeros_like(total)

    def peer_step(e, _):
        for s in range(SLOTS):
            at = s * MOVING
            total[pair[e, s]] += both(
                lambda h: returned[
                    e, h * SLOTS * MOVING + at : h * SLOTS * MOVING + at + MOVING
                ]
            )
        return 0

    lax.fori_loop(0, PEERS, peer_step, 0)
    copies[0].wait()
    full = planes_of(own, [4], 0, CELLS, CELL)[0] > 0.0
    gate[...] = jnp.where(full, active[...].astype(F32), 0.0)

    def cell_step(c, _):
        one = pl.ds(c, 1)
        open_to = gate[one, :]
        for k in range(4):
            out[k, one, :] = (near[k, one, :] + total[c, k : k + 1]) * open_to
        return 0

    lax.fori_loop(0, CELLS, cell_step, 0, unroll=8)


def finish(pair, near, returned, active, own):
    return pl.pallas_call(
        finish_kernel,
        in_specs=[SM, VM, VM, ANYWHERE, VM],
        out_specs=VM,
        out_shape=jax.ShapeDtypeStruct((4, CELLS, WIDTH), F32),
        scratch_shapes=[
            pltpu.VMEM((CELLS, 4, WIDTH), F32),
            pltpu.VMEM((CELLS, WIDTH), jnp.int32),
            pltpu.VMEM((CELLS, WIDTH), F32),
            pltpu.SemaphoreType.DMA((1,)),
        ],
        compiler_params=params(),
    )(pair, near, returned, active, own)


def to_peers(block):
    return lax.all_to_all(block, "dev", split_axis=0, concat_axis=0, tiled=True)


def with_neighbours(rows, size):
    count = lax.axis_size("region")
    up = [(i, (i + 1) % count) for i in range(count)]
    down = [(i, (i - 1) % count) for i in range(count)]
    return jnp.concatenate(
        [
            lax.ppermute(rows[..., (CELLS - FACE) * size : CELLS * size, :], "region", up),
            lax.ppermute(rows[..., : FACE * size, :], "region", down),
        ],
        -2,
    )


def local(
    positions, velocity, smoothing, masses, energy, occupancy, active, send_cells, send_fill,
    pair_cell,
):
    pair = pair_cell[0]
    own, listed = prepare(occupancy, pair, positions, velocity, smoothing, masses)
    arrived = to_peers(listed)
    faces = with_neighbours(own, CELL)
    rho, first, second, plan = local_density(0, occupancy, send_fill, send_cells[0], own)
    rho, back = cross_density(send_fill, plan, own, first, arrived, rho)
    returned = to_peers(back)
    rho = local_density(1, plan, own, first, second, faces, rho)
    density, term, leaving = pressure(pair, rho, returned, energy, own)
    arrived_moving = to_peers(leaving)
    face_terms = with_neighbours(term, 1)
    rows, sums = local_force(0, plan, own, first, second, term)
    sums, force_back = cross_force(
        send_fill, plan, own, first, rows, arrived, arrived_moving, sums, face_terms
    )
    returned_force = to_peers(force_back)
    sums = local_force(1, plan, own, first, second, term, faces, face_terms, rows, sums)
    forces = finish(pair, sums, returned_force, active, own)
    return (density, forces)


def solution(mesh):
    cells = P(("region", "dev"), None)
    vectors = P(None, ("region", "dev"), None)
    lists = P(("region", "dev"), None, None)
    in_specs = (
        vectors, vectors, cells, cells, cells, P(("region", "dev")), cells, lists, cells, lists,
    )
    return jax.shard_map(
        local, mesh=mesh, in_specs=in_specs, out_specs=(cells, vectors), check_vma=False
    )
```

```python
import functools
import math

import jax
import jax.numpy as jnp
from jax import lax
from jax.experimental import pallas as pl
from jax.experimental.pallas import tpu as pltpu
from jax.sharding import PartitionSpec as P

BF = jnp.bfloat16
F32 = jnp.float32
FACE = 4
CELLS = 64
WIDTH = 256
PEERS = 16
SLOTS = 16
LISTED = PEERS * SLOTS
GAMMA_LESS = 2.0 / 3.0
W_SCALE = 84.0 / math.pi
G_SCALE = 6720.0 / math.pi
TINY = 1e-14
EMPTY = 1e8
CHUNK = 32
CELL = 8
SUMS = 16
NN = (((1,), (0,)), ((), ()))
NT = (((1,), (1,)), ((), ()))
VM = pl.BlockSpec(memory_space=pltpu.VMEM)
SM = pl.BlockSpec(memory_space=pltpu.SMEM)
ROWS = 5
MOVING = 4
SPLIT = 40
SIZES = (160, 192, 224, 256)
KINDS = len(SIZES)
UNIT = 4
LOCAL_AT = 16
LOCAL_LEAD = 2
LOCAL_LIST = CELLS + 8
CROSS_AT = LOCAL_AT + 2 * LOCAL_LIST
CROSS_LEAD = 4
CROSS_LIST = LISTED + 16
PLAN = CROSS_AT + CROSS_LIST
PACK = 128
ANYWHERE = pl.BlockSpec(memory_space=pl.ANY)
OWN_ROWS = jax.ShapeDtypeStruct((2, (CELLS + 1) * CELL, 128), F32)


def params(mib=50):
    return pltpu.CompilerParams(vmem_limit_bytes=int(mib * 2**20))


def split2(x):
    a = x.astype(BF)
    return a, (x - a.astype(F32)).astype(BF)


def split3(x):
    a = x.astype(BF).astype(F32)
    rest = x - a
    b = rest.astype(BF).astype(F32)
    return a, b, rest - b


def pair_terms(x, y, z, h, m):
    norm = 4.0 * (x * x + y * y + z * z)
    root = lax.rsqrt(jnp.where(m > 0.0, m, 1.0))
    mu = jnp.where(m > 0.0, root * lax.rsqrt(root), EMPTY)
    one = jnp.ones_like(x)
    first = [-8.0 * x, -8.0 * y, -8.0 * z, norm, one, h * h * mu, 2.0 * h * mu, mu]
    second = [x, y, z, one, norm, mu, h * mu, h * h * mu]
    return first, second


def both(read):
    return jnp.concatenate([read(0), read(1)], -1)


def half(value, h):
    return value[..., 128 * h : 128 * (h + 1)]


def put(ref, planes, start, count, stride):
    for k, plane in enumerate(planes):
        for h in range(2):
            ref[h, pl.ds(start + k, count, stride=stride), :] = half(plane, h)


def planes_of(ref, ids, start, count, stride):
    return [both(lambda h: ref[h, pl.ds(start + k, count, stride=stride), :]) for k in ids]


def rows_at(index, size):
    return pl.ds(pl.multiple_of(index * size, size), size)


def block(ref, index, size):
    return both(lambda h: ref[h, rows_at(index, size), :])


def set_block(ref, index, size, value):
    for h in range(2):
        ref[h, rows_at(index, size), :] = half(value, h)


def add_block(ref, index, size, value):
    for h in range(2):
        ref[h, rows_at(index, size), :] += half(value, h)


def line(ref, index, size, k):
    return both(lambda h: ref[h, pl.ds(index * size + k, 1), :])


def listed_planes(listed, e, part, ids, size):
    step = SLOTS * size
    start = 8 * part * size
    return [
        both(lambda h: listed[e, pl.ds(h * step + start + k, 8, stride=size), :]) for k in ids
    ]


def listed_support(listed, slot):
    at = (slot & (SLOTS - 1)) * ROWS + 3
    return both(lambda h: listed[slot >> 4, pl.ds(h * SLOTS * ROWS + at, 1), :])


def first_operand(rows):
    a1, a2, a3 = split3(rows)
    return jnp.concatenate([a1, a1, a2, a2, a1, a3, jnp.zeros((80, WIDTH), F32)], 0).T.astype(BF)


def second_operands(rows, both):
    b1, b2, b3 = split3(rows)
    stacked = jnp.concatenate([b1, b2, b1, b2, b3, b1, jnp.zeros((80, WIDTH), F32)], 0)
    part = lax.broadcasted_iota(jnp.int32, stacked.shape, 0) % 8
    near = jnp.where(part < 5, stacked, 0.0).astype(BF)
    if not both:
        return near
    return near, jnp.where(part >= 5, stacked, 0.0).astype(BF)


def support_columns(row):
    return jnp.broadcast_to(row, (128, WIDTH)).T


def density_products(left, operands, s_ref, mix_ref):
    s_ref[...] = jnp.dot(left, operands[0], preferred_element_type=F32)
    mix_ref[...] = jnp.dot(left, operands[1], preferred_element_type=F32)


def weights_of(s, mix, columns, row):
    s = jnp.maximum(s, TINY)
    dist = s * lax.rsqrt(s)
    support = columns + row
    d = jnp.maximum(support - dist, 0.0)
    x = pl.reciprocal(mix, approx=True) * d
    x = x * x
    x = x * x
    return x * (support + 4.0 * dist)


def density_weights(count, s_ref, mix_ref, columns, row, one_sided):
    second = jnp.zeros((8, WIDTH), F32)
    firsts = []
    for start in range(0, count, CHUNK):
        part = slice(start, start + CHUNK)
        wide = columns[part]
        w = weights_of(s_ref[part], mix_ref[part], jnp.concatenate([wide, wide], 1), row)
        for k in range(CHUNK // 8):
            second = second + w[8 * k : 8 * k + 8]
        if not one_sided:
            firsts.append(w[:, :128] + w[:, 128:])
    if one_sided:
        return second
    if count < WIDTH:
        firsts.append(jnp.zeros((WIDTH - count, 128), F32))
    turned = jnp.concatenate(firsts, 0).T
    first = turned[:8]
    for k in range(1, 16):
        first = first + turned[8 * k : 8 * k + 8]
    return second, first


def inverse_mass(m):
    return jnp.where(m > 0.0, W_SCALE / jnp.where(m > 0.0, m, 1.0), 0.0)


def self_weights(count, s_ref, mix_ref, columns, row):
    sums = [jnp.zeros((8, 128), F32)] * 2
    crossing = []
    for start in range(0, count, CHUNK):
        part = slice(start, start + CHUNK)
        for h in range(0 if start < 128 else 1, 2):
            lanes = slice(128 * h, 128 * (h + 1))
            w = weights_of(s_ref[part, lanes], mix_ref[part, lanes], columns[part], half(row, h))
            for k in range(CHUNK // 8):
                sums[h] = sums[h] + w[8 * k : 8 * k + 8]
            if h and start < 128:
                crossing.append(w)
    turned = jnp.concatenate(crossing, 0).T
    for k in range(16):
        sums[0] = sums[0] + turned[8 * k : 8 * k + 8]
    return jnp.concatenate(sums, 1)


def fetch(pairs, sem):
    copies = [
        pltpu.make_async_copy(source, target, sem.at[k])
        for k, (source, target) in enumerate(pairs)
    ]
    for copy in copies:
        copy.start()
    return copies


def prepare_kernel(
    occ, pair, pos_in, vel_in, smooth_in, mass_in, own, out, pos, vel, smooth, mass, full, sem
):
    copies = fetch(
        [(pos_in, pos), (vel_in, vel), (smooth_in, smooth), (mass_in, mass)], sem
    )
    lane = lax.broadcasted_iota(jnp.int32, (1, WIDTH), 1)
    for c in range(CELLS):
        full[c : c + 1, :] = (lane < occ[c]).astype(F32)
    for copy in copies:
        copy.wait()
    place = [pos[k] - 0.5 for k in range(3)]
    m = jnp.where(full[...] > 0.0, mass[...], 0.0)
    put(own, place + [smooth[...], m] + [vel[k] for k in range(3)], 0, CELLS, CELL)
    blank = jnp.zeros((CELL, WIDTH), F32)
    wide = jnp.full((1, WIDTH), 0.5, F32)
    set_block(own, CELLS, CELL, jnp.concatenate([blank[:3], wide, blank[:4]], 0))

    def peer_step(e, _):
        for s in range(SLOTS):
            c = pair[e, s]
            for h in range(2):
                at = (h * SLOTS + s) * ROWS
                out[e, at : at + ROWS] = own[h, rows_at(c, CELL), :][:ROWS]
        return 0

    lax.fori_loop(0, PEERS, peer_step, 0)


def prepare(occ, pair, pos, vel, smooth, mass):
    plane = pltpu.VMEM((CELLS, WIDTH), F32)
    return pl.pallas_call(
        prepare_kernel,
        in_specs=[SM] * 2 + [ANYWHERE] * 4,
        out_specs=[VM] * 2,
        out_shape=[
            OWN_ROWS,
            jax.ShapeDtypeStruct((PEERS, 2 * SLOTS * ROWS, 128), F32),
        ],
        scratch_shapes=[
            pltpu.VMEM((3, CELLS, WIDTH), F32),
            pltpu.VMEM((3, CELLS, WIDTH), F32),
            plane,
            plane,
            plane,
            pltpu.SemaphoreType.DMA((4,)),
        ],
        compiler_params=params(60),
    )(occ, pair, pos, vel, smooth, mass)


def kind_of(size):
    return jnp.maximum(size - SIZES[0] + 31, 0) >> 5


def make_plan(occ, fill, cells, plan):
    def over_local(visit, part, carry):
        low, high = (SPLIT, CELLS) if part else (0, SPLIT)
        step = lambda c, carry: visit(kind_of(occ[c]), c, carry)
        return lax.fori_loop(low, high, step, carry, unroll=8)

    def over_pairs(visit, carry):
        def peer_step(e, carry):
            def slot_step(s, carry):
                cell = cells[e, s]
                return visit(kind_of(occ[cell]), (e * SLOTS + s) * PACK + cell, carry)

            return lax.fori_loop(0, fill[0, e], slot_step, carry)

        return lax.fori_loop(0, PEERS, peer_step, carry)

    unused = jnp.int32(0)
    for e in range(PEERS):
        unused = jnp.where(fill[0, e] == 0, e * SLOTS, unused)

    def one_of(kind):
        return jnp.left_shift(jnp.int32(1), 8 * kind)

    for group, (walk, start, lead, unit, blank) in enumerate(
        [
            (lambda v, x: over_local(v, 0, x), LOCAL_AT, LOCAL_LEAD, 2, CELLS),
            (lambda v, x: over_local(v, 1, x), LOCAL_AT + LOCAL_LIST, LOCAL_LEAD, 2, CELLS),
            (over_pairs, CROSS_AT, CROSS_LEAD, UNIT, unused * PACK + CELLS),
        ]
    ):
        counts = walk(lambda kind, value, packed: packed + one_of(kind), jnp.int32(0))
        total = jnp.int32(0)
        done = jnp.int32(0)
        places = jnp.int32(0)
        for k in range(KINDS):
            places = places + jnp.left_shift(total, 8 * k)
            total = total + ((counts >> (8 * k)) & 255)
            upto = (total + (unit - 1 if k == KINDS - 1 else 0)) >> (unit.bit_length() - 1)
            plan[group * KINDS + k] = upto - done
            done = upto
        for k in range(lead):
            plan[start + k] = blank
        for k in range(unit + 1):
            plan[start + lead + total + k] = blank

        def place(kind, value, packed, start=start + lead):
            plan[start + ((packed >> (8 * kind)) & 255)] = value
            return packed + one_of(kind)

        walk(place, places)


def fold(total, own, out, carried):
    mine = sum(planes_of(total, range(CELL), 0, CELLS, CELL))
    mass = planes_of(own, [4], 0, CELLS, CELL)[0]
    mine = mine * inverse_mass(mass)
    out[...] = mine if carried is None else carried[...] + mine


def make_face_first(faces, face_first):
    planes = planes_of(faces, range(ROWS), 0, 2 * FACE, CELL)
    put(face_first, pair_terms(*planes)[0], 0, 2 * FACE, CELL)


def face_cell(n):
    return jnp.where(n < FACE, n, CELLS - 2 * FACE + n)


def in_turns(trips, sizes, item, last, products, weights, slot_a, slot_b):
    products(item(0), slot_a)
    base = 0
    for count, size in zip(trips, sizes):

        def step(i, _, size=size):
            products(item(2 * i + 1), slot_b)
            weights(size, item(2 * i), slot_a)
            after = 2 * i + 2
            products(item(after if last is None else jnp.minimum(after, last - 1)), slot_a)
            weights(size, item(2 * i + 1), slot_b)
            return 0

        lax.fori_loop(base, base + count, step, 0)
        base = base + count


def cell_list(plan, part):
    start = LOCAL_AT + part * LOCAL_LIST + LOCAL_LEAD
    return [plan[part * KINDS + k] for k in range(KINDS)], lambda n: plan[start + n]


def pair_list(plan):
    start = CROSS_AT + CROSS_LEAD

    def item(n):
        entries = [plan[start + 2 * n + k] for k in range(2)]
        return [(entry >> 7, entry & (PACK - 1)) for entry in entries]

    return [plan[2 * KINDS + k] for k in range(KINDS)], item


def live_parts(fill, visit, other):
    def step(n, _):
        e, part = n >> 1, n & 1
        live = fill[0, e] > 8 * part

        @pl.when(live)
        def _():
            visit(e, part)

        if other is not None:

            @pl.when(jnp.logical_not(live))
            def _():
                other(e, part)

        return 0

    lax.fori_loop(0, 2 * PEERS, step, 0)


def local_density_kernel(part, *refs):
    if part:
        plan, own, first, second, faces, carried, rho, total, face_first, *slots = refs
    else:
        carried = None
        occ, fill, cells, own, rho, first, second, plan, total, *slots = refs
        make_plan(occ, fill, cells, plan)
        planes = planes_of(own, range(ROWS), 0, CELLS, CELL)
        blank = [jnp.zeros((1, WIDTH), F32)] * 3 + [jnp.full((1, WIDTH), 0.5, F32)]
        for ref, some, none in zip(
            (first, second), pair_terms(*planes), pair_terms(*blank, blank[0])
        ):
            put(ref, some, 0, CELLS, CELL)
            set_block(ref, CELLS, CELL, jnp.concatenate(none, 0))
    slot_a, slot_b = slots[:6], slots[6:]
    total[...] = jnp.zeros_like(total)

    def products(c, held):
        left = first_operand(block(first, c, CELL))
        after = jnp.minimum(c + 1, CELLS)
        held[4][...] = support_columns(line(own, c, CELL, 3))
        density_products(left, second_operands(block(second, c, CELL), True), *held[0:2])
        density_products(left, second_operands(block(second, after, CELL), True), *held[2:4])

    def weights(count, c, held):
        after = jnp.minimum(c + 1, CELLS)
        row, other = line(own, c, CELL, 3), line(own, after, CELL, 3)
        own_sum = self_weights(count, *held[0:2], held[4], row)
        there, here = density_weights(count, *held[2:4], held[4], other, False)
        add_block(total, c, CELL, own_sum + here)
        add_block(total, after, CELL, there)

    trips, item = cell_list(plan, part)
    in_turns(trips, SIZES, item, None, products, weights, slot_a, slot_b)

    if part:
        make_face_first(faces, face_first)

        def face_products(i, held):
            for k in range(2):
                n = 2 * i + k
                left = first_operand(block(face_first, n, CELL))
                operands = second_operands(block(second, face_cell(n), CELL), True)
                held[4 + k][...] = support_columns(line(faces, n, CELL, 3))
                density_products(left, operands, *held[2 * k : 2 * k + 2])

        def face_weights(size, i, held):
            for k in range(2):
                c = face_cell(2 * i + k)
                added = density_weights(
                    size, *held[2 * k : 2 * k + 2], held[4 + k], line(own, c, CELL, 3), True
                )
                add_block(total, c, CELL, added)

        in_turns(
            [FACE // 2], [WIDTH], lambda i: i, FACE, face_products, face_weights, slot_a, slot_b
        )

    fold(total, own, rho, carried)


DENSITY_SLOT = [pltpu.VMEM((WIDTH, WIDTH), F32)] * 4 + [pltpu.VMEM((WIDTH, 128), F32)] * 2


def local_density(part, *operands):
    plane = jax.ShapeDtypeStruct((CELLS, WIDTH), F32)
    if part:
        in_specs, out_specs, out_shape = [SM] + [VM] * 5, VM, plane
    else:
        in_specs, out_specs = [SM] * 3 + [VM], [VM] * 3 + [SM]
        out_shape = [plane, OWN_ROWS, OWN_ROWS, jax.ShapeDtypeStruct((PLAN,), jnp.int32)]
    return pl.pallas_call(
        functools.partial(local_density_kernel, part),
        in_specs=in_specs,
        out_specs=out_specs,
        out_shape=out_shape,
        scratch_shapes=[pltpu.VMEM((2, (CELLS + 1) * CELL, 128), F32)]
        + [pltpu.VMEM((2, 2 * FACE * CELL, 128), F32)] * part
        + DENSITY_SLOT * 2,
        cost_estimate=pl.CostEstimate(
            flops=64 * 65536 * 60, bytes_accessed=2 * 2**20, transcendentals=0
        ),
        compiler_params=params(),
    )(*operands)


def live_rows(fill, e, part):
    row = lax.broadcasted_iota(jnp.int32, (8, WIDTH), 0)
    return row < fill[0, e] - 8 * part


def cross_density_kernel(
    fill, plan, own, first, listed, carried, rho, back, total, theirs, there_of, *slots
):
    slot_a, slot_b = slots[:6], slots[6:]
    total[...] = jnp.zeros_like(total)

    def make(e, part):
        after = pair_terms(*listed_planes(listed, e, part, range(ROWS), ROWS))[1]
        put(theirs, after, (e * SLOTS + 8 * part) * CELL, 8, CELL)

    live_parts(fill, make, None)

    def products(pairs, held):
        for k, (slot, c) in enumerate(pairs):
            left = first_operand(block(first, c, CELL))
            held[4 + k][...] = support_columns(line(own, c, CELL, 3))
            operands = second_operands(block(theirs, slot, CELL), True)
            density_products(left, operands, *held[2 * k : 2 * k + 2])

    def weights(count, pairs, held):
        for k, (slot, c) in enumerate(pairs):
            support = listed_support(listed, slot)
            there, here = density_weights(
                count, *held[2 * k : 2 * k + 2], held[4 + k], support, False
            )
            add_block(total, c, CELL, here)
            set_block(there_of, slot, CELL, there)

    trips, item = pair_list(plan)
    in_turns(trips, SIZES, item, None, products, weights, slot_a, slot_b)

    def send(e, part):
        start = (e * SLOTS + 8 * part) * CELL
        summed = sum(planes_of(there_of, range(CELL), start, 8, CELL))
        mass = listed_planes(listed, e, part, [4], ROWS)[0]
        value = jnp.where(live_rows(fill, e, part), summed * inverse_mass(mass), 0.0)
        back[e, rows_at(part, 8), :] = value

    def send_none(e, part):
        back[e, rows_at(part, 8), :] = jnp.zeros((8, WIDTH), F32)

    live_parts(fill, send, send_none)
    fold(total, own, rho, carried)


def cross_density(fill, plan, own, first, listed, carried):
    return pl.pallas_call(
        cross_density_kernel,
        in_specs=[SM, SM] + [VM] * 4,
        out_specs=[VM, VM],
        out_shape=[
            jax.ShapeDtypeStruct((CELLS, WIDTH), F32),
            jax.ShapeDtypeStruct((PEERS, SLOTS, WIDTH), F32),
        ],
        scratch_shapes=[
            pltpu.VMEM((2, (CELLS + 1) * CELL, 128), F32),
            pltpu.VMEM((2, LISTED * CELL, 128), F32),
            pltpu.VMEM((2, LISTED * CELL, 128), F32),
        ]
        + DENSITY_SLOT * 2,
        cost_estimate=pl.CostEstimate(
            flops=80 * 65536 * 60, bytes_accessed=2 * 2**20, transcendentals=0
        ),
        compiler_params=params(),
    )(fill, plan, own, first, listed, carried)


def pressure_kernel(
    pair, near, returned, energy_in, own, density, term, out, energy, sum_of, moving, sem
):
    copies = fetch([(energy_in, energy)], sem)
    sum_of[...] = near[...]

    def peer_step(e, _):
        for s in range(SLOTS):
            sum_of[pl.ds(pair[e, s], 1), :] += returned[e, s : s + 1]
        return 0

    lax.fori_loop(0, PEERS, peer_step, 0)
    copies[0].wait()
    full = planes_of(own, [4], 0, CELLS, CELL)[0] > 0.0
    rho = jnp.where(full, sum_of[...], 0.0)
    density[...] = rho
    term[...] = jnp.where(full, GAMMA_LESS * energy[...] / jnp.where(full, rho, 1.0), 0.0)

    def cell_step(c, _):
        moving[c] = jnp.concatenate(
            [line(own, c, CELL, k) for k in (5, 6, 7)] + [term[pl.ds(c, 1), :]], 0
        )
        return 0

    lax.fori_loop(0, CELLS, cell_step, 0, unroll=8)

    def send_step(e, _):
        for s in range(SLOTS):
            cell = moving[pair[e, s]]
            for h in range(2):
                at = (h * SLOTS + s) * MOVING
                out[e, at : at + MOVING] = half(cell, h)
        return 0

    lax.fori_loop(0, PEERS, send_step, 0)


def pressure(pair, near, returned, energy, own):
    plane = jax.ShapeDtypeStruct((CELLS, WIDTH), F32)
    return pl.pallas_call(
        pressure_kernel,
        in_specs=[SM, VM, VM, ANYWHERE, VM],
        out_specs=[VM, VM, VM],
        out_shape=[
            plane,
            plane,
            jax.ShapeDtypeStruct((PEERS, 2 * SLOTS * MOVING, 128), F32),
        ],
        scratch_shapes=[
            pltpu.VMEM((CELLS, WIDTH), F32),
            pltpu.VMEM((CELLS, WIDTH), F32),
            pltpu.VMEM((CELLS, MOVING, WIDTH), F32),
            pltpu.SemaphoreType.DMA((1,)),
        ],
        compiler_params=params(),
    )(pair, near, returned, energy, own)


def force_terms(place, m, speed, term):
    mp = m * term
    turned = sum(a * b for a, b in zip(place, speed))
    return (
        [m] + [m * a for a in place] + [mp] + [mp * a for a in place]
        + [m * a for a in speed] + [m * turned]
    )


def forces_of(sums, place, speed, term):
    lean = [a * sums[0] - b for a, b in zip(place, sums[1:4])]
    acc = [term * a + (b * sums[4] - c) for a, b, c in zip(lean, place, sums[5:8])]
    mixed = sum(a * b - c * d for a, b, c, d in zip(speed, lean, place, sums[8:11]))
    return [G_SCALE * a for a in acc] + [-G_SCALE * term * (mixed + sums[11])]


def force_operand(ref, index):
    high, low = split2(block(ref, index, SUMS))
    return jnp.concatenate([high, low], 0)


def own_terms(own, term, rows):
    planes = planes_of(own, range(CELL), 0, CELLS, CELL)
    terms = force_terms(planes[0:3], planes[4], planes[5:8], term[...])
    put(rows, terms, 0, CELLS, SUMS)
    put(rows, [jnp.zeros((CELLS, WIDTH), F32)] * 4, 12, CELLS, SUMS)
    set_block(rows, CELLS, SUMS, jnp.zeros((SUMS, WIDTH), F32))


def slopes(s_ref, high, low, columns, row, count):
    for start in range(0, count, CHUNK):
        s = jnp.maximum(s_ref[start : start + CHUNK], TINY)
        dist = s * lax.rsqrt(s)
        wide = columns[start : start + CHUNK]
        support = jnp.concatenate([wide, wide], 1) + row
        d = jnp.maximum(support - dist, 0.0)
        e = pl.reciprocal(support * support, approx=True)
        x = e * d
        g = (x * x) * (x * e)
        top = g.astype(BF)
        high[start : start + CHUNK] = top
        low[start : start + CHUNK] = (g - top.astype(F32)).astype(BF)


def distances(left, rows, s_ref):
    s_ref[...] = jnp.dot(left, second_operands(rows, False), preferred_element_type=F32)


def slope_sums(rows, high, low, dims):
    top = lax.dot_general(rows, high, dims, preferred_element_type=F32)
    rest = lax.dot_general(rows[:SUMS], low, dims, preferred_element_type=F32)
    return top[:SUMS] + top[SUMS:] + rest


def to_seconds(rows, count, high, low):
    return slope_sums(rows[:, :count], high[0:count], low[0:count], NN)


def to_firsts(rows, count, high, low):
    return slope_sums(rows, high[0:count], low[0:count], NT)


def in_three_turns(trips, sizes, item, last, products, tiles, sums, slot_a, slot_b, lag):
    products(item(0), slot_a)
    base = 0
    for count, size in zip(trips, sizes):

        def step(i, _, size=size):
            after = 2 * i + 2
            if last is not None:
                after = jnp.minimum(after, last - 1)
            if lag == 1:
                sums(size, item(2 * i - 1), slot_b)
                tiles(size, item(2 * i), slot_a)
                products(item(2 * i + 1), slot_b)
                sums(size, item(2 * i), slot_a)
                tiles(size, item(2 * i + 1), slot_b)
                products(item(after), slot_a)
            else:
                products(item(2 * i + 1), slot_b)
                sums(size, item(2 * i - 2), slot_a)
                tiles(size, item(2 * i), slot_a)
                products(item(after), slot_a)
                sums(size, item(2 * i - 1), slot_b)
                tiles(size, item(2 * i + 1), slot_b)
            return 0

        lax.fori_loop(base, base + count, step, 0)
        base = base + count
    if lag == 2:
        sums(sizes[-1], item(2 * base - 2), slot_a)
    sums(sizes[-1], item(2 * base - 1), slot_b)


def clear(slots):
    for held in slots:
        held[SIZES[0] :, :] = jnp.zeros((WIDTH - SIZES[0], WIDTH), BF)


def add_forces(total, own, term, out, carried):
    planes = planes_of(own, range(CELL), 0, CELLS, CELL)
    sums = planes_of(total, range(12), 0, CELLS, SUMS)
    for k, force in enumerate(forces_of(sums, planes[0:3], planes[5:8], term[...])):
        out[k] = force if carried is None else carried[k] + force


def local_force_kernel(part, plan, own, first, second, term, *rest):
    if part:
        faces, face_terms, carried, out, rows, total, face_rows, face_first, *slots = rest
    else:
        carried = None
        out, rows, total, *slots = rest
    slot_a, slot_b = slots[:7], slots[7:]
    own_terms(own, term, rows)
    total[...] = jnp.zeros_like(total)
    clear([held[k] for held in (slot_a, slot_b) for k in (2, 3, 5, 6)])

    def products(c, held):
        left = first_operand(block(first, c, CELL))
        held[0][...] = support_columns(line(own, c, CELL, 3))
        distances(left, block(second, c, CELL), held[1])
        distances(left, block(second, jnp.minimum(c + 1, CELLS), CELL), held[4])

    def tiles(count, c, held):
        other = line(own, jnp.minimum(c + 1, CELLS), CELL, 3)
        slopes(*held[1:4], held[0], line(own, c, CELL, 3), count)
        slopes(*held[4:7], held[0], other, count)

    def sums(count, c, held):
        after = jnp.minimum(c + 1, CELLS)
        mine, other = force_operand(rows, c), force_operand(rows, after)
        added = to_firsts(other, count, *held[5:7])
        if count < WIDTH:
            added = jnp.concatenate([added, jnp.zeros((SUMS, WIDTH - count), F32)], 1)
        add_block(total, c, SUMS, to_seconds(mine, count, *held[2:4]) + added)
        add_block(total, after, SUMS, to_seconds(mine, count, *held[5:7]))

    trips, item = cell_list(plan, part)
    in_three_turns(trips, SIZES, item, None, products, tiles, sums, slot_a, slot_b, 1)

    if part:
        make_face_first(faces, face_first)
        planes = planes_of(faces, range(CELL), 0, 2 * FACE, CELL)
        terms = force_terms(planes[0:3], planes[4], planes[5:8], face_terms[...])
        blank = jnp.zeros((2 * FACE, WIDTH), F32)
        put(face_rows, terms + [blank] * 4, 0, 2 * FACE, SUMS)

        def face_products(i, held):
            for k in range(2):
                n = 2 * i + k
                left = first_operand(block(face_first, n, CELL))
                distances(left, block(second, face_cell(n), CELL), held[1 + 3 * k])

        def face_tiles(size, i, held):
            for k in range(2):
                n = 2 * i + k
                columns = support_columns(line(faces, n, CELL, 3))
                slopes(
                    *held[1 + 3 * k : 4 + 3 * k], columns, line(own, face_cell(n), CELL, 3), size
                )

        def face_sums(size, i, held):
            for k in range(2):
                n = jnp.maximum(2 * i, 0) + k
                c = jnp.where(i < 0, CELLS, face_cell(n))
                theirs = force_operand(face_rows, n)
                add_block(
                    total, c, SUMS, to_seconds(theirs, size, *held[2 + 3 * k : 4 + 3 * k])
                )

        in_three_turns(
            [FACE // 2], [WIDTH], lambda i: i, FACE, face_products, face_tiles, face_sums,
            slot_a, slot_b, 1,
        )

    add_forces(total, own, term, out, carried)


FORCE_PAIR = [
    pltpu.VMEM((WIDTH, WIDTH), F32),
    pltpu.VMEM((WIDTH, WIDTH), BF),
    pltpu.VMEM((WIDTH, WIDTH), BF),
]
FORCE_SLOT = [pltpu.VMEM((WIDTH, 128), F32)] + FORCE_PAIR * 2


def local_force(part, plan, own, first, second, term, *rest):
    scratch = [
        pltpu.VMEM((2, (CELLS + 1) * SUMS, 128), F32),
        pltpu.VMEM((2, (CELLS + 1) * SUMS, 128), F32),
    ]
    if part:
        scratch.append(pltpu.VMEM((2, 2 * FACE * SUMS, 128), F32))
        scratch.append(pltpu.VMEM((2, 2 * FACE * CELL, 128), F32))
    return pl.pallas_call(
        functools.partial(local_force_kernel, part),
        in_specs=[SM] + [VM] * (4 + len(rest)),
        out_specs=VM,
        out_shape=jax.ShapeDtypeStruct((4, CELLS, WIDTH), F32),
        scratch_shapes=scratch + FORCE_SLOT * 2,
        cost_estimate=pl.CostEstimate(
            flops=64 * 65536 * 80, bytes_accessed=2 * 2**20, transcendentals=0
        ),
        compiler_params=params(),
    )(plan, own, first, second, term, *rest)


def cross_force_kernel(
    fill, plan, own, first, term, listed, arrived, carried, _, out, back,
    rows, total, theirs, their_rows, sums_of, *slots
):
    slot_a, slot_b = slots[:8], slots[8:]
    own_terms(own, term, rows)
    total[...] = jnp.zeros_like(total)
    clear([held[k] for held in (slot_a, slot_b) for k in (3, 4, 6, 7)])

    def make(e, part):
        planes = listed_planes(listed, e, part, range(ROWS), ROWS)
        at = e * SLOTS + 8 * part
        put(theirs, pair_terms(*planes)[1], at * CELL, 8, CELL)
        *speed, pressed = listed_planes(arrived, e, part, range(MOVING), MOVING)
        terms = force_terms(planes[0:3], planes[4], speed, pressed)
        blank = jnp.zeros((8, WIDTH), F32)
        put(their_rows, terms + [blank] * 4, at * SUMS, 8, SUMS)

    live_parts(fill, make, None)

    def products(pairs, held):
        for k, (slot, c) in enumerate(pairs):
            held[k][...] = support_columns(line(own, c, CELL, 3))
            left = first_operand(block(first, c, CELL))
            distances(left, block(theirs, slot, CELL), held[2 + 3 * k])

    def tiles(count, pairs, held):
        for k, (slot, c) in enumerate(pairs):
            support = listed_support(listed, slot)
            slopes(*held[2 + 3 * k : 5 + 3 * k], held[k], support, count)

    def sums(count, pairs, held):
        for k, (slot, c) in enumerate(pairs):
            tile = held[3 + 3 * k : 5 + 3 * k]
            set_block(sums_of, slot, SUMS, to_seconds(force_operand(rows, c), count, *tile))
            added = to_firsts(force_operand(their_rows, slot), count, *tile)
            if count < WIDTH:
                added = jnp.concatenate([added, jnp.zeros((SUMS, WIDTH - count), F32)], 1)
            add_block(total, c, SUMS, added)

    trips, item = pair_list(plan)
    in_three_turns(trips, SIZES, item, None, products, tiles, sums, slot_a, slot_b, 2)

    def send(e, part):
        planes = listed_planes(listed, e, part, range(3), ROWS)
        *speed, pressed = listed_planes(arrived, e, part, range(MOVING), MOVING)
        summed = planes_of(sums_of, range(12), (e * SLOTS + 8 * part) * SUMS, 8, SUMS)
        live = live_rows(fill, e, part)
        send_rows(e, part, [jnp.where(live, f, 0.0) for f in forces_of(summed, planes, speed, pressed)])

    def send_none(e, part):
        send_rows(e, part, [jnp.zeros((8, WIDTH), F32)] * MOVING)

    def send_rows(e, part, forces):
        for k, force in enumerate(forces):
            for h in range(2):
                start = (h * SLOTS + 8 * part) * MOVING + k
                back[e, pl.ds(start, 8, stride=MOVING), :] = half(force, h)

    live_parts(fill, send, send_none)
    add_forces(total, own, term, out, carried)


def cross_force(fill, plan, own, first, term, listed, arrived, carried, after):
    return pl.pallas_call(
        cross_force_kernel,
        in_specs=[SM, SM] + [VM] * 6 + [ANYWHERE],
        out_specs=[VM, VM],
        out_shape=[
            jax.ShapeDtypeStruct((4, CELLS, WIDTH), F32),
            jax.ShapeDtypeStruct((PEERS, 2 * SLOTS * MOVING, 128), F32),
        ],
        scratch_shapes=[
            pltpu.VMEM((2, (CELLS + 1) * SUMS, 128), F32),
            pltpu.VMEM((2, (CELLS + 1) * SUMS, 128), F32),
            pltpu.VMEM((2, LISTED * CELL, 128), F32),
            pltpu.VMEM((2, LISTED * SUMS, 128), F32),
            pltpu.VMEM((2, LISTED * SUMS, 128), F32),
        ]
        + (FORCE_SLOT[:1] * 2 + FORCE_PAIR * 2) * 2,
        cost_estimate=pl.CostEstimate(
            flops=80 * 65536 * 80, bytes_accessed=2 * 2**20, transcendentals=0
        ),
        compiler_params=params(),
    )(fill, plan, own, first, term, listed, arrived, carried, after)


def finish_kernel(pair, near, returned, active_in, own, out, total, active, gate, sem):
    copies = fetch([(active_in, active)], sem)
    total[...] = jnp.zeros_like(total)

    def peer_step(e, _):
        for s in range(SLOTS):
            at = s * MOVING
            total[pair[e, s]] += both(
                lambda h: returned[
                    e, h * SLOTS * MOVING + at : h * SLOTS * MOVING + at + MOVING
                ]
            )
        return 0

    lax.fori_loop(0, PEERS, peer_step, 0)
    copies[0].wait()
    full = planes_of(own, [4], 0, CELLS, CELL)[0] > 0.0
    gate[...] = jnp.where(full, active[...].astype(F32), 0.0)

    def cell_step(c, _):
        one = pl.ds(c, 1)
        open_to = gate[one, :]
        for k in range(4):
            out[k, one, :] = (near[k, one, :] + total[c, k : k + 1]) * open_to
        return 0

    lax.fori_loop(0, CELLS, cell_step, 0, unroll=8)


def finish(pair, near, returned, active, own):
    return pl.pallas_call(
        finish_kernel,
        in_specs=[SM, VM, VM, ANYWHERE, VM],
        out_specs=VM,
        out_shape=jax.ShapeDtypeStruct((4, CELLS, WIDTH), F32),
        scratch_shapes=[
            pltpu.VMEM((CELLS, 4, WIDTH), F32),
            pltpu.VMEM((CELLS, WIDTH), jnp.int32),
            pltpu.VMEM((CELLS, WIDTH), F32),
            pltpu.SemaphoreType.DMA((1,)),
        ],
        compiler_params=params(),
    )(pair, near, returned, active, own)


def to_peers(block):
    return lax.all_to_all(block, "dev", split_axis=0, concat_axis=0, tiled=True)


def with_neighbours(rows, size):
    count = lax.axis_size("region")
    up = [(i, (i + 1) % count) for i in range(count)]
    down = [(i, (i - 1) % count) for i in range(count)]
    return jnp.concatenate(
        [
            lax.ppermute(rows[..., (CELLS - FACE) * size : CELLS * size, :], "region", up),
            lax.ppermute(rows[..., : FACE * size, :], "region", down),
        ],
        -2,
    )


def local(
    positions, velocity, smoothing, masses, energy, occupancy, active, send_cells, send_fill,
    pair_cell,
):
    pair = pair_cell[0]
    own, listed = prepare(occupancy, pair, positions, velocity, smoothing, masses)
    arrived = to_peers(listed)
    faces = with_neighbours(own, CELL)
    rho, first, second, plan = local_density(0, occupancy, send_fill, send_cells[0], own)
    rho, back = cross_density(send_fill, plan, own, first, arrived, rho)
    returned = to_peers(back)
    rho = local_density(1, plan, own, first, second, faces, rho)
    density, term, leaving = pressure(pair, rho, returned, energy, own)
    arrived_moving = to_peers(leaving)
    face_terms = with_neighbours(term, 1)
    sums = local_force(0, plan, own, first, second, term)
    sums, force_back = cross_force(
        send_fill, plan, own, first, term, arrived, arrived_moving, sums, face_terms
    )
    returned_force = to_peers(force_back)
    sums = local_force(1, plan, own, first, second, term, faces, face_terms, sums)
    forces = finish(pair, sums, returned_force, active, own)
    return (density, forces)


def solution(mesh):
    cells = P(("region", "dev"), None)
    vectors = P(None, ("region", "dev"), None)
    lists = P(("region", "dev"), None, None)
    in_specs = (
        vectors, vectors, cells, cells, cells, P(("region", "dev")), cells, lists, cells, lists,
    )
    return jax.shard_map(
        local, mesh=mesh, in_specs=in_specs, out_specs=(cells, vectors), check_vma=False
    )
```

```python
import functools
import math

import jax
import jax.numpy as jnp
from jax import lax
from jax.experimental import pallas as pl
from jax.experimental.pallas import tpu as pltpu
from jax.sharding import PartitionSpec as P

BF = jnp.bfloat16
F32 = jnp.float32
FACE = 4
CELLS = 64
WIDTH = 256
PEERS = 16
SLOTS = 16
LISTED = PEERS * SLOTS
GAMMA_LESS = 2.0 / 3.0
W_SCALE = 84.0 / math.pi
G_SCALE = 6720.0 / math.pi
TINY = 1e-14
EMPTY = 1e8
CHUNK = 32
CELL = 8
SUMS = 16
NN = (((1,), (0,)), ((), ()))
NT = (((1,), (1,)), ((), ()))
VM = pl.BlockSpec(memory_space=pltpu.VMEM)
SM = pl.BlockSpec(memory_space=pltpu.SMEM)
ROWS = 5
MOVING = 4
SPEEDS = 3
SPLITS = (40, 24)
SIZES = (160, 192, 224, 256)
KINDS = len(SIZES)
UNIT = 4
LOCAL_AT = 5 * KINDS
LOCAL_LEAD = 2
LOCAL_LIST = CELLS + 8
CROSS_AT = LOCAL_AT + 4 * LOCAL_LIST
CROSS_LEAD = 4
CROSS_LIST = LISTED + 16
PLAN = CROSS_AT + CROSS_LIST
PACK = 128
ANYWHERE = pl.BlockSpec(memory_space=pl.ANY)
OWN_ROWS = jax.ShapeDtypeStruct((2, (CELLS + 1) * CELL, 128), F32)


def params(mib=50):
    return pltpu.CompilerParams(vmem_limit_bytes=int(mib * 2**20))


def split2(x):
    a = x.astype(BF)
    return a, (x - a.astype(F32)).astype(BF)


def split3(x):
    a = x.astype(BF).astype(F32)
    rest = x - a
    b = rest.astype(BF).astype(F32)
    return a, b, rest - b


def pair_terms(x, y, z, h, m):
    norm = 4.0 * (x * x + y * y + z * z)
    root = lax.rsqrt(jnp.where(m > 0.0, m, 1.0))
    mu = jnp.where(m > 0.0, root * lax.rsqrt(root), EMPTY)
    one = jnp.ones_like(x)
    first = [-8.0 * x, -8.0 * y, -8.0 * z, norm, one, h * h * mu, 2.0 * h * mu, mu]
    second = [x, y, z, one, norm, mu, h * mu, h * h * mu]
    return first, second


def both(read):
    return jnp.concatenate([read(0), read(1)], -1)


def half(value, h):
    return value[..., 128 * h : 128 * (h + 1)]


def put(ref, planes, start, count, stride):
    for k, plane in enumerate(planes):
        for h in range(2):
            ref[h, pl.ds(start + k, count, stride=stride), :] = half(plane, h)


def planes_of(ref, ids, start, count, stride):
    return [both(lambda h: ref[h, pl.ds(start + k, count, stride=stride), :]) for k in ids]


def rows_at(index, size):
    return pl.ds(pl.multiple_of(index * size, size), size)


def block(ref, index, size):
    return both(lambda h: ref[h, rows_at(index, size), :])


def set_block(ref, index, size, value):
    for h in range(2):
        ref[h, rows_at(index, size), :] = half(value, h)


def add_block(ref, index, size, value):
    for h in range(2):
        ref[h, rows_at(index, size), :] += half(value, h)


def line(ref, index, size, k):
    return both(lambda h: ref[h, pl.ds(index * size + k, 1), :])


def listed_planes(listed, e, part, ids, size):
    step = SLOTS * size
    start = 8 * part * size
    return [
        both(lambda h: listed[e, pl.ds(h * step + start + k, 8, stride=size), :]) for k in ids
    ]


def listed_support(listed, slot):
    at = (slot & (SLOTS - 1)) * ROWS + 3
    return both(lambda h: listed[slot >> 4, pl.ds(h * SLOTS * ROWS + at, 1), :])


def first_operand(rows):
    a1, a2, a3 = split3(rows)
    return jnp.concatenate([a1, a1, a2, a2, a1, a3, jnp.zeros((80, WIDTH), F32)], 0).T.astype(BF)


def second_operands(rows, both):
    b1, b2, b3 = split3(rows)
    stacked = jnp.concatenate([b1, b2, b1, b2, b3, b1, jnp.zeros((80, WIDTH), F32)], 0)
    part = lax.broadcasted_iota(jnp.int32, stacked.shape, 0) % 8
    near = jnp.where(part < 5, stacked, 0.0).astype(BF)
    if not both:
        return near
    return near, jnp.where(part >= 5, stacked, 0.0).astype(BF)


def support_columns(row):
    return jnp.broadcast_to(row, (128, WIDTH)).T


def density_products(left, operands, s_ref, mix_ref):
    s_ref[...] = jnp.dot(left, operands[0], preferred_element_type=F32)
    mix_ref[...] = jnp.dot(left, operands[1], preferred_element_type=F32)


def weights_of(s, mix, columns, row):
    s = jnp.maximum(s, TINY)
    dist = s * lax.rsqrt(s)
    support = columns + row
    d = jnp.maximum(support - dist, 0.0)
    x = pl.reciprocal(mix, approx=True) * d
    x = x * x
    x = x * x
    return x * (support + 4.0 * dist)


def density_weights(count, s_ref, mix_ref, columns, row, one_sided):
    second = jnp.zeros((8, WIDTH), F32)
    firsts = []
    for start in range(0, count, CHUNK):
        part = slice(start, start + CHUNK)
        wide = columns[part]
        w = weights_of(s_ref[part], mix_ref[part], jnp.concatenate([wide, wide], 1), row)
        for k in range(CHUNK // 8):
            second = second + w[8 * k : 8 * k + 8]
        if not one_sided:
            firsts.append(w[:, :128] + w[:, 128:])
    if one_sided:
        return second
    if count < WIDTH:
        firsts.append(jnp.zeros((WIDTH - count, 128), F32))
    turned = jnp.concatenate(firsts, 0).T
    first = turned[:8]
    for k in range(1, 16):
        first = first + turned[8 * k : 8 * k + 8]
    return second, first


def inverse_mass(m):
    return jnp.where(m > 0.0, W_SCALE / jnp.where(m > 0.0, m, 1.0), 0.0)


def self_weights(count, s_ref, mix_ref, columns, row):
    sums = [jnp.zeros((8, 128), F32)] * 2
    crossing = []
    for start in range(0, count, CHUNK):
        part = slice(start, start + CHUNK)
        for h in range(0 if start < 128 else 1, 2):
            lanes = slice(128 * h, 128 * (h + 1))
            w = weights_of(s_ref[part, lanes], mix_ref[part, lanes], columns[part], half(row, h))
            for k in range(CHUNK // 8):
                sums[h] = sums[h] + w[8 * k : 8 * k + 8]
            if h and start < 128:
                crossing.append(w)
    turned = jnp.concatenate(crossing, 0).T
    for k in range(16):
        sums[0] = sums[0] + turned[8 * k : 8 * k + 8]
    return jnp.concatenate(sums, 1)


def fetch(pairs, sem):
    copies = [
        pltpu.make_async_copy(source, target, sem.at[k])
        for k, (source, target) in enumerate(pairs)
    ]
    for copy in copies:
        copy.start()
    return copies


def prepare_kernel(
    occ, pair, pos_in, vel_in, smooth_in, mass_in, own, out, pos, vel, smooth, mass, full, sem
):
    copies = fetch(
        [(pos_in, pos), (vel_in, vel), (smooth_in, smooth), (mass_in, mass)], sem
    )
    lane = lax.broadcasted_iota(jnp.int32, (1, WIDTH), 1)
    for c in range(CELLS):
        full[c : c + 1, :] = (lane < occ[c]).astype(F32)
    for copy in copies:
        copy.wait()
    place = [pos[k] - 0.5 for k in range(3)]
    m = jnp.where(full[...] > 0.0, mass[...], 0.0)
    put(own, place + [smooth[...], m] + [vel[k] for k in range(3)], 0, CELLS, CELL)
    blank = jnp.zeros((CELL, WIDTH), F32)
    wide = jnp.full((1, WIDTH), 0.5, F32)
    set_block(own, CELLS, CELL, jnp.concatenate([blank[:3], wide, blank[:4]], 0))

    def peer_step(e, _):
        for s in range(SLOTS):
            c = pair[e, s]
            for h in range(2):
                at = (h * SLOTS + s) * ROWS
                out[e, at : at + ROWS] = own[h, rows_at(c, CELL), :][:ROWS]
        return 0

    lax.fori_loop(0, PEERS, peer_step, 0)


def prepare(occ, pair, pos, vel, smooth, mass):
    plane = pltpu.VMEM((CELLS, WIDTH), F32)
    return pl.pallas_call(
        prepare_kernel,
        in_specs=[SM] * 2 + [ANYWHERE] * 4,
        out_specs=[VM] * 2,
        out_shape=[
            OWN_ROWS,
            jax.ShapeDtypeStruct((PEERS, 2 * SLOTS * ROWS, 128), F32),
        ],
        scratch_shapes=[
            pltpu.VMEM((3, CELLS, WIDTH), F32),
            pltpu.VMEM((3, CELLS, WIDTH), F32),
            plane,
            plane,
            plane,
            pltpu.SemaphoreType.DMA((4,)),
        ],
        compiler_params=params(60),
    )(occ, pair, pos, vel, smooth, mass)


def kind_of(size):
    return jnp.maximum(size - SIZES[0] + 31, 0) >> 5


def make_plan(occ, fill, cells, plan):
    def over_local(visit, group, carry):
        split = SPLITS[group // 2]
        low, high = (split, CELLS) if group % 2 else (0, split)
        step = lambda c, carry: visit(kind_of(occ[c]), c, carry)
        return lax.fori_loop(low, high, step, carry, unroll=8)

    def over_pairs(visit, carry):
        def peer_step(e, carry):
            def slot_step(s, carry):
                cell = cells[e, s]
                return visit(kind_of(occ[cell]), (e * SLOTS + s) * PACK + cell, carry)

            return lax.fori_loop(0, fill[0, e], slot_step, carry)

        return lax.fori_loop(0, PEERS, peer_step, carry)

    unused = jnp.int32(0)
    for e in range(PEERS):
        unused = jnp.where(fill[0, e] == 0, e * SLOTS, unused)

    def one_of(kind):
        return jnp.left_shift(jnp.int32(1), 8 * kind)

    groups = [
        (
            functools.partial(lambda g, v, x: over_local(v, g, x), g),
            LOCAL_AT + g * LOCAL_LIST, LOCAL_LEAD, 2, CELLS,
        )
        for g in range(4)
    ]
    groups.append((over_pairs, CROSS_AT, CROSS_LEAD, UNIT, unused * PACK + CELLS))
    for group, (walk, start, lead, unit, blank) in enumerate(groups):
        counts = walk(lambda kind, value, packed: packed + one_of(kind), jnp.int32(0))
        total = jnp.int32(0)
        done = jnp.int32(0)
        places = jnp.int32(0)
        for k in range(KINDS):
            places = places + jnp.left_shift(total, 8 * k)
            total = total + ((counts >> (8 * k)) & 255)
            upto = (total + (unit - 1 if k == KINDS - 1 else 0)) >> (unit.bit_length() - 1)
            plan[group * KINDS + k] = upto - done
            done = upto
        for k in range(lead):
            plan[start + k] = blank
        for k in range(unit + 1):
            plan[start + lead + total + k] = blank

        def place(kind, value, packed, start=start + lead):
            plan[start + ((packed >> (8 * kind)) & 255)] = value
            return packed + one_of(kind)

        walk(place, places)


def fold(total, own, out, carried):
    mine = sum(planes_of(total, range(CELL), 0, CELLS, CELL))
    mass = planes_of(own, [4], 0, CELLS, CELL)[0]
    mine = mine * inverse_mass(mass)
    out[...] = mine if carried is None else carried[...] + mine


def make_face_first(faces, face_first):
    planes = planes_of(faces, range(ROWS), 0, 2 * FACE, CELL)
    put(face_first, pair_terms(*planes)[0], 0, 2 * FACE, CELL)


def face_cell(n):
    return jnp.where(n < FACE, n, CELLS - 2 * FACE + n)


def in_turns(trips, sizes, item, last, products, weights, slot_a, slot_b):
    products(item(0), slot_a)
    base = 0
    for count, size in zip(trips, sizes):

        def step(i, _, size=size):
            products(item(2 * i + 1), slot_b)
            weights(size, item(2 * i), slot_a)
            after = 2 * i + 2
            products(item(after if last is None else jnp.minimum(after, last - 1)), slot_a)
            weights(size, item(2 * i + 1), slot_b)
            return 0

        lax.fori_loop(base, base + count, step, 0)
        base = base + count


def cell_list(plan, group):
    start = LOCAL_AT + group * LOCAL_LIST + LOCAL_LEAD
    return [plan[group * KINDS + k] for k in range(KINDS)], lambda n: plan[start + n]


def pair_list(plan):
    start = CROSS_AT + CROSS_LEAD

    def item(n):
        entries = [plan[start + 2 * n + k] for k in range(2)]
        return [(entry >> 7, entry & (PACK - 1)) for entry in entries]

    return [plan[4 * KINDS + k] for k in range(KINDS)], item


def live_parts(fill, visit, other):
    def step(n, _):
        e, part = n >> 1, n & 1
        live = fill[0, e] > 8 * part

        @pl.when(live)
        def _():
            visit(e, part)

        if other is not None:

            @pl.when(jnp.logical_not(live))
            def _():
                other(e, part)

        return 0

    lax.fori_loop(0, 2 * PEERS, step, 0)


def local_density_kernel(part, *refs):
    if part:
        plan, own, first, second, faces, carried, rho, total, face_first, *slots = refs
    else:
        carried = None
        occ, fill, cells, pair, own, rho, first, second, speeds, plan, total, *slots = refs
        make_plan(occ, fill, cells, plan)

        def peer_step(e, _):
            for s in range(SLOTS):
                c = pair[e, s]
                for h in range(2):
                    at = (h * SLOTS + s) * SPEEDS
                    speeds[e, at : at + SPEEDS] = own[h, rows_at(c, CELL), :][5:8]
            return 0

        lax.fori_loop(0, PEERS, peer_step, 0)
        planes = planes_of(own, range(ROWS), 0, CELLS, CELL)
        blank = [jnp.zeros((1, WIDTH), F32)] * 3 + [jnp.full((1, WIDTH), 0.5, F32)]
        for ref, some, none in zip(
            (first, second), pair_terms(*planes), pair_terms(*blank, blank[0])
        ):
            put(ref, some, 0, CELLS, CELL)
            set_block(ref, CELLS, CELL, jnp.concatenate(none, 0))
    slot_a, slot_b = slots[:6], slots[6:]
    total[...] = jnp.zeros_like(total)

    def products(c, held):
        left = first_operand(block(first, c, CELL))
        after = jnp.minimum(c + 1, CELLS)
        held[4][...] = support_columns(line(own, c, CELL, 3))
        density_products(left, second_operands(block(second, c, CELL), True), *held[0:2])
        density_products(left, second_operands(block(second, after, CELL), True), *held[2:4])

    def weights(count, c, held):
        after = jnp.minimum(c + 1, CELLS)
        row, other = line(own, c, CELL, 3), line(own, after, CELL, 3)
        own_sum = self_weights(count, *held[0:2], held[4], row)
        there, here = density_weights(count, *held[2:4], held[4], other, False)
        add_block(total, c, CELL, own_sum + here)
        add_block(total, after, CELL, there)

    trips, item = cell_list(plan, part)
    in_turns(trips, SIZES, item, None, products, weights, slot_a, slot_b)

    if part:
        make_face_first(faces, face_first)

        def face_products(i, held):
            for k in range(2):
                n = 2 * i + k
                left = first_operand(block(face_first, n, CELL))
                operands = second_operands(block(second, face_cell(n), CELL), True)
                held[4 + k][...] = support_columns(line(faces, n, CELL, 3))
                density_products(left, operands, *held[2 * k : 2 * k + 2])

        def face_weights(size, i, held):
            for k in range(2):
                c = face_cell(2 * i + k)
                added = density_weights(
                    size, *held[2 * k : 2 * k + 2], held[4 + k], line(own, c, CELL, 3), True
                )
                add_block(total, c, CELL, added)

        in_turns(
            [FACE // 2], [WIDTH], lambda i: i, FACE, face_products, face_weights, slot_a, slot_b
        )

    fold(total, own, rho, carried)


DENSITY_SLOT = [pltpu.VMEM((WIDTH, WIDTH), F32)] * 4 + [pltpu.VMEM((WIDTH, 128), F32)] * 2


def local_density(part, *operands):
    plane = jax.ShapeDtypeStruct((CELLS, WIDTH), F32)
    if part:
        in_specs, out_specs, out_shape = [SM] + [VM] * 5, VM, plane
    else:
        in_specs, out_specs = [SM] * 4 + [VM], [VM] * 4 + [SM]
        out_shape = [
            plane,
            OWN_ROWS,
            OWN_ROWS,
            jax.ShapeDtypeStruct((PEERS, 2 * SLOTS * SPEEDS, 128), F32),
            jax.ShapeDtypeStruct((PLAN,), jnp.int32),
        ]
    return pl.pallas_call(
        functools.partial(local_density_kernel, part),
        in_specs=in_specs,
        out_specs=out_specs,
        out_shape=out_shape,
        scratch_shapes=[pltpu.VMEM((2, (CELLS + 1) * CELL, 128), F32)]
        + [pltpu.VMEM((2, 2 * FACE * CELL, 128), F32)] * part
        + DENSITY_SLOT * 2,
        cost_estimate=pl.CostEstimate(
            flops=64 * 65536 * 60, bytes_accessed=2 * 2**20, transcendentals=0
        ),
        compiler_params=params(),
    )(*operands)


def live_rows(fill, e, part):
    row = lax.broadcasted_iota(jnp.int32, (8, WIDTH), 0)
    return row < fill[0, e] - 8 * part


def cross_density_kernel(
    fill, plan, own, first, listed, carried, rho, back, total, theirs, there_of, *slots
):
    slot_a, slot_b = slots[:6], slots[6:]
    total[...] = jnp.zeros_like(total)

    def make(e, part):
        after = pair_terms(*listed_planes(listed, e, part, range(ROWS), ROWS))[1]
        put(theirs, after, (e * SLOTS + 8 * part) * CELL, 8, CELL)

    live_parts(fill, make, None)

    def products(pairs, held):
        for k, (slot, c) in enumerate(pairs):
            left = first_operand(block(first, c, CELL))
            held[4 + k][...] = support_columns(line(own, c, CELL, 3))
            operands = second_operands(block(theirs, slot, CELL), True)
            density_products(left, operands, *held[2 * k : 2 * k + 2])

    def weights(count, pairs, held):
        for k, (slot, c) in enumerate(pairs):
            support = listed_support(listed, slot)
            there, here = density_weights(
                count, *held[2 * k : 2 * k + 2], held[4 + k], support, False
            )
            add_block(total, c, CELL, here)
            set_block(there_of, slot, CELL, there)

    trips, item = pair_list(plan)
    in_turns(trips, SIZES, item, None, products, weights, slot_a, slot_b)

    def send(e, part):
        start = (e * SLOTS + 8 * part) * CELL
        summed = sum(planes_of(there_of, range(CELL), start, 8, CELL))
        mass = listed_planes(listed, e, part, [4], ROWS)[0]
        value = jnp.where(live_rows(fill, e, part), summed * inverse_mass(mass), 0.0)
        back[e, rows_at(part, 8), :] = value

    def send_none(e, part):
        back[e, rows_at(part, 8), :] = jnp.zeros((8, WIDTH), F32)

    live_parts(fill, send, send_none)
    fold(total, own, rho, carried)


def cross_density(fill, plan, own, first, listed, carried):
    return pl.pallas_call(
        cross_density_kernel,
        in_specs=[SM, SM] + [VM] * 4,
        out_specs=[VM, VM],
        out_shape=[
            jax.ShapeDtypeStruct((CELLS, WIDTH), F32),
            jax.ShapeDtypeStruct((PEERS, SLOTS, WIDTH), F32),
        ],
        scratch_shapes=[
            pltpu.VMEM((2, (CELLS + 1) * CELL, 128), F32),
            pltpu.VMEM((2, LISTED * CELL, 128), F32),
            pltpu.VMEM((2, LISTED * CELL, 128), F32),
        ]
        + DENSITY_SLOT * 2,
        cost_estimate=pl.CostEstimate(
            flops=80 * 65536 * 60, bytes_accessed=2 * 2**20, transcendentals=0
        ),
        compiler_params=params(),
    )(fill, plan, own, first, listed, carried)


def pressure_kernel(
    pair, near, returned, energy_in, own, density, term, out, energy, sum_of, sem
):
    copies = fetch([(energy_in, energy)], sem)
    sum_of[...] = near[...]

    def peer_step(e, _):
        for s in range(SLOTS):
            sum_of[pl.ds(pair[e, s], 1), :] += returned[e, s : s + 1]
        return 0

    lax.fori_loop(0, PEERS, peer_step, 0)
    copies[0].wait()
    full = planes_of(own, [4], 0, CELLS, CELL)[0] > 0.0
    rho = jnp.where(full, sum_of[...], 0.0)
    density[...] = rho
    term[...] = jnp.where(full, GAMMA_LESS * energy[...] / jnp.where(full, rho, 1.0), 0.0)

    def send_step(e, _):
        for s in range(SLOTS):
            out[e, s : s + 1] = term[pl.ds(pair[e, s], 1), :]
        return 0

    lax.fori_loop(0, PEERS, send_step, 0)


def pressure(pair, near, returned, energy, own):
    plane = jax.ShapeDtypeStruct((CELLS, WIDTH), F32)
    return pl.pallas_call(
        pressure_kernel,
        in_specs=[SM, VM, VM, ANYWHERE, VM],
        out_specs=[VM, VM, VM],
        out_shape=[
            plane,
            plane,
            jax.ShapeDtypeStruct((PEERS, SLOTS, WIDTH), F32),
        ],
        scratch_shapes=[
            pltpu.VMEM((CELLS, WIDTH), F32),
            pltpu.VMEM((CELLS, WIDTH), F32),
            pltpu.SemaphoreType.DMA((1,)),
        ],
        compiler_params=params(),
    )(pair, near, returned, energy, own)


def force_terms(place, m, speed, term):
    mp = m * term
    turned = sum(a * b for a, b in zip(place, speed))
    return (
        [m] + [m * a for a in place] + [mp] + [mp * a for a in place]
        + [m * a for a in speed] + [m * turned]
    )


def forces_of(sums, place, speed, term):
    lean = [a * sums[0] - b for a, b in zip(place, sums[1:4])]
    acc = [term * a + (b * sums[4] - c) for a, b, c in zip(lean, place, sums[5:8])]
    mixed = sum(a * b - c * d for a, b, c, d in zip(speed, lean, place, sums[8:11]))
    return [G_SCALE * a for a in acc] + [-G_SCALE * term * (mixed + sums[11])]


def force_operand(ref, index):
    high, low = split2(block(ref, index, SUMS))
    return jnp.concatenate([high, low], 0)


def own_terms(own, term, rows):
    planes = planes_of(own, range(CELL), 0, CELLS, CELL)
    terms = force_terms(planes[0:3], planes[4], planes[5:8], term[...])
    put(rows, terms, 0, CELLS, SUMS)
    put(rows, [jnp.zeros((CELLS, WIDTH), F32)] * 4, 12, CELLS, SUMS)
    set_block(rows, CELLS, SUMS, jnp.zeros((SUMS, WIDTH), F32))


def slopes(s_ref, high, low, columns, row, count):
    for start in range(0, count, CHUNK):
        s = jnp.maximum(s_ref[start : start + CHUNK], TINY)
        dist = s * lax.rsqrt(s)
        wide = columns[start : start + CHUNK]
        support = jnp.concatenate([wide, wide], 1) + row
        d = jnp.maximum(support - dist, 0.0)
        e = pl.reciprocal(support * support, approx=True)
        x = e * d
        g = (x * x) * (x * e)
        top = g.astype(BF)
        high[start : start + CHUNK] = top
        low[start : start + CHUNK] = (g - top.astype(F32)).astype(BF)


def distances(left, rows, s_ref):
    s_ref[...] = jnp.dot(left, second_operands(rows, False), preferred_element_type=F32)


def slope_sums(rows, high, low, dims):
    top = lax.dot_general(rows, high, dims, preferred_element_type=F32)
    rest = lax.dot_general(rows[:SUMS], low, dims, preferred_element_type=F32)
    return top[:SUMS] + top[SUMS:] + rest


def to_seconds(rows, count, high, low):
    return slope_sums(rows[:, :count], high[0:count], low[0:count], NN)


def to_firsts(rows, count, high, low):
    return slope_sums(rows, high[0:count], low[0:count], NT)


def in_three_turns(trips, sizes, item, last, products, tiles, sums, slot_a, slot_b, lag):
    products(item(0), slot_a)
    base = 0
    for count, size in zip(trips, sizes):

        def step(i, _, size=size):
            after = 2 * i + 2
            if last is not None:
                after = jnp.minimum(after, last - 1)
            if lag == 1:
                sums(size, item(2 * i - 1), slot_b)
                tiles(size, item(2 * i), slot_a)
                products(item(2 * i + 1), slot_b)
                sums(size, item(2 * i), slot_a)
                tiles(size, item(2 * i + 1), slot_b)
                products(item(after), slot_a)
            else:
                products(item(2 * i + 1), slot_b)
                sums(size, item(2 * i - 2), slot_a)
                tiles(size, item(2 * i), slot_a)
                products(item(after), slot_a)
                sums(size, item(2 * i - 1), slot_b)
                tiles(size, item(2 * i + 1), slot_b)
            return 0

        lax.fori_loop(base, base + count, step, 0)
        base = base + count
    if lag == 2:
        sums(sizes[-1], item(2 * base - 2), slot_a)
    sums(sizes[-1], item(2 * base - 1), slot_b)


def clear(slots):
    for held in slots:
        held[SIZES[0] :, :] = jnp.zeros((WIDTH - SIZES[0], WIDTH), BF)


def add_forces(total, own, term, out, carried):
    planes = planes_of(own, range(CELL), 0, CELLS, CELL)
    sums = planes_of(total, range(12), 0, CELLS, SUMS)
    for k, force in enumerate(forces_of(sums, planes[0:3], planes[5:8], term[...])):
        out[k] = force if carried is None else carried[k] + force


def local_force_kernel(part, plan, own, first, second, term, *rest):
    if part:
        faces, face_terms, carried, out, rows, total, face_rows, face_first, *slots = rest
    else:
        carried = None
        out, rows, total, *slots = rest
    slot_a, slot_b = slots[:7], slots[7:]
    own_terms(own, term, rows)
    total[...] = jnp.zeros_like(total)
    clear([held[k] for held in (slot_a, slot_b) for k in (2, 3, 5, 6)])

    def products(c, held):
        left = first_operand(block(first, c, CELL))
        held[0][...] = support_columns(line(own, c, CELL, 3))
        distances(left, block(second, c, CELL), held[1])
        distances(left, block(second, jnp.minimum(c + 1, CELLS), CELL), held[4])

    def tiles(count, c, held):
        other = line(own, jnp.minimum(c + 1, CELLS), CELL, 3)
        slopes(*held[1:4], held[0], line(own, c, CELL, 3), count)
        slopes(*held[4:7], held[0], other, count)

    def sums(count, c, held):
        after = jnp.minimum(c + 1, CELLS)
        mine, other = force_operand(rows, c), force_operand(rows, after)
        added = to_firsts(other, count, *held[5:7])
        if count < WIDTH:
            added = jnp.concatenate([added, jnp.zeros((SUMS, WIDTH - count), F32)], 1)
        add_block(total, c, SUMS, to_seconds(mine, count, *held[2:4]) + added)
        add_block(total, after, SUMS, to_seconds(mine, count, *held[5:7]))

    trips, item = cell_list(plan, 2 + part)
    in_three_turns(trips, SIZES, item, None, products, tiles, sums, slot_a, slot_b, 1)

    if part:
        make_face_first(faces, face_first)
        planes = planes_of(faces, range(CELL), 0, 2 * FACE, CELL)
        terms = force_terms(planes[0:3], planes[4], planes[5:8], face_terms[...])
        blank = jnp.zeros((2 * FACE, WIDTH), F32)
        put(face_rows, terms + [blank] * 4, 0, 2 * FACE, SUMS)

        def face_products(i, held):
            for k in range(2):
                n = 2 * i + k
                left = first_operand(block(face_first, n, CELL))
                distances(left, block(second, face_cell(n), CELL), held[1 + 3 * k])

        def face_tiles(size, i, held):
            for k in range(2):
                n = 2 * i + k
                columns = support_columns(line(faces, n, CELL, 3))
                slopes(
                    *held[1 + 3 * k : 4 + 3 * k], columns, line(own, face_cell(n), CELL, 3), size
                )

        def face_sums(size, i, held):
            for k in range(2):
                n = jnp.maximum(2 * i, 0) + k
                c = jnp.where(i < 0, CELLS, face_cell(n))
                theirs = force_operand(face_rows, n)
                add_block(
                    total, c, SUMS, to_seconds(theirs, size, *held[2 + 3 * k : 4 + 3 * k])
                )

        in_three_turns(
            [FACE // 2], [WIDTH], lambda i: i, FACE, face_products, face_tiles, face_sums,
            slot_a, slot_b, 1,
        )

    add_forces(total, own, term, out, carried)


FORCE_PAIR = [
    pltpu.VMEM((WIDTH, WIDTH), F32),
    pltpu.VMEM((WIDTH, WIDTH), BF),
    pltpu.VMEM((WIDTH, WIDTH), BF),
]
FORCE_SLOT = [pltpu.VMEM((WIDTH, 128), F32)] + FORCE_PAIR * 2


def local_force(part, plan, own, first, second, term, *rest):
    scratch = [
        pltpu.VMEM((2, (CELLS + 1) * SUMS, 128), F32),
        pltpu.VMEM((2, (CELLS + 1) * SUMS, 128), F32),
    ]
    if part:
        scratch.append(pltpu.VMEM((2, 2 * FACE * SUMS, 128), F32))
        scratch.append(pltpu.VMEM((2, 2 * FACE * CELL, 128), F32))
    return pl.pallas_call(
        functools.partial(local_force_kernel, part),
        in_specs=[SM] + [VM] * (4 + len(rest)),
        out_specs=VM,
        out_shape=jax.ShapeDtypeStruct((4, CELLS, WIDTH), F32),
        scratch_shapes=scratch + FORCE_SLOT * 2,
        cost_estimate=pl.CostEstimate(
            flops=64 * 65536 * 80, bytes_accessed=2 * 2**20, transcendentals=0
        ),
        compiler_params=params(),
    )(plan, own, first, second, term, *rest)


def cross_force_kernel(
    fill, plan, own, first, term, listed, speeds, terms_of, carried, _, out, back,
    rows, total, theirs, their_rows, sums_of, *slots
):
    slot_a, slot_b = slots[:8], slots[8:]
    own_terms(own, term, rows)
    total[...] = jnp.zeros_like(total)
    clear([held[k] for held in (slot_a, slot_b) for k in (3, 4, 6, 7)])

    def make(e, part):
        planes = listed_planes(listed, e, part, range(ROWS), ROWS)
        at = e * SLOTS + 8 * part
        put(theirs, pair_terms(*planes)[1], at * CELL, 8, CELL)
        speed = listed_planes(speeds, e, part, range(SPEEDS), SPEEDS)
        pressed = terms_of[e, rows_at(part, 8), :]
        terms = force_terms(planes[0:3], planes[4], speed, pressed)
        blank = jnp.zeros((8, WIDTH), F32)
        put(their_rows, terms + [blank] * 4, at * SUMS, 8, SUMS)

    live_parts(fill, make, None)

    def products(pairs, held):
        for k, (slot, c) in enumerate(pairs):
            held[k][...] = support_columns(line(own, c, CELL, 3))
            left = first_operand(block(first, c, CELL))
            distances(left, block(theirs, slot, CELL), held[2 + 3 * k])

    def tiles(count, pairs, held):
        for k, (slot, c) in enumerate(pairs):
            support = listed_support(listed, slot)
            slopes(*held[2 + 3 * k : 5 + 3 * k], held[k], support, count)

    def sums(count, pairs, held):
        for k, (slot, c) in enumerate(pairs):
            tile = held[3 + 3 * k : 5 + 3 * k]
            set_block(sums_of, slot, SUMS, to_seconds(force_operand(rows, c), count, *tile))
            added = to_firsts(force_operand(their_rows, slot), count, *tile)
            if count < WIDTH:
                added = jnp.concatenate([added, jnp.zeros((SUMS, WIDTH - count), F32)], 1)
            add_block(total, c, SUMS, added)

    trips, item = pair_list(plan)
    in_three_turns(trips, SIZES, item, None, products, tiles, sums, slot_a, slot_b, 2)

    def send(e, part):
        planes = listed_planes(listed, e, part, range(3), ROWS)
        speed = listed_planes(speeds, e, part, range(SPEEDS), SPEEDS)
        pressed = terms_of[e, rows_at(part, 8), :]
        summed = planes_of(sums_of, range(12), (e * SLOTS + 8 * part) * SUMS, 8, SUMS)
        live = live_rows(fill, e, part)
        send_rows(e, part, [jnp.where(live, f, 0.0) for f in forces_of(summed, planes, speed, pressed)])

    def send_none(e, part):
        send_rows(e, part, [jnp.zeros((8, WIDTH), F32)] * MOVING)

    def send_rows(e, part, forces):
        for k, force in enumerate(forces):
            for h in range(2):
                start = (h * SLOTS + 8 * part) * MOVING + k
                back[e, pl.ds(start, 8, stride=MOVING), :] = half(force, h)

    live_parts(fill, send, send_none)
    add_forces(total, own, term, out, carried)


def cross_force(fill, plan, own, first, term, listed, speeds, terms, carried, after):
    return pl.pallas_call(
        cross_force_kernel,
        in_specs=[SM, SM] + [VM] * 7 + [ANYWHERE],
        out_specs=[VM, VM],
        out_shape=[
            jax.ShapeDtypeStruct((4, CELLS, WIDTH), F32),
            jax.ShapeDtypeStruct((PEERS, 2 * SLOTS * MOVING, 128), F32),
        ],
        scratch_shapes=[
            pltpu.VMEM((2, (CELLS + 1) * SUMS, 128), F32),
            pltpu.VMEM((2, (CELLS + 1) * SUMS, 128), F32),
            pltpu.VMEM((2, LISTED * CELL, 128), F32),
            pltpu.VMEM((2, LISTED * SUMS, 128), F32),
            pltpu.VMEM((2, LISTED * SUMS, 128), F32),
        ]
        + (FORCE_SLOT[:1] * 2 + FORCE_PAIR * 2) * 2,
        cost_estimate=pl.CostEstimate(
            flops=80 * 65536 * 80, bytes_accessed=2 * 2**20, transcendentals=0
        ),
        compiler_params=params(),
    )(fill, plan, own, first, term, listed, speeds, terms, carried, after)


def finish_kernel(pair, near, returned, active_in, own, out, total, active, gate, sem):
    copies = fetch([(active_in, active)], sem)
    total[...] = jnp.zeros_like(total)

    def peer_step(e, _):
        for s in range(SLOTS):
            at = s * MOVING
            total[pair[e, s]] += both(
                lambda h: returned[
                    e, h * SLOTS * MOVING + at : h * SLOTS * MOVING + at + MOVING
                ]
            )
        return 0

    lax.fori_loop(0, PEERS, peer_step, 0)
    copies[0].wait()
    full = planes_of(own, [4], 0, CELLS, CELL)[0] > 0.0
    gate[...] = jnp.where(full, active[...].astype(F32), 0.0)

    def cell_step(c, _):
        one = pl.ds(c, 1)
        open_to = gate[one, :]
        for k in range(4):
            out[k, one, :] = (near[k, one, :] + total[c, k : k + 1]) * open_to
        return 0

    lax.fori_loop(0, CELLS, cell_step, 0, unroll=8)


def finish(pair, near, returned, active, own):
    return pl.pallas_call(
        finish_kernel,
        in_specs=[SM, VM, VM, ANYWHERE, VM],
        out_specs=VM,
        out_shape=jax.ShapeDtypeStruct((4, CELLS, WIDTH), F32),
        scratch_shapes=[
            pltpu.VMEM((CELLS, 4, WIDTH), F32),
            pltpu.VMEM((CELLS, WIDTH), jnp.int32),
            pltpu.VMEM((CELLS, WIDTH), F32),
            pltpu.SemaphoreType.DMA((1,)),
        ],
        compiler_params=params(),
    )(pair, near, returned, active, own)


def to_peers(block):
    return lax.all_to_all(block, "dev", split_axis=0, concat_axis=0, tiled=True)


def with_neighbours(rows, size):
    count = lax.axis_size("region")
    up = [(i, (i + 1) % count) for i in range(count)]
    down = [(i, (i - 1) % count) for i in range(count)]
    return jnp.concatenate(
        [
            lax.ppermute(rows[..., (CELLS - FACE) * size : CELLS * size, :], "region", up),
            lax.ppermute(rows[..., : FACE * size, :], "region", down),
        ],
        -2,
    )


def local(
    positions, velocity, smoothing, masses, energy, occupancy, active, send_cells, send_fill,
    pair_cell,
):
    pair = pair_cell[0]
    own, listed = prepare(occupancy, pair, positions, velocity, smoothing, masses)
    arrived = to_peers(listed)
    faces = with_neighbours(own, CELL)
    rho, first, second, speeds, plan = local_density(
        0, occupancy, send_fill, send_cells[0], pair, own
    )
    arrived_speeds = to_peers(speeds)
    rho, back = cross_density(send_fill, plan, own, first, arrived, rho)
    returned = to_peers(back)
    rho = local_density(1, plan, own, first, second, faces, rho)
    density, term, leaving = pressure(pair, rho, returned, energy, own)
    arrived_terms = to_peers(leaving)
    face_terms = with_neighbours(term, 1)
    sums = local_force(0, plan, own, first, second, term)
    sums, force_back = cross_force(
        send_fill, plan, own, first, term, arrived, arrived_speeds, arrived_terms, sums,
        face_terms,
    )
    returned_force = to_peers(force_back)
    sums = local_force(1, plan, own, first, second, term, faces, face_terms, sums)
    forces = finish(pair, sums, returned_force, active, own)
    return (density, forces)


def solution(mesh):
    cells = P(("region", "dev"), None)
    vectors = P(None, ("region", "dev"), None)
    lists = P(("region", "dev"), None, None)
    in_specs = (
        vectors, vectors, cells, cells, cells, P(("region", "dev")), cells, lists, cells, lists,
    )
    return jax.shard_map(
        local, mesh=mesh, in_specs=in_specs, out_specs=(cells, vectors), check_vma=False
    )
```

```python
import functools
import math

import jax
import jax.numpy as jnp
from jax import lax
from jax.experimental import pallas as pl
from jax.experimental.pallas import tpu as pltpu
from jax.sharding import PartitionSpec as P

BF = jnp.bfloat16
F32 = jnp.float32
FACE = 4
CELLS = 64
WIDTH = 256
PEERS = 16
SLOTS = 16
LISTED = PEERS * SLOTS
GAMMA_LESS = 2.0 / 3.0
W_SCALE = 84.0 / math.pi
G_SCALE = 6720.0 / math.pi
TINY = 1e-14
EMPTY = 1e8
CHUNK = 32
CELL = 8
SUMS = 16
NN = (((1,), (0,)), ((), ()))
NT = (((1,), (1,)), ((), ()))
VM = pl.BlockSpec(memory_space=pltpu.VMEM)
SM = pl.BlockSpec(memory_space=pltpu.SMEM)
ROWS = 5
MOVING = 4
SPLITS = (44, 40)
SIZES = (160, 192, 224, 256)
KINDS = len(SIZES)
UNIT = 4
LOCAL_AT = 5 * KINDS
LOCAL_LEAD = 2
LOCAL_LIST = CELLS + 8
CROSS_AT = LOCAL_AT + 4 * LOCAL_LIST
CROSS_LEAD = 4
CROSS_LIST = LISTED + 16
PLAN = CROSS_AT + CROSS_LIST
PACK = 128
ANYWHERE = pl.BlockSpec(memory_space=pl.ANY)
OWN_ROWS = jax.ShapeDtypeStruct((2, (CELLS + 1) * CELL, 128), F32)


def params(mib=50):
    return pltpu.CompilerParams(vmem_limit_bytes=int(mib * 2**20))


def split2(x):
    a = x.astype(BF)
    return a, (x - a.astype(F32)).astype(BF)


def split3(x):
    a = x.astype(BF).astype(F32)
    rest = x - a
    b = rest.astype(BF).astype(F32)
    return a, b, rest - b


def pair_terms(x, y, z, h, m):
    norm = 4.0 * (x * x + y * y + z * z)
    root = lax.rsqrt(jnp.where(m > 0.0, m, 1.0))
    mu = jnp.where(m > 0.0, root * lax.rsqrt(root), EMPTY)
    one = jnp.ones_like(x)
    first = [-8.0 * x, -8.0 * y, -8.0 * z, norm, one, h * h * mu, 2.0 * h * mu, mu]
    second = [x, y, z, one, norm, mu, h * mu, h * h * mu]
    return first, second


def both(read):
    return jnp.concatenate([read(0), read(1)], -1)


def half(value, h):
    return value[..., 128 * h : 128 * (h + 1)]


def put(ref, planes, start, count, stride):
    for k, plane in enumerate(planes):
        for h in range(2):
            ref[h, pl.ds(start + k, count, stride=stride), :] = half(plane, h)


def planes_of(ref, ids, start, count, stride):
    return [both(lambda h: ref[h, pl.ds(start + k, count, stride=stride), :]) for k in ids]


def rows_at(index, size):
    return pl.ds(pl.multiple_of(index * size, size), size)


def block(ref, index, size):
    return both(lambda h: ref[h, rows_at(index, size), :])


def set_block(ref, index, size, value):
    for h in range(2):
        ref[h, rows_at(index, size), :] = half(value, h)


def add_block(ref, index, size, value):
    for h in range(2):
        ref[h, rows_at(index, size), :] += half(value, h)


def line(ref, index, size, k):
    return both(lambda h: ref[h, pl.ds(index * size + k, 1), :])


def listed_planes(listed, e, part, ids, size):
    step = SLOTS * size
    start = 8 * part * size
    return [
        both(lambda h: listed[e, pl.ds(h * step + start + k, 8, stride=size), :]) for k in ids
    ]


def listed_support(listed, slot):
    at = (slot & (SLOTS - 1)) * ROWS + 3
    return both(lambda h: listed[slot >> 4, pl.ds(h * SLOTS * ROWS + at, 1), :])


def first_operand(rows):
    a1, a2, a3 = split3(rows)
    return jnp.concatenate([a1, a1, a2, a2, a1, a3, jnp.zeros((80, WIDTH), F32)], 0).T.astype(BF)


def second_operands(rows, both):
    b1, b2, b3 = split3(rows)
    stacked = jnp.concatenate([b1, b2, b1, b2, b3, b1, jnp.zeros((80, WIDTH), F32)], 0)
    part = lax.broadcasted_iota(jnp.int32, stacked.shape, 0) % 8
    near = jnp.where(part < 5, stacked, 0.0).astype(BF)
    if not both:
        return near
    return near, jnp.where(part >= 5, stacked, 0.0).astype(BF)


def support_columns(row):
    return jnp.broadcast_to(row, (128, WIDTH)).T


def density_products(left, operands, s_ref, mix_ref):
    s_ref[...] = jnp.dot(left, operands[0], preferred_element_type=F32)
    mix_ref[...] = jnp.dot(left, operands[1], preferred_element_type=F32)


def weights_of(s, mix, columns, row):
    s = jnp.maximum(s, TINY)
    dist = s * lax.rsqrt(s)
    support = columns + row
    d = jnp.maximum(support - dist, 0.0)
    x = pl.reciprocal(mix, approx=True) * d
    x = x * x
    x = x * x
    return x * (support + 4.0 * dist)


def density_weights(count, s_ref, mix_ref, columns, row, one_sided):
    second = jnp.zeros((8, WIDTH), F32)
    firsts = []
    for start in range(0, count, CHUNK):
        part = slice(start, start + CHUNK)
        wide = columns[part]
        w = weights_of(s_ref[part], mix_ref[part], jnp.concatenate([wide, wide], 1), row)
        for k in range(CHUNK // 8):
            second = second + w[8 * k : 8 * k + 8]
        if not one_sided:
            firsts.append(w[:, :128] + w[:, 128:])
    if one_sided:
        return second
    if count < WIDTH:
        firsts.append(jnp.zeros((WIDTH - count, 128), F32))
    turned = jnp.concatenate(firsts, 0).T
    first = turned[:8]
    for k in range(1, 16):
        first = first + turned[8 * k : 8 * k + 8]
    return second, first


def inverse_mass(m):
    return jnp.where(m > 0.0, W_SCALE / jnp.where(m > 0.0, m, 1.0), 0.0)


def self_weights(count, s_ref, mix_ref, columns, row):
    sums = [jnp.zeros((8, 128), F32)] * 2
    crossing = []
    for start in range(0, count, CHUNK):
        part = slice(start, start + CHUNK)
        for h in range(0 if start < 128 else 1, 2):
            lanes = slice(128 * h, 128 * (h + 1))
            w = weights_of(s_ref[part, lanes], mix_ref[part, lanes], columns[part], half(row, h))
            for k in range(CHUNK // 8):
                sums[h] = sums[h] + w[8 * k : 8 * k + 8]
            if h and start < 128:
                crossing.append(w)
    turned = jnp.concatenate(crossing, 0).T
    for k in range(16):
        sums[0] = sums[0] + turned[8 * k : 8 * k + 8]
    return jnp.concatenate(sums, 1)


def fetch(pairs, sem):
    copies = [
        pltpu.make_async_copy(source, target, sem.at[k])
        for k, (source, target) in enumerate(pairs)
    ]
    for copy in copies:
        copy.start()
    return copies


def prepare_kernel(
    occ, pair, pos_in, vel_in, smooth_in, mass_in, own, out, pos, vel, smooth, mass, full, sem
):
    copies = fetch(
        [(pos_in, pos), (vel_in, vel), (smooth_in, smooth), (mass_in, mass)], sem
    )
    lane = lax.broadcasted_iota(jnp.int32, (1, WIDTH), 1)
    for c in range(CELLS):
        full[c : c + 1, :] = (lane < occ[c]).astype(F32)
    for copy in copies:
        copy.wait()
    place = [pos[k] - 0.5 for k in range(3)]
    m = jnp.where(full[...] > 0.0, mass[...], 0.0)
    put(own, place + [smooth[...], m] + [vel[k] for k in range(3)], 0, CELLS, CELL)
    blank = jnp.zeros((CELL, WIDTH), F32)
    wide = jnp.full((1, WIDTH), 0.5, F32)
    set_block(own, CELLS, CELL, jnp.concatenate([blank[:3], wide, blank[:4]], 0))

    def peer_step(e, _):
        for s in range(SLOTS):
            c = pair[e, s]
            for h in range(2):
                at = (h * SLOTS + s) * ROWS
                out[e, at : at + ROWS] = own[h, rows_at(c, CELL), :][:ROWS]
        return 0

    lax.fori_loop(0, PEERS, peer_step, 0)


def prepare(occ, pair, pos, vel, smooth, mass):
    plane = pltpu.VMEM((CELLS, WIDTH), F32)
    return pl.pallas_call(
        prepare_kernel,
        in_specs=[SM] * 2 + [ANYWHERE] * 4,
        out_specs=[VM] * 2,
        out_shape=[
            OWN_ROWS,
            jax.ShapeDtypeStruct((PEERS, 2 * SLOTS * ROWS, 128), F32),
        ],
        scratch_shapes=[
            pltpu.VMEM((3, CELLS, WIDTH), F32),
            pltpu.VMEM((3, CELLS, WIDTH), F32),
            plane,
            plane,
            plane,
            pltpu.SemaphoreType.DMA((4,)),
        ],
        compiler_params=params(60),
    )(occ, pair, pos, vel, smooth, mass)


def kind_of(size):
    return jnp.maximum(size - SIZES[0] + 31, 0) >> 5


def make_plan(occ, fill, cells, plan):
    def over_local(visit, group, carry):
        split = SPLITS[group // 2]
        low, high = (split, CELLS) if group % 2 else (0, split)
        step = lambda c, carry: visit(kind_of(occ[c]), c, carry)
        return lax.fori_loop(low, high, step, carry, unroll=4)

    def over_pairs(visit, carry):
        def peer_step(e, carry):
            def slot_step(s, carry):
                cell = cells[e, s]
                return visit(kind_of(occ[cell]), (e * SLOTS + s) * PACK + cell, carry)

            return lax.fori_loop(0, fill[0, e], slot_step, carry)

        return lax.fori_loop(0, PEERS, peer_step, carry)

    unused = jnp.int32(0)
    for e in range(PEERS):
        unused = jnp.where(fill[0, e] == 0, e * SLOTS, unused)

    def one_of(kind):
        return jnp.left_shift(jnp.int32(1), 8 * kind)

    groups = [
        (
            functools.partial(lambda g, v, x: over_local(v, g, x), g),
            LOCAL_AT + g * LOCAL_LIST, LOCAL_LEAD, 2, CELLS,
        )
        for g in range(4)
    ]
    groups.append((over_pairs, CROSS_AT, CROSS_LEAD, UNIT, unused * PACK + CELLS))
    for group, (walk, start, lead, unit, blank) in enumerate(groups):
        counts = walk(lambda kind, value, packed: packed + one_of(kind), jnp.int32(0))
        total = jnp.int32(0)
        done = jnp.int32(0)
        places = jnp.int32(0)
        for k in range(KINDS):
            places = places + jnp.left_shift(total, 8 * k)
            total = total + ((counts >> (8 * k)) & 255)
            upto = (total + (unit - 1 if k == KINDS - 1 else 0)) >> (unit.bit_length() - 1)
            plan[group * KINDS + k] = upto - done
            done = upto
        for k in range(lead):
            plan[start + k] = blank
        for k in range(unit + 1):
            plan[start + lead + total + k] = blank

        def place(kind, value, packed, start=start + lead):
            plan[start + ((packed >> (8 * kind)) & 255)] = value
            return packed + one_of(kind)

        walk(place, places)


def fold(total, own, out, carried):
    mine = sum(planes_of(total, range(CELL), 0, CELLS, CELL))
    mass = planes_of(own, [4], 0, CELLS, CELL)[0]
    mine = mine * inverse_mass(mass)
    out[...] = mine if carried is None else carried[...] + mine


def make_face_first(faces, face_first):
    planes = planes_of(faces, range(ROWS), 0, 2 * FACE, CELL)
    put(face_first, pair_terms(*planes)[0], 0, 2 * FACE, CELL)


def face_cell(n):
    return jnp.where(n < FACE, n, CELLS - 2 * FACE + n)


def in_turns(trips, sizes, item, last, products, weights, slot_a, slot_b):
    products(item(0), slot_a)
    base = 0
    for count, size in zip(trips, sizes):

        def step(i, _, size=size):
            products(item(2 * i + 1), slot_b)
            weights(size, item(2 * i), slot_a)
            after = 2 * i + 2
            products(item(after if last is None else jnp.minimum(after, last - 1)), slot_a)
            weights(size, item(2 * i + 1), slot_b)
            return 0

        lax.fori_loop(base, base + count, step, 0)
        base = base + count


def cell_list(plan, group):
    start = LOCAL_AT + group * LOCAL_LIST + LOCAL_LEAD
    return [plan[group * KINDS + k] for k in range(KINDS)], lambda n: plan[start + n]


def pair_list(plan):
    start = CROSS_AT + CROSS_LEAD

    def item(n):
        entries = [plan[start + 2 * n + k] for k in range(2)]
        return [(entry >> 7, entry & (PACK - 1)) for entry in entries]

    return [plan[4 * KINDS + k] for k in range(KINDS)], item


def live_parts(fill, visit, other):
    def step(n, _):
        e, part = n >> 1, n & 1
        live = fill[0, e] > 8 * part

        @pl.when(live)
        def _():
            visit(e, part)

        if other is not None:

            @pl.when(jnp.logical_not(live))
            def _():
                other(e, part)

        return 0

    lax.fori_loop(0, 2 * PEERS, step, 0)


def local_density_kernel(part, *refs):
    if part:
        plan, own, first, second, faces, carried, rho, total, face_first, *slots = refs
    else:
        carried = None
        occ, fill, cells, own, rho, first, second, plan, total, *slots = refs
        make_plan(occ, fill, cells, plan)
        planes = planes_of(own, range(ROWS), 0, CELLS, CELL)
        blank = [jnp.zeros((1, WIDTH), F32)] * 3 + [jnp.full((1, WIDTH), 0.5, F32)]
        for ref, some, none in zip(
            (first, second), pair_terms(*planes), pair_terms(*blank, blank[0])
        ):
            put(ref, some, 0, CELLS, CELL)
            set_block(ref, CELLS, CELL, jnp.concatenate(none, 0))
    slot_a, slot_b = slots[:6], slots[6:]
    total[...] = jnp.zeros_like(total)

    def products(c, held):
        left = first_operand(block(first, c, CELL))
        after = jnp.minimum(c + 1, CELLS)
        held[4][...] = support_columns(line(own, c, CELL, 3))
        density_products(left, second_operands(block(second, c, CELL), True), *held[0:2])
        density_products(left, second_operands(block(second, after, CELL), True), *held[2:4])

    def weights(count, c, held):
        after = jnp.minimum(c + 1, CELLS)
        row, other = line(own, c, CELL, 3), line(own, after, CELL, 3)
        own_sum = self_weights(count, *held[0:2], held[4], row)
        there, here = density_weights(count, *held[2:4], held[4], other, False)
        add_block(total, c, CELL, own_sum + here)
        add_block(total, after, CELL, there)

    trips, item = cell_list(plan, part)
    in_turns(trips, SIZES, item, None, products, weights, slot_a, slot_b)

    if part:
        make_face_first(faces, face_first)

        def face_products(i, held):
            for k in range(2):
                n = 2 * i + k
                left = first_operand(block(face_first, n, CELL))
                operands = second_operands(block(second, face_cell(n), CELL), True)
                held[4 + k][...] = support_columns(line(faces, n, CELL, 3))
                density_products(left, operands, *held[2 * k : 2 * k + 2])

        def face_weights(size, i, held):
            for k in range(2):
                c = face_cell(2 * i + k)
                added = density_weights(
                    size, *held[2 * k : 2 * k + 2], held[4 + k], line(own, c, CELL, 3), True
                )
                add_block(total, c, CELL, added)

        in_turns(
            [FACE // 2], [WIDTH], lambda i: i, FACE, face_products, face_weights, slot_a, slot_b
        )

    fold(total, own, rho, carried)


DENSITY_SLOT = [pltpu.VMEM((WIDTH, WIDTH), F32)] * 4 + [pltpu.VMEM((WIDTH, 128), F32)] * 2


def local_density(part, *operands):
    plane = jax.ShapeDtypeStruct((CELLS, WIDTH), F32)
    if part:
        in_specs, out_specs, out_shape = [SM] + [VM] * 5, VM, plane
    else:
        in_specs, out_specs = [SM] * 3 + [VM], [VM] * 3 + [SM]
        out_shape = [plane, OWN_ROWS, OWN_ROWS, jax.ShapeDtypeStruct((PLAN,), jnp.int32)]
    return pl.pallas_call(
        functools.partial(local_density_kernel, part),
        in_specs=in_specs,
        out_specs=out_specs,
        out_shape=out_shape,
        scratch_shapes=[pltpu.VMEM((2, (CELLS + 1) * CELL, 128), F32)]
        + [pltpu.VMEM((2, 2 * FACE * CELL, 128), F32)] * part
        + DENSITY_SLOT * 2,
        cost_estimate=pl.CostEstimate(
            flops=64 * 65536 * 60, bytes_accessed=2 * 2**20, transcendentals=0
        ),
        compiler_params=params(),
    )(*operands)


def live_rows(fill, e, part):
    row = lax.broadcasted_iota(jnp.int32, (8, WIDTH), 0)
    return row < fill[0, e] - 8 * part


def cross_density_kernel(
    fill, plan, own, first, listed, carried, rho, back, total, theirs, there_of, *slots
):
    slot_a, slot_b = slots[:6], slots[6:]
    total[...] = jnp.zeros_like(total)

    def make(e, part):
        after = pair_terms(*listed_planes(listed, e, part, range(ROWS), ROWS))[1]
        put(theirs, after, (e * SLOTS + 8 * part) * CELL, 8, CELL)

    live_parts(fill, make, None)

    def products(pairs, held):
        for k, (slot, c) in enumerate(pairs):
            left = first_operand(block(first, c, CELL))
            held[4 + k][...] = support_columns(line(own, c, CELL, 3))
            operands = second_operands(block(theirs, slot, CELL), True)
            density_products(left, operands, *held[2 * k : 2 * k + 2])

    def weights(count, pairs, held):
        for k, (slot, c) in enumerate(pairs):
            support = listed_support(listed, slot)
            there, here = density_weights(
                count, *held[2 * k : 2 * k + 2], held[4 + k], support, False
            )
            add_block(total, c, CELL, here)
            set_block(there_of, slot, CELL, there)

    trips, item = pair_list(plan)
    in_turns(trips, SIZES, item, None, products, weights, slot_a, slot_b)

    def send(e, part):
        start = (e * SLOTS + 8 * part) * CELL
        summed = sum(planes_of(there_of, range(CELL), start, 8, CELL))
        mass = listed_planes(listed, e, part, [4], ROWS)[0]
        value = jnp.where(live_rows(fill, e, part), summed * inverse_mass(mass), 0.0)
        back[e, rows_at(part, 8), :] = value

    def send_none(e, part):
        back[e, rows_at(part, 8), :] = jnp.zeros((8, WIDTH), F32)

    live_parts(fill, send, send_none)
    fold(total, own, rho, carried)


def cross_density(fill, plan, own, first, listed, carried):
    return pl.pallas_call(
        cross_density_kernel,
        in_specs=[SM, SM] + [VM] * 4,
        out_specs=[VM, VM],
        out_shape=[
            jax.ShapeDtypeStruct((CELLS, WIDTH), F32),
            jax.ShapeDtypeStruct((PEERS, SLOTS, WIDTH), F32),
        ],
        scratch_shapes=[
            pltpu.VMEM((2, (CELLS + 1) * CELL, 128), F32),
            pltpu.VMEM((2, LISTED * CELL, 128), F32),
            pltpu.VMEM((2, LISTED * CELL, 128), F32),
        ]
        + DENSITY_SLOT * 2,
        cost_estimate=pl.CostEstimate(
            flops=80 * 65536 * 60, bytes_accessed=2 * 2**20, transcendentals=0
        ),
        compiler_params=params(),
    )(fill, plan, own, first, listed, carried)


def pressure_kernel(
    pair, near, returned, energy_in, own, density, term, out, energy, moving, sem, *sums
):
    copies = fetch([(energy_in, energy)], sem)
    for ref in sums:
        ref[...] = jnp.zeros_like(ref)

    def peer_step(i, _):
        for s in range(SLOTS):
            for j in range(2):
                at = pl.ds(pair[2 * i + j, s], 1)
                row = returned[2 * i + j, s : s + 1]
                for h in range(2):
                    sums[2 * j + h][at, :] += half(row, h)
        return 0

    lax.fori_loop(0, PEERS // 2, peer_step, 0)
    copies[0].wait()
    sum_of = near[...] + both(lambda h: sums[h][...] + sums[2 + h][...])
    full = planes_of(own, [4], 0, CELLS, CELL)[0] > 0.0
    rho = jnp.where(full, sum_of, 0.0)
    density[...] = rho
    term[...] = jnp.where(full, GAMMA_LESS * energy[...] / jnp.where(full, rho, 1.0), 0.0)

    def cell_step(c, _):
        moving[c] = jnp.concatenate(
            [line(own, c, CELL, k) for k in (5, 6, 7)] + [term[pl.ds(c, 1), :]], 0
        )
        return 0

    lax.fori_loop(0, CELLS, cell_step, 0, unroll=8)

    def send_step(e, _):
        for s in range(SLOTS):
            cell = moving[pair[e, s]]
            for h in range(2):
                at = (h * SLOTS + s) * MOVING
                out[e, at : at + MOVING] = half(cell, h)
        return 0

    lax.fori_loop(0, PEERS, send_step, 0)


def pressure(pair, near, returned, energy, own):
    plane = jax.ShapeDtypeStruct((CELLS, WIDTH), F32)
    return pl.pallas_call(
        pressure_kernel,
        in_specs=[SM, VM, VM, ANYWHERE, VM],
        out_specs=[VM, VM, VM],
        out_shape=[
            plane,
            plane,
            jax.ShapeDtypeStruct((PEERS, 2 * SLOTS * MOVING, 128), F32),
        ],
        scratch_shapes=[
            pltpu.VMEM((CELLS, WIDTH), F32),
            pltpu.VMEM((CELLS, MOVING, WIDTH), F32),
            pltpu.SemaphoreType.DMA((1,)),
        ]
        + [pltpu.VMEM((CELLS, 128), F32)] * 4,
        compiler_params=params(),
    )(pair, near, returned, energy, own)


def force_terms(place, m, speed, term):
    mp = m * term
    turned = sum(a * b for a, b in zip(place, speed))
    return (
        [m] + [m * a for a in place] + [mp] + [mp * a for a in place]
        + [m * a for a in speed] + [m * turned]
    )


def forces_of(sums, place, speed, term):
    lean = [a * sums[0] - b for a, b in zip(place, sums[1:4])]
    acc = [term * a + (b * sums[4] - c) for a, b, c in zip(lean, place, sums[5:8])]
    mixed = sum(a * b - c * d for a, b, c, d in zip(speed, lean, place, sums[8:11]))
    return [G_SCALE * a for a in acc] + [-G_SCALE * term * (mixed + sums[11])]


def force_operand(ref, index):
    high, low = split2(block(ref, index, SUMS))
    return jnp.concatenate([high, low], 0)


def own_terms(own, term, rows):
    planes = planes_of(own, range(CELL), 0, CELLS, CELL)
    terms = force_terms(planes[0:3], planes[4], planes[5:8], term[...])
    put(rows, terms, 0, CELLS, SUMS)
    put(rows, [jnp.zeros((CELLS, WIDTH), F32)] * 4, 12, CELLS, SUMS)
    set_block(rows, CELLS, SUMS, jnp.zeros((SUMS, WIDTH), F32))


def slopes(s_ref, high, low, columns, row, count):
    for start in range(0, count, CHUNK):
        s = jnp.maximum(s_ref[start : start + CHUNK], TINY)
        dist = s * lax.rsqrt(s)
        wide = columns[start : start + CHUNK]
        support = jnp.concatenate([wide, wide], 1) + row
        d = jnp.maximum(support - dist, 0.0)
        e = pl.reciprocal(support * support, approx=True)
        x = e * d
        g = (x * x) * (x * e)
        top = g.astype(BF)
        high[start : start + CHUNK] = top
        low[start : start + CHUNK] = (g - top.astype(F32)).astype(BF)


def distances(left, rows, s_ref):
    s_ref[...] = jnp.dot(left, second_operands(rows, False), preferred_element_type=F32)


def slope_sums(rows, high, low, dims):
    top = lax.dot_general(rows, high, dims, preferred_element_type=F32)
    rest = lax.dot_general(rows[:SUMS], low, dims, preferred_element_type=F32)
    return top[:SUMS] + top[SUMS:] + rest


def to_seconds(rows, count, high, low):
    return slope_sums(rows[:, :count], high[0:count], low[0:count], NN)


def to_firsts(rows, count, high, low):
    return slope_sums(rows, high[0:count], low[0:count], NT)


def in_three_turns(trips, sizes, item, last, products, tiles, sums, slot_a, slot_b, lag):
    products(item(0), slot_a)
    base = 0
    for count, size in zip(trips, sizes):

        def step(i, _, size=size):
            after = 2 * i + 2
            if last is not None:
                after = jnp.minimum(after, last - 1)
            if lag == 1:
                sums(size, item(2 * i - 1), slot_b)
                tiles(size, item(2 * i), slot_a)
                products(item(2 * i + 1), slot_b)
                sums(size, item(2 * i), slot_a)
                tiles(size, item(2 * i + 1), slot_b)
                products(item(after), slot_a)
            else:
                products(item(2 * i + 1), slot_b)
                sums(size, item(2 * i - 2), slot_a)
                tiles(size, item(2 * i), slot_a)
                products(item(after), slot_a)
                sums(size, item(2 * i - 1), slot_b)
                tiles(size, item(2 * i + 1), slot_b)
            return 0

        lax.fori_loop(base, base + count, step, 0)
        base = base + count
    if lag == 2:
        sums(sizes[-1], item(2 * base - 2), slot_a)
    sums(sizes[-1], item(2 * base - 1), slot_b)


def clear(slots):
    for held in slots:
        held[SIZES[0] :, :] = jnp.zeros((WIDTH - SIZES[0], WIDTH), BF)


def add_forces(total, own, term, out, carried):
    planes = planes_of(own, range(CELL), 0, CELLS, CELL)
    sums = planes_of(total, range(12), 0, CELLS, SUMS)
    for k, force in enumerate(forces_of(sums, planes[0:3], planes[5:8], term[...])):
        out[k] = force if carried is None else carried[k] + force


def local_force_kernel(part, plan, own, first, second, term, *rest):
    if part:
        faces, face_terms, carried, out, rows, total, face_rows, face_first, *slots = rest
    else:
        carried = None
        out, rows, total, *slots = rest
    slot_a, slot_b = slots[:7], slots[7:]
    own_terms(own, term, rows)
    total[...] = jnp.zeros_like(total)
    clear([held[k] for held in (slot_a, slot_b) for k in (2, 3, 5, 6)])

    def products(c, held):
        left = first_operand(block(first, c, CELL))
        held[0][...] = support_columns(line(own, c, CELL, 3))
        distances(left, block(second, c, CELL), held[1])
        distances(left, block(second, jnp.minimum(c + 1, CELLS), CELL), held[4])

    def tiles(count, c, held):
        other = line(own, jnp.minimum(c + 1, CELLS), CELL, 3)
        slopes(*held[1:4], held[0], line(own, c, CELL, 3), count)
        slopes(*held[4:7], held[0], other, count)

    def sums(count, c, held):
        after = jnp.minimum(c + 1, CELLS)
        mine, other = force_operand(rows, c), force_operand(rows, after)
        added = to_firsts(other, count, *held[5:7])
        if count < WIDTH:
            added = jnp.concatenate([added, jnp.zeros((SUMS, WIDTH - count), F32)], 1)
        add_block(total, c, SUMS, to_seconds(mine, count, *held[2:4]) + added)
        add_block(total, after, SUMS, to_seconds(mine, count, *held[5:7]))

    trips, item = cell_list(plan, 2 + part)
    in_three_turns(trips, SIZES, item, None, products, tiles, sums, slot_a, slot_b, 1)

    if part:
        make_face_first(faces, face_first)
        planes = planes_of(faces, range(CELL), 0, 2 * FACE, CELL)
        terms = force_terms(planes[0:3], planes[4], planes[5:8], face_terms[...])
        blank = jnp.zeros((2 * FACE, WIDTH), F32)
        put(face_rows, terms + [blank] * 4, 0, 2 * FACE, SUMS)

        def face_products(i, held):
            for k in range(2):
                n = 2 * i + k
                left = first_operand(block(face_first, n, CELL))
                distances(left, block(second, face_cell(n), CELL), held[1 + 3 * k])

        def face_tiles(size, i, held):
            for k in range(2):
                n = 2 * i + k
                columns = support_columns(line(faces, n, CELL, 3))
                slopes(
                    *held[1 + 3 * k : 4 + 3 * k], columns, line(own, face_cell(n), CELL, 3), size
                )

        def face_sums(size, i, held):
            for k in range(2):
                n = jnp.maximum(2 * i, 0) + k
                c = jnp.where(i < 0, CELLS, face_cell(n))
                theirs = force_operand(face_rows, n)
                add_block(
                    total, c, SUMS, to_seconds(theirs, size, *held[2 + 3 * k : 4 + 3 * k])
                )

        in_three_turns(
            [FACE // 2], [WIDTH], lambda i: i, FACE, face_products, face_tiles, face_sums,
            slot_a, slot_b, 1,
        )

    add_forces(total, own, term, out, carried)


FORCE_PAIR = [
    pltpu.VMEM((WIDTH, WIDTH), F32),
    pltpu.VMEM((WIDTH, WIDTH), BF),
    pltpu.VMEM((WIDTH, WIDTH), BF),
]
FORCE_SLOT = [pltpu.VMEM((WIDTH, 128), F32)] + FORCE_PAIR * 2


def local_force(part, plan, own, first, second, term, *rest):
    scratch = [
        pltpu.VMEM((2, (CELLS + 1) * SUMS, 128), F32),
        pltpu.VMEM((2, (CELLS + 1) * SUMS, 128), F32),
    ]
    if part:
        scratch.append(pltpu.VMEM((2, 2 * FACE * SUMS, 128), F32))
        scratch.append(pltpu.VMEM((2, 2 * FACE * CELL, 128), F32))
    return pl.pallas_call(
        functools.partial(local_force_kernel, part),
        in_specs=[SM] + [VM] * (4 + len(rest)),
        out_specs=VM,
        out_shape=jax.ShapeDtypeStruct((4, CELLS, WIDTH), F32),
        scratch_shapes=scratch + FORCE_SLOT * 2,
        cost_estimate=pl.CostEstimate(
            flops=64 * 65536 * 80, bytes_accessed=2 * 2**20, transcendentals=0
        ),
        compiler_params=params(),
    )(plan, own, first, second, term, *rest)


def cross_force_kernel(
    fill, plan, own, first, term, listed, arrived, carried, _, out, back,
    rows, total, theirs, their_rows, sums_of, *slots
):
    slot_a, slot_b = slots[:8], slots[8:]
    own_terms(own, term, rows)
    total[...] = jnp.zeros_like(total)
    clear([held[k] for held in (slot_a, slot_b) for k in (3, 4, 6, 7)])

    def make(e, part):
        planes = listed_planes(listed, e, part, range(ROWS), ROWS)
        at = e * SLOTS + 8 * part
        put(theirs, pair_terms(*planes)[1], at * CELL, 8, CELL)
        *speed, pressed = listed_planes(arrived, e, part, range(MOVING), MOVING)
        terms = force_terms(planes[0:3], planes[4], speed, pressed)
        blank = jnp.zeros((8, WIDTH), F32)
        put(their_rows, terms + [blank] * 4, at * SUMS, 8, SUMS)

    live_parts(fill, make, None)

    def products(pairs, held):
        for k, (slot, c) in enumerate(pairs):
            held[k][...] = support_columns(line(own, c, CELL, 3))
            left = first_operand(block(first, c, CELL))
            distances(left, block(theirs, slot, CELL), held[2 + 3 * k])

    def tiles(count, pairs, held):
        for k, (slot, c) in enumerate(pairs):
            support = listed_support(listed, slot)
            slopes(*held[2 + 3 * k : 5 + 3 * k], held[k], support, count)

    def sums(count, pairs, held):
        for k, (slot, c) in enumerate(pairs):
            tile = held[3 + 3 * k : 5 + 3 * k]
            set_block(sums_of, slot, SUMS, to_seconds(force_operand(rows, c), count, *tile))
            added = to_firsts(force_operand(their_rows, slot), count, *tile)
            if count < WIDTH:
                added = jnp.concatenate([added, jnp.zeros((SUMS, WIDTH - count), F32)], 1)
            add_block(total, c, SUMS, added)

    trips, item = pair_list(plan)
    in_three_turns(trips, SIZES, item, None, products, tiles, sums, slot_a, slot_b, 2)

    def send(e, part):
        planes = listed_planes(listed, e, part, range(3), ROWS)
        *speed, pressed = listed_planes(arrived, e, part, range(MOVING), MOVING)
        summed = planes_of(sums_of, range(12), (e * SLOTS + 8 * part) * SUMS, 8, SUMS)
        live = live_rows(fill, e, part)
        send_rows(e, part, [jnp.where(live, f, 0.0) for f in forces_of(summed, planes, speed, pressed)])

    def send_none(e, part):
        send_rows(e, part, [jnp.zeros((8, WIDTH), F32)] * MOVING)

    def send_rows(e, part, forces):
        for k, force in enumerate(forces):
            for h in range(2):
                start = (h * SLOTS + 8 * part) * MOVING + k
                back[e, pl.ds(start, 8, stride=MOVING), :] = half(force, h)

    live_parts(fill, send, send_none)
    add_forces(total, own, term, out, carried)


def cross_force(fill, plan, own, first, term, listed, arrived, carried, after):
    return pl.pallas_call(
        cross_force_kernel,
        in_specs=[SM, SM] + [VM] * 6 + [ANYWHERE],
        out_specs=[VM, VM],
        out_shape=[
            jax.ShapeDtypeStruct((4, CELLS, WIDTH), F32),
            jax.ShapeDtypeStruct((PEERS, 2 * SLOTS * MOVING, 128), F32),
        ],
        scratch_shapes=[
            pltpu.VMEM((2, (CELLS + 1) * SUMS, 128), F32),
            pltpu.VMEM((2, (CELLS + 1) * SUMS, 128), F32),
            pltpu.VMEM((2, LISTED * CELL, 128), F32),
            pltpu.VMEM((2, LISTED * SUMS, 128), F32),
            pltpu.VMEM((2, LISTED * SUMS, 128), F32),
        ]
        + (FORCE_SLOT[:1] * 2 + FORCE_PAIR * 2) * 2,
        cost_estimate=pl.CostEstimate(
            flops=80 * 65536 * 80, bytes_accessed=2 * 2**20, transcendentals=0
        ),
        compiler_params=params(),
    )(fill, plan, own, first, term, listed, arrived, carried, after)


def finish_kernel(pair, near, returned, active_in, own, out, active, gate, sem, *sums):
    copies = fetch([(active_in, active)], sem)
    for ref in sums:
        ref[...] = jnp.zeros_like(ref)

    def peer_step(i, _):
        for s in range(SLOTS):
            for j in range(2):
                c = pair[2 * i + j, s]
                for h in range(2):
                    at = (h * SLOTS + s) * MOVING
                    sums[2 * j + h][c] += returned[2 * i + j, at : at + MOVING]
        return 0

    lax.fori_loop(0, PEERS // 2, peer_step, 0)
    copies[0].wait()
    full = planes_of(own, [4], 0, CELLS, CELL)[0] > 0.0
    gate[...] = jnp.where(full, active[...].astype(F32), 0.0)

    def cell_step(c, _):
        one = pl.ds(c, 1)
        open_to = gate[one, :]
        total = both(lambda h: sums[h][c] + sums[2 + h][c])
        for k in range(4):
            out[k, one, :] = (near[k, one, :] + total[k : k + 1]) * open_to
        return 0

    lax.fori_loop(0, CELLS, cell_step, 0, unroll=8)


def finish(pair, near, returned, active, own):
    return pl.pallas_call(
        finish_kernel,
        in_specs=[SM, VM, VM, ANYWHERE, VM],
        out_specs=VM,
        out_shape=jax.ShapeDtypeStruct((4, CELLS, WIDTH), F32),
        scratch_shapes=[
            pltpu.VMEM((CELLS, WIDTH), jnp.int32),
            pltpu.VMEM((CELLS, WIDTH), F32),
            pltpu.SemaphoreType.DMA((1,)),
        ]
        + [pltpu.VMEM((CELLS, MOVING, 128), F32)] * 4,
        compiler_params=params(),
    )(pair, near, returned, active, own)


def to_peers(block):
    return lax.all_to_all(block, "dev", split_axis=0, concat_axis=0, tiled=True)


def with_neighbours(rows, size):
    count = lax.axis_size("region")
    up = [(i, (i + 1) % count) for i in range(count)]
    down = [(i, (i - 1) % count) for i in range(count)]
    return jnp.concatenate(
        [
            lax.ppermute(rows[..., (CELLS - FACE) * size : CELLS * size, :], "region", up),
            lax.ppermute(rows[..., : FACE * size, :], "region", down),
        ],
        -2,
    )


def local(
    positions, velocity, smoothing, masses, energy, occupancy, active, send_cells, send_fill,
    pair_cell,
):
    pair = pair_cell[0]
    own, listed = prepare(occupancy, pair, positions, velocity, smoothing, masses)
    arrived = to_peers(listed)
    faces = with_neighbours(own, CELL)
    rho, first, second, plan = local_density(0, occupancy, send_fill, send_cells[0], own)
    rho, back = cross_density(send_fill, plan, own, first, arrived, rho)
    returned = to_peers(back)
    rho = local_density(1, plan, own, first, second, faces, rho)
    density, term, leaving = pressure(pair, rho, returned, energy, own)
    arrived_moving = to_peers(leaving)
    face_terms = with_neighbours(term, 1)
    sums = local_force(0, plan, own, first, second, term)
    sums, force_back = cross_force(
        send_fill, plan, own, first, term, arrived, arrived_moving, sums, face_terms
    )
    returned_force = to_peers(force_back)
    sums = local_force(1, plan, own, first, second, term, faces, face_terms, sums)
    forces = finish(pair, sums, returned_force, active, own)
    return (density, forces)


def solution(mesh):
    cells = P(("region", "dev"), None)
    vectors = P(None, ("region", "dev"), None)
    lists = P(("region", "dev"), None, None)
    in_specs = (
        vectors, vectors, cells, cells, cells, P(("region", "dev")), cells, lists, cells, lists,
    )
    return jax.shard_map(
        local, mesh=mesh, in_specs=in_specs, out_specs=(cells, vectors), check_vma=False
    )
```

```python
import functools
import math

import jax
import jax.numpy as jnp
from jax import lax
from jax.experimental import pallas as pl
from jax.experimental.pallas import tpu as pltpu
from jax.sharding import PartitionSpec as P

BF = jnp.bfloat16
F32 = jnp.float32
FACE = 4
CELLS = 64
WIDTH = 256
PEERS = 16
SLOTS = 16
LISTED = PEERS * SLOTS
GAMMA_LESS = 2.0 / 3.0
W_SCALE = 84.0 / math.pi
G_SCALE = 6720.0 / math.pi
TINY = 1e-14
EMPTY = 1e8
CHUNK = 32
CELL = 8
SUMS = 16
NN = (((1,), (0,)), ((), ()))
NT = (((1,), (1,)), ((), ()))
VM = pl.BlockSpec(memory_space=pltpu.VMEM)
SM = pl.BlockSpec(memory_space=pltpu.SMEM)
ROWS = 5
MOVING = 4
SPLITS = (44, 40)
SIZES = (160, 192, 224, 256)
KINDS = len(SIZES)
UNIT = 4
LOCAL_AT = 5 * KINDS
LOCAL_LEAD = 2
LOCAL_LIST = CELLS + 16
CROSS_AT = LOCAL_AT + 4 * LOCAL_LIST
CROSS_LEAD = 4
CROSS_LIST = LISTED + 16
PLAN = CROSS_AT + CROSS_LIST
PACK = 128
ANYWHERE = pl.BlockSpec(memory_space=pl.ANY)
OWN_ROWS = jax.ShapeDtypeStruct((2, (CELLS + 1) * CELL, 128), F32)


def params(mib=50):
    return pltpu.CompilerParams(vmem_limit_bytes=int(mib * 2**20))


def split2(x):
    a = x.astype(BF)
    return a, (x - a.astype(F32)).astype(BF)


def split3(x):
    a = x.astype(BF).astype(F32)
    rest = x - a
    b = rest.astype(BF).astype(F32)
    return a, b, rest - b


def pair_terms(x, y, z, h, m):
    norm = 4.0 * (x * x + y * y + z * z)
    root = lax.rsqrt(jnp.where(m > 0.0, m, 1.0))
    mu = jnp.where(m > 0.0, root * lax.rsqrt(root), EMPTY)
    one = jnp.ones_like(x)
    first = [-8.0 * x, -8.0 * y, -8.0 * z, norm, one, h * h * mu, 2.0 * h * mu, mu]
    second = [x, y, z, one, norm, mu, h * mu, h * h * mu]
    return first, second


def both(read):
    return jnp.concatenate([read(0), read(1)], -1)


def half(value, h):
    return value[..., 128 * h : 128 * (h + 1)]


def put(ref, planes, start, count, stride):
    for k, plane in enumerate(planes):
        for h in range(2):
            ref[h, pl.ds(start + k, count, stride=stride), :] = half(plane, h)


def planes_of(ref, ids, start, count, stride):
    return [both(lambda h: ref[h, pl.ds(start + k, count, stride=stride), :]) for k in ids]


def rows_at(index, size):
    return pl.ds(pl.multiple_of(index * size, size), size)


def block(ref, index, size):
    return both(lambda h: ref[h, rows_at(index, size), :])


def set_block(ref, index, size, value):
    for h in range(2):
        ref[h, rows_at(index, size), :] = half(value, h)


def add_block(ref, index, size, value):
    for h in range(2):
        ref[h, rows_at(index, size), :] += half(value, h)


def line(ref, index, size, k):
    return both(lambda h: ref[h, pl.ds(index * size + k, 1), :])


def listed_planes(listed, e, part, ids, size):
    step = SLOTS * size
    start = 8 * part * size
    return [
        both(lambda h: listed[e, pl.ds(h * step + start + k, 8, stride=size), :]) for k in ids
    ]


def listed_support(listed, slot):
    at = (slot & (SLOTS - 1)) * ROWS + 3
    return both(lambda h: listed[slot >> 4, pl.ds(h * SLOTS * ROWS + at, 1), :])


def first_operand(rows):
    a1, a2, a3 = split3(rows)
    return jnp.concatenate([a1, a1, a2, a2, a1, a3, jnp.zeros((80, WIDTH), F32)], 0).T.astype(BF)


def second_operands(rows, both):
    b1, b2, b3 = split3(rows)
    stacked = jnp.concatenate([b1, b2, b1, b2, b3, b1, jnp.zeros((80, WIDTH), F32)], 0)
    part = lax.broadcasted_iota(jnp.int32, stacked.shape, 0) % 8
    near = jnp.where(part < 5, stacked, 0.0).astype(BF)
    if not both:
        return near
    return near, jnp.where(part >= 5, stacked, 0.0).astype(BF)


def support_columns(row):
    return jnp.broadcast_to(row, (128, WIDTH)).T


def density_products(left, operands, s_ref, mix_ref):
    s_ref[...] = jnp.dot(left, operands[0], preferred_element_type=F32)
    mix_ref[...] = jnp.dot(left, operands[1], preferred_element_type=F32)


def weights_of(s, mix, columns, row):
    s = jnp.maximum(s, TINY)
    dist = s * lax.rsqrt(s)
    support = columns + row
    d = jnp.maximum(support - dist, 0.0)
    x = pl.reciprocal(mix, approx=True) * d
    x = x * x
    x = x * x
    return x * (support + 4.0 * dist)


def density_weights(count, s_ref, mix_ref, columns, row, one_sided):
    second = jnp.zeros((8, WIDTH), F32)
    firsts = []
    for start in range(0, count, CHUNK):
        part = slice(start, start + CHUNK)
        wide = columns[part]
        w = weights_of(s_ref[part], mix_ref[part], jnp.concatenate([wide, wide], 1), row)
        for k in range(CHUNK // 8):
            second = second + w[8 * k : 8 * k + 8]
        if not one_sided:
            firsts.append(w[:, :128] + w[:, 128:])
    if one_sided:
        return second
    if count < WIDTH:
        firsts.append(jnp.zeros((WIDTH - count, 128), F32))
    turned = jnp.concatenate(firsts, 0).T
    first = turned[:8]
    for k in range(1, 16):
        first = first + turned[8 * k : 8 * k + 8]
    return second, first


def inverse_mass(m):
    return jnp.where(m > 0.0, W_SCALE / jnp.where(m > 0.0, m, 1.0), 0.0)


def self_weights(count, s_ref, mix_ref, columns, row):
    sums = [jnp.zeros((8, 128), F32)] * 2
    crossing = []
    for start in range(0, count, CHUNK):
        part = slice(start, start + CHUNK)
        for h in range(0 if start < 128 else 1, 2):
            lanes = slice(128 * h, 128 * (h + 1))
            w = weights_of(s_ref[part, lanes], mix_ref[part, lanes], columns[part], half(row, h))
            for k in range(CHUNK // 8):
                sums[h] = sums[h] + w[8 * k : 8 * k + 8]
            if h and start < 128:
                crossing.append(w)
    turned = jnp.concatenate(crossing, 0).T
    for k in range(16):
        sums[0] = sums[0] + turned[8 * k : 8 * k + 8]
    return jnp.concatenate(sums, 1)


def fetch(pairs, sem):
    copies = [
        pltpu.make_async_copy(source, target, sem.at[k])
        for k, (source, target) in enumerate(pairs)
    ]
    for copy in copies:
        copy.start()
    return copies


def prepare_kernel(
    occ, pair, pos_in, vel_in, smooth_in, mass_in, own, out, pos, vel, smooth, mass, full, sem
):
    copies = fetch(
        [(pos_in, pos), (vel_in, vel), (smooth_in, smooth), (mass_in, mass)], sem
    )
    lane = lax.broadcasted_iota(jnp.int32, (1, WIDTH), 1)
    for c in range(CELLS):
        full[c : c + 1, :] = (lane < occ[c]).astype(F32)
    for copy in copies:
        copy.wait()
    place = [pos[k] - 0.5 for k in range(3)]
    m = jnp.where(full[...] > 0.0, mass[...], 0.0)
    put(own, place + [smooth[...], m] + [vel[k] for k in range(3)], 0, CELLS, CELL)
    blank = jnp.zeros((CELL, WIDTH), F32)
    wide = jnp.full((1, WIDTH), 0.5, F32)
    set_block(own, CELLS, CELL, jnp.concatenate([blank[:3], wide, blank[:4]], 0))

    def peer_step(e, _):
        for s in range(SLOTS):
            c = pair[e, s]
            for h in range(2):
                at = (h * SLOTS + s) * ROWS
                out[e, at : at + ROWS] = own[h, rows_at(c, CELL), :][:ROWS]
        return 0

    lax.fori_loop(0, PEERS, peer_step, 0)


def prepare(occ, pair, pos, vel, smooth, mass):
    plane = pltpu.VMEM((CELLS, WIDTH), F32)
    return pl.pallas_call(
        prepare_kernel,
        in_specs=[SM] * 2 + [ANYWHERE] * 4,
        out_specs=[VM] * 2,
        out_shape=[
            OWN_ROWS,
            jax.ShapeDtypeStruct((PEERS, 2 * SLOTS * ROWS, 128), F32),
        ],
        scratch_shapes=[
            pltpu.VMEM((3, CELLS, WIDTH), F32),
            pltpu.VMEM((3, CELLS, WIDTH), F32),
            plane,
            plane,
            plane,
            pltpu.SemaphoreType.DMA((4,)),
        ],
        compiler_params=params(60),
    )(occ, pair, pos, vel, smooth, mass)


def kind_of(size):
    return jnp.maximum(size - SIZES[0] + 31, 0) >> 5


def make_plan(occ, fill, cells, plan):
    def over_local(visit, group, carry):
        split = SPLITS[group // 2]
        low, high = (split, CELLS) if group % 2 else (0, split)
        step = lambda c, carry: visit(kind_of(occ[c]), c, carry)
        return lax.fori_loop(low, high, step, carry, unroll=4)

    def over_pairs(visit, carry):
        def peer_step(e, carry):
            def slot_step(s, carry):
                cell = cells[e, s]
                return visit(kind_of(occ[cell]), (e * SLOTS + s) * PACK + cell, carry)

            return lax.fori_loop(0, fill[0, e], slot_step, carry)

        return lax.fori_loop(0, PEERS, peer_step, carry)

    unused = jnp.int32(0)
    for e in range(PEERS):
        unused = jnp.where(fill[0, e] == 0, e * SLOTS, unused)

    def one_of(kind):
        return jnp.left_shift(jnp.int32(1), 8 * kind)

    groups = [
        (
            functools.partial(lambda g, v, x: over_local(v, g, x), g),
            LOCAL_AT + g * LOCAL_LIST, LOCAL_LEAD, 2, CELLS,
        )
        for g in range(4)
    ]
    groups.append((over_pairs, CROSS_AT, CROSS_LEAD, UNIT, unused * PACK + CELLS))
    for group, (walk, start, lead, unit, blank) in enumerate(groups):
        counts = walk(lambda kind, value, packed: packed + one_of(kind), jnp.int32(0))
        total = jnp.int32(0)
        done = jnp.int32(0)
        places = jnp.int32(0)
        for k in range(KINDS):
            places = places + jnp.left_shift(total, 8 * k)
            total = total + ((counts >> (8 * k)) & 255)
            upto = (total + (unit - 1 if k == KINDS - 1 else 0)) >> (unit.bit_length() - 1)
            plan[group * KINDS + k] = upto - done
            done = upto
        for k in range(lead):
            plan[start + k] = blank
        for k in range(unit + 5):
            plan[start + lead + total + k] = blank

        def place(kind, value, packed, start=start + lead):
            plan[start + ((packed >> (8 * kind)) & 255)] = value
            return packed + one_of(kind)

        walk(place, places)


def fold(total, own, out, carried):
    mine = sum(planes_of(total, range(CELL), 0, CELLS, CELL))
    mass = planes_of(own, [4], 0, CELLS, CELL)[0]
    mine = mine * inverse_mass(mass)
    out[...] = mine if carried is None else carried[...] + mine


def make_face_first(faces, face_first):
    planes = planes_of(faces, range(ROWS), 0, 2 * FACE, CELL)
    put(face_first, pair_terms(*planes)[0], 0, 2 * FACE, CELL)


def face_cell(n):
    return jnp.where(n < FACE, n, CELLS - 2 * FACE + n)


def in_turns(trips, sizes, item, products, weights, slot_a, slot_b):
    read, decode = item
    products(decode(read(0)), slot_a)
    base = 0
    held = tuple(read(n) for n in range(3))
    for count, size in zip(trips, sizes):

        def step(i, held, size=size):
            ahead = (read(2 * i + 3), read(2 * i + 4))
            now, then, after = [decode(entry) for entry in held]
            products(then, slot_b)
            weights(size, now, slot_a)
            products(after, slot_a)
            weights(size, then, slot_b)
            return held[2:] + ahead

        held = lax.fori_loop(base, base + count, step, held)
        base = base + count


def cell_list(plan, group):
    start = LOCAL_AT + group * LOCAL_LIST + LOCAL_LEAD
    trips = [plan[group * KINDS + k] for k in range(KINDS)]
    return trips, (lambda n: plan[start + n], lambda entry: entry)


def pair_list(plan):
    start = CROSS_AT + CROSS_LEAD

    def read(n):
        return tuple(plan[start + 2 * n + k] for k in range(2))

    def decode(entries):
        return [(entry >> 7, entry & (PACK - 1)) for entry in entries]

    return [plan[4 * KINDS + k] for k in range(KINDS)], (read, decode)


def face_list(n):
    return jnp.minimum(n, FACE - 1)


FACES = (face_list, lambda n: n)


def live_parts(fill, visit, other):
    def step(n, _):
        e, part = n >> 1, n & 1
        live = fill[0, e] > 8 * part

        @pl.when(live)
        def _():
            visit(e, part)

        if other is not None:

            @pl.when(jnp.logical_not(live))
            def _():
                other(e, part)

        return 0

    lax.fori_loop(0, 2 * PEERS, step, 0)


def local_density_kernel(part, *refs):
    if part:
        plan, own, first, second, faces, carried, rho, total, face_first, *slots = refs
    else:
        carried = None
        occ, fill, cells, own, rho, first, second, plan, total, *slots = refs
        make_plan(occ, fill, cells, plan)
        planes = planes_of(own, range(ROWS), 0, CELLS, CELL)
        blank = [jnp.zeros((1, WIDTH), F32)] * 3 + [jnp.full((1, WIDTH), 0.5, F32)]
        for ref, some, none in zip(
            (first, second), pair_terms(*planes), pair_terms(*blank, blank[0])
        ):
            put(ref, some, 0, CELLS, CELL)
            set_block(ref, CELLS, CELL, jnp.concatenate(none, 0))
    slot_a, slot_b = slots[:6], slots[6:]
    total[...] = jnp.zeros_like(total)

    def products(c, held):
        left = first_operand(block(first, c, CELL))
        after = jnp.minimum(c + 1, CELLS)
        held[4][...] = support_columns(line(own, c, CELL, 3))
        density_products(left, second_operands(block(second, c, CELL), True), *held[0:2])
        density_products(left, second_operands(block(second, after, CELL), True), *held[2:4])

    def weights(count, c, held):
        after = jnp.minimum(c + 1, CELLS)
        row, other = line(own, c, CELL, 3), line(own, after, CELL, 3)
        own_sum = self_weights(count, *held[0:2], held[4], row)
        there, here = density_weights(count, *held[2:4], held[4], other, False)
        add_block(total, c, CELL, own_sum + here)
        add_block(total, after, CELL, there)

    trips, item = cell_list(plan, part)
    in_turns(trips, SIZES, item, products, weights, slot_a, slot_b)

    if part:
        make_face_first(faces, face_first)

        def face_products(i, held):
            for k in range(2):
                n = 2 * i + k
                left = first_operand(block(face_first, n, CELL))
                operands = second_operands(block(second, face_cell(n), CELL), True)
                held[4 + k][...] = support_columns(line(faces, n, CELL, 3))
                density_products(left, operands, *held[2 * k : 2 * k + 2])

        def face_weights(size, i, held):
            for k in range(2):
                c = face_cell(2 * i + k)
                added = density_weights(
                    size, *held[2 * k : 2 * k + 2], held[4 + k], line(own, c, CELL, 3), True
                )
                add_block(total, c, CELL, added)

        in_turns(
            [FACE // 2], [WIDTH], FACES, face_products, face_weights, slot_a, slot_b
        )

    fold(total, own, rho, carried)


DENSITY_SLOT = [pltpu.VMEM((WIDTH, WIDTH), F32)] * 4 + [pltpu.VMEM((WIDTH, 128), F32)] * 2


def local_density(part, *operands):
    plane = jax.ShapeDtypeStruct((CELLS, WIDTH), F32)
    if part:
        in_specs, out_specs, out_shape = [SM] + [VM] * 5, VM, plane
    else:
        in_specs, out_specs = [SM] * 3 + [VM], [VM] * 3 + [SM]
        out_shape = [plane, OWN_ROWS, OWN_ROWS, jax.ShapeDtypeStruct((PLAN,), jnp.int32)]
    return pl.pallas_call(
        functools.partial(local_density_kernel, part),
        in_specs=in_specs,
        out_specs=out_specs,
        out_shape=out_shape,
        scratch_shapes=[pltpu.VMEM((2, (CELLS + 1) * CELL, 128), F32)]
        + [pltpu.VMEM((2, 2 * FACE * CELL, 128), F32)] * part
        + DENSITY_SLOT * 2,
        cost_estimate=pl.CostEstimate(
            flops=64 * 65536 * 60, bytes_accessed=2 * 2**20, transcendentals=0
        ),
        compiler_params=params(),
    )(*operands)


def live_rows(fill, e, part):
    row = lax.broadcasted_iota(jnp.int32, (8, WIDTH), 0)
    return row < fill[0, e] - 8 * part


def cross_density_kernel(
    fill, plan, own, first, listed, carried, rho, back, total, theirs, there_of, *slots
):
    slot_a, slot_b = slots[:6], slots[6:]
    total[...] = jnp.zeros_like(total)

    def make(e, part):
        after = pair_terms(*listed_planes(listed, e, part, range(ROWS), ROWS))[1]
        put(theirs, after, (e * SLOTS + 8 * part) * CELL, 8, CELL)

    live_parts(fill, make, None)

    def products(pairs, held):
        for k, (slot, c) in enumerate(pairs):
            left = first_operand(block(first, c, CELL))
            held[4 + k][...] = support_columns(line(own, c, CELL, 3))
            operands = second_operands(block(theirs, slot, CELL), True)
            density_products(left, operands, *held[2 * k : 2 * k + 2])

    def weights(count, pairs, held):
        for k, (slot, c) in enumerate(pairs):
            support = listed_support(listed, slot)
            there, here = density_weights(
                count, *held[2 * k : 2 * k + 2], held[4 + k], support, False
            )
            add_block(total, c, CELL, here)
            set_block(there_of, slot, CELL, there)

    trips, item = pair_list(plan)
    in_turns(trips, SIZES, item, products, weights, slot_a, slot_b)

    def send(e, part):
        start = (e * SLOTS + 8 * part) * CELL
        summed = sum(planes_of(there_of, range(CELL), start, 8, CELL))
        mass = listed_planes(listed, e, part, [4], ROWS)[0]
        value = jnp.where(live_rows(fill, e, part), summed * inverse_mass(mass), 0.0)
        back[e, rows_at(part, 8), :] = value

    def send_none(e, part):
        back[e, rows_at(part, 8), :] = jnp.zeros((8, WIDTH), F32)

    live_parts(fill, send, send_none)
    fold(total, own, rho, carried)


def cross_density(fill, plan, own, first, listed, carried):
    return pl.pallas_call(
        cross_density_kernel,
        in_specs=[SM, SM] + [VM] * 4,
        out_specs=[VM, VM],
        out_shape=[
            jax.ShapeDtypeStruct((CELLS, WIDTH), F32),
            jax.ShapeDtypeStruct((PEERS, SLOTS, WIDTH), F32),
        ],
        scratch_shapes=[
            pltpu.VMEM((2, (CELLS + 1) * CELL, 128), F32),
            pltpu.VMEM((2, LISTED * CELL, 128), F32),
            pltpu.VMEM((2, LISTED * CELL, 128), F32),
        ]
        + DENSITY_SLOT * 2,
        cost_estimate=pl.CostEstimate(
            flops=80 * 65536 * 60, bytes_accessed=2 * 2**20, transcendentals=0
        ),
        compiler_params=params(),
    )(fill, plan, own, first, listed, carried)


def pressure_kernel(
    pair, near, returned, energy_in, own, density, term, out, energy, moving, sem, *sums
):
    copies = fetch([(energy_in, energy)], sem)
    for ref in sums:
        ref[...] = jnp.zeros_like(ref)

    def peer_step(i, _):
        for s in range(SLOTS):
            for j in range(2):
                at = pl.ds(pair[2 * i + j, s], 1)
                row = returned[2 * i + j, s : s + 1]
                for h in range(2):
                    sums[2 * j + h][at, :] += half(row, h)
        return 0

    lax.fori_loop(0, PEERS // 2, peer_step, 0)
    copies[0].wait()
    sum_of = near[...] + both(lambda h: sums[h][...] + sums[2 + h][...])
    full = planes_of(own, [4], 0, CELLS, CELL)[0] > 0.0
    rho = jnp.where(full, sum_of, 0.0)
    density[...] = rho
    term[...] = jnp.where(full, GAMMA_LESS * energy[...] / jnp.where(full, rho, 1.0), 0.0)

    put(moving, planes_of(own, (5, 6, 7), 0, CELLS, CELL) + [term[...]], 0, CELLS, CELL)

    def send_step(e, _):
        for s in range(SLOTS):
            cell = pl.ds(pl.multiple_of(pair[e, s] * CELL, CELL), MOVING)
            for h in range(2):
                at = (h * SLOTS + s) * MOVING
                out[e, at : at + MOVING] = moving[h, cell, :]
        return 0

    lax.fori_loop(0, PEERS, send_step, 0)


def pressure(pair, near, returned, energy, own):
    plane = jax.ShapeDtypeStruct((CELLS, WIDTH), F32)
    return pl.pallas_call(
        pressure_kernel,
        in_specs=[SM, VM, VM, ANYWHERE, VM],
        out_specs=[VM, VM, VM],
        out_shape=[
            plane,
            plane,
            jax.ShapeDtypeStruct((PEERS, 2 * SLOTS * MOVING, 128), F32),
        ],
        scratch_shapes=[
            pltpu.VMEM((CELLS, WIDTH), F32),
            pltpu.VMEM((2, CELLS * CELL, 128), F32),
            pltpu.SemaphoreType.DMA((1,)),
        ]
        + [pltpu.VMEM((CELLS, 128), F32)] * 4,
        compiler_params=params(),
    )(pair, near, returned, energy, own)


def force_terms(place, m, speed, term):
    mp = m * term
    turned = sum(a * b for a, b in zip(place, speed))
    return (
        [m] + [m * a for a in place] + [mp] + [mp * a for a in place]
        + [m * a for a in speed] + [m * turned]
    )


def forces_of(sums, place, speed, term):
    lean = [a * sums[0] - b for a, b in zip(place, sums[1:4])]
    acc = [term * a + (b * sums[4] - c) for a, b, c in zip(lean, place, sums[5:8])]
    mixed = sum(a * b - c * d for a, b, c, d in zip(speed, lean, place, sums[8:11]))
    return [G_SCALE * a for a in acc] + [-G_SCALE * term * (mixed + sums[11])]


def force_operand(ref, index):
    high, low = split2(block(ref, index, SUMS))
    return jnp.concatenate([high, low], 0)


def own_terms(own, term, rows):
    planes = planes_of(own, range(CELL), 0, CELLS, CELL)
    terms = force_terms(planes[0:3], planes[4], planes[5:8], term[...])
    put(rows, terms, 0, CELLS, SUMS)
    put(rows, [jnp.zeros((CELLS, WIDTH), F32)] * 4, 12, CELLS, SUMS)
    set_block(rows, CELLS, SUMS, jnp.zeros((SUMS, WIDTH), F32))


def slopes(s_ref, high, low, columns, row, count):
    for start in range(0, count, CHUNK):
        s = jnp.maximum(s_ref[start : start + CHUNK], TINY)
        dist = s * lax.rsqrt(s)
        wide = columns[start : start + CHUNK]
        support = jnp.concatenate([wide, wide], 1) + row
        d = jnp.maximum(support - dist, 0.0)
        e = pl.reciprocal(support * support, approx=True)
        x = e * d
        g = (x * x) * (x * e)
        top = g.astype(BF)
        high[start : start + CHUNK] = top
        low[start : start + CHUNK] = (g - top.astype(F32)).astype(BF)


def distances(left, rows, s_ref):
    s_ref[...] = jnp.dot(left, second_operands(rows, False), preferred_element_type=F32)


def slope_sums(rows, high, low, dims):
    top = lax.dot_general(rows, high, dims, preferred_element_type=F32)
    rest = lax.dot_general(rows[:SUMS], low, dims, preferred_element_type=F32)
    return top[:SUMS] + top[SUMS:] + rest


def to_seconds(rows, count, high, low):
    return slope_sums(rows[:, :count], high[0:count], low[0:count], NN)


def to_firsts(rows, count, high, low):
    return slope_sums(rows, high[0:count], low[0:count], NT)


def in_three_turns(trips, sizes, item, products, tiles, sums, slot_a, slot_b, lag):
    read, decode = item
    products(decode(read(0)), slot_a)
    base = 0
    held = tuple(read(n) for n in range(-2, 3))
    for count, size in zip(trips, sizes):

        def step(i, held, size=size):
            ahead = (read(2 * i + 3), read(2 * i + 4))
            before, last, now, then, after = [decode(entry) for entry in held]
            if lag == 1:
                sums(size, last, slot_b)
                tiles(size, now, slot_a)
                products(then, slot_b)
                sums(size, now, slot_a)
                tiles(size, then, slot_b)
                products(after, slot_a)
            else:
                products(then, slot_b)
                sums(size, before, slot_a)
                tiles(size, now, slot_a)
                products(after, slot_a)
                sums(size, last, slot_b)
                tiles(size, then, slot_b)
            return held[2:] + ahead

        held = lax.fori_loop(base, base + count, step, held)
        base = base + count
    if lag == 2:
        sums(sizes[-1], decode(held[0]), slot_a)
    sums(sizes[-1], decode(held[1]), slot_b)


def clear(slots):
    for held in slots:
        held[SIZES[0] :, :] = jnp.zeros((WIDTH - SIZES[0], WIDTH), BF)


def add_forces(total, own, term, out, carried):
    planes = planes_of(own, range(CELL), 0, CELLS, CELL)
    sums = planes_of(total, range(12), 0, CELLS, SUMS)
    for k, force in enumerate(forces_of(sums, planes[0:3], planes[5:8], term[...])):
        out[k] = force if carried is None else carried[k] + force


def local_force_kernel(part, plan, own, first, second, term, *rest):
    if part:
        faces, face_terms, carried, out, rows, total, face_rows, face_first, *slots = rest
    else:
        carried = None
        out, rows, total, *slots = rest
    slot_a, slot_b = slots[:7], slots[7:]
    own_terms(own, term, rows)
    total[...] = jnp.zeros_like(total)
    clear([held[k] for held in (slot_a, slot_b) for k in (2, 3, 5, 6)])

    def products(c, held):
        left = first_operand(block(first, c, CELL))
        held[0][...] = support_columns(line(own, c, CELL, 3))
        distances(left, block(second, c, CELL), held[1])
        distances(left, block(second, jnp.minimum(c + 1, CELLS), CELL), held[4])

    def tiles(count, c, held):
        other = line(own, jnp.minimum(c + 1, CELLS), CELL, 3)
        slopes(*held[1:4], held[0], line(own, c, CELL, 3), count)
        slopes(*held[4:7], held[0], other, count)

    def sums(count, c, held):
        after = jnp.minimum(c + 1, CELLS)
        mine, other = force_operand(rows, c), force_operand(rows, after)
        added = to_firsts(other, count, *held[5:7])
        if count < WIDTH:
            added = jnp.concatenate([added, jnp.zeros((SUMS, WIDTH - count), F32)], 1)
        add_block(total, c, SUMS, to_seconds(mine, count, *held[2:4]) + added)
        add_block(total, after, SUMS, to_seconds(mine, count, *held[5:7]))

    trips, item = cell_list(plan, 2 + part)
    in_three_turns(trips, SIZES, item, products, tiles, sums, slot_a, slot_b, 1)

    if part:
        make_face_first(faces, face_first)
        planes = planes_of(faces, range(CELL), 0, 2 * FACE, CELL)
        terms = force_terms(planes[0:3], planes[4], planes[5:8], face_terms[...])
        blank = jnp.zeros((2 * FACE, WIDTH), F32)
        put(face_rows, terms + [blank] * 4, 0, 2 * FACE, SUMS)

        def face_products(i, held):
            for k in range(2):
                n = 2 * i + k
                left = first_operand(block(face_first, n, CELL))
                distances(left, block(second, face_cell(n), CELL), held[1 + 3 * k])

        def face_tiles(size, i, held):
            for k in range(2):
                n = 2 * i + k
                columns = support_columns(line(faces, n, CELL, 3))
                slopes(
                    *held[1 + 3 * k : 4 + 3 * k], columns, line(own, face_cell(n), CELL, 3), size
                )

        def face_sums(size, i, held):
            for k in range(2):
                n = jnp.maximum(2 * i, 0) + k
                c = jnp.where(i < 0, CELLS, face_cell(n))
                theirs = force_operand(face_rows, n)
                add_block(
                    total, c, SUMS, to_seconds(theirs, size, *held[2 + 3 * k : 4 + 3 * k])
                )

        in_three_turns(
            [FACE // 2], [WIDTH], FACES, face_products, face_tiles, face_sums,
            slot_a, slot_b, 1,
        )

    add_forces(total, own, term, out, carried)


FORCE_PAIR = [
    pltpu.VMEM((WIDTH, WIDTH), F32),
    pltpu.VMEM((WIDTH, WIDTH), BF),
    pltpu.VMEM((WIDTH, WIDTH), BF),
]
FORCE_SLOT = [pltpu.VMEM((WIDTH, 128), F32)] + FORCE_PAIR * 2


def local_force(part, plan, own, first, second, term, *rest):
    scratch = [
        pltpu.VMEM((2, (CELLS + 1) * SUMS, 128), F32),
        pltpu.VMEM((2, (CELLS + 1) * SUMS, 128), F32),
    ]
    if part:
        scratch.append(pltpu.VMEM((2, 2 * FACE * SUMS, 128), F32))
        scratch.append(pltpu.VMEM((2, 2 * FACE * CELL, 128), F32))
    return pl.pallas_call(
        functools.partial(local_force_kernel, part),
        in_specs=[SM] + [VM] * (4 + len(rest)),
        out_specs=VM,
        out_shape=jax.ShapeDtypeStruct((4, CELLS, WIDTH), F32),
        scratch_shapes=scratch + FORCE_SLOT * 2,
        cost_estimate=pl.CostEstimate(
            flops=64 * 65536 * 80, bytes_accessed=2 * 2**20, transcendentals=0
        ),
        compiler_params=params(),
    )(plan, own, first, second, term, *rest)


def cross_force_kernel(
    fill, plan, own, first, term, listed, arrived, carried, _, out, back,
    rows, total, theirs, their_rows, sums_of, *slots
):
    slot_a, slot_b = slots[:8], slots[8:]
    own_terms(own, term, rows)
    total[...] = jnp.zeros_like(total)
    clear([held[k] for held in (slot_a, slot_b) for k in (3, 4, 6, 7)])

    def make(e, part):
        planes = listed_planes(listed, e, part, range(ROWS), ROWS)
        at = e * SLOTS + 8 * part
        put(theirs, pair_terms(*planes)[1], at * CELL, 8, CELL)
        *speed, pressed = listed_planes(arrived, e, part, range(MOVING), MOVING)
        terms = force_terms(planes[0:3], planes[4], speed, pressed)
        blank = jnp.zeros((8, WIDTH), F32)
        put(their_rows, terms + [blank] * 4, at * SUMS, 8, SUMS)

    live_parts(fill, make, None)

    def products(pairs, held):
        for k, (slot, c) in enumerate(pairs):
            held[k][...] = support_columns(line(own, c, CELL, 3))
            left = first_operand(block(first, c, CELL))
            distances(left, block(theirs, slot, CELL), held[2 + 3 * k])

    def tiles(count, pairs, held):
        for k, (slot, c) in enumerate(pairs):
            support = listed_support(listed, slot)
            slopes(*held[2 + 3 * k : 5 + 3 * k], held[k], support, count)

    def sums(count, pairs, held):
        for k, (slot, c) in enumerate(pairs):
            tile = held[3 + 3 * k : 5 + 3 * k]
            set_block(sums_of, slot, SUMS, to_seconds(force_operand(rows, c), count, *tile))
            added = to_firsts(force_operand(their_rows, slot), count, *tile)
            if count < WIDTH:
                added = jnp.concatenate([added, jnp.zeros((SUMS, WIDTH - count), F32)], 1)
            add_block(total, c, SUMS, added)

    trips, item = pair_list(plan)
    in_three_turns(trips, SIZES, item, products, tiles, sums, slot_a, slot_b, 2)

    def send(e, part):
        planes = listed_planes(listed, e, part, range(3), ROWS)
        *speed, pressed = listed_planes(arrived, e, part, range(MOVING), MOVING)
        summed = planes_of(sums_of, range(12), (e * SLOTS + 8 * part) * SUMS, 8, SUMS)
        live = live_rows(fill, e, part)
        send_rows(e, part, [jnp.where(live, f, 0.0) for f in forces_of(summed, planes, speed, pressed)])

    def send_none(e, part):
        send_rows(e, part, [jnp.zeros((8, WIDTH), F32)] * MOVING)

    def send_rows(e, part, forces):
        for k, force in enumerate(forces):
            for h in range(2):
                start = (h * SLOTS + 8 * part) * MOVING + k
                back[e, pl.ds(start, 8, stride=MOVING), :] = half(force, h)

    live_parts(fill, send, send_none)
    add_forces(total, own, term, out, carried)


def cross_force(fill, plan, own, first, term, listed, arrived, carried, after):
    return pl.pallas_call(
        cross_force_kernel,
        in_specs=[SM, SM] + [VM] * 6 + [ANYWHERE],
        out_specs=[VM, VM],
        out_shape=[
            jax.ShapeDtypeStruct((4, CELLS, WIDTH), F32),
            jax.ShapeDtypeStruct((PEERS, 2 * SLOTS * MOVING, 128), F32),
        ],
        scratch_shapes=[
            pltpu.VMEM((2, (CELLS + 1) * SUMS, 128), F32),
            pltpu.VMEM((2, (CELLS + 1) * SUMS, 128), F32),
            pltpu.VMEM((2, LISTED * CELL, 128), F32),
            pltpu.VMEM((2, LISTED * SUMS, 128), F32),
            pltpu.VMEM((2, LISTED * SUMS, 128), F32),
        ]
        + (FORCE_SLOT[:1] * 2 + FORCE_PAIR * 2) * 2,
        cost_estimate=pl.CostEstimate(
            flops=80 * 65536 * 80, bytes_accessed=2 * 2**20, transcendentals=0
        ),
        compiler_params=params(),
    )(fill, plan, own, first, term, listed, arrived, carried, after)


def finish_kernel(pair, near, returned, active_in, own, out, active, sem, *sums):
    copies = fetch([(active_in, active)], sem)
    for ref in sums:
        ref[...] = jnp.zeros_like(ref)

    def peer_step(i, _):
        for s in range(SLOTS):
            for j in range(2):
                cell = pl.ds(pl.multiple_of(pair[2 * i + j, s] * CELL, CELL), MOVING)
                for h in range(2):
                    at = (h * SLOTS + s) * MOVING
                    sums[2 * j + h][cell, :] += returned[2 * i + j, at : at + MOVING]
        return 0

    lax.fori_loop(0, PEERS // 2, peer_step, 0)
    copies[0].wait()
    full = planes_of(own, [4], 0, CELLS, CELL)[0] > 0.0
    gate = jnp.where(full, active[...].astype(F32), 0.0)
    for k in range(4):
        at = pl.ds(k, CELLS, stride=CELL)
        total = both(lambda h: sums[h][at, :] + sums[2 + h][at, :])
        out[k] = (near[k] + total) * gate


def finish(pair, near, returned, active, own):
    return pl.pallas_call(
        finish_kernel,
        in_specs=[SM, VM, VM, ANYWHERE, VM],
        out_specs=VM,
        out_shape=jax.ShapeDtypeStruct((4, CELLS, WIDTH), F32),
        scratch_shapes=[
            pltpu.VMEM((CELLS, WIDTH), jnp.int32),
            pltpu.SemaphoreType.DMA((1,)),
        ]
        + [pltpu.VMEM((CELLS * CELL, 128), F32)] * 4,
        compiler_params=params(),
    )(pair, near, returned, active, own)


def to_peers(block):
    return lax.all_to_all(block, "dev", split_axis=0, concat_axis=0, tiled=True)


def with_neighbours(rows, size):
    count = lax.axis_size("region")
    up = [(i, (i + 1) % count) for i in range(count)]
    down = [(i, (i - 1) % count) for i in range(count)]
    return jnp.concatenate(
        [
            lax.ppermute(rows[..., (CELLS - FACE) * size : CELLS * size, :], "region", up),
            lax.ppermute(rows[..., : FACE * size, :], "region", down),
        ],
        -2,
    )


def local(
    positions, velocity, smoothing, masses, energy, occupancy, active, send_cells, send_fill,
    pair_cell,
):
    pair = pair_cell[0]
    own, listed = prepare(occupancy, pair, positions, velocity, smoothing, masses)
    arrived = to_peers(listed)
    faces = with_neighbours(own, CELL)
    rho, first, second, plan = local_density(0, occupancy, send_fill, send_cells[0], own)
    rho, back = cross_density(send_fill, plan, own, first, arrived, rho)
    returned = to_peers(back)
    rho = local_density(1, plan, own, first, second, faces, rho)
    density, term, leaving = pressure(pair, rho, returned, energy, own)
    arrived_moving = to_peers(leaving)
    face_terms = with_neighbours(term, 1)
    sums = local_force(0, plan, own, first, second, term)
    sums, force_back = cross_force(
        send_fill, plan, own, first, term, arrived, arrived_moving, sums, face_terms
    )
    returned_force = to_peers(force_back)
    sums = local_force(1, plan, own, first, second, term, faces, face_terms, sums)
    forces = finish(pair, sums, returned_force, active, own)
    return (density, forces)


def solution(mesh):
    cells = P(("region", "dev"), None)
    vectors = P(None, ("region", "dev"), None)
    lists = P(("region", "dev"), None, None)
    in_specs = (
        vectors, vectors, cells, cells, cells, P(("region", "dev")), cells, lists, cells, lists,
    )
    return jax.shard_map(
        local, mesh=mesh, in_specs=in_specs, out_specs=(cells, vectors), check_vma=False
    )
```

```python
import functools
import math

import jax
import jax.numpy as jnp
from jax import lax
from jax.experimental import pallas as pl
from jax.experimental.pallas import tpu as pltpu
from jax.sharding import PartitionSpec as P

BF = jnp.bfloat16
F32 = jnp.float32
FACE = 4
CELLS = 64
WIDTH = 256
PEERS = 16
SLOTS = 16
LISTED = PEERS * SLOTS
GAMMA_LESS = 2.0 / 3.0
W_SCALE = 84.0 / math.pi
G_SCALE = 6720.0 / math.pi
TINY = 1e-14
EMPTY = 1e8
CHUNK = 32
CELL = 8
SUMS = 16
NN = (((1,), (0,)), ((), ()))
NT = (((1,), (1,)), ((), ()))
VM = pl.BlockSpec(memory_space=pltpu.VMEM)
SM = pl.BlockSpec(memory_space=pltpu.SMEM)
ROWS = 5
MOVING = 4
SPLITS = (44, 36)
SIZES = (160, 192, 224, 256)
KINDS = len(SIZES)
UNIT = 4
LOCAL_AT = 5 * KINDS
LOCAL_LEAD = 2
LOCAL_LIST = CELLS + 16
CROSS_AT = LOCAL_AT + 4 * LOCAL_LIST
CROSS_LEAD = 4
CROSS_LIST = LISTED + 16
PLAN = CROSS_AT + CROSS_LIST
PACK = 128
ANYWHERE = pl.BlockSpec(memory_space=pl.ANY)
OWN_ROWS = jax.ShapeDtypeStruct((2, (CELLS + 1) * CELL, 128), F32)


def params(mib=50):
    return pltpu.CompilerParams(vmem_limit_bytes=int(mib * 2**20))


def split2(x):
    a = x.astype(BF)
    return a, (x - a.astype(F32)).astype(BF)


def split3(x):
    a = x.astype(BF).astype(F32)
    rest = x - a
    b = rest.astype(BF).astype(F32)
    return a, b, rest - b


def pair_terms(x, y, z, h, m):
    norm = 4.0 * (x * x + y * y + z * z)
    root = lax.rsqrt(jnp.where(m > 0.0, m, 1.0))
    mu = jnp.where(m > 0.0, root * lax.rsqrt(root), EMPTY)
    one = jnp.ones_like(x)
    first = [-8.0 * x, -8.0 * y, -8.0 * z, norm, one, h * h * mu, 2.0 * h * mu, mu]
    second = [x, y, z, one, norm, mu, h * mu, h * h * mu]
    return first, second


def both(read):
    return jnp.concatenate([read(0), read(1)], -1)


def half(value, h):
    return value[..., 128 * h : 128 * (h + 1)]


def put(ref, planes, start, count, stride):
    for k, plane in enumerate(planes):
        for h in range(2):
            ref[h, pl.ds(start + k, count, stride=stride), :] = half(plane, h)


def planes_of(ref, ids, start, count, stride):
    return [both(lambda h: ref[h, pl.ds(start + k, count, stride=stride), :]) for k in ids]


def rows_at(index, size):
    return pl.ds(pl.multiple_of(index * size, size), size)


def block(ref, index, size):
    return both(lambda h: ref[h, rows_at(index, size), :])


def set_block(ref, index, size, value):
    for h in range(2):
        ref[h, rows_at(index, size), :] = half(value, h)


def add_block(ref, index, size, value):
    for h in range(2):
        ref[h, rows_at(index, size), :] += half(value, h)


def line(ref, index, size, k):
    return both(lambda h: ref[h, pl.ds(index * size + k, 1), :])


def listed_planes(listed, e, part, ids, size):
    step = SLOTS * size
    start = 8 * part * size
    return [
        both(lambda h: listed[e, pl.ds(h * step + start + k, 8, stride=size), :]) for k in ids
    ]


def listed_support(listed, slot):
    at = (slot & (SLOTS - 1)) * ROWS + 3
    return both(lambda h: listed[slot >> 4, pl.ds(h * SLOTS * ROWS + at, 1), :])


def first_operand(rows):
    a1, a2, a3 = split3(rows)
    return jnp.concatenate([a1, a1, a2, a2, a1, a3, jnp.zeros((80, WIDTH), F32)], 0).T.astype(BF)


def second_operands(rows, both):
    b1, b2, b3 = split3(rows)
    stacked = jnp.concatenate([b1, b2, b1, b2, b3, b1, jnp.zeros((80, WIDTH), F32)], 0)
    part = lax.broadcasted_iota(jnp.int32, stacked.shape, 0) % 8
    near = jnp.where(part < 5, stacked, 0.0).astype(BF)
    if not both:
        return near
    return near, jnp.where(part >= 5, stacked, 0.0).astype(BF)


def support_columns(row):
    return jnp.broadcast_to(row, (128, WIDTH)).T


def density_products(left, operands, s_ref, mix_ref):
    s_ref[...] = jnp.dot(left, operands[0], preferred_element_type=F32)
    mix_ref[...] = jnp.dot(left, operands[1], preferred_element_type=F32)


def weights_of(s, mix, columns, row):
    s = jnp.maximum(s, TINY)
    dist = s * lax.rsqrt(s)
    support = columns + row
    d = jnp.maximum(support - dist, 0.0)
    x = pl.reciprocal(mix, approx=True) * d
    x = x * x
    x = x * x
    return x * (support + 4.0 * dist)


def density_weights(count, s_ref, mix_ref, columns, row, one_sided):
    second = jnp.zeros((8, WIDTH), F32)
    firsts = []
    for start in range(0, count, CHUNK):
        part = slice(start, start + CHUNK)
        wide = columns[part]
        w = weights_of(s_ref[part], mix_ref[part], jnp.concatenate([wide, wide], 1), row)
        for k in range(CHUNK // 8):
            second = second + w[8 * k : 8 * k + 8]
        if not one_sided:
            firsts.append(w[:, :128] + w[:, 128:])
    if one_sided:
        return second
    if count < WIDTH:
        firsts.append(jnp.zeros((WIDTH - count, 128), F32))
    turned = jnp.concatenate(firsts, 0).T
    first = turned[:8]
    for k in range(1, 16):
        first = first + turned[8 * k : 8 * k + 8]
    return second, first


def inverse_mass(m):
    return jnp.where(m > 0.0, W_SCALE / jnp.where(m > 0.0, m, 1.0), 0.0)


def self_weights(count, s_ref, mix_ref, columns, row):
    sums = [jnp.zeros((8, 128), F32)] * 2
    crossing = []
    for start in range(0, count, CHUNK):
        part = slice(start, start + CHUNK)
        for h in range(0 if start < 128 else 1, 2):
            lanes = slice(128 * h, 128 * (h + 1))
            w = weights_of(s_ref[part, lanes], mix_ref[part, lanes], columns[part], half(row, h))
            for k in range(CHUNK // 8):
                sums[h] = sums[h] + w[8 * k : 8 * k + 8]
            if h and start < 128:
                crossing.append(w)
    turned = jnp.concatenate(crossing, 0).T
    for k in range(16):
        sums[0] = sums[0] + turned[8 * k : 8 * k + 8]
    return jnp.concatenate(sums, 1)


def fetch(pairs, sem):
    copies = [
        pltpu.make_async_copy(source, target, sem.at[k])
        for k, (source, target) in enumerate(pairs)
    ]
    for copy in copies:
        copy.start()
    return copies


def prepare_kernel(
    occ, pair, pos_in, vel_in, smooth_in, mass_in, own, out, pos, vel, smooth, mass, full, sem
):
    copies = fetch(
        [(pos_in, pos), (vel_in, vel), (smooth_in, smooth), (mass_in, mass)], sem
    )
    lane = lax.broadcasted_iota(jnp.int32, (1, WIDTH), 1)
    for c in range(CELLS):
        full[c : c + 1, :] = (lane < occ[c]).astype(F32)
    for copy in copies:
        copy.wait()
    place = [pos[k] - 0.5 for k in range(3)]
    m = jnp.where(full[...] > 0.0, mass[...], 0.0)
    put(own, place + [smooth[...], m] + [vel[k] for k in range(3)], 0, CELLS, CELL)
    blank = jnp.zeros((CELL, WIDTH), F32)
    wide = jnp.full((1, WIDTH), 0.5, F32)
    set_block(own, CELLS, CELL, jnp.concatenate([blank[:3], wide, blank[:4]], 0))

    def peer_step(e, _):
        for s in range(SLOTS):
            c = pair[e, s]
            for h in range(2):
                at = (h * SLOTS + s) * ROWS
                out[e, at : at + ROWS] = own[h, rows_at(c, CELL), :][:ROWS]
        return 0

    lax.fori_loop(0, PEERS, peer_step, 0)


def prepare(occ, pair, pos, vel, smooth, mass):
    plane = pltpu.VMEM((CELLS, WIDTH), F32)
    return pl.pallas_call(
        prepare_kernel,
        in_specs=[SM] * 2 + [ANYWHERE] * 4,
        out_specs=[VM] * 2,
        out_shape=[
            OWN_ROWS,
            jax.ShapeDtypeStruct((PEERS, 2 * SLOTS * ROWS, 128), F32),
        ],
        scratch_shapes=[
            pltpu.VMEM((3, CELLS, WIDTH), F32),
            pltpu.VMEM((3, CELLS, WIDTH), F32),
            plane,
            plane,
            plane,
            pltpu.SemaphoreType.DMA((4,)),
        ],
        compiler_params=params(60),
    )(occ, pair, pos, vel, smooth, mass)


def kind_of(size):
    return jnp.maximum(size - SIZES[0] + 31, 0) >> 5


def make_plan(occ, fill, cells, plan):
    def over_local(visit, group, carry):
        split = SPLITS[group // 2]
        low, high = (split, CELLS) if group % 2 else (0, split)
        step = lambda c, carry: visit(kind_of(occ[c]), c, carry)
        return lax.fori_loop(low, high, step, carry, unroll=4)

    def over_pairs(visit, carry):
        def peer_step(e, carry):
            def slot_step(s, carry):
                cell = cells[e, s]
                return visit(kind_of(occ[cell]), (e * SLOTS + s) * PACK + cell, carry)

            return lax.fori_loop(0, fill[0, e], slot_step, carry)

        return lax.fori_loop(0, PEERS, peer_step, carry)

    unused = jnp.int32(0)
    for e in range(PEERS):
        unused = jnp.where(fill[0, e] == 0, e * SLOTS, unused)

    def one_of(kind):
        return jnp.left_shift(jnp.int32(1), 8 * kind)

    groups = [
        (
            functools.partial(lambda g, v, x: over_local(v, g, x), g),
            LOCAL_AT + g * LOCAL_LIST, LOCAL_LEAD, 2, CELLS,
        )
        for g in range(4)
    ]
    groups.append((over_pairs, CROSS_AT, CROSS_LEAD, UNIT, unused * PACK + CELLS))
    for group, (walk, start, lead, unit, blank) in enumerate(groups):
        counts = walk(lambda kind, value, packed: packed + one_of(kind), jnp.int32(0))
        total = jnp.int32(0)
        done = jnp.int32(0)
        places = jnp.int32(0)
        for k in range(KINDS):
            places = places + jnp.left_shift(total, 8 * k)
            total = total + ((counts >> (8 * k)) & 255)
            upto = (total + (unit - 1 if k == KINDS - 1 else 0)) >> (unit.bit_length() - 1)
            plan[group * KINDS + k] = upto - done
            done = upto
        for k in range(lead):
            plan[start + k] = blank
        for k in range(unit + 5):
            plan[start + lead + total + k] = blank

        def place(kind, value, packed, start=start + lead):
            plan[start + ((packed >> (8 * kind)) & 255)] = value
            return packed + one_of(kind)

        walk(place, places)


def fold(total, own, out, carried):
    mine = sum(planes_of(total, range(CELL), 0, CELLS, CELL))
    mass = planes_of(own, [4], 0, CELLS, CELL)[0]
    mine = mine * inverse_mass(mass)
    out[...] = mine if carried is None else carried[...] + mine


def make_face_first(faces, face_first):
    planes = planes_of(faces, range(ROWS), 0, 2 * FACE, CELL)
    put(face_first, pair_terms(*planes)[0], 0, 2 * FACE, CELL)


def face_cell(n):
    return jnp.where(n < FACE, n, CELLS - 2 * FACE + n)


def in_turns(trips, sizes, item, products, weights, slot_a, slot_b):
    read, decode = item
    products(decode(read(0)), slot_a)
    base = 0
    held = tuple(read(n) for n in range(3))
    for count, size in zip(trips, sizes):

        def step(i, held, size=size):
            ahead = (read(2 * i + 3), read(2 * i + 4))
            now, then, after = [decode(entry) for entry in held]
            products(then, slot_b)
            weights(size, now, slot_a)
            products(after, slot_a)
            weights(size, then, slot_b)
            return held[2:] + ahead

        held = lax.fori_loop(base, base + count, step, held)
        base = base + count


def cell_list(plan, group):
    start = LOCAL_AT + group * LOCAL_LIST + LOCAL_LEAD
    trips = [plan[group * KINDS + k] for k in range(KINDS)]
    return trips, (lambda n: plan[start + n], lambda entry: entry)


def pair_list(plan):
    start = CROSS_AT + CROSS_LEAD

    def read(n):
        return tuple(plan[start + 2 * n + k] for k in range(2))

    def decode(entries):
        return [(entry >> 7, entry & (PACK - 1)) for entry in entries]

    return [plan[4 * KINDS + k] for k in range(KINDS)], (read, decode)


def face_list(n):
    return jnp.minimum(n, FACE - 1)


FACES = (face_list, lambda n: n)


def live_parts(fill, visit, other):
    def step(n, _):
        e, part = n >> 1, n & 1
        live = fill[0, e] > 8 * part

        @pl.when(live)
        def _():
            visit(e, part)

        if other is not None:

            @pl.when(jnp.logical_not(live))
            def _():
                other(e, part)

        return 0

    lax.fori_loop(0, 2 * PEERS, step, 0)


def local_density_kernel(part, *refs):
    if part:
        plan, own, first, second, faces, carried, rho, total, face_first, *slots = refs
    else:
        carried = None
        occ, fill, cells, own, rho, first, second, plan, total, *slots = refs
        make_plan(occ, fill, cells, plan)
        planes = planes_of(own, range(ROWS), 0, CELLS, CELL)
        blank = [jnp.zeros((1, WIDTH), F32)] * 3 + [jnp.full((1, WIDTH), 0.5, F32)]
        for ref, some, none in zip(
            (first, second), pair_terms(*planes), pair_terms(*blank, blank[0])
        ):
            put(ref, some, 0, CELLS, CELL)
            set_block(ref, CELLS, CELL, jnp.concatenate(none, 0))
    slot_a, slot_b = slots[:6], slots[6:]
    total[...] = jnp.zeros_like(total)

    def products(c, held):
        left = first_operand(block(first, c, CELL))
        after = jnp.minimum(c + 1, CELLS)
        held[4][...] = support_columns(line(own, c, CELL, 3))
        density_products(left, second_operands(block(second, c, CELL), True), *held[0:2])
        density_products(left, second_operands(block(second, after, CELL), True), *held[2:4])

    def weights(count, c, held):
        after = jnp.minimum(c + 1, CELLS)
        row, other = line(own, c, CELL, 3), line(own, after, CELL, 3)
        own_sum = self_weights(count, *held[0:2], held[4], row)
        there, here = density_weights(count, *held[2:4], held[4], other, False)
        add_block(total, c, CELL, own_sum + here)
        add_block(total, after, CELL, there)

    trips, item = cell_list(plan, part)
    in_turns(trips, SIZES, item, products, weights, slot_a, slot_b)

    if part:
        make_face_first(faces, face_first)

        def face_products(i, held):
            for k in range(2):
                n = 2 * i + k
                left = first_operand(block(face_first, n, CELL))
                operands = second_operands(block(second, face_cell(n), CELL), True)
                held[4 + k][...] = support_columns(line(faces, n, CELL, 3))
                density_products(left, operands, *held[2 * k : 2 * k + 2])

        def face_weights(size, i, held):
            for k in range(2):
                c = face_cell(2 * i + k)
                added = density_weights(
                    size, *held[2 * k : 2 * k + 2], held[4 + k], line(own, c, CELL, 3), True
                )
                add_block(total, c, CELL, added)

        in_turns(
            [FACE // 2], [WIDTH], FACES, face_products, face_weights, slot_a, slot_b
        )

    fold(total, own, rho, carried)


DENSITY_SLOT = [pltpu.VMEM((WIDTH, WIDTH), F32)] * 4 + [pltpu.VMEM((WIDTH, 128), F32)] * 2


def local_density(part, *operands):
    plane = jax.ShapeDtypeStruct((CELLS, WIDTH), F32)
    if part:
        in_specs, out_specs, out_shape = [SM] + [VM] * 5, VM, plane
    else:
        in_specs, out_specs = [SM] * 3 + [VM], [VM] * 3 + [SM]
        out_shape = [plane, OWN_ROWS, OWN_ROWS, jax.ShapeDtypeStruct((PLAN,), jnp.int32)]
    return pl.pallas_call(
        functools.partial(local_density_kernel, part),
        in_specs=in_specs,
        out_specs=out_specs,
        out_shape=out_shape,
        scratch_shapes=[pltpu.VMEM((2, (CELLS + 1) * CELL, 128), F32)]
        + [pltpu.VMEM((2, 2 * FACE * CELL, 128), F32)] * part
        + DENSITY_SLOT * 2,
        cost_estimate=pl.CostEstimate(
            flops=64 * 65536 * 60, bytes_accessed=2 * 2**20, transcendentals=0
        ),
        compiler_params=params(),
    )(*operands)


def live_rows(fill, e, part):
    row = lax.broadcasted_iota(jnp.int32, (8, WIDTH), 0)
    return row < fill[0, e] - 8 * part


def cross_density_kernel(
    fill, plan, own, first, listed, carried, rho, back, total, theirs, there_of, *slots
):
    slot_a, slot_b = slots[:6], slots[6:]
    total[...] = jnp.zeros_like(total)

    def make(e, part):
        after = pair_terms(*listed_planes(listed, e, part, range(ROWS), ROWS))[1]
        put(theirs, after, (e * SLOTS + 8 * part) * CELL, 8, CELL)

    live_parts(fill, make, None)

    def products(pairs, held):
        for k, (slot, c) in enumerate(pairs):
            left = first_operand(block(first, c, CELL))
            held[4 + k][...] = support_columns(line(own, c, CELL, 3))
            operands = second_operands(block(theirs, slot, CELL), True)
            density_products(left, operands, *held[2 * k : 2 * k + 2])

    def weights(count, pairs, held):
        for k, (slot, c) in enumerate(pairs):
            support = listed_support(listed, slot)
            there, here = density_weights(
                count, *held[2 * k : 2 * k + 2], held[4 + k], support, False
            )
            add_block(total, c, CELL, here)
            set_block(there_of, slot, CELL, there)

    trips, item = pair_list(plan)
    in_turns(trips, SIZES, item, products, weights, slot_a, slot_b)

    def send(e, part):
        start = (e * SLOTS + 8 * part) * CELL
        summed = sum(planes_of(there_of, range(CELL), start, 8, CELL))
        mass = listed_planes(listed, e, part, [4], ROWS)[0]
        value = jnp.where(live_rows(fill, e, part), summed * inverse_mass(mass), 0.0)
        back[e, rows_at(part, 8), :] = value

    def send_none(e, part):
        back[e, rows_at(part, 8), :] = jnp.zeros((8, WIDTH), F32)

    live_parts(fill, send, send_none)
    fold(total, own, rho, carried)


def cross_density(fill, plan, own, first, listed, carried):
    return pl.pallas_call(
        cross_density_kernel,
        in_specs=[SM, SM] + [VM] * 4,
        out_specs=[VM, VM],
        out_shape=[
            jax.ShapeDtypeStruct((CELLS, WIDTH), F32),
            jax.ShapeDtypeStruct((PEERS, SLOTS, WIDTH), F32),
        ],
        scratch_shapes=[
            pltpu.VMEM((2, (CELLS + 1) * CELL, 128), F32),
            pltpu.VMEM((2, LISTED * CELL, 128), F32),
            pltpu.VMEM((2, LISTED * CELL, 128), F32),
        ]
        + DENSITY_SLOT * 2,
        cost_estimate=pl.CostEstimate(
            flops=80 * 65536 * 60, bytes_accessed=2 * 2**20, transcendentals=0
        ),
        compiler_params=params(),
    )(fill, plan, own, first, listed, carried)


def pressure_kernel(
    pair, near, returned, energy_in, own, density, term, out, energy, moving, sem, *sums
):
    copies = fetch([(energy_in, energy)], sem)
    for ref in sums:
        ref[...] = jnp.zeros_like(ref)

    def peer_step(i, _):
        for s in range(SLOTS):
            for j in range(2):
                at = pl.ds(pair[2 * i + j, s], 1)
                row = returned[2 * i + j, s : s + 1]
                for h in range(2):
                    sums[2 * j + h][at, :] += half(row, h)
        return 0

    lax.fori_loop(0, PEERS // 2, peer_step, 0)
    copies[0].wait()
    sum_of = near[...] + both(lambda h: sums[h][...] + sums[2 + h][...])
    full = planes_of(own, [4], 0, CELLS, CELL)[0] > 0.0
    rho = jnp.where(full, sum_of, 0.0)
    density[...] = rho
    term[...] = jnp.where(full, GAMMA_LESS * energy[...] / jnp.where(full, rho, 1.0), 0.0)

    put(moving, planes_of(own, (5, 6, 7), 0, CELLS, CELL) + [term[...]], 0, CELLS, CELL)

    def send_step(e, _):
        for s in range(SLOTS):
            cell = pl.ds(pl.multiple_of(pair[e, s] * CELL, CELL), MOVING)
            for h in range(2):
                at = (h * SLOTS + s) * MOVING
                out[e, at : at + MOVING] = moving[h, cell, :]
        return 0

    lax.fori_loop(0, PEERS, send_step, 0)


def pressure(pair, near, returned, energy, own):
    plane = jax.ShapeDtypeStruct((CELLS, WIDTH), F32)
    return pl.pallas_call(
        pressure_kernel,
        in_specs=[SM, VM, VM, ANYWHERE, VM],
        out_specs=[VM, VM, VM],
        out_shape=[
            plane,
            plane,
            jax.ShapeDtypeStruct((PEERS, 2 * SLOTS * MOVING, 128), F32),
        ],
        scratch_shapes=[
            pltpu.VMEM((CELLS, WIDTH), F32),
            pltpu.VMEM((2, CELLS * CELL, 128), F32),
            pltpu.SemaphoreType.DMA((1,)),
        ]
        + [pltpu.VMEM((CELLS, 128), F32)] * 4,
        compiler_params=params(),
    )(pair, near, returned, energy, own)


def force_terms(place, m, speed, term):
    mp = m * term
    turned = sum(a * b for a, b in zip(place, speed))
    return (
        [m] + [m * a for a in place] + [mp] + [mp * a for a in place]
        + [m * a for a in speed] + [m * turned]
    )


def forces_of(sums, place, speed, term):
    lean = [a * sums[0] - b for a, b in zip(place, sums[1:4])]
    acc = [term * a + (b * sums[4] - c) for a, b, c in zip(lean, place, sums[5:8])]
    mixed = sum(a * b - c * d for a, b, c, d in zip(speed, lean, place, sums[8:11]))
    return [G_SCALE * a for a in acc] + [-G_SCALE * term * (mixed + sums[11])]


def force_operand(ref, index):
    high, low = split2(block(ref, index, SUMS))
    return jnp.concatenate([high, low], 0)


def own_terms(own, term, rows):
    planes = planes_of(own, range(CELL), 0, CELLS, CELL)
    terms = force_terms(planes[0:3], planes[4], planes[5:8], term[...])
    put(rows, terms, 0, CELLS, SUMS)
    put(rows, [jnp.zeros((CELLS, WIDTH), F32)] * 4, 12, CELLS, SUMS)
    set_block(rows, CELLS, SUMS, jnp.zeros((SUMS, WIDTH), F32))


def slopes(s_ref, high, low, columns, row, count):
    for start in range(0, count, CHUNK):
        s = jnp.maximum(s_ref[start : start + CHUNK], TINY)
        dist = s * lax.rsqrt(s)
        wide = columns[start : start + CHUNK]
        support = jnp.concatenate([wide, wide], 1) + row
        d = jnp.maximum(support - dist, 0.0)
        e = pl.reciprocal(support * support, approx=True)
        x = e * d
        g = (x * x) * (x * e)
        top = g.astype(BF)
        high[start : start + CHUNK] = top
        low[start : start + CHUNK] = (g - top.astype(F32)).astype(BF)


def distances(left, rows, s_ref):
    s_ref[...] = jnp.dot(left, second_operands(rows, False), preferred_element_type=F32)


def slope_sums(rows, high, low, dims):
    top = lax.dot_general(rows, high, dims, preferred_element_type=F32)
    rest = lax.dot_general(rows[:SUMS], low, dims, preferred_element_type=F32)
    return top[:SUMS] + top[SUMS:] + rest


def to_seconds(rows, count, high, low):
    return slope_sums(rows[:, :count], high[0:count], low[0:count], NN)


def to_firsts(rows, count, high, low):
    return slope_sums(rows, high[0:count], low[0:count], NT)


def in_three_turns(trips, sizes, item, products, tiles, sums, slot_a, slot_b, lag):
    read, decode = item
    products(decode(read(0)), slot_a)
    base = 0
    held = tuple(read(n) for n in range(-2, 3))
    for count, size in zip(trips, sizes):

        def step(i, held, size=size):
            ahead = (read(2 * i + 3), read(2 * i + 4))
            before, last, now, then, after = [decode(entry) for entry in held]
            if lag == 1:
                sums(size, last, slot_b)
                tiles(size, now, slot_a)
                products(then, slot_b)
                sums(size, now, slot_a)
                tiles(size, then, slot_b)
                products(after, slot_a)
            else:
                products(then, slot_b)
                sums(size, before, slot_a)
                tiles(size, now, slot_a)
                products(after, slot_a)
                sums(size, last, slot_b)
                tiles(size, then, slot_b)
            return held[2:] + ahead

        held = lax.fori_loop(base, base + count, step, held)
        base = base + count
    if lag == 2:
        sums(sizes[-1], decode(held[0]), slot_a)
    sums(sizes[-1], decode(held[1]), slot_b)


def clear(slots):
    for held in slots:
        held[SIZES[0] :, :] = jnp.zeros((WIDTH - SIZES[0], WIDTH), BF)


def add_forces(total, own, term, out, carried):
    planes = planes_of(own, range(CELL), 0, CELLS, CELL)
    sums = planes_of(total, range(12), 0, CELLS, SUMS)
    for k, force in enumerate(forces_of(sums, planes[0:3], planes[5:8], term[...])):
        out[k] = force if carried is None else carried[k] + force


def local_force_kernel(part, plan, own, first, second, term, *rest):
    if part:
        faces, face_terms, carried, out, rows, total, face_rows, face_first, *slots = rest
    else:
        carried = None
        out, rows, total, *slots = rest
    slot_a, slot_b = slots[:7], slots[7:]
    own_terms(own, term, rows)
    total[...] = jnp.zeros_like(total)
    clear([held[k] for held in (slot_a, slot_b) for k in (2, 3, 5, 6)])

    def products(c, held):
        left = first_operand(block(first, c, CELL))
        held[0][...] = support_columns(line(own, c, CELL, 3))
        distances(left, block(second, c, CELL), held[1])
        distances(left, block(second, jnp.minimum(c + 1, CELLS), CELL), held[4])

    def tiles(count, c, held):
        other = line(own, jnp.minimum(c + 1, CELLS), CELL, 3)
        slopes(*held[1:4], held[0], line(own, c, CELL, 3), count)
        slopes(*held[4:7], held[0], other, count)

    def sums(count, c, held):
        after = jnp.minimum(c + 1, CELLS)
        mine, other = force_operand(rows, c), force_operand(rows, after)
        added = to_firsts(other, count, *held[5:7])
        if count < WIDTH:
            added = jnp.concatenate([added, jnp.zeros((SUMS, WIDTH - count), F32)], 1)
        add_block(total, c, SUMS, to_seconds(mine, count, *held[2:4]) + added)
        add_block(total, after, SUMS, to_seconds(mine, count, *held[5:7]))

    trips, item = cell_list(plan, 2 + part)
    in_three_turns(trips, SIZES, item, products, tiles, sums, slot_a, slot_b, 1)

    if part:
        make_face_first(faces, face_first)
        planes = planes_of(faces, range(CELL), 0, 2 * FACE, CELL)
        terms = force_terms(planes[0:3], planes[4], planes[5:8], face_terms[...])
        blank = jnp.zeros((2 * FACE, WIDTH), F32)
        put(face_rows, terms + [blank] * 4, 0, 2 * FACE, SUMS)

        def face_products(i, held):
            for k in range(2):
                n = 2 * i + k
                left = first_operand(block(face_first, n, CELL))
                distances(left, block(second, face_cell(n), CELL), held[1 + 3 * k])

        def face_tiles(size, i, held):
            for k in range(2):
                n = 2 * i + k
                columns = support_columns(line(faces, n, CELL, 3))
                slopes(
                    *held[1 + 3 * k : 4 + 3 * k], columns, line(own, face_cell(n), CELL, 3), size
                )

        def face_sums(size, i, held):
            for k in range(2):
                n = jnp.maximum(2 * i, 0) + k
                c = jnp.where(i < 0, CELLS, face_cell(n))
                theirs = force_operand(face_rows, n)
                add_block(
                    total, c, SUMS, to_seconds(theirs, size, *held[2 + 3 * k : 4 + 3 * k])
                )

        in_three_turns(
            [FACE // 2], [WIDTH], FACES, face_products, face_tiles, face_sums,
            slot_a, slot_b, 1,
        )

    add_forces(total, own, term, out, carried)


FORCE_PAIR = [
    pltpu.VMEM((WIDTH, WIDTH), F32),
    pltpu.VMEM((WIDTH, WIDTH), BF),
    pltpu.VMEM((WIDTH, WIDTH), BF),
]
FORCE_SLOT = [pltpu.VMEM((WIDTH, 128), F32)] + FORCE_PAIR * 2


def local_force(part, plan, own, first, second, term, *rest):
    scratch = [
        pltpu.VMEM((2, (CELLS + 1) * SUMS, 128), F32),
        pltpu.VMEM((2, (CELLS + 1) * SUMS, 128), F32),
    ]
    if part:
        scratch.append(pltpu.VMEM((2, 2 * FACE * SUMS, 128), F32))
        scratch.append(pltpu.VMEM((2, 2 * FACE * CELL, 128), F32))
    return pl.pallas_call(
        functools.partial(local_force_kernel, part),
        in_specs=[SM] + [VM] * (4 + len(rest)),
        out_specs=VM,
        out_shape=jax.ShapeDtypeStruct((4, CELLS, WIDTH), F32),
        scratch_shapes=scratch + FORCE_SLOT * 2,
        cost_estimate=pl.CostEstimate(
            flops=64 * 65536 * 80, bytes_accessed=2 * 2**20, transcendentals=0
        ),
        compiler_params=params(),
    )(plan, own, first, second, term, *rest)


def cross_force_kernel(
    fill, plan, own, first, term, listed, arrived, carried, _, out, back,
    rows, total, theirs, their_rows, sums_of, *slots
):
    slot_a, slot_b = slots[:8], slots[8:]
    own_terms(own, term, rows)
    total[...] = jnp.zeros_like(total)
    clear([held[k] for held in (slot_a, slot_b) for k in (3, 4, 6, 7)])

    def make(e, part):
        planes = listed_planes(listed, e, part, range(ROWS), ROWS)
        at = e * SLOTS + 8 * part
        put(theirs, pair_terms(*planes)[1], at * CELL, 8, CELL)
        *speed, pressed = listed_planes(arrived, e, part, range(MOVING), MOVING)
        terms = force_terms(planes[0:3], planes[4], speed, pressed)
        blank = jnp.zeros((8, WIDTH), F32)
        put(their_rows, terms + [blank] * 4, at * SUMS, 8, SUMS)

    live_parts(fill, make, None)

    def products(pairs, held):
        for k, (slot, c) in enumerate(pairs):
            held[k][...] = support_columns(line(own, c, CELL, 3))
            left = first_operand(block(first, c, CELL))
            distances(left, block(theirs, slot, CELL), held[2 + 3 * k])

    def tiles(count, pairs, held):
        for k, (slot, c) in enumerate(pairs):
            support = listed_support(listed, slot)
            slopes(*held[2 + 3 * k : 5 + 3 * k], held[k], support, count)

    def sums(count, pairs, held):
        for k, (slot, c) in enumerate(pairs):
            tile = held[3 + 3 * k : 5 + 3 * k]
            set_block(sums_of, slot, SUMS, to_seconds(force_operand(rows, c), count, *tile))
            added = to_firsts(force_operand(their_rows, slot), count, *tile)
            if count < WIDTH:
                added = jnp.concatenate([added, jnp.zeros((SUMS, WIDTH - count), F32)], 1)
            add_block(total, c, SUMS, added)

    trips, item = pair_list(plan)
    in_three_turns(trips, SIZES, item, products, tiles, sums, slot_a, slot_b, 2)

    def send(e, part):
        planes = listed_planes(listed, e, part, range(3), ROWS)
        *speed, pressed = listed_planes(arrived, e, part, range(MOVING), MOVING)
        summed = planes_of(sums_of, range(12), (e * SLOTS + 8 * part) * SUMS, 8, SUMS)
        live = live_rows(fill, e, part)
        send_rows(e, part, [jnp.where(live, f, 0.0) for f in forces_of(summed, planes, speed, pressed)])

    def send_none(e, part):
        send_rows(e, part, [jnp.zeros((8, WIDTH), F32)] * MOVING)

    def send_rows(e, part, forces):
        for k, force in enumerate(forces):
            for h in range(2):
                start = (h * SLOTS + 8 * part) * MOVING + k
                back[e, pl.ds(start, 8, stride=MOVING), :] = half(force, h)

    live_parts(fill, send, send_none)
    add_forces(total, own, term, out, carried)


def cross_force(fill, plan, own, first, term, listed, arrived, carried, after):
    return pl.pallas_call(
        cross_force_kernel,
        in_specs=[SM, SM] + [VM] * 6 + [ANYWHERE],
        out_specs=[VM, VM],
        out_shape=[
            jax.ShapeDtypeStruct((4, CELLS, WIDTH), F32),
            jax.ShapeDtypeStruct((PEERS, 2 * SLOTS * MOVING, 128), F32),
        ],
        scratch_shapes=[
            pltpu.VMEM((2, (CELLS + 1) * SUMS, 128), F32),
            pltpu.VMEM((2, (CELLS + 1) * SUMS, 128), F32),
            pltpu.VMEM((2, LISTED * CELL, 128), F32),
            pltpu.VMEM((2, LISTED * SUMS, 128), F32),
            pltpu.VMEM((2, LISTED * SUMS, 128), F32),
        ]
        + (FORCE_SLOT[:1] * 2 + FORCE_PAIR * 2) * 2,
        cost_estimate=pl.CostEstimate(
            flops=80 * 65536 * 80, bytes_accessed=2 * 2**20, transcendentals=0
        ),
        compiler_params=params(),
    )(fill, plan, own, first, term, listed, arrived, carried, after)


def finish_kernel(pair, near, returned, active_in, own, out, active, sem, *sums):
    copies = fetch([(active_in, active)], sem)
    for ref in sums:
        ref[...] = jnp.zeros_like(ref)

    def peer_step(i, _):
        for s in range(SLOTS):
            for j in range(2):
                cell = pl.ds(pl.multiple_of(pair[2 * i + j, s] * CELL, CELL), MOVING)
                for h in range(2):
                    at = (h * SLOTS + s) * MOVING
                    sums[2 * j + h][cell, :] += returned[2 * i + j, at : at + MOVING]
        return 0

    lax.fori_loop(0, PEERS // 2, peer_step, 0)
    copies[0].wait()
    full = planes_of(own, [4], 0, CELLS, CELL)[0] > 0.0
    gate = jnp.where(full, active[...].astype(F32), 0.0)
    for k in range(4):
        at = pl.ds(k, CELLS, stride=CELL)
        total = both(lambda h: sums[h][at, :] + sums[2 + h][at, :])
        out[k] = (near[k] + total) * gate


def finish(pair, near, returned, active, own):
    return pl.pallas_call(
        finish_kernel,
        in_specs=[SM, VM, VM, ANYWHERE, VM],
        out_specs=VM,
        out_shape=jax.ShapeDtypeStruct((4, CELLS, WIDTH), F32),
        scratch_shapes=[
            pltpu.VMEM((CELLS, WIDTH), jnp.int32),
            pltpu.SemaphoreType.DMA((1,)),
        ]
        + [pltpu.VMEM((CELLS * CELL, 128), F32)] * 4,
        compiler_params=params(),
    )(pair, near, returned, active, own)


def to_peers(block):
    return lax.all_to_all(block, "dev", split_axis=0, concat_axis=0, tiled=True)


def with_neighbours(rows, size):
    count = lax.axis_size("region")
    up = [(i, (i + 1) % count) for i in range(count)]
    down = [(i, (i - 1) % count) for i in range(count)]
    return jnp.concatenate(
        [
            lax.ppermute(rows[..., (CELLS - FACE) * size : CELLS * size, :], "region", up),
            lax.ppermute(rows[..., : FACE * size, :], "region", down),
        ],
        -2,
    )


def local(
    positions, velocity, smoothing, masses, energy, occupancy, active, send_cells, send_fill,
    pair_cell,
):
    pair = pair_cell[0]
    own, listed = prepare(occupancy, pair, positions, velocity, smoothing, masses)
    arrived = to_peers(listed)
    faces = with_neighbours(own, CELL)
    rho, first, second, plan = local_density(0, occupancy, send_fill, send_cells[0], own)
    rho, back = cross_density(send_fill, plan, own, first, arrived, rho)
    returned = to_peers(back)
    rho = local_density(1, plan, own, first, second, faces, rho)
    density, term, leaving = pressure(pair, rho, returned, energy, own)
    arrived_moving = to_peers(leaving)
    face_terms = with_neighbours(term, 1)
    sums = local_force(0, plan, own, first, second, term)
    sums, force_back = cross_force(
        send_fill, plan, own, first, term, arrived, arrived_moving, sums, face_terms
    )
    returned_force = to_peers(force_back)
    sums = local_force(1, plan, own, first, second, term, faces, face_terms, sums)
    forces = finish(pair, sums, returned_force, active, own)
    return (density, forces)


def solution(mesh):
    cells = P(("region", "dev"), None)
    vectors = P(None, ("region", "dev"), None)
    lists = P(("region", "dev"), None, None)
    in_specs = (
        vectors, vectors, cells, cells, cells, P(("region", "dev")), cells, lists, cells, lists,
    )
    return jax.shard_map(
        local, mesh=mesh, in_specs=in_specs, out_specs=(cells, vectors), check_vma=False
    )
```
